32 devices in a mesh: section: 2 (over core), batch: 16 (over z, y, x).
Axes of the slice: x: 2, y: 2, z: 4, core: 2. Of those that a mesh axis runs over, the one named last changes fastest.
Arguments:
- x_query: bfloat16 [128, 32, 768], P('batch'), may hold values from -6 to 6
- x_passage: bfloat16 [32, 256, 768], P('batch'), may hold values from -6 to 6
- len_query: int32 [128], P('batch'), may hold values from 16 to 32, as said below
- len_passage: int32 [32], P('batch'), may hold values from 33 to 256, as said below
- positive: int32 [128], P('batch'), may hold values from 0 to 31
- cot_query: bfloat16 [128, 32, 768], P('batch'), may hold values from -6 to 6
- cot_passage: bfloat16 [32, 256, 768], P('batch'), may hold values from -6 to 6
- w_qkv: bfloat16 [2, 768, 2304], P('section'), may hold values from -0.21875 to 0.21875
- b_qv: float32 [2, 1536], P('section'), may hold values from -3 to 3
- w_o: bfloat16 [2, 768, 768], P('section'), may hold values from -1.75 to 1.75
- b_o: float32 [2, 768], P('section'), may hold values from -3 to 3
- g_attn: float32 [2, 768], P('section'), may hold values from 0.5 to 1.5
- c_attn: float32 [2, 768], P('section'), may hold values from -2 to 2
- w_in: bfloat16 [2, 768, 3072], P('section'), may hold values from -0.21875 to 0.21875
- b_in: float32 [2, 3072], P('section'), may hold values from -3 to 3
- w_out: bfloat16 [2, 3072, 768], P('section'), may hold values from -0.109375 to 0.109375
- b_out: float32 [2, 768], P('section'), may hold values from -3 to 3
- g_ffn: float32 [2, 768], P('section'), may hold values from 0.5 to 1.5
- c_ffn: float32 [2, 768], P('section'), may hold values from -2 to 2
Outputs:
- hidden_query: bfloat16 [2, 128, 32, 768], P('section', 'batch')
- hidden_passage: bfloat16 [2, 32, 256, 768], P('section', 'batch')
- grad_query: float32 [2, 128, 32, 768], P('section', 'batch')
- grad_passage: float32 [2, 32, 256, 768], P('section', 'batch')
- loss_value: float32 [], replicated
- d_w_qkv: float32 [2, 768, 2304], P('section', 'batch')
- d_b_qv: float32 [2, 1536], P('section', 'batch')
- d_w_o: float32 [2, 768, 768], P('section', 'batch')
- d_b_o: float32 [2, 768], P('section', 'batch')
- d_g_attn: float32 [2, 768], P('section', 'batch')
- d_c_attn: float32 [2, 768], P('section', 'batch')
- d_w_in: float32 [2, 768, 3072], P('section', 'batch')
- d_b_in: float32 [2, 3072], P('section', 'batch')
- d_w_out: float32 [2, 3072, 768], P('section', 'batch')
- d_b_out: float32 [2, 768], P('section', 'batch')
- d_g_ffn: float32 [2, 768], P('section', 'batch')
- d_c_ffn: float32 [2, 768], P('section', 'batch')
The draws below stay inside these ranges and needn't reach their ends.
Inputs may be any that keep to these rules, and one draw needn't show every extreme that they name: `len_query`: valid tokens of each query, from the start of its 32 slots; some query has exactly 32. `len_passage`: valid tokens of each passage, from the start of its 256 slots; most are short, some fill all 256; some passage has exactly 256.
All inputs are finite; a program needn't handle non-finite values.
Results may differ from the reference program's by a relative error of at most 0.028.
Values may be sent and summed in bfloat16 or wider, within the bound.
A program may use at most 256 MiB of HBM per device.

```python
import math
import jax
import jax.numpy as jnp
from jax import lax

D = 768
HEADS = 12
HD = 64
FF = 3072
QLEN = 32
PLEN = 256
QUERIES = 128
PASSAGES = 32


def draw_len_query(key, part):
    key = jax.random.fold_in(key, 11)
    key_one, key_two = jax.random.split(key)
    lengths = jax.random.randint(key_one, (QUERIES,), QLEN // 2, QLEN + 1)
    chosen = jax.random.randint(key_two, (), 0, QUERIES)
    return jnp.where(jnp.arange(QUERIES) == chosen, QLEN, lengths).astype(jnp.int32)


def draw_len_passage(key, part):
    key = jax.random.fold_in(key, 23)
    key_one, key_two, key_three, key_four = jax.random.split(key, 4)
    long_bucket = jax.random.randint(key_one, (PASSAGES,), 0, 1248) < 224
    short_lengths = jax.random.randint(key_two, (PASSAGES,), PLEN // 8 + 1, PLEN // 4 + 1)
    long_lengths = jax.random.randint(key_three, (PASSAGES,), PLEN // 2 + 1, PLEN + 1)
    chosen = jax.random.randint(key_four, (), 0, PASSAGES)
    lengths = jnp.where(long_bucket, long_lengths, short_lengths)
    return jnp.where(jnp.arange(PASSAGES) == chosen, PLEN, lengths).astype(jnp.int32)


def plant(entries, own_key, smallest, top_value):
    spot = [jax.random.randint(jax.random.fold_in(own_key, axis), (), 0, length) for axis, length in enumerate(entries.shape)]
    widest = entries.shape.index(max(entries.shape))
    next_to = spot[:widest] + [(spot[widest] + 1) % entries.shape[widest]] + spot[widest + 1:]
    return entries.at[tuple(spot)].set(smallest).at[tuple(next_to)].set(top_value)


def levels(rng, extent, cuts, smallest, top_value):
    gain, own = 1.0, jax.random.fold_in(rng, 6)
    for dim, parts in cuts:
        steps = jnp.exp(jax.random.uniform(jax.random.fold_in(own, dim), (parts,), jnp.float32, smallest / len(cuts), top_value / len(cuts)))
        gain = gain * jnp.repeat(steps, extent[dim] // parts).reshape([-1 if axis == dim else 1 for axis in range(len(extent))])
    return gain


def scatter_about(key, extent, scale, bound, shards=(), kind=jnp.bfloat16):
    values = jax.random.normal(key, extent, jnp.float32) * scale
    if len(shards) > 0:
        values = levels(key, extent, shards, -0.22, 0.18) * values
    return jnp.clip(values, min=-bound, max=bound).astype(kind)


def setup_inputs(seed: int = 0) -> dict:
    keys = jax.random.split(jax.random.key(seed), 20)
    return {
        "x_query": scatter_about(keys[0], (QUERIES, QLEN, D), 1.0, 6.0, ((0, 16),)),
        "x_passage": scatter_about(keys[1], (PASSAGES, PLEN, D), 1.0, 6.0, ((0, 16),)),
        "len_query": draw_len_query(jax.random.fold_in(keys[19], 71), 0),
        "len_passage": draw_len_passage(jax.random.fold_in(keys[19], 71), 0),
        "positive": plant(jax.random.randint(keys[4], (QUERIES,), 0, PASSAGES), jax.random.fold_in(keys[4], 1), 0, PASSAGES - 1).astype(jnp.int32),
        "cot_query": scatter_about(keys[5], (QUERIES, QLEN, D), 1.0, 6.0, ((0, 16),)),
        "cot_passage": scatter_about(keys[6], (PASSAGES, PLEN, D), 1.0, 6.0, ((0, 16),)),
        "w_qkv": scatter_about(keys[7], (2, D, 3 * D), D ** -0.5, 0.21875, ((0, 2),)),
        "b_qv": scatter_about(keys[8], (2, 2 * D), 0.5, 3.0, ((0, 2),), jnp.float32),
        "w_o": scatter_about(keys[9], (2, D, D), (D // 64) ** -0.5, 1.75, ((0, 2),)),
        "b_o": scatter_about(keys[10], (2, D), 0.5, 3.0, ((0, 2),), jnp.float32),
        "g_attn": jnp.clip(1.0 + 0.1 * jax.random.normal(keys[11], (2, D), jnp.float32), 0.5, 1.5),
        "c_attn": scatter_about(keys[12], (2, D), 0.3, 2.0, ((0, 2),), jnp.float32),
        "w_in": scatter_about(keys[13], (2, D, FF), D ** -0.5, 0.21875, ((0, 2),)),
        "b_in": scatter_about(keys[14], (2, FF), 0.5, 3.0, ((0, 2),), jnp.float32),
        "w_out": scatter_about(keys[15], (2, FF, D), FF ** -0.5, 0.109375, ((0, 2),)),
        "b_out": scatter_about(keys[16], (2, D), 0.5, 3.0, ((0, 2),), jnp.float32),
        "g_ffn": jnp.clip(1.0 + 0.1 * jax.random.normal(keys[17], (2, D), jnp.float32), 0.5, 1.5),
        "c_ffn": scatter_about(keys[18], (2, D), 0.3, 2.0, ((0, 2),), jnp.float32),
    }


highest = lax.Precision.HIGHEST
norm_eps = 1e-05

@jax.custom_vjp
def low(v):
    return lax.optimization_barrier(v.astype(jnp.bfloat16)).astype(jnp.float32)

@jax.custom_vjp
def low_back(v):
    return v

def low_keep(v):
    return (low(v), None)

def low_pass(kept, grad):
    return (grad,)

def back_keep(v):
    return (v, None)

def back_low(kept, grad):
    return (low(grad),)
low.defvjp(low_keep, low_pass)
low_back.defvjp(back_keep, back_low)

def product(left, right):
    return jnp.dot(left, right, precision=highest)

def normalize(inputs, gain_vec, shift_vec):
    mean_val = lax.optimization_barrier(jnp.mean(inputs, -1, keepdims=True))
    centred = inputs - mean_val
    spread = lax.optimization_barrier(jnp.mean(centred * centred, -1, keepdims=True))
    return centred * lax.rsqrt(spread + norm_eps) * gain_vec + shift_vec

def exact_gelu(inputs):
    return jax.nn.gelu(inputs, approximate=False)

def one_sequence(packed):
    queries, key_rows, values, length = packed
    scores = low_back(jnp.einsum('qhd,khd->hqk', queries, key_rows, precision=highest) * HD ** (-0.5))
    valid_mask = jnp.arange(queries.shape[0]) < length
    scores = jnp.where(valid_mask[None, None, :], scores, -1000000000.0)
    top_score = lax.optimization_barrier(jnp.max(scores, -1, keepdims=True))
    weights = jnp.exp(scores - top_score)
    probs_low = low(weights / lax.optimization_barrier(jnp.sum(weights, -1, keepdims=True)))
    mixed = jnp.einsum('hqk,khd->qhd', probs_low, values, precision=highest)
    return mixed.reshape(queries.shape[0], HEADS * HD)

def group_attend(queries, key_rows, values, lengths, length):
    seq_count = lengths.shape[0]
    shaped = tuple((member.reshape(seq_count, length, HEADS, HD) for member in (queries, key_rows, values)))
    mixed = lax.map(jax.checkpoint(one_sequence), shaped + (lengths,))
    return mixed.reshape(seq_count * length, HEADS * HD)

def layer(token_rows, query_lens, passage_lens, params):
    w_qkv, b_qv, w_o, b_o, g_attn, c_attn, w_in, b_in, w_out, b_out, g_ffn, c_ffn = params
    projected = product(token_rows, w_qkv)
    queries = low(low_back(projected[:, :D] + b_qv[:D]))
    key_rows = low(low_back(projected[:, D:2 * D]))
    values = low(low_back(projected[:, 2 * D:] + b_qv[D:]))
    query_rows = query_lens.shape[0] * QLEN
    mixed = jnp.concatenate([group_attend(queries[:query_rows], key_rows[:query_rows], values[:query_rows], query_lens, QLEN), group_attend(queries[query_rows:], key_rows[query_rows:], values[query_rows:], passage_lens, PLEN)], 0)
    mixed = low(low_back(mixed))
    pre_attn = token_rows + low_back(product(mixed, w_o)) + b_o
    normed = normalize(pre_attn, g_attn, c_attn)
    up_proj = low_back(product(low(normed), w_in) + b_in)
    act_low = low(exact_gelu(up_proj))
    pre_ffn = normed + low_back(product(act_low, w_out)) + b_out
    return normalize(pre_ffn, g_ffn, c_ffn)

def reference(x_query, x_passage, len_query, len_passage, positive, cot_query, cot_passage, w_qkv, b_qv, w_o, b_o, g_attn, c_attn, w_in, b_in, w_out, b_out, g_ffn, c_ffn):
    weights = tuple((member.astype(jnp.float32) for member in (w_qkv, b_qv, w_o, b_o, g_attn, c_attn, w_in, b_in, w_out, b_out, g_ffn, c_ffn)))
    query_rows = QUERIES * QLEN
    token_rows = jnp.concatenate([x_query.astype(jnp.float32).reshape(-1, D), x_passage.astype(jnp.float32).reshape(-1, D)], 0)
    mask_query = jnp.arange(QLEN)[None, :] < len_query[:, None]
    mask_passage = jnp.arange(PLEN)[None, :] < len_passage[:, None]
    cot_rows = jnp.concatenate([jnp.where(mask_query[:, :, None], cot_query.astype(jnp.float32), 0.0).reshape(-1, D), jnp.where(mask_passage[:, :, None], cot_passage.astype(jnp.float32), 0.0).reshape(-1, D)], 0)
    chosen = positive[:, None] == jnp.arange(PASSAGES)[None, :]
    score_scale = 2.0 / math.sqrt(D)

    def forward(rows_zero, shift_rows, params):
        first_params = tuple((member[0] for member in params))
        second_params = tuple((member[1] for member in params))
        first_out = layer(rows_zero, len_query, len_passage, first_params)
        rows_one = low(low_back(first_out)) + shift_rows
        second_out = layer(rows_one, len_query, len_passage, second_params)
        cls_query = low(second_out[:query_rows].reshape(QUERIES, QLEN, D)[:, 0])
        cls_passage = low(second_out[query_rows:].reshape(PASSAGES, PLEN, D)[:, 0])
        logits = low_back(product(cls_query, cls_passage.T) * score_scale)
        top_score = lax.optimization_barrier(jnp.max(logits, -1, keepdims=True))
        log_total = top_score[:, 0] + jnp.log(lax.optimization_barrier(jnp.sum(jnp.exp(logits - top_score), -1)))
        term_values = log_total - lax.optimization_barrier(jnp.sum(jnp.where(chosen, logits, 0.0), -1))
        objective = jnp.sum(second_out * cot_rows) + jnp.sum(term_values)
        return (objective, (first_out, second_out, jnp.mean(term_values)))
    objective, back_fn, extra = jax.vjp(forward, token_rows, jnp.zeros_like(token_rows), weights, has_aux=True)
    grad_rows, grad_shift, grad_weights = back_fn(jnp.ones_like(objective))
    first_out, second_out, loss_value = extra

    def split_query(array):
        return array[:query_rows].reshape(QUERIES, QLEN, D)

    def split_passage(array):
        return array[query_rows:].reshape(PASSAGES, PLEN, D)
    hidden_query = jnp.stack([split_query(first_out), split_query(second_out)]).astype(jnp.bfloat16)
    hidden_passage = jnp.stack([split_passage(first_out), split_passage(second_out)]).astype(jnp.bfloat16)
    grad_query = jnp.stack([split_query(grad_rows), split_query(grad_shift)])
    grad_passage = jnp.stack([split_passage(grad_rows), split_passage(grad_shift)])
    return (hidden_query, hidden_passage, grad_query, grad_passage, loss_value, grad_weights[0], grad_weights[1], grad_weights[2], grad_weights[3], grad_weights[4], grad_weights[5], grad_weights[6], grad_weights[7], grad_weights[8], grad_weights[9], grad_weights[10], grad_weights[11])
```

```python
import functools
import math

import jax
import jax.numpy as jnp
from jax import lax
from jax.experimental import pallas as pl
from jax.experimental.pallas import tpu as pltpu
from jax.sharding import PartitionSpec as P

HEADS = 12
QLEN = 32
PLEN = 256


norm_eps = 1e-05


def normalize(inputs, gain_vec, shift_vec):
    mean_val = jnp.mean(inputs, -1, keepdims=True)
    centred = inputs - mean_val
    spread = jnp.mean(centred * centred, -1, keepdims=True)
    return centred * lax.rsqrt(spread + norm_eps) * gain_vec + shift_vec


def exact_gelu(inputs):
    return jax.nn.gelu(inputs, approximate=False)


def head_split(rows, seq_count, length):
    return rows.reshape(seq_count, length, HEADS, rows.shape[1] // HEADS)


def masked_scores(q_heads, k_heads, lengths, length):
    head_size = q_heads.shape[3]
    scores = jnp.einsum(
        "sqhd,skhd->shqk", q_heads, k_heads, preferred_element_type=jnp.float32
    ) * head_size ** (-0.5)
    valid_mask = jnp.arange(length)[None, :] < lengths[:, None]
    return jnp.where(valid_mask[:, None, None, :], scores, -1000000000.0)


def attend_forward(queries, key_rows, values, lengths, length):
    seq_count = lengths.shape[0]
    q_heads = head_split(queries, seq_count, length)
    k_heads = head_split(key_rows, seq_count, length)
    v_heads = head_split(values, seq_count, length)
    scores = masked_scores(q_heads, k_heads, lengths, length)
    top_score = jnp.max(scores, -1, keepdims=True)
    weights = jnp.exp(scores - top_score)
    total_sum = jnp.sum(weights, -1, keepdims=True)
    probs_low = (weights / total_sum).astype(jnp.bfloat16)
    mixed = jnp.einsum("shqk,skhd->sqhd", probs_low, v_heads, preferred_element_type=jnp.float32)
    return (mixed.reshape(queries.shape).astype(jnp.bfloat16), top_score + jnp.log(total_sum))


def attend_backward(queries, key_rows, values, lengths, length, log_sums, grad_mixed):
    seq_count = lengths.shape[0]
    q_heads = head_split(queries, seq_count, length)
    k_heads = head_split(key_rows, seq_count, length)
    v_heads = head_split(values, seq_count, length)
    head_scale = q_heads.shape[3] ** (-0.5)
    probs_full = jnp.exp(masked_scores(q_heads, k_heads, lengths, length) - log_sums)
    grad_heads = head_split(grad_mixed, seq_count, length)
    grad_probs = jnp.einsum(
        "sqhd,skhd->shqk", grad_heads, v_heads, preferred_element_type=jnp.float32
    )
    grad_values = jnp.einsum(
        "shqk,sqhd->skhd",
        probs_full.astype(jnp.bfloat16),
        grad_heads,
        preferred_element_type=jnp.float32,
    )
    inner_sum = jnp.sum(grad_probs * probs_full, -1, keepdims=True)
    grad_scores = (probs_full * (grad_probs - inner_sum)).astype(jnp.bfloat16)
    grad_queries = (
        jnp.einsum("shqk,skhd->sqhd", grad_scores, k_heads, preferred_element_type=jnp.float32)
        * head_scale
    )
    grad_keys = (
        jnp.einsum("shqk,sqhd->skhd", grad_scores, q_heads, preferred_element_type=jnp.float32)
        * head_scale
    )
    return tuple(
        (
            member.reshape(queries.shape).astype(jnp.bfloat16)
            for member in (grad_queries, grad_keys, grad_values)
        )
    )


def layer_forward(token_rows, query_lens, passage_lens, params):
    w_qkv, b_qv, w_o, b_o, g_attn, c_attn, w_in, b_in, w_out, b_out, g_ffn, c_ffn = params
    features = token_rows.shape[1]
    projected = jnp.dot(token_rows, w_qkv, preferred_element_type=jnp.float32)
    queries = (projected[:, :features] + b_qv[:features]).astype(jnp.bfloat16)
    key_rows = projected[:, features : 2 * features].astype(jnp.bfloat16)
    values = (projected[:, 2 * features :] + b_qv[features:]).astype(jnp.bfloat16)
    query_rows = query_lens.shape[0] * QLEN
    mixed_q, sums_q = attend_forward(
        queries[:query_rows], key_rows[:query_rows], values[:query_rows], query_lens, QLEN
    )
    mixed_p, sums_p = attend_forward(
        queries[query_rows:], key_rows[query_rows:], values[query_rows:], passage_lens, PLEN
    )
    mixed_rows = jnp.concatenate([mixed_q, mixed_p], 0)
    pre_attn = (
        token_rows.astype(jnp.float32)
        + jnp.dot(mixed_rows, w_o, preferred_element_type=jnp.float32)
        + b_o
    )
    normed = normalize(pre_attn, g_attn, c_attn)
    normed_low = normed.astype(jnp.bfloat16)
    up_proj = jnp.dot(normed_low, w_in, preferred_element_type=jnp.float32) + b_in
    act_low = exact_gelu(up_proj).astype(jnp.bfloat16)
    pre_ffn = normed + jnp.dot(act_low, w_out, preferred_element_type=jnp.float32) + b_out
    kept_state = (
        token_rows,
        queries,
        key_rows,
        values,
        mixed_rows,
        sums_q,
        sums_p,
        pre_attn,
        normed_low,
        up_proj,
        act_low,
        pre_ffn,
        query_lens,
        passage_lens,
    )
    return (normalize(pre_ffn, g_ffn, c_ffn), kept_state)


def layer_backward(kept_state, params, grad_out):
    (
        token_rows,
        queries,
        key_rows,
        values,
        mixed_rows,
        sums_q,
        sums_p,
        pre_attn,
        normed_low,
        up_proj,
        act_low,
        pre_ffn,
        query_lens,
        passage_lens,
    ) = kept_state
    w_qkv, b_qv, w_o, b_o, g_attn, c_attn, w_in, b_in, w_out, b_out, g_ffn, c_ffn = params
    unused, ffn_norm_back = jax.vjp(normalize, pre_ffn, g_ffn, c_ffn)
    grad_pre_ffn, grad_g_ffn, grad_c_ffn = ffn_norm_back(grad_out)
    grad_ffn_low = grad_pre_ffn.astype(jnp.bfloat16)
    grad_b_out = jnp.sum(grad_pre_ffn, 0)
    grad_act = jnp.einsum("rd,fd->rf", grad_ffn_low, w_out, preferred_element_type=jnp.float32)
    unused, gelu_back = jax.vjp(exact_gelu, up_proj)
    grad_up = gelu_back(grad_act)[0].astype(jnp.bfloat16)
    grad_b_in = jnp.sum(grad_up.astype(jnp.float32), 0)
    grad_normed = grad_pre_ffn + jnp.einsum(
        "rf,df->rd", grad_up, w_in, preferred_element_type=jnp.float32
    )
    unused, attn_norm_back = jax.vjp(normalize, pre_attn, g_attn, c_attn)
    grad_pre_attn, grad_g_attn, grad_c_attn = attn_norm_back(grad_normed)
    grad_attn_low = grad_pre_attn.astype(jnp.bfloat16)
    grad_b_o = jnp.sum(grad_pre_attn, 0)
    grad_mixed = jnp.einsum(
        "rd,ed->re", grad_attn_low, w_o, preferred_element_type=jnp.float32
    ).astype(jnp.bfloat16)
    query_rows = query_lens.shape[0] * QLEN
    grads_q = attend_backward(
        queries[:query_rows],
        key_rows[:query_rows],
        values[:query_rows],
        query_lens,
        QLEN,
        sums_q,
        grad_mixed[:query_rows],
    )
    grads_p = attend_backward(
        queries[query_rows:],
        key_rows[query_rows:],
        values[query_rows:],
        passage_lens,
        PLEN,
        sums_p,
        grad_mixed[query_rows:],
    )
    stacked = tuple((jnp.concatenate([left, right], 0) for left, right in zip(grads_q, grads_p)))
    grad_proj = jnp.concatenate(stacked, 1)
    grad_b_qv = jnp.concatenate(
        [jnp.sum(stacked[0].astype(jnp.float32), 0), jnp.sum(stacked[2].astype(jnp.float32), 0)]
    )
    grad_rows = grad_pre_attn + jnp.einsum(
        "re,de->rd", grad_proj, w_qkv, preferred_element_type=jnp.float32
    )
    lefts = (token_rows, mixed_rows, normed_low, act_low)
    rights = (grad_proj, grad_attn_low, grad_up, grad_ffn_low)
    vectors = (
        grad_b_qv,
        grad_b_o,
        grad_g_attn,
        grad_c_attn,
        grad_b_in,
        grad_b_out,
        grad_g_ffn,
        grad_c_ffn,
    )
    return (grad_rows, lefts, rights, vectors)


def contrast(logits, targets):
    top_score = jnp.max(logits, -1, keepdims=True)
    log_total = top_score[:, 0] + jnp.log(jnp.sum(jnp.exp(logits - top_score), -1))
    chosen = targets[:, None] == jnp.arange(logits.shape[1])[None, :]
    term_values = log_total - jnp.sum(jnp.where(chosen, logits, 0.0), -1)
    grad_logits = (jnp.exp(logits - log_total[:, None]) - chosen.astype(jnp.float32)).astype(
        jnp.bfloat16
    )
    return (term_values, grad_logits)


MESH = pl.DeviceIdType.MESH
CHUNK = 384
COUNT = 12
BLOCK = 48


def swap(value):
    return lax.ppermute(value, "section", [(0, 1), (1, 0)])


def chunk_left(ch):
    return (ch >= 3).astype(jnp.int32) + (ch >= 4).astype(jnp.int32) + jnp.maximum(ch - 7, 0)


def chunk_right(ch):
    return jnp.minimum(ch, 8)


def reduce_kernel(
    at1, pat1, g1, pg1, at0, pat0, g0, pg0, vec,
    o_qkv, o_o, o_in, o_out, o_vec,
    a_buf, g_buf, s1, r1, s2, r2, s3, r3, v1, w1, v2, w2, v3, w3,
    load, s1s, r1s, s2s, r2s, s3s, r3s, vs, vr, v3s, v3r,
):
    core = lax.axis_index("section")
    me = lax.axis_index("batch")
    x, y, z = me % 2, (me // 2) % 2, me // 4
    px, py = me + 1 - 2 * x, me + 2 - 4 * y

    loads = []
    for layer, parts in ((1, (at1, pat1, g1, pg1)), (0, (at0, pat0, g0, pg0))):
        for spot, part in enumerate(parts):
            lo = (spot % 2) * CHUNK
            if spot < 2:
                dst = a_buf.at[layer, :, :, :, pl.ds(lo, CHUNK)]
            else:
                dst = g_buf.at[layer, :, pl.ds(lo, CHUNK)]
            loads.append(pltpu.make_async_copy(part, dst, load.at[layer, spot]))
            loads[-1].start()
    vload = pltpu.make_async_copy(vec, v1, load.at[2, 0])
    vload.start()

    barrier = pltpu.get_barrier_semaphore()
    for who in (px, py):
        pl.semaphore_signal(barrier, inc=1, device_id={"batch": who}, device_id_type=MESH)
    for step in (1, 2, 3):
        other = ((z + step) % 4) * 4 + me % 4
        for sec in (0, 1):
            pl.semaphore_signal(
                barrier, inc=1, device_id={"section": sec, "batch": other}, device_id_type=MESH
            )
    pl.semaphore_signal(barrier, inc=1, device_id={"section": 1 - core}, device_id_type=MESH)
    pl.semaphore_wait(barrier, 9)

    def remote(src, dst, send, recv, where):
        return pltpu.make_async_remote_copy(
            src_ref=src, dst_ref=dst, send_sem=send, recv_sem=recv,
            device_id=where, device_id_type=MESH,
        )

    def first(k, par):
        return remote(
            s1.at[k % 4], r1.at[k], s1s.at[k], r1s.at[k], {"batch": px if par == 0 else py}
        )

    def second(k, par):
        return remote(
            s2.at[k % 4], r2.at[k], s2s.at[k], r2s.at[k], {"batch": py if par == 0 else px}
        )

    def third(k, step, src_core):
        layer = 1 - k // COUNT
        zt = (z + step) % 4
        return remote(
            s3.at[k % 4, zt],
            r3.at[src_core, k % COUNT, z],
            s3s.at[k, step],
            r3s.at[src_core, k % COUNT, z],
            {"section": layer, "batch": zt * 4 + me % 4},
        )

    def third_in(k, step, src_core):
        layer = 1 - k // COUNT
        zs = (z + 4 - step) % 4
        return remote(
            s3.at[k % 4, zs],
            r3.at[src_core, k % COUNT, zs],
            s3s.at[k, step],
            r3s.at[src_core, k % COUNT, zs],
            {"section": 1 - core, "batch": me},
        )

    def product(k, left, rows):
        ch, layer = k % COUNT, 1 - k // COUNT
        right = g_buf[layer, chunk_right(ch)]
        return jnp.dot(
            left.reshape(rows, 2 * CHUNK), right, preferred_element_type=jnp.float32
        )

    def left_of(k):
        return a_buf.at[1 - k // COUNT, chunk_left(k % COUNT)]

    def part_one(k, par):
        ref = left_of(k).reshape(4, 2, 2, BLOCK, 2 * CHUNK)
        left = ref[:, :, 1 - x] if par == 0 else ref[:, 1 - y]
        out = product(k, left, 8 * BLOCK)
        s1[k % 4] = out.astype(jnp.bfloat16).reshape(4, 2, BLOCK, CHUNK)
        first(k, par).start()

    def part_two(k, par):
        first(k, par).wait()
        ref = left_of(k).reshape(4, 2, 2, BLOCK, 2 * CHUNK)
        if par == 0:
            left, came = ref[:, 1 - y, x], r1[k, :, 1 - y]
        else:
            left, came = ref[:, y, 1 - x], r1[k, :, 1 - x]
        out = product(k, left, 4 * BLOCK).reshape(4, BLOCK, CHUNK) + came.astype(jnp.float32)
        s2[k % 4] = out.astype(jnp.bfloat16)
        second(k, par).start()

    def part_three(k, par):
        second(k, par).wait()
        layer = 1 - k // COUNT
        ref = left_of(k).reshape(4, 2, 2, BLOCK, 2 * CHUNK)
        came = r1[k, :, y] if par == 0 else r1[k, :, x]
        out = (
            product(k, ref[:, y, x], 4 * BLOCK).reshape(4, BLOCK, CHUNK)
            + came.astype(jnp.float32)
            + r2[k].astype(jnp.float32)
        )
        s3[k % 4] = out.astype(jnp.bfloat16)
        for step in (1, 2, 3):
            third(k, step, core).start()

        @pl.when(core != layer)
        def _():
            third(k, 0, core).start()

        @pl.when(core == layer)
        def _():
            r3[core, k % COUNT, z] = s3[k % 4, z]

    def part_four(k):
        layer = 1 - k // COUNT
        ch = k % COUNT
        for step in (1, 2, 3):
            third(k, step, core).wait_send()

        @pl.when(core != layer)
        def _():
            third(k, 0, core).wait_send()

        @pl.when(core == layer)
        def _():
            for step in (1, 2, 3):
                for src_core in (0, 1):
                    third_in(k, step, src_core).wait_recv()
            third_in(k, 0, 1 - core).wait_recv()
            for src_core in (0, 1):
                total = jnp.sum(r3[src_core, ch].astype(jnp.float32), 0)

                @pl.when(ch < 3)
                def _():
                    start = pl.multiple_of(ch * CHUNK + src_core * 1152, 128)
                    o_qkv[:, pl.ds(start, CHUNK)] = total

                @pl.when(ch == 3)
                def _():
                    o_o[:, pl.ds(src_core * CHUNK, CHUNK)] = total

                @pl.when((ch >= 4) & (ch < 8))
                def _():
                    start = pl.multiple_of((ch - 4) * CHUNK + src_core * 1536, 128)
                    o_in[:, pl.ds(start, CHUNK)] = total

                @pl.when(ch >= 8)
                def _():
                    o_out[ch - 8, :, pl.ds(src_core * CHUNK, CHUNK)] = total

    def vec_first():
        return remote(v2.at[0], w1, vs.at[0], vr.at[0], {"batch": px})

    def vec_second():
        return remote(v2.at[1, :, :, 0], w2, vs.at[1], vr.at[1], {"batch": py})

    def vec_third(layer, step):
        zt = (z + step) % 4
        return remote(
            v3.at[layer, zt], w3.at[core, z], v3s.at[layer, step], v3r.at[core, z],
            {"section": layer, "batch": zt * 4 + me % 4},
        )

    def vec_third_in(src_core, step):
        zs = (z + 4 - step) % 4
        return remote(
            v3.at[core, zs], w3.at[src_core, zs], v3s.at[core, step], v3r.at[src_core, zs],
            {"section": 1 - core, "batch": me},
        )

    for spot in range(4):
        loads[spot].wait()
    vload.wait()
    v2[0] = v1[:, :, :, 1 - x]
    vec_first().start()

    steps = 2 * COUNT + 6

    def pair(kk, carry):
        for par in (0, 1):
            k = 2 * kk + par

            @pl.when(k == COUNT)
            def _():
                for spot in range(4, 8):
                    loads[spot].wait()

            @pl.when(k < 2 * COUNT)
            def _():
                part_one(k, par)

            @pl.when((k >= 2) & (k < 2 * COUNT + 2))
            def _():
                part_two(k - 2, par)

            @pl.when((k >= 4) & (k < 2 * COUNT + 4))
            def _():
                part_three(k - 4, par)

            @pl.when(k >= 6)
            def _():
                part_four(k - 6)

        return carry

    lax.fori_loop(0, 3, pair, 0)
    vec_first().wait()
    v2[1, :, :, 0] = v1[:, :, 1 - y, x] + w1[:, :, 1 - y]
    vec_second().start()
    lax.fori_loop(3, 6, pair, 0)
    vec_second().wait()
    v3[...] = v1[:, :, y, x] + w1[:, :, y] + w2[...]
    for layer in (0, 1):
        for step in (1, 2, 3):
            vec_third(layer, step).start()

        @pl.when(core != layer)
        def _():
            vec_third(layer, 0).start()

        @pl.when(core == layer)
        def _():
            w3[core, z] = v3[layer, z]

    lax.fori_loop(6, steps // 2, pair, 0)
    for layer in (0, 1):
        for step in (1, 2, 3):
            vec_third(layer, step).wait_send()

        @pl.when(core != layer)
        def _():
            vec_third(layer, 0).wait_send()

    for step in (1, 2, 3):
        for src_core in (0, 1):
            vec_third_in(src_core, step).wait_recv()
    vec_third_in(1 - core, 0).wait_recv()
    o_vec[...] = jnp.sum(w3[...], (0, 1))


def reduce_all(packed, vec):
    low, full = jnp.bfloat16, jnp.float32
    steps = 2 * COUNT
    anywhere = pl.BlockSpec(memory_space=pl.ANY)
    vmem = pl.BlockSpec(memory_space=pltpu.VMEM)
    dma = pltpu.SemaphoreType.DMA
    return pl.pallas_call(
        reduce_kernel,
        out_shape=(
            jax.ShapeDtypeStruct((BLOCK, 2304), full),
            jax.ShapeDtypeStruct((BLOCK, 768), full),
            jax.ShapeDtypeStruct((BLOCK, 3072), full),
            jax.ShapeDtypeStruct((4, BLOCK, 768), full),
            jax.ShapeDtypeStruct((8, 128), full),
        ),
        in_specs=[anywhere] * 9,
        out_specs=(vmem,) * 5,
        scratch_shapes=[
            pltpu.VMEM((2, 7, 16, BLOCK, 2 * CHUNK), low),
            pltpu.VMEM((2, 9, 2 * CHUNK, CHUNK), low),
            pltpu.VMEM((4, 4, 2, BLOCK, CHUNK), low),
            pltpu.VMEM((steps, 4, 2, BLOCK, CHUNK), low),
            pltpu.VMEM((4, 4, BLOCK, CHUNK), low),
            pltpu.VMEM((steps, 4, BLOCK, CHUNK), low),
            pltpu.VMEM((4, 4, BLOCK, CHUNK), low),
            pltpu.VMEM((2, COUNT, 4, BLOCK, CHUNK), low),
            pltpu.VMEM((2, 4, 2, 2, 8, 128), full),
            pltpu.VMEM((2, 4, 2, 8, 128), full),
            pltpu.VMEM((2, 2, 4, 2, 8, 128), full),
            pltpu.VMEM((2, 4, 8, 128), full),
            pltpu.VMEM((2, 4, 8, 128), full),
            pltpu.VMEM((2, 4, 8, 128), full),
            dma((3, 4)),
            dma((steps,)),
            dma((steps,)),
            dma((steps,)),
            dma((steps,)),
            dma((steps, 4)),
            dma((2, COUNT, 4)),
            dma((2,)),
            dma((2,)),
            dma((2, 4)),
            dma((2, 4)),
        ],
        compiler_params=pltpu.CompilerParams(
            collective_id=1, has_side_effects=True, vmem_limit_bytes=56 * 1024 * 1024
        ),
    )(*packed, vec)


def pack_left(lefts):
    token_rows, mixed_rows, normed_low, act_low = (member.T for member in lefts)
    rows = token_rows.shape[1]
    shaped = [member.reshape(1, 16, BLOCK, rows) for member in (token_rows, mixed_rows, normed_low)]
    shaped.append(act_low.reshape(16, 4, BLOCK, rows).transpose(1, 0, 2, 3))
    return jnp.concatenate(shaped, 0)


def pack_right(rights, core):
    rows = rights[0].shape[0]
    parts = []
    for member in rights:
        width = member.shape[1] // 2
        half = lax.dynamic_slice_in_dim(member, core * width, width, 1)
        parts.append(half.reshape(rows, width // CHUNK, CHUNK).transpose(1, 0, 2))
    return jnp.concatenate(parts, 0)


def pack_vectors(vectors, parts):
    flat = jnp.concatenate([member.reshape(parts, -1) for member in vectors], 1)
    flat = jnp.pad(flat, ((0, 0), (0, 1024 - flat.shape[1])))
    return flat.reshape(parts, 8, 128)


def gather_kernel(parts, own, out, send, recv, here):
    core = lax.axis_index("section")
    me = lax.axis_index("batch")
    mine = core * parts + me
    total = 2 * parts
    barrier = pltpu.get_barrier_semaphore()

    def greet(step, carry):
        other = (mine + step) % total
        pl.semaphore_signal(
            barrier, inc=1, device_id={"section": other // parts, "batch": other % parts},
            device_id_type=MESH,
        )
        return carry

    lax.fori_loop(1, total, greet, 0)
    pl.semaphore_wait(barrier, total - 1)

    def copy(step, slot):
        other = (mine + step) % total
        return pltpu.make_async_remote_copy(
            src_ref=own, dst_ref=out.at[slot], send_sem=send.at[step], recv_sem=recv.at[slot],
            device_id={"section": other // parts, "batch": other % parts}, device_id_type=MESH,
        )

    def start(step, carry):
        copy(step, mine).start()
        return carry

    lax.fori_loop(1, total, start, 0)
    local = pltpu.make_async_copy(own, out.at[mine], here)
    local.start()
    local.wait()

    def finish(step, carry):
        copy(step, mine).wait_send()
        copy(step, (mine + total - step) % total).wait_recv()
        return carry

    lax.fori_loop(1, total, finish, 0)


def gather_all(own, parts):
    vmem = pl.BlockSpec(memory_space=pltpu.VMEM)
    return pl.pallas_call(
        functools.partial(gather_kernel, parts),
        out_shape=jax.ShapeDtypeStruct((2 * parts,) + own.shape, own.dtype),
        in_specs=[vmem],
        out_specs=vmem,
        scratch_shapes=[
            pltpu.SemaphoreType.DMA((2 * parts,)),
            pltpu.SemaphoreType.DMA((2 * parts,)),
            pltpu.SemaphoreType.DMA,
        ],
        compiler_params=pltpu.CompilerParams(collective_id=0, has_side_effects=True),
    )(own)


def per_device(
    parts,
    x_query,
    x_passage,
    len_query,
    len_passage,
    positive,
    cot_query,
    cot_passage,
    *weights,
):
    core = lax.axis_index("section")
    on_first = core == 0
    own_set = tuple(member[0] for member in weights)
    other_set = tuple(swap(member) for member in own_set)
    params = (
        tuple(jnp.where(on_first, a, b) for a, b in zip(own_set, other_set)),
        tuple(jnp.where(on_first, b, a) for a, b in zip(own_set, other_set)),
    )
    features = x_query.shape[2]
    half_q, half_p = x_query.shape[0] // 2, x_passage.shape[0] // 2
    split = half_q * QLEN

    def own_half(array):
        half = array.shape[0] // 2
        return lax.dynamic_slice_in_dim(array, core * half, half, 0)

    def rows_of(query, passage):
        return jnp.concatenate(
            [own_half(query).reshape(-1, features), own_half(passage).reshape(-1, features)], 0
        )

    query_lens, passage_lens = own_half(len_query), own_half(len_passage)
    out0, kept0 = layer_forward(rows_of(x_query, x_passage), query_lens, passage_lens, params[0])
    rows1 = out0.astype(jnp.bfloat16)
    out1, kept1 = layer_forward(rows1, query_lens, passage_lens, params[1])
    final = out1.astype(jnp.bfloat16)

    def join(first, second):
        mine = jnp.where(on_first, first, second)
        came = swap(jnp.where(on_first, second, first))
        low, high = jnp.where(on_first, mine, came), jnp.where(on_first, came, mine)
        query = jnp.concatenate([low[:split], high[:split]], 0)
        passage = jnp.concatenate([low[split:], high[split:]], 0)
        return query.reshape(x_query.shape)[None], passage.reshape(x_passage.shape)[None]

    hidden_q, hidden_p = join(rows1, final)

    cls_own = jnp.concatenate(
        [
            final[:split].reshape(half_q, QLEN, features)[:, 0],
            final[split:].reshape(half_p, PLEN, features)[:, 0],
        ],
        0,
    )
    targets = lax.all_gather(positive, "batch", axis=0, tiled=True)
    count = half_q + half_p
    if parts == 16:
        flat = jnp.pad(cls_own.reshape(-1, 128), ((0, 2), (0, 0)))
        every = gather_all(flat, parts)[:, : count * features // 128]
        every = every.reshape(2, parts, count, features)
    else:
        every = lax.all_gather(cls_own, ("section", "batch"), axis=0, tiled=True)
        every = every.reshape(2, parts, count, features)
    every = every.transpose(1, 0, 2, 3)
    cls_query = every[:, :, :half_q].reshape(-1, features)
    cls_passage = every[:, :, half_q:].reshape(-1, features)
    score_scale = 2.0 / math.sqrt(features)
    logits = (
        jnp.einsum("qd,pd->qp", cls_query, cls_passage, preferred_element_type=jnp.float32)
        * score_scale
    )
    term_values, grad_logits = contrast(logits, targets)
    loss_value = jnp.mean(term_values)
    mine = lax.axis_index("batch") * 2 + core
    own_logits = lax.dynamic_slice_in_dim(grad_logits, mine * half_q, half_q, 0)
    grad_cls_q = (
        jnp.einsum("qp,pd->qd", own_logits, cls_passage, preferred_element_type=jnp.float32)
        * score_scale
    )
    own_columns = lax.dynamic_slice_in_dim(grad_logits, mine * half_p, half_p, 1)
    grad_cls_p = (
        jnp.einsum("qp,qd->pd", own_columns, cls_query, preferred_element_type=jnp.float32)
        * score_scale
    )
    rows_list = []
    for cot, lens, cls_grad, length in (
        (cot_query, query_lens, grad_cls_q, QLEN),
        (cot_passage, passage_lens, grad_cls_p, PLEN),
    ):
        block = own_half(cot).astype(jnp.float32)
        valid_mask = jnp.arange(length)[None, :] < lens[:, None]
        masked = jnp.where(valid_mask[:, :, None], block, 0.0)
        rows_list.append(masked.at[:, 0].add(cls_grad).reshape(-1, features))
    grad_out1 = jnp.concatenate(rows_list, 0)

    grad1, lefts1, rights1, vectors1 = layer_backward(kept1, params[1], grad_out1)
    grad_low = grad1.astype(jnp.bfloat16).astype(jnp.float32)
    grad0, lefts0, rights0, vectors0 = layer_backward(kept0, params[0], grad_low)
    grad_q, grad_p = join(grad0, grad1)

    if parts == 16:
        packed = []
        for lefts, rights in ((lefts1, rights1), (lefts0, rights0)):
            left = pack_left(lefts)
            packed += [left, swap(left), pack_right(rights, core), swap(pack_right(rights, 1 - core))]
        vec = jnp.stack([pack_vectors(vectors0, parts), pack_vectors(vectors1, parts)])
        d_qkv, d_o, d_in, d_out, d_vec = reduce_all(packed, vec.reshape(2, 4, 2, 2, 8, 128))
        d_out = d_out.reshape(4 * BLOCK, 768)
        flat = d_vec.reshape(-1)
        sizes = [member.shape[0] // parts for member in vectors0]
        small, at = [], 0
        for size in sizes:
            small.append(flat[at : at + size])
            at += size
    else:

        def total(first, second):
            kept = jnp.where(on_first, first, second)
            both = kept + swap(jnp.where(on_first, second, first))
            return lax.psum_scatter(both, "batch", scatter_dimension=0, tiled=True)

        def product(left, right):
            return jnp.einsum("rd,re->de", left, right, preferred_element_type=jnp.float32)

        d_qkv, d_o, d_in, d_out = (
            total(product(la, ra), product(lb, rb))
            for la, ra, lb, rb in zip(lefts0, rights0, lefts1, rights1)
        )
        small = [total(first, second) for first, second in zip(vectors0, vectors1)]
    d_b_qv, d_b_o, d_g_attn, d_c_attn, d_b_in, d_b_out, d_g_ffn, d_c_ffn = small
    outs = (
        d_qkv, d_b_qv, d_o, d_b_o, d_g_attn, d_c_attn, d_in, d_b_in, d_out, d_b_out, d_g_ffn,
        d_c_ffn,
    )
    return (hidden_q, hidden_p, grad_q, grad_p, loss_value) + tuple(item[None] for item in outs)


def solution(mesh):
    in_specs = (
        P("batch", None, None),
        P("batch", None, None),
        P("batch"),
        P("batch"),
        P("batch"),
        P("batch", None, None),
        P("batch", None, None),
        P("section", None, None),
        P("section", None),
        P("section", None, None),
        P("section", None),
        P("section", None),
        P("section", None),
        P("section", None, None),
        P("section", None),
        P("section", None, None),
        P("section", None),
        P("section", None),
        P("section", None),
    )
    out_specs = (
        P("section", "batch", None, None),
        P("section", "batch", None, None),
        P("section", "batch", None, None),
        P("section", "batch", None, None),
        P(),
        P("section", "batch", None),
        P("section", "batch"),
        P("section", "batch", None),
        P("section", "batch"),
        P("section", "batch"),
        P("section", "batch"),
        P("section", "batch", None),
        P("section", "batch"),
        P("section", "batch", None),
        P("section", "batch"),
        P("section", "batch"),
        P("section", "batch"),
    )
    return jax.shard_map(
        functools.partial(per_device, mesh.shape["batch"]), mesh=mesh, in_specs=in_specs, out_specs=out_specs, check_vma=False
    )
```

```python
import functools
import math

import jax
import jax.numpy as jnp
from jax import lax
from jax.experimental import pallas as pl
from jax.experimental.pallas import tpu as pltpu
from jax.sharding import PartitionSpec as P

HEADS = 12
QLEN = 32
PLEN = 256


norm_eps = 1e-05


def contrast(logits, targets):
    top_score = jnp.max(logits, -1, keepdims=True)
    log_total = top_score[:, 0] + jnp.log(jnp.sum(jnp.exp(logits - top_score), -1))
    chosen = targets[:, None] == jnp.arange(logits.shape[1])[None, :]
    term_values = log_total - jnp.sum(jnp.where(chosen, logits, 0.0), -1)
    grad_logits = (jnp.exp(logits - log_total[:, None]) - chosen.astype(jnp.float32)).astype(
        jnp.bfloat16
    )
    return (term_values, grad_logits)


MESH = pl.DeviceIdType.MESH
CHUNK = 384
COUNT = 12
BLOCK = 48


def swap(value):
    return lax.ppermute(value, "section", [(0, 1), (1, 0)])


LOW = jnp.bfloat16
FULL = jnp.float32
ROWS = 16
TILE = 256
LAST = (((1,), (1,)), ((), ()))
FIRST = (((0,), (0,)), ((), ()))


def dot(left, right):
    return jnp.dot(left, right, preferred_element_type=FULL)


def dot_last(left, right):
    return lax.dot_general(left, right, LAST, preferred_element_type=FULL)


def dot_first(left, right):
    return lax.dot_general(left, right, FIRST, preferred_element_type=FULL)


def over(count, body):
    def step(index, carry):
        body(index)
        return carry

    lax.fori_loop(0, count, step, 0)


def row_range(index):
    return pl.ds(pl.multiple_of(index * ROWS, ROWS), ROWS)


def lane_range(index, width):
    return pl.ds(pl.multiple_of(index * width, 128), width)


def moments(block):
    centred = block - jnp.mean(block, -1, keepdims=True)
    spread = jnp.mean(centred * centred, -1, keepdims=True)
    inverse = lax.rsqrt(spread + norm_eps)
    return centred * inverse, inverse


def gelu_pair(block):
    size = jnp.abs(block)
    t = 1.0 / (1.0 + (0.3275911 * math.sqrt(0.5)) * size)
    bell = jnp.exp(-0.5 * block * block)
    poly = 0.5 * 1.061405429
    for term in (-1.453152027, 1.421413741, -0.284496736, 0.254829592):
        poly = poly * t + 0.5 * term
    tail = poly * t * bell
    phi = jnp.where(block > 0, 1.0 - tail, tail)
    return block * phi, phi + block * bell * (1.0 / math.sqrt(2.0 * math.pi))


def head_lanes(rows, head):
    lane = lax.broadcasted_iota(jnp.int32, (rows, 128), 1)
    return (lane < 64) if head == 0 else (lane >= 64)


def query_mask(lens, count):
    rows = count * QLEN
    row = lax.broadcasted_iota(jnp.int32, (rows, rows), 0)
    column = lax.broadcasted_iota(jnp.int32, (rows, rows), 1)
    limit = jnp.zeros((rows, rows), jnp.int32)
    for item in range(count):
        limit = jnp.where(column // QLEN == item, item * QLEN + lens[item], limit)
    return (row // QLEN == column // QLEN) & (column < limit)


def fetch_weights(core, layer, own, other, buffers, sem):
    def copies(source):
        return [
            pltpu.make_async_copy(a, b, sem.at[spot])
            for spot, (a, b) in enumerate(zip(source, buffers))
        ]

    @pl.when(core == layer)
    def _():
        for copy in copies(own):
            copy.start()

    @pl.when(core != layer)
    def _():
        for copy in copies(other):
            copy.start()

    return copies(own)


def forward_kernel(
    layer, x, qlens, plens, par, wqkv, wo, win, wout, xqkv, xo, xin, xout,
    o_qkv, o_pq, o_pp, o_mixed, o_pre, o_normed, o_act, o_slope, o_ffn, o_out,
    bqkv, bo, bin_, bout, qkv, pq, pp, mixed, pre, normed_full, normed, up, act, slope, ffn,
    load, save,
):
    core = lax.axis_index("section")
    features = x.shape[1]
    total = x.shape[0]
    count_q, count_p = qlens.shape[0], plens.shape[0]
    split = count_q * QLEN
    waits = fetch_weights(
        core, layer, (wqkv, wo, win, wout), (xqkv, xo, xin, xout), (bqkv, bo, bin_, bout), load
    )
    saves = []

    def keep(source, target):
        saves.append(pltpu.make_async_copy(source, target, save.at[len(saves)]))
        saves[-1].start()

    waits[0].wait()

    def project(tile):
        lanes = lane_range(tile, TILE)
        out = dot(x[...], bqkv[:, lanes])
        third = features // TILE
        bias_row = jnp.where(tile < third, par[0:1, lane_range(tile % third, TILE)], 0.0)
        bias_row = jnp.where(tile >= 2 * third, par[1:2, lane_range(tile % third, TILE)], bias_row)
        qkv[:, lanes] = (out + bias_row).astype(LOW)

    over(3 * features // TILE, project)
    keep(qkv, o_qkv)

    def attend(lo, rows, mask, probs, base):
        def pair(hp):
            def part(offset):
                return qkv[pl.ds(lo, rows), pl.ds(pl.multiple_of(offset + hp * 128, 128), 128)]

            queries = part(0) * LOW(0.125)
            keys, values = part(features), part(2 * features)
            outs = []
            for head in (0, 1):
                masked = jnp.where(head_lanes(rows, head), queries, LOW(0))
                scores = jnp.where(mask, dot_last(masked, keys), -1000000000.0)
                weights = jnp.exp(scores - jnp.max(scores, -1, keepdims=True))
                inverse = 1.0 / jnp.sum(weights, -1, keepdims=True)
                low = (weights * inverse).astype(LOW)
                probs[base + 2 * hp + head] = low
                outs.append(dot(low, values))
            both = jnp.where(head_lanes(rows, 0), outs[0], outs[1])
            mixed[pl.ds(lo, rows), pl.ds(pl.multiple_of(hp * 128, 128), 128)] = both.astype(LOW)

        over(features // 128, pair)

    attend(0, split, query_mask(qlens, count_q), pq, 0)
    for item in range(count_p):
        column = lax.broadcasted_iota(jnp.int32, (PLEN, PLEN), 1)
        attend(split + item * PLEN, PLEN, column < plens[item], pp, item * HEADS)
    keep(pq, o_pq)
    keep(pp, o_pp)
    keep(mixed, o_mixed)

    waits[1].wait()

    def mix(tile):
        lanes = lane_range(tile, TILE)
        pre[:, lanes] = (
            dot(mixed[...], bo[:, lanes]) + x[:, lanes].astype(FULL) + par[2:3, lanes]
        )

    over(features // TILE, mix)
    keep(pre, o_pre)

    def norm_one(index):
        rows = row_range(index)
        block = moments(pre[rows])[0] * par[3:4] + par[4:5]
        normed_full[rows] = block
        normed[rows] = block.astype(LOW)

    over(total // ROWS, norm_one)
    keep(normed, o_normed)
    waits[2].wait()

    def expand(tile):
        lanes = lane_range(tile, features)
        up[...] = dot(normed[...], bin_[:, lanes]) + par[pl.ds(5 + tile, 1)]

        def bend(index):
            rows = row_range(index)
            value, steep = gelu_pair(up[rows])
            act[rows, lanes] = value.astype(LOW)
            slope[rows, lanes] = steep.astype(LOW)

        over(total // ROWS, bend)

    over(4, expand)
    keep(act, o_act)
    keep(slope, o_slope)
    waits[3].wait()

    def contract(tile):
        lanes = lane_range(tile, TILE)
        ffn[:, lanes] = dot(act[...], bout[:, lanes]) + normed_full[:, lanes] + par[9:10, lanes]

    over(features // TILE, contract)
    keep(ffn, o_ffn)

    def norm_two(index):
        rows = row_range(index)
        o_out[rows] = (moments(ffn[rows])[0] * par[10:11] + par[11:12]).astype(LOW)

    over(total // ROWS, norm_two)
    for copy in saves:
        copy.wait()


VMEM_LIMIT = 56 * 1024 * 1024


def forward_layer(layer, x, qlens, plens, par, own, other):
    total, features = x.shape
    wide = own[2].shape[1]
    count_q, count_p = qlens.shape[0], plens.shape[0]
    split = count_q * QLEN
    kept = [
        ((total, 3 * features), LOW),
        ((HEADS, split, split), LOW),
        ((HEADS * count_p, PLEN, PLEN), LOW),
        ((total, features), LOW),
        ((total, features), FULL),
        ((total, features), LOW),
        ((total, wide), LOW),
        ((total, wide), LOW),
        ((total, features), FULL),
    ]
    anywhere = pl.BlockSpec(memory_space=pl.ANY)
    vmem = pl.BlockSpec(memory_space=pltpu.VMEM)
    smem = pl.BlockSpec(memory_space=pltpu.SMEM)
    buffers = [pltpu.VMEM(shape, kind) for shape, kind in kept]
    buffers = (
        buffers[:5]
        + [pltpu.VMEM((total, features), FULL)]
        + buffers[5:6]
        + [pltpu.VMEM((total, features), FULL)]
        + buffers[6:]
    )
    return pl.pallas_call(
        functools.partial(forward_kernel, layer),
        out_shape=[jax.ShapeDtypeStruct(shape, kind) for shape, kind in kept]
        + [jax.ShapeDtypeStruct((total, features), LOW)],
        in_specs=[vmem, smem, smem, vmem] + [anywhere] * 8,
        out_specs=[anywhere] * 9 + [vmem],
        scratch_shapes=[pltpu.VMEM(item.shape, item.dtype) for item in own]
        + buffers
        + [pltpu.SemaphoreType.DMA((4,)), pltpu.SemaphoreType.DMA((9,))],
        compiler_params=pltpu.CompilerParams(vmem_limit_bytes=VMEM_LIMIT),
    )(x, qlens, plens, par, *own, *other)


def add_rows(block):
    return jnp.sum(block.reshape(ROWS // 8, 8, block.shape[1]), 0)


def norm_back(source, grad_of, gain, total, store):
    features = source.shape[1]
    zero = jnp.zeros((8, features), FULL)

    def step(index, carry):
        rows = row_range(index)
        grad = grad_of(rows)
        unit, inverse = moments(source[rows])
        scaled = grad * gain
        back = inverse * (
            scaled
            - jnp.mean(scaled, -1, keepdims=True)
            - unit * jnp.mean(scaled * unit, -1, keepdims=True)
        )
        store(rows, back)
        return (
            carry[0] + add_rows(grad * unit),
            carry[1] + add_rows(grad),
            carry[2] + add_rows(back),
        )

    sums = lax.fori_loop(0, total // ROWS, step, (zero, zero, zero))
    return [jnp.sum(item, 0, keepdims=True) for item in sums]


def backward_kernel(
    layer, grad, par, wqkv, wo, win, wout, xqkv, xo, xin, xout,
    h_qkv, h_pq, h_pp, h_pre, h_slope, h_ffn,
    o_proj, o_attn, o_up, o_flow, o_rows, o_par,
    bqkv, bo, bin_, bout, qkv, pq, pp, pre, slope, ffn,
    proj, attn_full, attn, steep, gup, flow_full, flow, gmixed,
    load, fetch, save,
):
    core = lax.axis_index("section")
    total, features = grad.shape
    split = pq.shape[1]
    count_p = pp.shape[0] // HEADS
    gets = [
        pltpu.make_async_copy(a, b, fetch.at[spot])
        for spot, (a, b) in enumerate(
            zip((h_ffn, h_slope, h_pre, h_qkv, h_pq, h_pp), (ffn, slope, pre, qkv, pq, pp))
        )
    ]
    gets[0].start()
    waits = fetch_weights(
        core, layer, (wout, win, wo, wqkv), (xout, xin, xo, xqkv), (bout, bin_, bo, bqkv), load
    )
    for copy in gets[1:]:
        copy.start()
    saves = []

    def keep(source, target):
        saves.append(pltpu.make_async_copy(source, target, save.at[len(saves)]))
        saves[-1].start()

    gets[0].wait()

    def store_ffn(rows, back):
        flow_full[rows] = back
        flow[rows] = back.astype(LOW)

    gain, shift, bias = norm_back(ffn, lambda rows: grad[rows], par[10:11], total, store_ffn)
    o_par[10:11], o_par[11:12], o_par[9:10] = gain, shift, bias
    keep(flow, o_flow)
    gets[1].wait()
    waits[0].wait()

    def shrink(tile):
        lanes = lane_range(tile, features)
        rows_of = pl.ds(pl.multiple_of(tile * features, 128), features)
        steep[...] = dot_last(flow[...], bout[rows_of])

        def bend(index, carry):
            rows = row_range(index)
            low = (steep[rows] * slope[rows, lanes].astype(FULL)).astype(LOW)
            gup[rows, lanes] = low
            return carry + add_rows(low.astype(FULL))

        sums = lax.fori_loop(0, total // ROWS, bend, jnp.zeros((8, features), FULL))
        o_par[pl.ds(5 + tile, 1)] = jnp.sum(sums, 0, keepdims=True)

    over(4, shrink)
    keep(gup, o_up)
    waits[1].wait()

    def widen(tile):
        rows_of = pl.ds(pl.multiple_of(tile * TILE, TILE), TILE)
        lanes = lane_range(tile, TILE)
        flow_full[:, lanes] += dot_last(gup[...], bin_[rows_of])

    over(features // TILE, widen)
    gets[2].wait()

    def store_attn(rows, back):
        attn_full[rows] = back
        attn[rows] = back.astype(LOW)

    gain, shift, bias = norm_back(pre, lambda rows: flow_full[rows], par[3:4], total, store_attn)
    o_par[3:4], o_par[4:5], o_par[2:3] = gain, shift, bias
    keep(attn, o_attn)
    waits[2].wait()

    def unmix(tile):
        rows_of = pl.ds(pl.multiple_of(tile * TILE, TILE), TILE)
        gmixed[:, lane_range(tile, TILE)] = dot_last(attn[...], bo[rows_of]).astype(LOW)

    over(features // TILE, unmix)
    for copy in gets[3:]:
        copy.wait()

    def attend(lo, rows, probs, base):
        def pair(hp):
            def spot(offset):
                return (
                    pl.ds(lo, rows),
                    pl.ds(pl.multiple_of(offset + hp * 128, 128), 128),
                )

            queries, keys, values = (qkv[spot(item * features)] for item in range(3))
            back = gmixed[spot(0)]
            parts = []
            for head in (0, 1):
                masked = jnp.where(head_lanes(rows, head), back, LOW(0))
                low = probs[base + 2 * hp + head]
                full = low.astype(FULL)
                grad_probs = dot_last(masked, values)
                inner = jnp.sum(grad_probs * full, -1, keepdims=True)
                grad_scores = (full * (grad_probs - inner)).astype(LOW)
                parts.append(
                    (
                        dot(grad_scores, keys) * 0.125,
                        dot_first(grad_scores, queries) * 0.125,
                        dot_first(low, back),
                    )
                )
            first = head_lanes(rows, 0)
            for item in range(3):
                both = jnp.where(first, parts[0][item], parts[1][item])
                proj[spot(item * features)] = both.astype(LOW)

        over(features // 128, pair)

    attend(0, split, pq, 0)
    for item in range(count_p):
        attend(split + item * PLEN, PLEN, pp, item * HEADS)
    keep(proj, o_proj)

    def bias_sums(index, carry):
        rows = row_range(index)
        return (
            carry[0] + add_rows(proj[rows, pl.ds(0, features)].astype(FULL)),
            carry[1] + add_rows(proj[rows, pl.ds(2 * features, features)].astype(FULL)),
        )

    zero = jnp.zeros((8, features), FULL)
    sums = lax.fori_loop(0, total // ROWS, bias_sums, (zero, zero))
    o_par[0:1] = jnp.sum(sums[0], 0, keepdims=True)
    o_par[1:2] = jnp.sum(sums[1], 0, keepdims=True)
    o_par[12:16] = jnp.zeros((4, features), FULL)
    waits[3].wait()

    def finish(tile):
        rows_of = pl.ds(pl.multiple_of(tile * TILE, TILE), TILE)
        lanes = lane_range(tile, TILE)
        o_rows[:, lanes] = attn_full[:, lanes] + dot_last(proj[...], bqkv[rows_of])

    over(features // TILE, finish)
    for copy in saves:
        copy.wait()


def backward_layer(layer, grad, par, own, other, kept):
    total, features = grad.shape
    wide = own[2].shape[1]
    h_qkv, h_pq, h_pp, h_mixed, h_pre, h_normed, h_act, h_slope, h_ffn = kept
    held = (h_qkv, h_pq, h_pp, h_pre, h_slope, h_ffn)
    anywhere = pl.BlockSpec(memory_space=pl.ANY)
    vmem = pl.BlockSpec(memory_space=pltpu.VMEM)
    shape = jax.ShapeDtypeStruct
    scratch = [pltpu.VMEM(item.shape, item.dtype) for item in tuple(own) + held]
    scratch += [
        pltpu.VMEM((total, 3 * features), LOW),
        pltpu.VMEM((total, features), FULL),
        pltpu.VMEM((total, features), LOW),
        pltpu.VMEM((total, features), FULL),
        pltpu.VMEM((total, wide), LOW),
        pltpu.VMEM((total, features), FULL),
        pltpu.VMEM((total, features), LOW),
        pltpu.VMEM((total, features), LOW),
        pltpu.SemaphoreType.DMA((4,)),
        pltpu.SemaphoreType.DMA((6,)),
        pltpu.SemaphoreType.DMA((4,)),
    ]
    return pl.pallas_call(
        functools.partial(backward_kernel, layer),
        out_shape=[
            shape((total, 3 * features), LOW),
            shape((total, features), LOW),
            shape((total, wide), LOW),
            shape((total, features), LOW),
            shape((total, features), FULL),
            shape((16, features), FULL),
        ],
        in_specs=[vmem, vmem] + [anywhere] * 14,
        out_specs=[anywhere] * 4 + [vmem] * 2,
        scratch_shapes=scratch,
        compiler_params=pltpu.CompilerParams(vmem_limit_bytes=VMEM_LIMIT),
    )(grad, par, *own, *other, *held)


def chunk_left(ch):
    return (ch >= 3).astype(jnp.int32) + (ch >= 4).astype(jnp.int32) + jnp.maximum(ch - 7, 0)


def chunk_right(ch):
    return jnp.minimum(ch, 8)


def reduce_kernel(
    tok1, mix1, nor1, act1, pro1, att1, gup1, flo1,
    tok0, mix0, nor0, act0, pro0, att0, gup0, flo0, vec,
    o_qkv, o_o, o_in, o_out, o_vec, land,
    a_buf, g_buf, stage, s1, r1, s2, r2, s3, r3, v1, w1, v2, w2, v3, w3,
    load, s1s, r1s, s2s, r2s, s3s, r3s, vs, vr, v3s, v3r, gl, gs, gr, ls, lr, sl,
):
    core = lax.axis_index("section")
    me = lax.axis_index("batch")
    x, y, z = me % 2, (me // 2) % 2, me // 4
    px, py = me + 1 - 2 * x, me + 2 - 4 * y
    rows = tok1.shape[0]
    features = tok1.shape[1]

    vload = pltpu.make_async_copy(vec, v1, load)
    vload.start()
    groups, rights = [], []
    for layer, lefts, grads in (
        (1, (tok1, mix1, nor1, act1), (pro1, att1, gup1, flo1)),
        (0, (tok0, mix0, nor0, act0), (pro0, att0, gup0, flo0)),
    ):
        for spot in range(7):
            ref = lefts[min(spot, 3)]
            lanes = pl.ds(max(spot - 3, 0) * features, features)
            groups.append((layer, spot, ref.at[:, lanes]))
        spot = 0
        for ref in grads:
            width = ref.shape[1] // 2
            for item in range(width // CHUNK):
                rights.append((layer, spot, ref, width, item))
                spot += 1

    def right_here(entry):
        layer, spot, ref, width, item = entry
        lanes = pl.ds(pl.multiple_of(core * width + item * CHUNK, 128), CHUNK)
        return pltpu.make_async_copy(
            ref.at[:, lanes], g_buf.at[layer, spot, pl.ds(0, rows)], gl.at[layer, spot]
        )

    def right_there(entry):
        layer, spot, ref, width, item = entry
        lanes = pl.ds(pl.multiple_of((1 - core) * width + item * CHUNK, 128), CHUNK)
        return remote(
            ref.at[:, lanes], g_buf.at[layer, spot, pl.ds(rows, rows)],
            gs.at[layer, spot], gr.at[layer, spot], {"section": 1 - core},
        )

    def left_there(entry):
        layer, spot, ref = entry
        return remote(
            ref, land.at[layer, spot], ls.at[layer, spot], lr.at[layer, spot],
            {"section": 1 - core},
        )

    def stage_own(number):
        layer, spot, ref = groups[number]
        return pltpu.make_async_copy(ref, stage.at[number % 2, 0], sl.at[number % 2, 0])

    def stage_peer(number):
        layer, spot, ref = groups[number]
        return pltpu.make_async_copy(
            land.at[layer, spot], stage.at[number % 2, 1], sl.at[number % 2, 1]
        )

    def stage_start(number):
        if number < len(groups):
            stage_own(number).start()
            left_there(groups[number]).wait_recv()
            stage_peer(number).start()

    def stage_wait(number):
        stage_start(number + 1)
        stage_own(number).wait()
        stage_peer(number).wait()

    def turn(number):
        layer, spot, unused = groups[number]
        stage_wait(number)
        for side in (0, 1):
            lanes = pl.ds(side * rows, rows)
            for half in range(features // CHUNK):
                block = stage[number % 2, side, :, pl.ds(half * CHUNK, CHUNK)].T
                if spot < 3:
                    a_buf[layer, spot, pl.ds(8 * half, 8), :, lanes] = block.reshape(
                        8, BLOCK, rows
                    )
                else:
                    shaped = block.reshape(2, 4, BLOCK, rows)
                    for item in range(4):
                        a_buf[
                            layer, 3 + item, pl.ds(4 * (spot - 3) + 2 * half, 2), :, lanes
                        ] = shaped[:, item]

    barrier = pltpu.get_barrier_semaphore()
    for who in (px, py):
        pl.semaphore_signal(barrier, inc=1, device_id={"batch": who}, device_id_type=MESH)
    for step in (1, 2, 3):
        other = ((z + step) % 4) * 4 + me % 4
        for sec in (0, 1):
            pl.semaphore_signal(
                barrier, inc=1, device_id={"section": sec, "batch": other}, device_id_type=MESH
            )
    pl.semaphore_signal(barrier, inc=1, device_id={"section": 1 - core}, device_id_type=MESH)
    pl.semaphore_wait(barrier, 9)

    def remote(src, dst, send, recv, where):
        return pltpu.make_async_remote_copy(
            src_ref=src, dst_ref=dst, send_sem=send, recv_sem=recv,
            device_id=where, device_id_type=MESH,
        )

    def first(k, par):
        return remote(
            s1.at[k % 4], r1.at[k], s1s.at[k], r1s.at[k], {"batch": px if par == 0 else py}
        )

    def second(k, par):
        return remote(
            s2.at[k % 4], r2.at[k], s2s.at[k], r2s.at[k], {"batch": py if par == 0 else px}
        )

    def third(k, step, src_core):
        layer = 1 - k // COUNT
        zt = (z + step) % 4
        return remote(
            s3.at[k % 4, zt],
            r3.at[src_core, k % COUNT, z],
            s3s.at[k, step],
            r3s.at[src_core, k % COUNT, z],
            {"section": layer, "batch": zt * 4 + me % 4},
        )

    def third_in(k, step, src_core):
        layer = 1 - k // COUNT
        zs = (z + 4 - step) % 4
        return remote(
            s3.at[k % 4, zs],
            r3.at[src_core, k % COUNT, zs],
            s3s.at[k, step],
            r3s.at[src_core, k % COUNT, zs],
            {"section": 1 - core, "batch": me},
        )

    def product(k, left, rows):
        ch, layer = k % COUNT, 1 - k // COUNT
        right = g_buf[layer, chunk_right(ch)]
        return jnp.dot(
            left.reshape(rows, 2 * CHUNK), right, preferred_element_type=jnp.float32
        )

    def left_of(k):
        return a_buf.at[1 - k // COUNT, chunk_left(k % COUNT)]

    def ready(k, par):
        layer, ch = 1 - k // COUNT, k % COUNT

        @pl.when(ch <= 8)
        def _():
            mine = g_buf.at[layer, ch, pl.ds(0, rows)]
            pltpu.make_async_copy(mine, mine, gl.at[layer, ch]).wait()
            theirs = g_buf.at[layer, ch, pl.ds(rows, rows)]
            remote(
                theirs, theirs, gs.at[layer, ch], gr.at[layer, ch], {"section": 1 - core}
            ).wait_recv()

        for number, (owner, spot, unused) in enumerate(groups):
            when = (1 - owner) * COUNT + (0, 3, 4, 8, 8, 8, 8)[spot]
            if when % 2 == par:

                @pl.when(k == when)
                def _():
                    turn(number)

    def part_one(k, par):
        ready(k, par)
        ref = left_of(k).reshape(4, 2, 2, BLOCK, 2 * CHUNK)
        left = ref[:, :, 1 - x] if par == 0 else ref[:, 1 - y]
        out = product(k, left, 8 * BLOCK)
        s1[k % 4] = out.astype(jnp.bfloat16).reshape(4, 2, BLOCK, CHUNK)
        first(k, par).start()

    def part_two(k, par):
        first(k, par).wait()
        ref = left_of(k).reshape(4, 2, 2, BLOCK, 2 * CHUNK)
        if par == 0:
            left, came = ref[:, 1 - y, x], r1[k, :, 1 - y]
        else:
            left, came = ref[:, y, 1 - x], r1[k, :, 1 - x]
        out = product(k, left, 4 * BLOCK).reshape(4, BLOCK, CHUNK) + came.astype(jnp.float32)
        s2[k % 4] = out.astype(jnp.bfloat16)
        second(k, par).start()

    def part_three(k, par):
        second(k, par).wait()
        layer = 1 - k // COUNT
        ref = left_of(k).reshape(4, 2, 2, BLOCK, 2 * CHUNK)
        came = r1[k, :, y] if par == 0 else r1[k, :, x]
        out = (
            product(k, ref[:, y, x], 4 * BLOCK).reshape(4, BLOCK, CHUNK)
            + came.astype(jnp.float32)
            + r2[k].astype(jnp.float32)
        )
        s3[k % 4] = out.astype(jnp.bfloat16)
        for step in (1, 2, 3):
            third(k, step, core).start()

        @pl.when(core != layer)
        def _():
            third(k, 0, core).start()

        @pl.when(core == layer)
        def _():
            r3[core, k % COUNT, z] = s3[k % 4, z]

    def part_four(k):
        layer = 1 - k // COUNT
        ch = k % COUNT
        for step in (1, 2, 3):
            third(k, step, core).wait_send()

        @pl.when(core != layer)
        def _():
            third(k, 0, core).wait_send()

        @pl.when(core == layer)
        def _():
            for step in (1, 2, 3):
                for src_core in (0, 1):
                    third_in(k, step, src_core).wait_recv()
            third_in(k, 0, 1 - core).wait_recv()
            for src_core in (0, 1):
                total = jnp.sum(r3[src_core, ch].astype(jnp.float32), 0)

                @pl.when(ch < 3)
                def _():
                    start = pl.multiple_of(ch * CHUNK + src_core * 1152, 128)
                    o_qkv[:, pl.ds(start, CHUNK)] = total

                @pl.when(ch == 3)
                def _():
                    o_o[:, pl.ds(src_core * CHUNK, CHUNK)] = total

                @pl.when((ch >= 4) & (ch < 8))
                def _():
                    start = pl.multiple_of((ch - 4) * CHUNK + src_core * 1536, 128)
                    o_in[:, pl.ds(start, CHUNK)] = total

                @pl.when(ch >= 8)
                def _():
                    o_out[ch - 8, :, pl.ds(src_core * CHUNK, CHUNK)] = total

    def vec_first():
        return remote(v2.at[0], w1, vs.at[0], vr.at[0], {"batch": px})

    def vec_second():
        return remote(v2.at[1, :, :, 0], w2, vs.at[1], vr.at[1], {"batch": py})

    def vec_third(layer, step):
        zt = (z + step) % 4
        return remote(
            v3.at[layer, zt], w3.at[core, z], v3s.at[layer, step], v3r.at[core, z],
            {"section": layer, "batch": zt * 4 + me % 4},
        )

    def vec_third_in(src_core, step):
        zs = (z + 4 - step) % 4
        return remote(
            v3.at[core, zs], w3.at[src_core, zs], v3s.at[core, step], v3r.at[src_core, zs],
            {"section": 1 - core, "batch": me},
        )

    order = (0, 3, 4, 8, 8, 8, 8)
    for entry in groups:
        layer, spot = entry[:2]
        for right in rights:
            begin = right[1] == 0 if spot == 0 else order[spot - 1] < right[1] <= order[spot]
            if right[0] == layer and begin:
                right_here(right).start()
                right_there(right).start()
        left_there(entry).start()
    stage_start(0)
    vload.wait()
    v2[0] = v1[:, :, :, 1 - x]
    vec_first().start()

    steps = 2 * COUNT + 6

    def pair(kk, carry):
        for par in (0, 1):
            k = 2 * kk + par

            @pl.when(k < 2 * COUNT)
            def _():
                part_one(k, par)

            @pl.when((k >= 2) & (k < 2 * COUNT + 2))
            def _():
                part_two(k - 2, par)

            @pl.when((k >= 4) & (k < 2 * COUNT + 4))
            def _():
                part_three(k - 4, par)

            @pl.when(k >= 6)
            def _():
                part_four(k - 6)

        return carry

    lax.fori_loop(0, 3, pair, 0)
    vec_first().wait()
    v2[1, :, :, 0] = v1[:, :, 1 - y, x] + w1[:, :, 1 - y]
    vec_second().start()
    lax.fori_loop(3, 6, pair, 0)
    vec_second().wait()
    v3[...] = v1[:, :, y, x] + w1[:, :, y] + w2[...]
    for layer in (0, 1):
        for step in (1, 2, 3):
            vec_third(layer, step).start()

        @pl.when(core != layer)
        def _():
            vec_third(layer, 0).start()

        @pl.when(core == layer)
        def _():
            w3[core, z] = v3[layer, z]

    lax.fori_loop(6, steps // 2, pair, 0)
    for layer in (0, 1):
        for step in (1, 2, 3):
            vec_third(layer, step).wait_send()

        @pl.when(core != layer)
        def _():
            vec_third(layer, 0).wait_send()

    for step in (1, 2, 3):
        for src_core in (0, 1):
            vec_third_in(src_core, step).wait_recv()
    vec_third_in(1 - core, 0).wait_recv()
    o_vec[...] = jnp.sum(w3[...], (0, 1))
    for entry in rights:
        right_there(entry).wait_send()
    for entry in groups:
        left_there(entry).wait_send()


def reduce_all(packed, vec):
    low, full = jnp.bfloat16, jnp.float32
    steps = 2 * COUNT
    anywhere = pl.BlockSpec(memory_space=pl.ANY)
    vmem = pl.BlockSpec(memory_space=pltpu.VMEM)
    dma = pltpu.SemaphoreType.DMA
    return pl.pallas_call(
        reduce_kernel,
        out_shape=(
            jax.ShapeDtypeStruct((BLOCK, 2304), full),
            jax.ShapeDtypeStruct((BLOCK, 768), full),
            jax.ShapeDtypeStruct((BLOCK, 3072), full),
            jax.ShapeDtypeStruct((4, BLOCK, 768), full),
            jax.ShapeDtypeStruct((8, 128), full),
            jax.ShapeDtypeStruct((2, 7, CHUNK, 768), low),
        ),
        in_specs=[anywhere] * 17,
        out_specs=(vmem,) * 5 + (anywhere,),
        scratch_shapes=[
            pltpu.VMEM((2, 7, 16, BLOCK, 2 * CHUNK), low),
            pltpu.VMEM((2, 9, 2 * CHUNK, CHUNK), low),
            pltpu.VMEM((2, 2, CHUNK, 768), low),
            pltpu.VMEM((4, 4, 2, BLOCK, CHUNK), low),
            pltpu.VMEM((steps, 4, 2, BLOCK, CHUNK), low),
            pltpu.VMEM((4, 4, BLOCK, CHUNK), low),
            pltpu.VMEM((steps, 4, BLOCK, CHUNK), low),
            pltpu.VMEM((4, 4, BLOCK, CHUNK), low),
            pltpu.VMEM((2, COUNT, 4, BLOCK, CHUNK), low),
            pltpu.VMEM((2, 4, 2, 2, 8, 128), full),
            pltpu.VMEM((2, 4, 2, 8, 128), full),
            pltpu.VMEM((2, 2, 4, 2, 8, 128), full),
            pltpu.VMEM((2, 4, 8, 128), full),
            pltpu.VMEM((2, 4, 8, 128), full),
            pltpu.VMEM((2, 4, 8, 128), full),
            dma,
            dma((steps,)),
            dma((steps,)),
            dma((steps,)),
            dma((steps,)),
            dma((steps, 4)),
            dma((2, COUNT, 4)),
            dma((2,)),
            dma((2,)),
            dma((2, 4)),
            dma((2, 4)),
            dma((2, 9)),
            dma((2, 9)),
            dma((2, 9)),
            dma((2, 7)),
            dma((2, 7)),
            dma((2, 2)),
        ],
        compiler_params=pltpu.CompilerParams(
            collective_id=1, has_side_effects=True, vmem_limit_bytes=56 * 1024 * 1024
        ),
    )(*packed, vec)


def pack_vectors(par, parts):
    rows = (par[0:2], par[2], par[3], par[4], par[5:9], par[9], par[10], par[11])
    flat = jnp.concatenate([member.reshape(parts, -1) for member in rows], 1)
    flat = jnp.pad(flat, ((0, 0), (0, 1024 - flat.shape[1])))
    return flat.reshape(parts, 8, 128)


def gather_kernel(parts, own, out, send, recv, here):
    core = lax.axis_index("section")
    me = lax.axis_index("batch")
    mine = core * parts + me
    total = 2 * parts
    barrier = pltpu.get_barrier_semaphore()

    def greet(step, carry):
        other = (mine + step) % total
        pl.semaphore_signal(
            barrier, inc=1, device_id={"section": other // parts, "batch": other % parts},
            device_id_type=MESH,
        )
        return carry

    lax.fori_loop(1, total, greet, 0)
    pl.semaphore_wait(barrier, total - 1)

    def copy(step, slot):
        other = (mine + step) % total
        return pltpu.make_async_remote_copy(
            src_ref=own, dst_ref=out.at[slot], send_sem=send.at[step], recv_sem=recv.at[slot],
            device_id={"section": other // parts, "batch": other % parts}, device_id_type=MESH,
        )

    def start(step, carry):
        copy(step, mine).start()
        return carry

    lax.fori_loop(1, total, start, 0)
    local = pltpu.make_async_copy(own, out.at[mine], here)
    local.start()
    local.wait()

    def finish(step, carry):
        copy(step, mine).wait_send()
        copy(step, (mine + total - step) % total).wait_recv()
        return carry

    lax.fori_loop(1, total, finish, 0)


def gather_all(own, parts):
    vmem = pl.BlockSpec(memory_space=pltpu.VMEM)
    return pl.pallas_call(
        functools.partial(gather_kernel, parts),
        out_shape=jax.ShapeDtypeStruct((2 * parts,) + own.shape, own.dtype),
        in_specs=[vmem],
        out_specs=vmem,
        scratch_shapes=[
            pltpu.SemaphoreType.DMA((2 * parts,)),
            pltpu.SemaphoreType.DMA((2 * parts,)),
            pltpu.SemaphoreType.DMA,
        ],
        compiler_params=pltpu.CompilerParams(collective_id=0, has_side_effects=True),
    )(own)


def per_device(
    parts,
    x_query,
    x_passage,
    len_query,
    len_passage,
    positive,
    cot_query,
    cot_passage,
    *weights,
):
    core = lax.axis_index("section")
    on_first = core == 0
    own_set = [member[0] for member in weights]
    own = [own_set[item] for item in (0, 2, 6, 8)]
    other = [swap(member) for member in own]
    own_par = jnp.concatenate([own_set[item].reshape(-1) for item in (1, 3, 4, 5, 7, 9, 10, 11)])
    own_par = jnp.pad(own_par, (0, 16 * 768 - own_par.shape[0])).reshape(16, 768)
    other_par = swap(own_par)
    params = (
        jnp.where(on_first, own_par, other_par),
        jnp.where(on_first, other_par, own_par),
    )
    features = x_query.shape[2]
    half_q, half_p = x_query.shape[0] // 2, x_passage.shape[0] // 2
    split = half_q * QLEN

    def own_half(array):
        half = array.shape[0] // 2
        return lax.dynamic_slice_in_dim(array, core * half, half, 0)

    def rows_of(query, passage):
        return jnp.concatenate(
            [own_half(query).reshape(-1, features), own_half(passage).reshape(-1, features)], 0
        )

    query_lens, passage_lens = own_half(len_query), own_half(len_passage)
    rows0 = rows_of(x_query, x_passage)
    *kept0, rows1 = forward_layer(0, rows0, query_lens, passage_lens, params[0], own, other)
    *kept1, final = forward_layer(1, rows1, query_lens, passage_lens, params[1], own, other)

    def join(first, second):
        mine = jnp.where(on_first, first, second)
        came = swap(jnp.where(on_first, second, first))
        low, high = jnp.where(on_first, mine, came), jnp.where(on_first, came, mine)
        query = jnp.concatenate([low[:split], high[:split]], 0)
        passage = jnp.concatenate([low[split:], high[split:]], 0)
        return query.reshape(x_query.shape)[None], passage.reshape(x_passage.shape)[None]

    hidden_q, hidden_p = join(rows1, final)

    cls_own = jnp.concatenate(
        [
            final[:split].reshape(half_q, QLEN, features)[:, 0],
            final[split:].reshape(half_p, PLEN, features)[:, 0],
        ],
        0,
    )
    targets = lax.all_gather(positive, "batch", axis=0, tiled=True)
    count = half_q + half_p
    if parts == 16:
        flat = jnp.pad(cls_own.reshape(-1, 128), ((0, 2), (0, 0)))
        every = gather_all(flat, parts)[:, : count * features // 128]
        every = every.reshape(2, parts, count, features)
    else:
        every = lax.all_gather(cls_own, ("section", "batch"), axis=0, tiled=True)
        every = every.reshape(2, parts, count, features)
    every = every.transpose(1, 0, 2, 3)
    cls_query = every[:, :, :half_q].reshape(-1, features)
    cls_passage = every[:, :, half_q:].reshape(-1, features)
    score_scale = 2.0 / math.sqrt(features)
    logits = (
        jnp.einsum("qd,pd->qp", cls_query, cls_passage, preferred_element_type=jnp.float32)
        * score_scale
    )
    term_values, grad_logits = contrast(logits, targets)
    loss_value = jnp.mean(term_values)
    mine = lax.axis_index("batch") * 2 + core
    own_logits = lax.dynamic_slice_in_dim(grad_logits, mine * half_q, half_q, 0)
    grad_cls_q = (
        jnp.einsum("qp,pd->qd", own_logits, cls_passage, preferred_element_type=jnp.float32)
        * score_scale
    )
    own_columns = lax.dynamic_slice_in_dim(grad_logits, mine * half_p, half_p, 1)
    grad_cls_p = (
        jnp.einsum("qp,qd->pd", own_columns, cls_query, preferred_element_type=jnp.float32)
        * score_scale
    )
    rows_list = []
    for cot, lens, cls_grad, length in (
        (cot_query, query_lens, grad_cls_q, QLEN),
        (cot_passage, passage_lens, grad_cls_p, PLEN),
    ):
        block = own_half(cot).astype(jnp.float32)
        valid_mask = jnp.arange(length)[None, :] < lens[:, None]
        masked = jnp.where(valid_mask[:, :, None], block, 0.0)
        rows_list.append(masked.at[:, 0].add(cls_grad).reshape(-1, features))
    grad_out1 = jnp.concatenate(rows_list, 0)

    *rights1, grad1, vectors1 = backward_layer(1, grad_out1, params[1], own, other, kept1)
    grad_low = grad1.astype(jnp.bfloat16).astype(jnp.float32)
    *rights0, grad0, vectors0 = backward_layer(0, grad_low, params[0], own, other, kept0)
    lefts1 = (rows1, kept1[3], kept1[5], kept1[6])
    lefts0 = (rows0, kept0[3], kept0[5], kept0[6])
    grad_q, grad_p = join(grad0, grad1)

    if parts == 16:
        packed = [*lefts1, *rights1, *lefts0, *rights0]
        vec = jnp.stack([pack_vectors(vectors0, parts), pack_vectors(vectors1, parts)])
        d_qkv, d_o, d_in, d_out, d_vec, unused = reduce_all(packed, vec.reshape(2, 4, 2, 2, 8, 128))
        d_out = d_out.reshape(4 * BLOCK, 768)
        flat = d_vec.reshape(-1)
        small, at = [], 0
        for count in (2, 1, 1, 1, 4, 1, 1, 1):
            size = count * features // parts
            small.append(flat[at : at + size])
            at += size
    else:

        def total(first, second):
            kept = jnp.where(on_first, first, second)
            both = kept + swap(jnp.where(on_first, second, first))
            return lax.psum_scatter(both, "batch", scatter_dimension=0, tiled=True)

        def product(left, right):
            return jnp.einsum("rd,re->de", left, right, preferred_element_type=jnp.float32)

        d_qkv, d_o, d_in, d_out = (
            total(product(la, ra), product(lb, rb))
            for la, ra, lb, rb in zip(lefts0, rights0, lefts1, rights1)
        )
        sums = [
            (first.reshape(-1), second.reshape(-1))
            for first, second in zip(jnp.split(vectors0, 16), jnp.split(vectors1, 16))
        ]
        groups = ((0, 1), (2,), (3,), (4,), (5, 6, 7, 8), (9,), (10,), (11,))
        small = [
            total(
                jnp.concatenate([sums[item][0] for item in group]),
                jnp.concatenate([sums[item][1] for item in group]),
            )
            for group in groups
        ]
    d_b_qv, d_b_o, d_g_attn, d_c_attn, d_b_in, d_b_out, d_g_ffn, d_c_ffn = small
    outs = (
        d_qkv, d_b_qv, d_o, d_b_o, d_g_attn, d_c_attn, d_in, d_b_in, d_out, d_b_out, d_g_ffn,
        d_c_ffn,
    )
    return (hidden_q, hidden_p, grad_q, grad_p, loss_value) + tuple(item[None] for item in outs)


def solution(mesh):
    in_specs = (
        P("batch", None, None),
        P("batch", None, None),
        P("batch"),
        P("batch"),
        P("batch"),
        P("batch", None, None),
        P("batch", None, None),
        P("section", None, None),
        P("section", None),
        P("section", None, None),
        P("section", None),
        P("section", None),
        P("section", None),
        P("section", None, None),
        P("section", None),
        P("section", None, None),
        P("section", None),
        P("section", None),
        P("section", None),
    )
    out_specs = (
        P("section", "batch", None, None),
        P("section", "batch", None, None),
        P("section", "batch", None, None),
        P("section", "batch", None, None),
        P(),
        P("section", "batch", None),
        P("section", "batch"),
        P("section", "batch", None),
        P("section", "batch"),
        P("section", "batch"),
        P("section", "batch"),
        P("section", "batch", None),
        P("section", "batch"),
        P("section", "batch", None),
        P("section", "batch"),
        P("section", "batch"),
        P("section", "batch"),
    )
    return jax.shard_map(
        functools.partial(per_device, mesh.shape["batch"]), mesh=mesh, in_specs=in_specs, out_specs=out_specs, check_vma=False
    )
```

```python
import functools
import math

import jax
import jax.numpy as jnp
from jax import lax
from jax.experimental import pallas as pl
from jax.experimental.pallas import tpu as pltpu
from jax.sharding import PartitionSpec as P

HEADS = 12
QLEN = 32
PLEN = 256


norm_eps = 1e-05


def contrast(logits, targets):
    top_score = jnp.max(logits, -1, keepdims=True)
    log_total = top_score[:, 0] + jnp.log(jnp.sum(jnp.exp(logits - top_score), -1))
    chosen = targets[:, None] == jnp.arange(logits.shape[1])[None, :]
    term_values = log_total - jnp.sum(jnp.where(chosen, logits, 0.0), -1)
    grad_logits = (jnp.exp(logits - log_total[:, None]) - chosen.astype(jnp.float32)).astype(
        jnp.bfloat16
    )
    return (term_values, grad_logits)


MESH = pl.DeviceIdType.MESH
CHUNK = 384
COUNT = 12
BLOCK = 48


def swap(value):
    return lax.ppermute(value, "section", [(0, 1), (1, 0)])


LOW = jnp.bfloat16
FULL = jnp.float32
ROWS = 32
TILE = 768
LAST = (((1,), (1,)), ((), ()))
FIRST = (((0,), (0,)), ((), ()))


def dot(left, right):
    return jnp.dot(left, right, preferred_element_type=FULL)


def dot_last(left, right):
    return lax.dot_general(left, right, LAST, preferred_element_type=FULL)


def dot_first(left, right):
    return lax.dot_general(left, right, FIRST, preferred_element_type=FULL)


UNROLL = 4
PAIRS = 3


def over(count, body, unroll=1):
    def step(index, carry):
        body(index)
        return carry

    lax.fori_loop(0, count, step, 0, unroll=unroll)


def row_range(index):
    return pl.ds(pl.multiple_of(index * ROWS, ROWS), ROWS)


def lane_range(index, width):
    return pl.ds(pl.multiple_of(index * width, 128), width)


def moments(block):
    centred = block - jnp.mean(block, -1, keepdims=True)
    spread = jnp.mean(centred * centred, -1, keepdims=True)
    inverse = lax.rsqrt(spread + norm_eps)
    return centred * inverse, inverse


def gelu_pair(block):
    size = jnp.abs(block)
    t = 1.0 / (1.0 + (0.3275911 * math.sqrt(0.5)) * size)
    bell = jnp.exp(-0.5 * block * block)
    poly = 0.5 * 1.061405429
    for term in (-1.453152027, 1.421413741, -0.284496736, 0.254829592):
        poly = poly * t + 0.5 * term
    tail = poly * t * bell
    phi = jnp.where(block > 0, 1.0 - tail, tail)
    return block * phi, phi + block * bell * (1.0 / math.sqrt(2.0 * math.pi))


def head_lanes(rows, head):
    lane = lax.broadcasted_iota(jnp.int32, (rows, 128), 1)
    return (lane < 64) if head == 0 else (lane >= 64)


def query_mask(lens, start, count):
    rows = count * QLEN
    row = lax.broadcasted_iota(jnp.int32, (rows, rows), 0)
    column = lax.broadcasted_iota(jnp.int32, (rows, rows), 1)
    limit = jnp.zeros((rows, rows), jnp.int32)
    for item in range(count):
        limit = jnp.where(column // QLEN == item, item * QLEN + lens[start + item], limit)
    return (row // QLEN == column // QLEN) & (row < limit)


VMEM_LIMIT = 58 * 1024 * 1024


def remote(src, dst, send, recv, where):
    return pltpu.make_async_remote_copy(
        src_ref=src, dst_ref=dst, send_sem=send, recv_sem=recv,
        device_id=where, device_id_type=MESH,
    )


def greet(targets):
    barrier = pltpu.get_barrier_semaphore()
    for where in targets:
        pl.semaphore_signal(barrier, inc=1, device_id=where, device_id_type=MESH)
    pl.semaphore_wait(barrier, len(targets))


def forward_kernel(
    parts, x_query, x_passage, qlens, plens, positive, par, wqkv, wo, win, wout,
    o_tok, o_qkv, o_pq, o_pp, o_mixed, o_pre, o_normed, o_act, o_slope, o_ffn,
    l_qkv, l_o, l_in, l_out, hid_q, hid_p, gcls, loss,
    tok, out, bqkv, bo, bin_, bout, qkv, pq, pp, mixed, pre, normed_full, normed, up, act,
    slope, ffn, rows8, rows48, packed, every, stack,
    load, save, xload, wsend, wrecv, hsend, hrecv, hlocal, gsend, grecv, psend, precv,
):
    core = lax.axis_index("section")
    me = lax.axis_index("batch")
    peer = {"section": 1 - core}
    features = wo.shape[0]
    count_q, count_p = x_query.shape[0] // 2, x_passage.shape[0] // 2
    split = count_q * QLEN
    tall = count_p
    total = (count_q + count_p) * QLEN
    own = (wqkv, wo, win, wout)
    land = (l_qkv, l_o, l_in, l_out)
    buffers = (bqkv, bo, bin_, bout)

    gets = [
        pltpu.make_async_copy(
            x_query.at[pl.ds(core * count_q, count_q)], tok.at[0, pl.ds(0, count_q)], xload.at[0]
        ),
        pltpu.make_async_copy(
            x_passage.at[pl.ds(core * tall, tall)], tok.at[0, pl.ds(count_q, tall)], xload.at[1]
        ),
    ]
    for copy in gets:
        copy.start()

    def local(source, spot):
        return pltpu.make_async_copy(source[spot], buffers[spot], load.at[spot])

    def stash(spot):
        return pltpu.make_async_copy(buffers[spot], land[spot], load.at[4 + spot])

    def give_first(spot):
        return remote(own[spot], buffers[spot], wsend.at[spot], wrecv.at[spot], peer)

    def give_second(spot):
        return remote(own[spot], land[spot], wsend.at[spot], wrecv.at[spot], peer)

    others = [peer]
    if parts == 16:
        for step in range(1, parts):
            others.append({"batch": (me + step) % parts})

    @pl.when(core == 0)
    def _():
        for spot in range(4):
            local(own, spot).start()

    greet(others)

    @pl.when(core == 0)
    def _():
        for spot in range(4):
            give_first(spot).start()

    @pl.when(core == 1)
    def _():
        for spot in range(4):
            give_second(spot).start()

    def weight_first(spot):
        @pl.when(core == 0)
        def _():
            local(own, spot).wait()

        @pl.when(core == 1)
        def _():
            give_first(spot).wait_recv()
            stash(spot).start()

    def fetch_second(spot):
        @pl.when(core == 0)
        def _():
            give_second(spot).wait_recv()
            local(land, spot).start()

        @pl.when(core == 1)
        def _():
            stash(spot).wait()
            local(own, spot).start()

    def weight(layer, spot):
        if layer == 0:
            weight_first(spot)
        else:
            local(own, spot).wait()

    saves = {}

    def keep(name, layer, source, target):
        saves[name, layer] = pltpu.make_async_copy(
            source, target.at[layer], save.at[len(saves)]
        )
        saves[name, layer].start()

    def free(name, layer):
        if layer == 1:
            saves[name, 0].wait()

    for copy in gets:
        copy.wait()

    blocks = [(0, split, query_mask(qlens, core * count_q, count_q), pq, 0)]
    for item in range(count_p * QLEN // PLEN):
        row = lax.broadcasted_iota(jnp.int32, (PLEN, PLEN), 0)
        limit = plens[core * (count_p * QLEN // PLEN) + item]
        blocks.append((split + item * PLEN, PLEN, row < limit, pp, item * HEADS))

    for layer in (0, 1):
        base_row = layer * 16
        x = tok.at[layer].reshape(total, features)
        keep("tok", layer, x, o_tok)
        weight(layer, 0)
        free("qkv", layer)

        def project(tile):
            lanes = lane_range(tile, features)
            bias = jnp.where(tile == 0, par[base_row : base_row + 1], 0.0)
            bias = jnp.where(tile == 2, par[base_row + 1 : base_row + 2], bias)
            qkv[:, lanes] = (dot(x[...], bqkv[:, lanes]) + bias).astype(LOW)

        over(3, project)
        keep("qkv", layer, qkv, o_qkv)
        if layer == 1:
            fetch_second(3)
        for name in ("pq", "pp", "mixed"):
            free(name, layer)

        def attend(index):
            tasks = []
            for step in range(PAIRS):
                for lo, rows, mask, probs, base in blocks:
                    tasks.append((index * PAIRS + step, lo, rows, mask, probs, base))

            def part(task, offset):
                hp, lo, rows = task[:3]
                return qkv[pl.ds(lo, rows), pl.ds(pl.multiple_of(offset + hp * 128, 128), 128)]

            scores = []
            for task in tasks:
                queries, keys = part(task, 0) * LOW(0.125), part(task, features)
                for head in (0, 1):
                    masked = jnp.where(head_lanes(task[2], head), keys, LOW(0))
                    scores.append(dot_last(masked, queries))
            lows = []
            for spot, value in enumerate(scores):
                hp, lo, rows, mask, probs, base = tasks[spot // 2]
                value = jnp.where(mask, value, -1000000000.0)
                weights = jnp.exp(value - jnp.max(value, 0, keepdims=True))
                inverse = 1.0 / jnp.sum(weights, 0, keepdims=True)
                low = (weights * inverse).astype(LOW)
                probs[base + 2 * hp + spot % 2] = low
                lows.append(low)
            for spot, task in enumerate(tasks):
                hp, lo, rows = task[:3]
                values = part(task, 2 * features).T
                outs = [
                    dot(values[64 * head : 64 * head + 64], lows[2 * spot + head])
                    for head in (0, 1)
                ]
                both = jnp.concatenate(outs, 0).astype(LOW).T
                mixed[pl.ds(lo, rows), pl.ds(pl.multiple_of(hp * 128, 128), 128)] = both

        over(features // 128 // PAIRS, attend)
        keep("pq", layer, pq, o_pq)
        keep("pp", layer, pp, o_pp)
        keep("mixed", layer, mixed, o_mixed)
        weight(layer, 1)
        free("pre", layer)
        pre[...] = (
            dot(mixed[...], bo[...]) + x[...].astype(FULL) + par[base_row + 2 : base_row + 3]
        )
        keep("pre", layer, pre, o_pre)
        if layer == 0:
            fetch_second(0)
            fetch_second(1)
        free("normed", layer)

        def norm_one(index):
            rows = row_range(index)
            block = moments(pre[rows])[0] * par[base_row + 3 : base_row + 4]
            block = block + par[base_row + 4 : base_row + 5]
            normed_full[rows] = block
            normed[rows] = block.astype(LOW)

        over(total // ROWS, norm_one, UNROLL)
        keep("normed", layer, normed, o_normed)
        weight(layer, 2)
        free("act", layer)
        free("slope", layer)
        step_width = 256
        tiles = win.shape[1] // step_width

        def expand(tile):
            lanes = lane_range(tile, step_width)
            bias_lanes = lane_range(tile % 3, step_width)
            up[tile % 2] = (
                dot(normed[...], bin_[:, lanes])
                + par[pl.ds(base_row + 5 + tile // 3, 1), bias_lanes]
            )

        def bend(tile):
            lanes = lane_range(tile, step_width)
            for index in range(total // ROWS):
                rows = pl.ds(index * ROWS, ROWS)
                value, steep = gelu_pair(up[tile % 2, rows])
                act[rows, lanes] = value.astype(LOW)
                slope[rows, lanes] = steep.astype(LOW)

        expand(0)

        def grow(index):
            expand(index + 1)
            bend(index)

        over(tiles - 1, grow)
        bend(tiles - 1)
        keep("act", layer, act, o_act)
        keep("slope", layer, slope, o_slope)
        weight(layer, 3)
        free("ffn", layer)
        ffn[...] = (
            dot(act[...], bout[...]) + normed_full[...] + par[base_row + 9 : base_row + 10]
        )
        keep("ffn", layer, ffn, o_ffn)
        if layer == 0:
            fetch_second(2)
        target = tok.at[1] if layer == 0 else out
        flat = target.reshape(total, features)

        def norm_two(index):
            rows = row_range(index)
            block = moments(ffn[rows])[0] * par[base_row + 10 : base_row + 11]
            flat[rows] = (block + par[base_row + 11 : base_row + 12]).astype(LOW)

        over(total // ROWS, norm_two, UNROLL)
        sides = (
            (target.at[pl.ds(0, count_q)], hid_q.at[pl.ds(core * count_q, count_q)]),
            (target.at[pl.ds(count_q, tall)], hid_p.at[pl.ds(core * tall, tall)]),
        )

        @pl.when(core == layer)
        def _():
            for spot, (src, dst) in enumerate(sides):
                pltpu.make_async_copy(src, dst, hlocal.at[spot]).start()

        @pl.when(core != layer)
        def _():
            for spot, (src, dst) in enumerate(sides):
                remote(src, dst, hsend.at[spot], hrecv.at[spot], peer).start()

    if parts == 16:
        lead = [item * QLEN for item in range(count_q)] + [split]
        rows8[...] = jnp.zeros_like(rows8)
        for spot, row in enumerate(lead):
            rows8[spot : spot + 1] = flat[pl.ds(row, 16)].astype(FULL)[0:1]
        for tile in range(6):
            rows48[8 * tile : 8 * tile + 8] = rows8[:, 128 * tile : 128 * tile + 128]
        for item in range(count_q):
            value = positive[core * count_q + item].astype(FULL)
            rows48[8 * item + 5 : 8 * item + 6] = jnp.full((1, 128), value)
        packed[...] = rows48[...].astype(LOW)

        def share(step, slot):
            return remote(
                packed, every.at[core, slot], gsend.at[step], grecv.at[slot],
                {"batch": (me + step) % parts},
            )

        for step in range(1, parts):
            share(step, me).start()
        every[core, me] = packed[...]
        for step in range(1, parts):
            share(step, (me + parts - step) % parts).wait_recv()
        pass_on = remote(every.at[core], every.at[core], psend, precv, peer)
        pass_on.start()
        remote(every.at[core], every.at[1 - core], psend, precv, peer).wait_recv()
        pass_on.wait_send()
        for step in range(1, parts):
            share(step, me).wait_send()

        wide = 2 * parts * 8
        grid = every[...].astype(FULL).reshape(2 * parts, 48, 128)
        inner = lax.broadcasted_iota(jnp.int32, (2 * parts, 8, 128), 1)
        goal = jnp.zeros((2 * parts, 8, 128), FULL)
        for tile in range(6):
            block = grid[:, 8 * tile : 8 * tile + 8]
            stack[:, 128 * tile : 128 * tile + 128] = block.reshape(wide, 128).astype(LOW)
            if tile < count_q:
                found = jnp.sum(jnp.where(inner == 5, block, 0.0), 1, keepdims=True)
                goal = jnp.where(inner == tile, found, goal)
        row = lax.broadcasted_iota(jnp.int32, (wide, wide), 0)
        column = lax.broadcasted_iota(jnp.int32, (wide, wide), 1)
        scale = 2.0 / math.sqrt(features)
        logits = dot_last(stack[...], stack[...]) * scale
        device = column // 8
        passage = (device % parts) * 2 + device // parts
        is_passage = column % 8 == count_q
        is_query = row % 8 < count_q
        kept = jnp.where(is_passage, logits, -1e30)
        top = jnp.max(kept, -1, keepdims=True)
        log_total = top + jnp.log(jnp.sum(jnp.exp(kept - top), -1, keepdims=True))
        chosen = is_passage & (passage.astype(FULL) == goal.reshape(wide, 128)[:, 0:1])
        picked = jnp.sum(jnp.where(chosen, logits, 0.0), -1, keepdims=True)
        terms = jnp.where(is_query[:, 0:1], log_total - picked, 0.0)
        count = count_q * 2 * parts
        loss[...] = jnp.full((8, 128), jnp.sum(terms) / count)
        grads = jnp.exp(kept - log_total) - chosen.astype(FULL)
        grads = jnp.where(is_query & is_passage, grads, 0.0)
        up[0, 0:wide, 0:wide] = grads + grads.T
        mine = pl.multiple_of((core * parts + me) * 8, 8)
        picked_rows = up[0, pl.ds(mine, 8), 0:wide]
        gcls[...] = dot(picked_rows.astype(LOW), stack[...]) * scale

    for spot, (src, dst) in enumerate(sides):
        pltpu.make_async_copy(src, dst, hlocal.at[spot]).wait()
    theirs = (
        hid_q.at[pl.ds((1 - core) * count_q, count_q)],
        hid_p.at[pl.ds((1 - core) * tall, tall)],
    )
    for spot, (src, dst) in enumerate(zip((item[0] for item in sides), theirs)):
        remote(src, dst, hsend.at[spot], hrecv.at[spot], peer).wait()
    for spot in range(4):
        give_second(spot).wait_send()
    for (name, layer), copy in saves.items():
        if layer == 1:
            copy.wait()
    saves["tok", 0].wait()


def forward_both(parts, x_query, x_passage, qlens, plens, positive, par, own):
    queries, features = x_query.shape[0], x_query.shape[2]
    passages = x_passage.shape[0]
    total = (queries + passages) // 2 * QLEN
    wide = own[2].shape[1]
    split = queries // 2 * QLEN
    heads_p = HEADS * (passages // 2 * QLEN // PLEN)
    kept = [
        ((total, features), LOW),
        ((total, 3 * features), LOW),
        ((HEADS, split, split), LOW),
        ((heads_p, PLEN, PLEN), LOW),
        ((total, features), LOW),
        ((total, features), FULL),
        ((total, features), LOW),
        ((total, wide), LOW),
        ((total, wide), LOW),
        ((total, features), FULL),
    ]
    shape = jax.ShapeDtypeStruct
    anywhere = pl.BlockSpec(memory_space=pl.ANY)
    vmem = pl.BlockSpec(memory_space=pltpu.VMEM)
    smem = pl.BlockSpec(memory_space=pltpu.SMEM)
    dma = pltpu.SemaphoreType.DMA
    scratch = [
        pltpu.VMEM((2, total // QLEN, QLEN, features), LOW),
        pltpu.VMEM((total // QLEN, QLEN, features), LOW),
    ]
    scratch += [pltpu.VMEM(item.shape, item.dtype) for item in own]
    buffers = [pltpu.VMEM(size, kind) for size, kind in kept[1:]]
    scratch += buffers[:5]
    scratch += [pltpu.VMEM((total, features), FULL), buffers[5]]
    scratch += [pltpu.VMEM((2, total, 256), FULL)] + buffers[6:]
    scratch += [
        pltpu.VMEM((8, features), FULL),
        pltpu.VMEM((48, 128), FULL),
        pltpu.VMEM((48, 128), LOW),
        pltpu.VMEM((2, 16, 48, 128), LOW),
        pltpu.VMEM((256, features), LOW),
        dma((8,)),
        dma((20,)),
        dma((2,)),
        dma((4,)),
        dma((4,)),
        dma((2,)),
        dma((2,)),
        dma((2,)),
        dma((16,)),
        dma((16,)),
        dma,
        dma,
    ]
    return pl.pallas_call(
        functools.partial(forward_kernel, parts),
        out_shape=[shape((2,) + size, kind) for size, kind in kept]
        + [shape(item.shape, item.dtype) for item in own]
        + [
            shape(x_query.shape, LOW),
            shape(x_passage.shape, LOW),
            shape((8, features), FULL),
            shape((8, 128), FULL),
        ],
        in_specs=[anywhere, anywhere, smem, smem, smem, vmem] + [anywhere] * 4,
        out_specs=[anywhere] * 16 + [vmem] * 2,
        scratch_shapes=scratch,
        compiler_params=pltpu.CompilerParams(
            collective_id=2, has_side_effects=True, vmem_limit_bytes=VMEM_LIMIT
        ),
    )(x_query, x_passage, qlens, plens, positive, par, *own)


def fetch_weights(core, layer, own, other, buffers, sem):
    def copies(source):
        return [
            pltpu.make_async_copy(a, b, sem.at[spot])
            for spot, (a, b) in enumerate(zip(source, buffers))
        ]

    @pl.when(core == layer)
    def _():
        for copy in copies(own):
            copy.start()

    @pl.when(core != layer)
    def _():
        for copy in copies(other):
            copy.start()

    return copies(own)


def add_rows(block):
    return jnp.sum(block.reshape(ROWS // 8, 8, block.shape[1]), 0)


def norm_back(source, grad_of, gain, total, store):
    features = source.shape[1]
    zero = jnp.zeros((8, features), FULL)

    def step(index, carry):
        rows = row_range(index)
        grad = grad_of(rows)
        unit, inverse = moments(source[rows])
        scaled = grad * gain
        back = inverse * (
            scaled
            - jnp.mean(scaled, -1, keepdims=True)
            - unit * jnp.mean(scaled * unit, -1, keepdims=True)
        )
        store(rows, back)
        return (
            carry[0] + add_rows(grad * unit),
            carry[1] + add_rows(grad),
            carry[2] + add_rows(back),
        )

    sums = lax.fori_loop(0, total // ROWS, step, (zero, zero, zero), unroll=UNROLL)
    return [jnp.sum(item, 0, keepdims=True) for item in sums]


def backward_kernel(
    layer, grad, par, wqkv, wo, win, wout, xqkv, xo, xin, xout,
    h_qkv, h_pq, h_pp, h_pre, h_slope, h_ffn,
    o_proj, o_attn, o_up, o_flow, o_rows, o_par,
    bqkv, bo, bin_, bout, qkv, pq, pp, pre, slope, ffn,
    proj, attn_full, attn, steep, gup, flow_full, flow, gmixed,
    load, fetch, save,
):
    core = lax.axis_index("section")
    total, features = grad.shape
    split = pq.shape[1]
    count_p = pp.shape[0] // HEADS
    gets = [
        pltpu.make_async_copy(a, b, fetch.at[spot])
        for spot, (a, b) in enumerate(
            zip(
                (item.at[layer] for item in (h_ffn, h_slope, h_pre, h_qkv, h_pq, h_pp)),
                (ffn, slope, pre, qkv, pq, pp),
            )
        )
    ]
    gets[0].start()
    waits = fetch_weights(
        core, layer, (wout, win, wo, wqkv), (xout, xin, xo, xqkv), (bout, bin_, bo, bqkv), load
    )
    for copy in gets[1:]:
        copy.start()
    saves = []

    def keep(source, target):
        saves.append(pltpu.make_async_copy(source, target, save.at[len(saves)]))
        saves[-1].start()

    gets[0].wait()

    def store_ffn(rows, back):
        flow_full[rows] = back
        flow[rows] = back.astype(LOW)

    gain, shift, bias = norm_back(ffn, lambda rows: grad[rows], par[10:11], total, store_ffn)
    o_par[10:11], o_par[11:12], o_par[9:10] = gain, shift, bias
    keep(flow, o_flow)
    gets[1].wait()
    waits[0].wait()

    def shrink(tile):
        lanes = lane_range(tile, features)
        rows_of = pl.ds(pl.multiple_of(tile * features, 128), features)
        steep[...] = dot_last(flow[...], bout[rows_of])

        def bend(index, carry):
            rows = row_range(index)
            low = (steep[rows] * slope[rows, lanes].astype(FULL)).astype(LOW)
            gup[rows, lanes] = low
            return carry + add_rows(low.astype(FULL))

        sums = lax.fori_loop(0, total // ROWS, bend, jnp.zeros((8, features), FULL), unroll=2)
        o_par[pl.ds(5 + tile, 1)] = jnp.sum(sums, 0, keepdims=True)

    over(4, shrink)
    keep(gup, o_up)
    waits[1].wait()

    def widen(tile):
        rows_of = pl.ds(pl.multiple_of(tile * TILE, TILE), TILE)
        lanes = lane_range(tile, TILE)
        flow_full[:, lanes] += dot_last(gup[...], bin_[rows_of])

    over(features // TILE, widen)
    gets[2].wait()

    def store_attn(rows, back):
        attn_full[rows] = back
        attn[rows] = back.astype(LOW)

    gain, shift, bias = norm_back(pre, lambda rows: flow_full[rows], par[3:4], total, store_attn)
    o_par[3:4], o_par[4:5], o_par[2:3] = gain, shift, bias
    keep(attn, o_attn)
    waits[2].wait()

    def unmix(tile):
        rows_of = pl.ds(pl.multiple_of(tile * TILE, TILE), TILE)
        gmixed[:, lane_range(tile, TILE)] = dot_last(attn[...], bo[rows_of]).astype(LOW)

    over(features // TILE, unmix)
    for copy in gets[3:]:
        copy.wait()

    blocks = [(0, split, pq, 0)]
    for item in range(count_p):
        blocks.append((split + item * PLEN, PLEN, pp, item * HEADS))

    def attend(index):
        tasks = []
        for step in range(PAIRS):
            for block in blocks:
                tasks.append((index * PAIRS + step,) + block)

        def spot_of(task, offset):
            hp, lo, rows = task[:3]
            return (pl.ds(lo, rows), pl.ds(pl.multiple_of(offset + hp * 128, 128), 128))

        grads = []
        for task in tasks:
            values, back = qkv[spot_of(task, 2 * features)], gmixed[spot_of(task, 0)]
            for head in (0, 1):
                masked = jnp.where(head_lanes(task[2], head), values, LOW(0))
                grads.append(dot_last(masked, back))
        lows = []
        for spot, grad_probs in enumerate(grads):
            hp, lo, rows, probs, base = tasks[spot // 2]
            full = probs[base + 2 * hp + spot % 2].astype(FULL)
            inner = jnp.sum(grad_probs * full, 0, keepdims=True)
            lows.append((full * (grad_probs - inner)).astype(LOW))
        for spot, task in enumerate(tasks):
            hp, lo, rows, probs, base = task
            queries, keys = qkv[spot_of(task, 0)], qkv[spot_of(task, features)]
            back = gmixed[spot_of(task, 0)]
            turned = keys.T
            parts = []
            for head in (0, 1):
                grad_scores = lows[2 * spot + head]
                parts.append(
                    (
                        dot(turned[64 * head : 64 * head + 64], grad_scores) * 0.125,
                        dot(grad_scores, queries) * 0.125,
                        dot(probs[base + 2 * hp + head], back),
                    )
                )
            first = head_lanes(rows, 0)
            both = jnp.concatenate([parts[0][0], parts[1][0]], 0)
            proj[spot_of(task, 0)] = both.astype(LOW).T
            for item in (1, 2):
                both = jnp.where(first, parts[0][item], parts[1][item])
                proj[spot_of(task, item * features)] = both.astype(LOW)

    over(features // 128 // PAIRS, attend)
    keep(proj, o_proj)

    def bias_sums(index, carry):
        rows = row_range(index)
        return (
            carry[0] + add_rows(proj[rows, pl.ds(0, features)].astype(FULL)),
            carry[1] + add_rows(proj[rows, pl.ds(2 * features, features)].astype(FULL)),
        )

    zero = jnp.zeros((8, features), FULL)
    sums = lax.fori_loop(0, total // ROWS, bias_sums, (zero, zero))
    o_par[0:1] = jnp.sum(sums[0], 0, keepdims=True)
    o_par[1:2] = jnp.sum(sums[1], 0, keepdims=True)
    o_par[12:16] = jnp.zeros((4, features), FULL)
    waits[3].wait()

    def finish(tile):
        rows_of = pl.ds(pl.multiple_of(tile * TILE, TILE), TILE)
        lanes = lane_range(tile, TILE)
        o_rows[:, lanes] = attn_full[:, lanes] + dot_last(proj[...], bqkv[rows_of])

    over(features // TILE, finish)
    for copy in saves:
        copy.wait()


def backward_layer(layer, grad, par, own, other, kept):
    total, features = grad.shape
    wide = own[2].shape[1]
    h_tok, h_qkv, h_pq, h_pp, h_mixed, h_pre, h_normed, h_act, h_slope, h_ffn = kept
    held = (h_qkv, h_pq, h_pp, h_pre, h_slope, h_ffn)
    anywhere = pl.BlockSpec(memory_space=pl.ANY)
    vmem = pl.BlockSpec(memory_space=pltpu.VMEM)
    shape = jax.ShapeDtypeStruct
    scratch = [pltpu.VMEM(item.shape, item.dtype) for item in own]
    scratch += [pltpu.VMEM(item.shape[1:], item.dtype) for item in held]
    scratch += [
        pltpu.VMEM((total, 3 * features), LOW),
        pltpu.VMEM((total, features), FULL),
        pltpu.VMEM((total, features), LOW),
        pltpu.VMEM((total, features), FULL),
        pltpu.VMEM((total, wide), LOW),
        pltpu.VMEM((total, features), FULL),
        pltpu.VMEM((total, features), LOW),
        pltpu.VMEM((total, features), LOW),
        pltpu.SemaphoreType.DMA((4,)),
        pltpu.SemaphoreType.DMA((6,)),
        pltpu.SemaphoreType.DMA((4,)),
    ]
    return pl.pallas_call(
        functools.partial(backward_kernel, layer),
        out_shape=[
            shape((total, 3 * features), LOW),
            shape((total, features), LOW),
            shape((total, wide), LOW),
            shape((total, features), LOW),
            shape((total, features), FULL),
            shape((16, features), FULL),
        ],
        in_specs=[vmem, vmem] + [anywhere] * 14,
        out_specs=[anywhere] * 4 + [vmem] * 2,
        scratch_shapes=scratch,
        compiler_params=pltpu.CompilerParams(vmem_limit_bytes=VMEM_LIMIT),
    )(grad, par, *own, *other, *held)


def chunk_left(ch):
    return (ch >= 3).astype(jnp.int32) + (ch >= 4).astype(jnp.int32) + jnp.maximum(ch - 7, 0)


def chunk_right(ch):
    return jnp.minimum(ch, 8)


def reduce_kernel(
    tok, mix, nor, act, pro1, att1, gup1, flo1, pro0, att0, gup0, flo0, vec,
    o_qkv, o_o, o_in, o_out, o_vec, land,
    a_buf, g_buf, stage, s1, r1, s2, r2, s3, r3, v1, w1, v2, w2, v3, w3,
    load, s1s, r1s, s2s, r2s, s3s, r3s, vs, vr, v3s, v3r, gl, gs, gr, ls, lr, sl,
):
    core = lax.axis_index("section")
    me = lax.axis_index("batch")
    x, y, z = me % 2, (me // 2) % 2, me // 4
    px, py = me + 1 - 2 * x, me + 2 - 4 * y
    rows, features = tok.shape[1:]

    vload = pltpu.make_async_copy(vec, v1, load)
    vload.start()
    groups, rights = [], []
    for layer, grads in ((1, (pro1, att1, gup1, flo1)), (0, (pro0, att0, gup0, flo0))):
        for spot in range(7):
            ref = (tok, mix, nor, act)[min(spot, 3)]
            lanes = pl.ds(max(spot - 3, 0) * features, features)
            groups.append((layer, spot, ref.at[layer, :, lanes]))
        spot = 0
        for ref in grads:
            width = ref.shape[1] // 2
            for item in range(width // CHUNK):
                rights.append((layer, spot, ref, width, item))
                spot += 1

    def right_here(entry):
        layer, spot, ref, width, item = entry
        lanes = pl.ds(pl.multiple_of(core * width + item * CHUNK, 128), CHUNK)
        return pltpu.make_async_copy(
            ref.at[:, lanes], g_buf.at[layer, spot, pl.ds(0, rows)], gl.at[layer, spot]
        )

    def right_there(entry):
        layer, spot, ref, width, item = entry
        lanes = pl.ds(pl.multiple_of((1 - core) * width + item * CHUNK, 128), CHUNK)
        return remote(
            ref.at[:, lanes], g_buf.at[layer, spot, pl.ds(rows, rows)],
            gs.at[layer, spot], gr.at[layer, spot], {"section": 1 - core},
        )

    def left_there(entry):
        layer, spot, ref = entry
        return remote(
            ref, land.at[layer, spot], ls.at[layer, spot], lr.at[layer, spot],
            {"section": 1 - core},
        )

    def stage_own(number):
        layer, spot, ref = groups[number]
        return pltpu.make_async_copy(ref, stage.at[number % 2, 0], sl.at[number % 2, 0])

    def stage_peer(number):
        layer, spot, ref = groups[number]
        return pltpu.make_async_copy(
            land.at[layer, spot], stage.at[number % 2, 1], sl.at[number % 2, 1]
        )

    def stage_start(number):
        if number < len(groups):
            stage_own(number).start()
            left_there(groups[number]).wait_recv()
            stage_peer(number).start()

    def stage_wait(number):
        stage_start(number + 1)
        stage_own(number).wait()
        stage_peer(number).wait()

    def turn(number):
        layer, spot, unused = groups[number]
        stage_wait(number)
        for side in (0, 1):
            lanes = pl.ds(side * rows, rows)
            for half in range(features // CHUNK):
                block = stage[number % 2, side, :, pl.ds(half * CHUNK, CHUNK)].T
                if spot < 3:
                    a_buf[layer, spot, pl.ds(8 * half, 8), :, lanes] = block.reshape(
                        8, BLOCK, rows
                    )
                else:
                    shaped = block.reshape(2, 4, BLOCK, rows)
                    for item in range(4):
                        a_buf[
                            layer, 3 + item, pl.ds(4 * (spot - 3) + 2 * half, 2), :, lanes
                        ] = shaped[:, item]

    barrier = pltpu.get_barrier_semaphore()
    for who in (px, py):
        pl.semaphore_signal(barrier, inc=1, device_id={"batch": who}, device_id_type=MESH)
    for step in (1, 2, 3):
        other = ((z + step) % 4) * 4 + me % 4
        for sec in (0, 1):
            pl.semaphore_signal(
                barrier, inc=1, device_id={"section": sec, "batch": other}, device_id_type=MESH
            )
    pl.semaphore_signal(barrier, inc=1, device_id={"section": 1 - core}, device_id_type=MESH)
    pl.semaphore_wait(barrier, 9)

    def first(k, par):
        return remote(
            s1.at[k % 4], r1.at[k], s1s.at[k], r1s.at[k], {"batch": px if par == 0 else py}
        )

    def second(k, par):
        return remote(
            s2.at[k % 4], r2.at[k], s2s.at[k], r2s.at[k], {"batch": py if par == 0 else px}
        )

    def third(k, step, src_core):
        layer = 1 - k // COUNT
        zt = (z + step) % 4
        return remote(
            s3.at[k % 4, zt],
            r3.at[src_core, k % COUNT, z],
            s3s.at[k, step],
            r3s.at[src_core, k % COUNT, z],
            {"section": layer, "batch": zt * 4 + me % 4},
        )

    def third_in(k, step, src_core):
        layer = 1 - k // COUNT
        zs = (z + 4 - step) % 4
        return remote(
            s3.at[k % 4, zs],
            r3.at[src_core, k % COUNT, zs],
            s3s.at[k, step],
            r3s.at[src_core, k % COUNT, zs],
            {"section": 1 - core, "batch": me},
        )

    def product(k, left, rows):
        ch, layer = k % COUNT, 1 - k // COUNT
        right = g_buf[layer, chunk_right(ch)]
        return jnp.dot(
            left.reshape(rows, 2 * CHUNK), right, preferred_element_type=jnp.float32
        )

    def left_of(k):
        return a_buf.at[1 - k // COUNT, chunk_left(k % COUNT)]

    def ready(k, par):
        layer, ch = 1 - k // COUNT, k % COUNT

        @pl.when(ch <= 8)
        def _():
            mine = g_buf.at[layer, ch, pl.ds(0, rows)]
            pltpu.make_async_copy(mine, mine, gl.at[layer, ch]).wait()
            theirs = g_buf.at[layer, ch, pl.ds(rows, rows)]
            remote(
                theirs, theirs, gs.at[layer, ch], gr.at[layer, ch], {"section": 1 - core}
            ).wait_recv()

        for number, (owner, spot, unused) in enumerate(groups):
            when = (1 - owner) * COUNT + (0, 3, 4, 8, 8, 8, 8)[spot]
            if when % 2 == par:

                @pl.when(k == when)
                def _():
                    turn(number)

    def part_one(k, par):
        ready(k, par)
        ref = left_of(k).reshape(4, 2, 2, BLOCK, 2 * CHUNK)
        left = ref[:, :, 1 - x] if par == 0 else ref[:, 1 - y]
        out = product(k, left, 8 * BLOCK)
        s1[k % 4] = out.astype(jnp.bfloat16).reshape(4, 2, BLOCK, CHUNK)
        first(k, par).start()

    def part_two(k, par):
        first(k, par).wait()
        ref = left_of(k).reshape(4, 2, 2, BLOCK, 2 * CHUNK)
        if par == 0:
            left, came = ref[:, 1 - y, x], r1[k, :, 1 - y]
        else:
            left, came = ref[:, y, 1 - x], r1[k, :, 1 - x]
        out = product(k, left, 4 * BLOCK).reshape(4, BLOCK, CHUNK) + came.astype(jnp.float32)
        s2[k % 4] = out.astype(jnp.bfloat16)
        second(k, par).start()

    def part_three(k, par):
        second(k, par).wait()
        layer = 1 - k // COUNT
        ref = left_of(k).reshape(4, 2, 2, BLOCK, 2 * CHUNK)
        came = r1[k, :, y] if par == 0 else r1[k, :, x]
        out = (
            product(k, ref[:, y, x], 4 * BLOCK).reshape(4, BLOCK, CHUNK)
            + came.astype(jnp.float32)
            + r2[k].astype(jnp.float32)
        )
        s3[k % 4] = out.astype(jnp.bfloat16)
        for step in (1, 2, 3):
            third(k, step, core).start()

        @pl.when(core != layer)
        def _():
            third(k, 0, core).start()

        @pl.when(core == layer)
        def _():
            r3[core, k % COUNT, z] = s3[k % 4, z]

    def part_four(k):
        layer = 1 - k // COUNT
        ch = k % COUNT
        for step in (1, 2, 3):
            third(k, step, core).wait_send()

        @pl.when(core != layer)
        def _():
            third(k, 0, core).wait_send()

        @pl.when(core == layer)
        def _():
            for step in (1, 2, 3):
                for src_core in (0, 1):
                    third_in(k, step, src_core).wait_recv()
            third_in(k, 0, 1 - core).wait_recv()
            for src_core in (0, 1):
                total = jnp.sum(r3[src_core, ch].astype(jnp.float32), 0)

                @pl.when(ch < 3)
                def _():
                    start = pl.multiple_of(ch * CHUNK + src_core * 1152, 128)
                    o_qkv[:, pl.ds(start, CHUNK)] = total

                @pl.when(ch == 3)
                def _():
                    o_o[:, pl.ds(src_core * CHUNK, CHUNK)] = total

                @pl.when((ch >= 4) & (ch < 8))
                def _():
                    start = pl.multiple_of((ch - 4) * CHUNK + src_core * 1536, 128)
                    o_in[:, pl.ds(start, CHUNK)] = total

                @pl.when(ch >= 8)
                def _():
                    o_out[ch - 8, :, pl.ds(src_core * CHUNK, CHUNK)] = total

    def vec_first():
        return remote(v2.at[0], w1, vs.at[0], vr.at[0], {"batch": px})

    def vec_second():
        return remote(v2.at[1, :, :, 0], w2, vs.at[1], vr.at[1], {"batch": py})

    def vec_third(layer, step):
        zt = (z + step) % 4
        return remote(
            v3.at[layer, zt], w3.at[core, z], v3s.at[layer, step], v3r.at[core, z],
            {"section": layer, "batch": zt * 4 + me % 4},
        )

    def vec_third_in(src_core, step):
        zs = (z + 4 - step) % 4
        return remote(
            v3.at[core, zs], w3.at[src_core, zs], v3s.at[core, step], v3r.at[src_core, zs],
            {"section": 1 - core, "batch": me},
        )

    order = (0, 3, 4, 8, 8, 8, 8)
    for entry in groups:
        layer, spot = entry[:2]
        for right in rights:
            begin = right[1] == 0 if spot == 0 else order[spot - 1] < right[1] <= order[spot]
            if right[0] == layer and begin:
                right_here(right).start()
                right_there(right).start()
        left_there(entry).start()
    stage_start(0)
    vload.wait()
    v2[0] = v1[:, :, :, 1 - x]
    vec_first().start()

    steps = 2 * COUNT + 6

    def pair(kk, carry):
        for par in (0, 1):
            k = 2 * kk + par

            @pl.when(k < 2 * COUNT)
            def _():
                part_one(k, par)

            @pl.when((k >= 2) & (k < 2 * COUNT + 2))
            def _():
                part_two(k - 2, par)

            @pl.when((k >= 4) & (k < 2 * COUNT + 4))
            def _():
                part_three(k - 4, par)

            @pl.when(k >= 6)
            def _():
                part_four(k - 6)

        return carry

    lax.fori_loop(0, 3, pair, 0)
    vec_first().wait()
    v2[1, :, :, 0] = v1[:, :, 1 - y, x] + w1[:, :, 1 - y]
    vec_second().start()
    lax.fori_loop(3, 6, pair, 0)
    vec_second().wait()
    v3[...] = v1[:, :, y, x] + w1[:, :, y] + w2[...]
    for layer in (0, 1):
        for step in (1, 2, 3):
            vec_third(layer, step).start()

        @pl.when(core != layer)
        def _():
            vec_third(layer, 0).start()

        @pl.when(core == layer)
        def _():
            w3[core, z] = v3[layer, z]

    lax.fori_loop(6, steps // 2, pair, 0)
    for layer in (0, 1):
        for step in (1, 2, 3):
            vec_third(layer, step).wait_send()

        @pl.when(core != layer)
        def _():
            vec_third(layer, 0).wait_send()

    for step in (1, 2, 3):
        for src_core in (0, 1):
            vec_third_in(src_core, step).wait_recv()
    vec_third_in(1 - core, 0).wait_recv()
    o_vec[...] = jnp.sum(w3[...], (0, 1))
    for entry in rights:
        right_there(entry).wait_send()
    for entry in groups:
        left_there(entry).wait_send()


def reduce_all(packed, vec):
    low, full = jnp.bfloat16, jnp.float32
    steps = 2 * COUNT
    anywhere = pl.BlockSpec(memory_space=pl.ANY)
    vmem = pl.BlockSpec(memory_space=pltpu.VMEM)
    dma = pltpu.SemaphoreType.DMA
    return pl.pallas_call(
        reduce_kernel,
        out_shape=(
            jax.ShapeDtypeStruct((BLOCK, 2304), full),
            jax.ShapeDtypeStruct((BLOCK, 768), full),
            jax.ShapeDtypeStruct((BLOCK, 3072), full),
            jax.ShapeDtypeStruct((4, BLOCK, 768), full),
            jax.ShapeDtypeStruct((8, 128), full),
            jax.ShapeDtypeStruct((2, 7, CHUNK, 768), low),
        ),
        in_specs=[anywhere] * 13,
        out_specs=(vmem,) * 5 + (anywhere,),
        scratch_shapes=[
            pltpu.VMEM((2, 7, 16, BLOCK, 2 * CHUNK), low),
            pltpu.VMEM((2, 9, 2 * CHUNK, CHUNK), low),
            pltpu.VMEM((2, 2, CHUNK, 768), low),
            pltpu.VMEM((4, 4, 2, BLOCK, CHUNK), low),
            pltpu.VMEM((steps, 4, 2, BLOCK, CHUNK), low),
            pltpu.VMEM((4, 4, BLOCK, CHUNK), low),
            pltpu.VMEM((steps, 4, BLOCK, CHUNK), low),
            pltpu.VMEM((4, 4, BLOCK, CHUNK), low),
            pltpu.VMEM((2, COUNT, 4, BLOCK, CHUNK), low),
            pltpu.VMEM((2, 4, 2, 2, 8, 128), full),
            pltpu.VMEM((2, 4, 2, 8, 128), full),
            pltpu.VMEM((2, 2, 4, 2, 8, 128), full),
            pltpu.VMEM((2, 4, 8, 128), full),
            pltpu.VMEM((2, 4, 8, 128), full),
            pltpu.VMEM((2, 4, 8, 128), full),
            dma,
            dma((steps,)),
            dma((steps,)),
            dma((steps,)),
            dma((steps,)),
            dma((steps, 4)),
            dma((2, COUNT, 4)),
            dma((2,)),
            dma((2,)),
            dma((2, 4)),
            dma((2, 4)),
            dma((2, 9)),
            dma((2, 9)),
            dma((2, 9)),
            dma((2, 7)),
            dma((2, 7)),
            dma((2, 2)),
        ],
        compiler_params=pltpu.CompilerParams(
            collective_id=1, has_side_effects=True, vmem_limit_bytes=56 * 1024 * 1024
        ),
    )(*packed, vec)


def pack_vectors(par, parts):
    rows = (par[0:2], par[2], par[3], par[4], par[5:9], par[9], par[10], par[11])
    flat = jnp.concatenate([member.reshape(parts, -1) for member in rows], 1)
    flat = jnp.pad(flat, ((0, 0), (0, 1024 - flat.shape[1])))
    return flat.reshape(parts, 8, 128)


def per_device(
    parts,
    x_query,
    x_passage,
    len_query,
    len_passage,
    positive,
    cot_query,
    cot_passage,
    *weights,
):
    core = lax.axis_index("section")
    on_first = core == 0
    own_set = [member[0] for member in weights]
    own = [own_set[item] for item in (0, 2, 6, 8)]
    own_par = jnp.concatenate([own_set[item].reshape(-1) for item in (1, 3, 4, 5, 7, 9, 10, 11)])
    own_par = jnp.pad(own_par, (0, 16 * 768 - own_par.shape[0])).reshape(16, 768)
    other_par = swap(own_par)
    params = (
        jnp.where(on_first, own_par, other_par),
        jnp.where(on_first, other_par, own_par),
    )
    features = x_query.shape[2]
    half_q, half_p = x_query.shape[0] // 2, x_passage.shape[0] // 2
    split = half_q * QLEN

    def own_half(array):
        half = array.shape[0] // 2
        return lax.dynamic_slice_in_dim(array, core * half, half, 0)

    query_lens, passage_lens = own_half(len_query), own_half(len_passage)
    *kept, l_qkv, l_o, l_in, l_out, hidden_q, hidden_p, grad_cls, loss = forward_both(
        parts,
        x_query,
        x_passage.reshape(-1, QLEN, features),
        len_query,
        len_passage,
        positive,
        jnp.concatenate(params, 0),
        own,
    )
    other = (l_qkv, l_o, l_in, l_out)
    hidden_q, hidden_p = hidden_q[None], hidden_p.reshape(x_passage.shape)[None]
    if parts == 16:
        loss_value = loss[0, 0]
        grad_cls_q, grad_cls_p = grad_cls[:half_q], grad_cls[half_q : half_q + half_p]
    else:
        targets = lax.all_gather(positive, "batch", axis=0, tiled=True)
        own_q = hidden_q[0, :, 0]
        own_p = hidden_p[0, :, 0]
        last_q, last_p = (jnp.where(on_first, swap(item), item) for item in (own_q, own_p))
        cls_query = lax.all_gather(last_q, "batch", axis=0, tiled=True)
        cls_passage = lax.all_gather(last_p, "batch", axis=0, tiled=True)
        score_scale = 2.0 / math.sqrt(features)
        logits = (
            jnp.einsum("qd,pd->qp", cls_query, cls_passage, preferred_element_type=jnp.float32)
            * score_scale
        )
        term_values, grad_logits = contrast(logits, targets)
        loss_value = jnp.mean(term_values)
        mine = lax.axis_index("batch") * 2 + core
        own_logits = lax.dynamic_slice_in_dim(grad_logits, mine * half_q, half_q, 0)
        grad_cls_q = (
            jnp.einsum("qp,pd->qd", own_logits, cls_passage, preferred_element_type=jnp.float32)
            * score_scale
        )
        own_columns = lax.dynamic_slice_in_dim(grad_logits, mine * half_p, half_p, 1)
        grad_cls_p = (
            jnp.einsum("qp,qd->pd", own_columns, cls_query, preferred_element_type=jnp.float32)
            * score_scale
        )

    def join(first, second):
        mine = jnp.where(on_first, first, second)
        came = swap(jnp.where(on_first, second, first))
        low, high = jnp.where(on_first, mine, came), jnp.where(on_first, came, mine)
        query = jnp.concatenate([low[:split], high[:split]], 0)
        passage = jnp.concatenate([low[split:], high[split:]], 0)
        return query.reshape(x_query.shape)[None], passage.reshape(x_passage.shape)[None]

    rows_list = []
    for cot, lens, cls_grad, length in (
        (cot_query, query_lens, grad_cls_q, QLEN),
        (cot_passage, passage_lens, grad_cls_p, PLEN),
    ):
        block = own_half(cot).astype(jnp.float32)
        valid_mask = jnp.arange(length)[None, :] < lens[:, None]
        masked = jnp.where(valid_mask[:, :, None], block, 0.0)
        rows_list.append(masked.at[:, 0].add(cls_grad).reshape(-1, features))
    grad_out1 = jnp.concatenate(rows_list, 0)

    *rights1, grad1, vectors1 = backward_layer(1, grad_out1, params[1], own, other, kept)
    grad_low = grad1.astype(jnp.bfloat16).astype(jnp.float32)
    *rights0, grad0, vectors0 = backward_layer(0, grad_low, params[0], own, other, kept)
    grad_q, grad_p = join(grad0, grad1)

    if parts == 16:
        packed = [kept[item] for item in (0, 4, 6, 7)] + [*rights1, *rights0]
        vec = jnp.stack([pack_vectors(vectors0, parts), pack_vectors(vectors1, parts)])
        d_qkv, d_o, d_in, d_out, d_vec, unused = reduce_all(packed, vec.reshape(2, 4, 2, 2, 8, 128))
        d_out = d_out.reshape(4 * BLOCK, 768)
        flat = d_vec.reshape(-1)
        small, at = [], 0
        for count in (2, 1, 1, 1, 4, 1, 1, 1):
            size = count * features // parts
            small.append(flat[at : at + size])
            at += size
    else:

        lefts1, lefts0 = (
            [kept[item][layer] for item in (0, 4, 6, 7)] for layer in (1, 0)
        )

        def total(first, second):
            kept = jnp.where(on_first, first, second)
            both = kept + swap(jnp.where(on_first, second, first))
            return lax.psum_scatter(both, "batch", scatter_dimension=0, tiled=True)

        def product(left, right):
            return jnp.einsum("rd,re->de", left, right, preferred_element_type=jnp.float32)

        d_qkv, d_o, d_in, d_out = (
            total(product(la, ra), product(lb, rb))
            for la, ra, lb, rb in zip(lefts0, rights0, lefts1, rights1)
        )
        sums = [
            (first.reshape(-1), second.reshape(-1))
            for first, second in zip(jnp.split(vectors0, 16), jnp.split(vectors1, 16))
        ]
        groups = ((0, 1), (2,), (3,), (4,), (5, 6, 7, 8), (9,), (10,), (11,))
        small = [
            total(
                jnp.concatenate([sums[item][0] for item in group]),
                jnp.concatenate([sums[item][1] for item in group]),
            )
            for group in groups
        ]
    d_b_qv, d_b_o, d_g_attn, d_c_attn, d_b_in, d_b_out, d_g_ffn, d_c_ffn = small
    outs = (
        d_qkv, d_b_qv, d_o, d_b_o, d_g_attn, d_c_attn, d_in, d_b_in, d_out, d_b_out, d_g_ffn,
        d_c_ffn,
    )
    return (hidden_q, hidden_p, grad_q, grad_p, loss_value) + tuple(item[None] for item in outs)


def solution(mesh):
    in_specs = (
        P("batch", None, None),
        P("batch", None, None),
        P("batch"),
        P("batch"),
        P("batch"),
        P("batch", None, None),
        P("batch", None, None),
        P("section", None, None),
        P("section", None),
        P("section", None, None),
        P("section", None),
        P("section", None),
        P("section", None),
        P("section", None, None),
        P("section", None),
        P("section", None, None),
        P("section", None),
        P("section", None),
        P("section", None),
    )
    out_specs = (
        P("section", "batch", None, None),
        P("section", "batch", None, None),
        P("section", "batch", None, None),
        P("section", "batch", None, None),
        P(),
        P("section", "batch", None),
        P("section", "batch"),
        P("section", "batch", None),
        P("section", "batch"),
        P("section", "batch"),
        P("section", "batch"),
        P("section", "batch", None),
        P("section", "batch"),
        P("section", "batch", None),
        P("section", "batch"),
        P("section", "batch"),
        P("section", "batch"),
    )
    return jax.shard_map(
        functools.partial(per_device, mesh.shape["batch"]), mesh=mesh, in_specs=in_specs, out_specs=out_specs, check_vma=False
    )
```

```python
import functools
import math

import jax
import jax.numpy as jnp
from jax import lax
from jax.experimental import pallas as pl
from jax.experimental.pallas import tpu as pltpu
from jax.sharding import PartitionSpec as P

HEADS = 12
QLEN = 32
PLEN = 256


norm_eps = 1e-05


def contrast(logits, targets):
    top_score = jnp.max(logits, -1, keepdims=True)
    log_total = top_score[:, 0] + jnp.log(jnp.sum(jnp.exp(logits - top_score), -1))
    chosen = targets[:, None] == jnp.arange(logits.shape[1])[None, :]
    term_values = log_total - jnp.sum(jnp.where(chosen, logits, 0.0), -1)
    grad_logits = (jnp.exp(logits - log_total[:, None]) - chosen.astype(jnp.float32)).astype(
        jnp.bfloat16
    )
    return (term_values, grad_logits)


MESH = pl.DeviceIdType.MESH
CHUNK = 384
COUNT = 12
BLOCK = 48


def swap(value):
    return lax.ppermute(value, "section", [(0, 1), (1, 0)])


LOW = jnp.bfloat16
FULL = jnp.float32
ROWS = 32
TILE = 768
LAST = (((1,), (1,)), ((), ()))
FIRST = (((0,), (0,)), ((), ()))


def dot(left, right):
    return jnp.dot(left, right, preferred_element_type=FULL)


def dot_last(left, right):
    return lax.dot_general(left, right, LAST, preferred_element_type=FULL)


def dot_first(left, right):
    return lax.dot_general(left, right, FIRST, preferred_element_type=FULL)


UNROLL = 4
PAIRS = 3


def over(count, body, unroll=1):
    def step(index, carry):
        body(index)
        return carry

    lax.fori_loop(0, count, step, 0, unroll=unroll)


def row_range(index):
    return pl.ds(pl.multiple_of(index * ROWS, ROWS), ROWS)


def lane_range(index, width):
    return pl.ds(pl.multiple_of(index * width, 128), width)


def moments(block):
    centred = block - jnp.mean(block, -1, keepdims=True)
    spread = jnp.mean(centred * centred, -1, keepdims=True)
    inverse = lax.rsqrt(spread + norm_eps)
    return centred * inverse, inverse


def gelu_pair(block):
    size = jnp.abs(block)
    t = 1.0 / (1.0 + (0.3275911 * math.sqrt(0.5)) * size)
    bell = jnp.exp(-0.5 * block * block)
    poly = 0.5 * 1.061405429
    for term in (-1.453152027, 1.421413741, -0.284496736, 0.254829592):
        poly = poly * t + 0.5 * term
    tail = poly * t * bell
    phi = jnp.where(block > 0, 1.0 - tail, tail)
    return block * phi, phi + block * bell * (1.0 / math.sqrt(2.0 * math.pi))


def head_lanes(rows, head):
    lane = lax.broadcasted_iota(jnp.int32, (rows, 128), 1)
    return (lane < 64) if head == 0 else (lane >= 64)


def query_mask(lens, start, count):
    rows = count * QLEN
    row = lax.broadcasted_iota(jnp.int32, (rows, rows), 0)
    column = lax.broadcasted_iota(jnp.int32, (rows, rows), 1)
    limit = jnp.zeros((rows, rows), jnp.int32)
    for item in range(count):
        limit = jnp.where(column // QLEN == item, item * QLEN + lens[start + item], limit)
    return (row // QLEN == column // QLEN) & (row < limit)


VMEM_LIMIT = 58 * 1024 * 1024


def remote(src, dst, send, recv, where):
    return pltpu.make_async_remote_copy(
        src_ref=src, dst_ref=dst, send_sem=send, recv_sem=recv,
        device_id=where, device_id_type=MESH,
    )


def greet(targets):
    barrier = pltpu.get_barrier_semaphore()
    for where in targets:
        pl.semaphore_signal(barrier, inc=1, device_id=where, device_id_type=MESH)
    pl.semaphore_wait(barrier, len(targets))


def forward_kernel(
    parts, x_query, x_passage, qlens, plens, positive,
    b_qv, b_o, g_attn, c_attn, b_in, b_out, g_ffn, c_ffn, wqkv, wo, win, wout,
    o_left, o_qkv, o_pq, o_pp, o_pre, o_slope, o_ffn, both_par,
    l_qkv, l_o, l_in, l_out, hid_q, hid_p, gcls, loss,
    tok, out, bqkv, bo, bin_, bout, qkv, pq, pp, mixed, pre, normed_full, normed, up, act,
    slope, ffn, rows8, rows48, packed, every, stack,
    load, save, xload, parsend, parrecv, wsend, wrecv, hsend, hrecv, hlocal, gsend, grecv, psend, precv,
):
    core = lax.axis_index("section")
    me = lax.axis_index("batch")
    peer = {"section": 1 - core}
    features = wo.shape[0]
    count_q, count_p = x_query.shape[0] // 2, x_passage.shape[0] // 2
    split = count_q * QLEN
    tall = count_p
    total = (count_q + count_p) * QLEN
    own = (wqkv, wo, win, wout)
    land = (l_qkv, l_o, l_in, l_out)
    buffers = (bqkv, bo, bin_, bout)

    gets = [
        pltpu.make_async_copy(
            x_query.at[pl.ds(core * count_q, count_q)], tok.at[0, pl.ds(0, count_q)], xload.at[0]
        ),
        pltpu.make_async_copy(
            x_passage.at[pl.ds(core * tall, tall)], tok.at[0, pl.ds(count_q, tall)], xload.at[1]
        ),
    ]
    for copy in gets:
        copy.start()

    def local(source, spot):
        return pltpu.make_async_copy(source[spot], buffers[spot], load.at[spot])

    def stash(spot):
        return pltpu.make_async_copy(buffers[spot], land[spot], load.at[4 + spot])

    def give_first(spot):
        return remote(own[spot], buffers[spot], wsend.at[spot], wrecv.at[spot], peer)

    def give_second(spot):
        return remote(own[spot], land[spot], wsend.at[spot], wrecv.at[spot], peer)

    others = [peer]
    if parts == 16:
        for step in range(1, parts):
            others.append({"batch": (me + step) % parts})

    @pl.when(core == 0)
    def _():
        for spot in range(4):
            local(own, spot).start()

    vectors = (b_qv, b_o, g_attn, c_attn, b_in, b_out, g_ffn, c_ffn)
    spot = 0
    for ref in vectors:
        for item in range(ref.shape[1] // features):
            both_par[core, spot : spot + 1] = ref[:, item * features : (item + 1) * features]
            spot += 1
    both_par[core, spot:16] = jnp.zeros((16 - spot, features), FULL)
    greet(others)
    give_par = remote(both_par.at[core], both_par.at[core], parsend, parrecv, peer)
    give_par.start()

    @pl.when(core == 0)
    def _():
        for spot in range(4):
            give_first(spot).start()

    @pl.when(core == 1)
    def _():
        for spot in range(4):
            give_second(spot).start()

    def weight_first(spot):
        @pl.when(core == 0)
        def _():
            local(own, spot).wait()

        @pl.when(core == 1)
        def _():
            give_first(spot).wait_recv()
            stash(spot).start()

    def fetch_second(spot):
        @pl.when(core == 0)
        def _():
            give_second(spot).wait_recv()
            local(land, spot).start()

        @pl.when(core == 1)
        def _():
            stash(spot).wait()
            local(own, spot).start()

    def weight(layer, spot):
        if layer == 0:
            weight_first(spot)
        else:
            local(own, spot).wait()

    saves = {}

    def keep(name, layer, source, target):
        saves[name, layer] = pltpu.make_async_copy(
            source, target, save.at[len(saves)]
        )
        saves[name, layer].start()

    def free(name, layer):
        if layer == 1:
            saves[name, 0].wait()

    for copy in gets:
        copy.wait()

    remote(both_par.at[core], both_par.at[1 - core], parsend, parrecv, peer).wait_recv()
    blocks = [(0, split, query_mask(qlens, core * count_q, count_q), pq, 0)]
    for item in range(count_p * QLEN // PLEN):
        row = lax.broadcasted_iota(jnp.int32, (PLEN, PLEN), 0)
        limit = plens[core * (count_p * QLEN // PLEN) + item]
        blocks.append((split + item * PLEN, PLEN, row < limit, pp, item * HEADS))

    for layer in (0, 1):
        base_row = 0
        par = both_par.at[layer]
        x = tok.at[layer].reshape(total, features)
        keep("tok", layer, x, o_left.at[layer, 6])
        weight(layer, 0)
        free("qkv", layer)

        def project(tile):
            lanes = lane_range(tile, features)
            bias = jnp.where(tile == 0, par[base_row : base_row + 1], 0.0)
            bias = jnp.where(tile == 2, par[base_row + 1 : base_row + 2], bias)
            qkv[:, lanes] = (dot(x[...], bqkv[:, lanes]) + bias).astype(LOW)

        over(3, project)
        keep("qkv", layer, qkv, o_qkv.at[layer])
        if layer == 1:
            fetch_second(3)
        for name in ("pq", "pp", "mixed"):
            free(name, layer)

        def attend(index):
            tasks = []
            for step in range(PAIRS):
                for lo, rows, mask, probs, base in blocks:
                    tasks.append((index * PAIRS + step, lo, rows, mask, probs, base))

            def part(task, offset):
                hp, lo, rows = task[:3]
                return qkv[pl.ds(lo, rows), pl.ds(pl.multiple_of(offset + hp * 128, 128), 128)]

            scores = []
            for task in tasks:
                queries, keys = part(task, 0) * LOW(0.125), part(task, features)
                for head in (0, 1):
                    masked = jnp.where(head_lanes(task[2], head), keys, LOW(0))
                    scores.append(dot_last(masked, queries))
            lows = []
            for spot, value in enumerate(scores):
                hp, lo, rows, mask, probs, base = tasks[spot // 2]
                value = jnp.where(mask, value, -1000000000.0)
                weights = jnp.exp(value - jnp.max(value, 0, keepdims=True))
                inverse = 1.0 / jnp.sum(weights, 0, keepdims=True)
                low = (weights * inverse).astype(LOW)
                probs[base + 2 * hp + spot % 2] = low
                lows.append(low)
            for spot, task in enumerate(tasks):
                hp, lo, rows = task[:3]
                values = part(task, 2 * features).T
                outs = [
                    dot(values[64 * head : 64 * head + 64], lows[2 * spot + head])
                    for head in (0, 1)
                ]
                both = jnp.concatenate(outs, 0).astype(LOW).T
                mixed[pl.ds(lo, rows), pl.ds(pl.multiple_of(hp * 128, 128), 128)] = both

        over(features // 128 // PAIRS, attend)
        keep("pq", layer, pq, o_pq.at[layer])
        keep("pp", layer, pp, o_pp.at[layer])
        keep("mixed", layer, mixed, o_left.at[layer, 5])
        weight(layer, 1)
        free("pre", layer)
        pre[...] = (
            dot(mixed[...], bo[...]) + x[...].astype(FULL) + par[base_row + 2 : base_row + 3]
        )
        keep("pre", layer, pre, o_pre.at[layer])
        if layer == 0:
            fetch_second(0)
            fetch_second(1)
        free("normed", layer)

        def norm_one(index):
            rows = row_range(index)
            block = moments(pre[rows])[0] * par[base_row + 3 : base_row + 4]
            block = block + par[base_row + 4 : base_row + 5]
            normed_full[rows] = block
            normed[rows] = block.astype(LOW)

        over(total // ROWS, norm_one, UNROLL)
        keep("normed", layer, normed, o_left.at[layer, 4])
        weight(layer, 2)
        for item in range(4):
            free("act%d" % item, layer)
        free("slope", layer)
        step_width = 256
        tiles = win.shape[1] // step_width

        def expand(tile):
            lanes = lane_range(tile, step_width)
            bias_lanes = lane_range(tile % 3, step_width)
            up[tile % 2] = (
                dot(normed[...], bin_[:, lanes])
                + par[pl.ds(base_row + 5 + tile // 3, 1), bias_lanes]
            )

        def bend(tile):
            lanes = lane_range(tile, step_width)
            for index in range(total // ROWS):
                rows = pl.ds(index * ROWS, ROWS)
                value, steep = gelu_pair(up[tile % 2, rows])
                act[rows, lanes] = value.astype(LOW)
                slope[rows, lanes] = steep.astype(LOW)

        expand(0)

        def grow(index):
            expand(index + 1)
            bend(index)

        over(tiles - 1, grow)
        bend(tiles - 1)
        for item in range(4):
            lanes = pl.ds(item * features, features)
            keep("act%d" % item, layer, act.at[:, lanes], o_left.at[layer, item])
        keep("slope", layer, slope, o_slope.at[layer])
        weight(layer, 3)
        free("ffn", layer)
        ffn[...] = (
            dot(act[...], bout[...]) + normed_full[...] + par[base_row + 9 : base_row + 10]
        )
        keep("ffn", layer, ffn, o_ffn.at[layer])
        if layer == 0:
            fetch_second(2)
        target = tok.at[1] if layer == 0 else out
        flat = target.reshape(total, features)

        def norm_two(index):
            rows = row_range(index)
            block = moments(ffn[rows])[0] * par[base_row + 10 : base_row + 11]
            flat[rows] = (block + par[base_row + 11 : base_row + 12]).astype(LOW)

        over(total // ROWS, norm_two, UNROLL)
        sides = (
            (target.at[pl.ds(0, count_q)], hid_q.at[pl.ds(core * count_q, count_q)]),
            (target.at[pl.ds(count_q, tall)], hid_p.at[pl.ds(core * tall, tall)]),
        )

        @pl.when(core == layer)
        def _():
            for spot, (src, dst) in enumerate(sides):
                pltpu.make_async_copy(src, dst, hlocal.at[spot]).start()

        @pl.when(core != layer)
        def _():
            for spot, (src, dst) in enumerate(sides):
                remote(src, dst, hsend.at[spot], hrecv.at[spot], peer).start()

    if parts == 16:
        lead = [item * QLEN for item in range(count_q)] + [split]
        rows8[...] = jnp.zeros_like(rows8)
        for spot, row in enumerate(lead):
            rows8[spot : spot + 1] = flat[pl.ds(row, 16)].astype(FULL)[0:1]
        for tile in range(6):
            rows48[8 * tile : 8 * tile + 8] = rows8[:, 128 * tile : 128 * tile + 128]
        for item in range(count_q):
            value = positive[core * count_q + item].astype(FULL)
            rows48[8 * item + 5 : 8 * item + 6] = jnp.full((1, 128), value)
        packed[...] = rows48[...].astype(LOW)

        def share(step, slot):
            return remote(
                packed, every.at[core, slot], gsend.at[step], grecv.at[slot],
                {"batch": (me + step) % parts},
            )

        for step in range(1, parts):
            share(step, me).start()
        every[core, me] = packed[...]
        for step in range(1, parts):
            share(step, (me + parts - step) % parts).wait_recv()
        pass_on = remote(every.at[core], every.at[core], psend, precv, peer)
        pass_on.start()
        remote(every.at[core], every.at[1 - core], psend, precv, peer).wait_recv()
        pass_on.wait_send()
        for step in range(1, parts):
            share(step, me).wait_send()

        wide = 2 * parts * 8
        grid = every[...].astype(FULL).reshape(2 * parts, 48, 128)
        inner = lax.broadcasted_iota(jnp.int32, (2 * parts, 8, 128), 1)
        goal = jnp.zeros((2 * parts, 8, 128), FULL)
        for tile in range(6):
            block = grid[:, 8 * tile : 8 * tile + 8]
            stack[:, 128 * tile : 128 * tile + 128] = block.reshape(wide, 128).astype(LOW)
            if tile < count_q:
                found = jnp.sum(jnp.where(inner == 5, block, 0.0), 1, keepdims=True)
                goal = jnp.where(inner == tile, found, goal)
        row = lax.broadcasted_iota(jnp.int32, (wide, wide), 0)
        column = lax.broadcasted_iota(jnp.int32, (wide, wide), 1)
        scale = 2.0 / math.sqrt(features)
        logits = dot_last(stack[...], stack[...]) * scale
        device = column // 8
        passage = (device % parts) * 2 + device // parts
        is_passage = column % 8 == count_q
        is_query = row % 8 < count_q
        kept = jnp.where(is_passage, logits, -1e30)
        top = jnp.max(kept, -1, keepdims=True)
        log_total = top + jnp.log(jnp.sum(jnp.exp(kept - top), -1, keepdims=True))
        chosen = is_passage & (passage.astype(FULL) == goal.reshape(wide, 128)[:, 0:1])
        picked = jnp.sum(jnp.where(chosen, logits, 0.0), -1, keepdims=True)
        terms = jnp.where(is_query[:, 0:1], log_total - picked, 0.0)
        count = count_q * 2 * parts
        loss[...] = jnp.full((8, 128), jnp.sum(terms) / count)
        grads = jnp.exp(kept - log_total) - chosen.astype(FULL)
        grads = jnp.where(is_query & is_passage, grads, 0.0)
        up[0, 0:wide, 0:wide] = grads + grads.T
        mine = pl.multiple_of((core * parts + me) * 8, 8)
        picked_rows = up[0, pl.ds(mine, 8), 0:wide]
        gcls[...] = dot(picked_rows.astype(LOW), stack[...]) * scale

    for spot, (src, dst) in enumerate(sides):
        pltpu.make_async_copy(src, dst, hlocal.at[spot]).wait()
    theirs = (
        hid_q.at[pl.ds((1 - core) * count_q, count_q)],
        hid_p.at[pl.ds((1 - core) * tall, tall)],
    )
    for spot, (src, dst) in enumerate(zip((item[0] for item in sides), theirs)):
        remote(src, dst, hsend.at[spot], hrecv.at[spot], peer).wait()
    for spot in range(4):
        give_second(spot).wait_send()
    give_par.wait_send()
    for (name, layer), copy in saves.items():
        if layer == 1:
            copy.wait()
    saves["tok", 0].wait()


def forward_both(parts, x_query, x_passage, qlens, plens, positive, vectors, own):
    queries, features = x_query.shape[0], x_query.shape[2]
    passages = x_passage.shape[0]
    total = (queries + passages) // 2 * QLEN
    wide = own[2].shape[1]
    split = queries // 2 * QLEN
    heads_p = HEADS * (passages // 2 * QLEN // PLEN)
    kept = [
        ((7, total, features), LOW),
        ((total, 3 * features), LOW),
        ((HEADS, split, split), LOW),
        ((heads_p, PLEN, PLEN), LOW),
        ((total, features), FULL),
        ((total, wide), LOW),
        ((total, features), FULL),
        ((16, features), FULL),
    ]
    shape = jax.ShapeDtypeStruct
    anywhere = pl.BlockSpec(memory_space=pl.ANY)
    vmem = pl.BlockSpec(memory_space=pltpu.VMEM)
    smem = pl.BlockSpec(memory_space=pltpu.SMEM)
    dma = pltpu.SemaphoreType.DMA
    scratch = [
        pltpu.VMEM((2, total // QLEN, QLEN, features), LOW),
        pltpu.VMEM((total // QLEN, QLEN, features), LOW),
    ]
    scratch += [pltpu.VMEM(item.shape, item.dtype) for item in own]
    scratch += [pltpu.VMEM(size, kind) for size, kind in kept[1:4]]
    scratch += [
        pltpu.VMEM((total, features), LOW),
        pltpu.VMEM((total, features), FULL),
        pltpu.VMEM((total, features), FULL),
        pltpu.VMEM((total, features), LOW),
        pltpu.VMEM((2, total, 256), FULL),
        pltpu.VMEM((total, wide), LOW),
        pltpu.VMEM((total, wide), LOW),
        pltpu.VMEM((total, features), FULL),
    ]
    scratch += [
        pltpu.VMEM((8, features), FULL),
        pltpu.VMEM((48, 128), FULL),
        pltpu.VMEM((48, 128), LOW),
        pltpu.VMEM((2, 16, 48, 128), LOW),
        pltpu.VMEM((256, features), LOW),
        dma((8,)),
        dma((26,)),
        dma((2,)),
        dma,
        dma,
        dma((4,)),
        dma((4,)),
        dma((2,)),
        dma((2,)),
        dma((2,)),
        dma((16,)),
        dma((16,)),
        dma,
        dma,
    ]
    return pl.pallas_call(
        functools.partial(forward_kernel, parts),
        out_shape=[shape((2,) + size, kind) for size, kind in kept]
        + [shape(item.shape, item.dtype) for item in own]
        + [
            shape(x_query.shape, LOW),
            shape(x_passage.shape, LOW),
            shape((8, features), FULL),
            shape((8, 128), FULL),
        ],
        in_specs=[anywhere, anywhere, smem, smem, smem] + [vmem] * 8 + [anywhere] * 4,
        out_specs=[anywhere] * 7 + [vmem] + [anywhere] * 6 + [vmem] * 2,
        scratch_shapes=scratch,
        compiler_params=pltpu.CompilerParams(
            collective_id=2, has_side_effects=True, vmem_limit_bytes=VMEM_LIMIT
        ),
    )(x_query, x_passage, qlens, plens, positive, *vectors, *own)


def add_rows(block):
    return jnp.sum(block.reshape(block.shape[0] // 8, 8, block.shape[1]), 0)


def norm_back(source, grad_of, gain, total, store):
    features = source.shape[1]
    zero = jnp.zeros((8, features), FULL)

    def step(index, carry):
        rows = row_range(index)
        grad = grad_of(index)
        unit, inverse = moments(source[rows])
        scaled = grad * gain
        back = inverse * (
            scaled
            - jnp.mean(scaled, -1, keepdims=True)
            - unit * jnp.mean(scaled * unit, -1, keepdims=True)
        )
        store(rows, back)
        return (
            carry[0] + add_rows(grad * unit),
            carry[1] + add_rows(grad),
            carry[2] + add_rows(back),
        )

    sums = lax.fori_loop(0, total // ROWS, step, (zero, zero, zero), unroll=UNROLL)
    return [jnp.sum(item, 0, keepdims=True) for item in sums]


def left_index(ch):
    return (
        jnp.minimum(ch, 4) + (ch >= 8).astype(jnp.int32) + (ch >= 9).astype(jnp.int32)
    )


def right_index(ch):
    return jnp.maximum(ch - 3, 0)


def backward_kernel(parts, *refs):
    small = parts == 16
    refs = list(refs)

    def take(count):
        front = refs[:count]
        del refs[:count]
        return front

    cot_query, cot_passage, qlens, plens, gcls, par = take(6)
    own, land = take(4), take(4)
    left, h_qkv, h_pq, h_pp, h_pre, h_slope, h_ffn = take(7)
    if small:
        o_qkv, o_o, o_in, o_out, o_vec, o_gq, o_gp, land_a, land_g, own_g = take(10)
    else:
        vpar, o_gq, o_gp, f_pro, f_att, f_up, f_flo = take(7)
    buffers = take(4)
    bqkv, bo, bin_, bout = buffers
    qkv, pq, pp, source, slope, gsrc = take(6)
    attn_full, attn, steep, flow_full, flow, gmixed, grow = take(7)
    wload, fetch, cload, hsend, hrecv, hlocal, ksem = take(7)
    if small:
        vpar, a_buf, g_buf, stage, s1, r1, s2, r2, s3, r3 = take(10)
        va, ra, vb, rb, vc, rc, rz = take(7)
        s1s, r1s, s2s, r2s, s3s, r3s, vsend, vrecv, zsend, zrecv = take(10)
        gs, gr, ls, lr, sl, gl = take(6)

    core = lax.axis_index("section")
    me = lax.axis_index("batch")
    peer = {"section": 1 - core}
    features = gcls.shape[1]
    total = flow.shape[0]
    split = pq.shape[1]
    count_q, tall = cot_query.shape[0] // 2, cot_passage.shape[0] // 2
    heads_p = pp.shape[0]
    blocks_p = PLEN // QLEN

    def weight_copy(spot, source_set):
        return pltpu.make_async_copy(source_set[spot], buffers[spot], wload.at[spot])

    def weight_start(layer, spot):
        @pl.when(core == layer)
        def _():
            weight_copy(spot, own).start()

        @pl.when(core != layer)
        def _():
            weight_copy(spot, land).start()

    def weight_wait(spot):
        weight_copy(spot, own).wait()

    saved = ((h_ffn, source), (h_slope, slope), (h_pre, source), (h_qkv, qkv), (h_pq, pq), (h_pp, pp))

    def saved_copy(layer, spot):
        src, dst = saved[spot]
        return pltpu.make_async_copy(src.at[layer], dst, fetch.at[spot])

    cots = [
        pltpu.make_async_copy(
            cot_query.at[pl.ds(core * count_q, count_q)], gsrc.at[pl.ds(0, count_q)], cload.at[0]
        ),
        pltpu.make_async_copy(
            cot_passage.at[pl.ds(core * tall, tall)], gsrc.at[pl.ds(count_q, tall)], cload.at[1]
        ),
    ]
    saved_copy(1, 0).start()
    for copy in cots:
        copy.start()
    weight_start(1, 3)
    saved_copy(1, 1).start()

    widths = ((flow, 1), (slope, 4), (attn, 1), (qkv, 3))

    def pieces_of(slot):
        base = (0, 1, 5, 6)[slot]
        ref, count = widths[slot]
        return [(base + item, ref, ref.shape[1] // 2, item) for item in range(count)]

    def own_piece(layer, piece):
        spot, ref, width, item = piece
        lanes = pl.ds(pl.multiple_of(core * width + item * CHUNK, 128), CHUNK)
        return pltpu.make_async_copy(ref.at[:, lanes], own_g.at[layer, spot], ksem.at[spot])

    def peer_piece(layer, piece):
        spot, ref, width, item = piece
        lanes = pl.ds(pl.multiple_of((1 - core) * width + item * CHUNK, 128), CHUNK)
        return remote(
            ref.at[:, lanes], land_g.at[layer, spot], gs.at[layer, spot], gr.at[layer, spot], peer
        )

    def whole_piece(layer, slot):
        ref = widths[slot][0]
        target = (f_flo, f_up, f_att, f_pro)[slot]
        return pltpu.make_async_copy(ref, target.at[layer], ksem.at[slot])

    def give(layer, slot):
        if small:
            for piece in pieces_of(slot):
                peer_piece(layer, piece).start()
                own_piece(layer, piece).start()
        else:
            whole_piece(layer, slot).start()

    def given(layer, slot):
        if small:
            for piece in pieces_of(slot):
                peer_piece(layer, piece).wait_send()
                if slot > 0:
                    own_piece(layer, piece).wait()
                else:

                    @pl.when(layer == 0)
                    def _():
                        own_piece(layer, piece).wait()
        else:
            whole_piece(layer, slot).wait()

    def slot_zero(layer):
        saved_copy(layer, 0).wait()
        gains = par.at[layer]
        last = layer == 1

        def grad_of(index):
            block = gsrc[index].astype(FULL)
            beyond = jnp.maximum(index - count_q, 0)
            item = beyond // blocks_p
            query_limit = qlens[core * count_q + jnp.minimum(index, count_q - 1)]
            passage_limit = (
                plens[core * (tall // blocks_p) + item] - (beyond % blocks_p) * QLEN
            )
            limit = jnp.where(index < count_q, query_limit, passage_limit)
            limit = jnp.where(last, limit, QLEN)
            lead = jnp.where(index < count_q, index, count_q + item)
            starts = (index < count_q) | (beyond % blocks_p == 0)
            row = lax.broadcasted_iota(jnp.int32, block.shape, 0)
            block = jnp.where(row < limit, block, 0.0)
            extra = gcls[pl.ds(lead, 1)] * jnp.where(starts & last, 1.0, 0.0)
            return block + jnp.where(row == 0, extra, 0.0)

        def store(rows, back):
            flow_full[rows] = back
            flow[rows] = back.astype(LOW)

        gain, shift, bias = norm_back(source, grad_of, gains[10:11], total, store)
        sums = vpar.at[layer]
        sums[10:11], sums[11:12], sums[9:10] = gain, shift, bias
        give(layer, 0)
        saved_copy(layer, 2).start()

    width = 256
    tiles = bout.shape[0] // width

    def slot_one(layer):
        saved_copy(layer, 1).wait()
        weight_wait(3)
        sums = vpar.at[layer]

        def shrink(tile):
            rows_of = pl.ds(pl.multiple_of(tile * width, width), width)
            steep[tile % 2] = dot_last(flow[...], bout[rows_of])

        def bend(tile):
            lanes = lane_range(tile, width)
            acc = jnp.zeros((8, width), FULL)
            for index in range(total // ROWS):
                rows = pl.ds(index * ROWS, ROWS)
                low = (steep[tile % 2, rows] * slope[rows, lanes].astype(FULL)).astype(LOW)
                slope[rows, lanes] = low
                acc = acc + add_rows(low.astype(FULL))
            sums[pl.ds(5 + tile // 3, 1), lane_range(tile % 3, width)] = jnp.sum(
                acc, 0, keepdims=True
            )

        shrink(0)

        def both(index):
            shrink(index + 1)
            bend(index)

        over(tiles - 1, both)
        bend(tiles - 1)
        give(layer, 1)

        @pl.when(layer == 1)
        def _():
            weight_start(0, 3)

    def slot_two(layer):
        weight_wait(2)
        flow_full[...] += dot_last(slope[...], bin_[...])
        saved_copy(layer, 2).wait()
        gains, sums = par.at[layer], vpar.at[layer]

        def store(rows, back):
            attn_full[rows] = back
            attn[rows] = back.astype(LOW)

        gain, shift, bias = norm_back(
            source, lambda index: flow_full[row_range(index)], gains[3:4], total, store
        )
        sums[3:4], sums[4:5], sums[2:3] = gain, shift, bias
        give(layer, 2)
        weight_wait(1)
        gmixed[...] = dot_last(attn[...], bo[...]).astype(LOW)

        @pl.when(layer == 1)
        def _():
            weight_start(0, 2)
            weight_start(0, 1)
            saved_copy(0, 0).start()
            saved_copy(0, 1).start()

    blocks = [(0, split, pq, 0)]
    for item in range(heads_p // HEADS):
        blocks.append((split + item * PLEN, PLEN, pp, item * HEADS))

    def attend(index):
        tasks = []
        for step in range(PAIRS):
            for block in blocks:
                tasks.append((index * PAIRS + step,) + block)

        def spot_of(task, offset):
            hp, lo, rows = task[:3]
            return (pl.ds(lo, rows), pl.ds(pl.multiple_of(offset + hp * 128, 128), 128))

        grads = []
        for task in tasks:
            values, back = qkv[spot_of(task, 2 * features)], gmixed[spot_of(task, 0)]
            for head in (0, 1):
                masked = jnp.where(head_lanes(task[2], head), values, LOW(0))
                grads.append(dot_last(masked, back))
        lows = []
        for spot, grad_probs in enumerate(grads):
            hp, lo, rows, probs, base = tasks[spot // 2]
            full = probs[base + 2 * hp + spot % 2].astype(FULL)
            inner = jnp.sum(grad_probs * full, 0, keepdims=True)
            lows.append((full * (grad_probs - inner)).astype(LOW))
        for spot, task in enumerate(tasks):
            hp, lo, rows, probs, base = task
            queries, keys = qkv[spot_of(task, 0)], qkv[spot_of(task, features)]
            back = gmixed[spot_of(task, 0)]
            turned = keys.T
            outs = []
            for head in (0, 1):
                grad_scores = lows[2 * spot + head]
                outs.append(
                    (
                        dot(turned[64 * head : 64 * head + 64], grad_scores) * 0.125,
                        dot(grad_scores, queries) * 0.125,
                        dot(probs[base + 2 * hp + head], back),
                    )
                )
            first = head_lanes(rows, 0)
            both = jnp.concatenate([outs[0][0], outs[1][0]], 0)
            qkv[spot_of(task, 0)] = both.astype(LOW).T
            for item in (1, 2):
                both = jnp.where(first, outs[0][item], outs[1][item])
                qkv[spot_of(task, item * features)] = both.astype(LOW)

    def grads_here(spot):
        lo, count, target = ((0, count_q, o_gq), (count_q, tall, o_gp))[spot]
        return pltpu.make_async_copy(
            grow.at[pl.ds(lo, count)], target.at[pl.ds(core * count, count)], hlocal.at[spot]
        )

    def grads_there(spot):
        lo, count, target = ((0, count_q, o_gq), (count_q, tall, o_gp))[spot]
        return remote(
            grow.at[pl.ds(lo, count)],
            target.at[pl.ds(core * count, count)],
            hsend.at[spot],
            hrecv.at[spot],
            peer,
        )

    def slot_three(layer):
        for spot in (3, 4, 5):
            saved_copy(layer, spot).wait()
        over(features // 128 // PAIRS, attend)
        give(layer, 3)
        sums = vpar.at[layer]

        def bias_sums(index, carry):
            rows = row_range(index)
            return (
                carry[0] + add_rows(qkv[rows, pl.ds(0, features)].astype(FULL)),
                carry[1] + add_rows(qkv[rows, pl.ds(2 * features, features)].astype(FULL)),
            )

        zero = jnp.zeros((8, features), FULL)
        found = lax.fori_loop(0, total // ROWS, bias_sums, (zero, zero), unroll=2)
        sums[0:1] = jnp.sum(found[0], 0, keepdims=True)
        sums[1:2] = jnp.sum(found[1], 0, keepdims=True)
        sums[12:16] = jnp.zeros((4, features), FULL)
        weight_wait(0)
        rows_all = attn_full[...] + dot_last(qkv[...], bqkv[...])
        grow[...] = rows_all.reshape(grow.shape)
        gsrc[...] = rows_all.astype(LOW).reshape(gsrc.shape)

        @pl.when(core == layer)
        def _():
            for spot in (0, 1):
                grads_here(spot).start()

        @pl.when(core != layer)
        def _():
            for spot in (0, 1):
                grads_there(spot).start()

        @pl.when(layer == 1)
        def _():
            weight_start(0, 0)

    def grads_given(layer):
        @pl.when(core == layer)
        def _():
            for spot in (0, 1):
                grads_here(spot).wait()

        @pl.when(core != layer)
        def _():
            for spot in (0, 1):
                grads_there(spot).wait_send()

    slots = (slot_zero, slot_one, slot_two, slot_three)

    def reload(layer, slot):
        @pl.when(layer == 1)
        def _():
            if slot == 3:
                for spot in (3, 4, 5):
                    saved_copy(0, spot).start()

    def rest_of_loads():
        for spot in (2, 1, 0):
            weight_start(1, spot)
        for spot in (3, 4, 5):
            saved_copy(1, spot).start()

    def grads_came():
        lands = ((o_gq, count_q), (o_gp, tall))
        for spot, (target, count) in enumerate(lands):
            there = target.at[pl.ds((1 - core) * count, count)]
            remote(there, there, hsend.at[spot], hrecv.at[spot], peer).wait_recv()

    if not small:
        greet([peer])
        rest_of_loads()
        for copy in cots:
            copy.wait()
        for layer in (1, 0):
            for slot in range(4):
                slots[slot](layer)
                given(layer, slot)
                reload(layer, slot)
            grads_given(layer)
        grads_came()
        return

    x, y, z = me % 2, (me // 2) % 2, me // 4
    px, py = me + 1 - 2 * x, me + 2 - 4 * y
    targets = [{"batch": px}, {"batch": py}, peer]
    for step in (1, 2, 3):
        other = ((z + step) % 4) * 4 + me % 4
        targets += [{"section": sec, "batch": other} for sec in (0, 1)]
    greet(targets)

    def left_there(layer, spot):
        return remote(
            left.at[layer, spot], land_a.at[layer, spot], ls.at[layer, spot], lr.at[layer, spot],
            peer,
        )

    def stage_copy(number, side):
        layer, spot = 1 - number // 7, number % 7
        src = left if side == 0 else land_a
        return pltpu.make_async_copy(
            src.at[layer, spot], stage.at[number % 2, side], sl.at[number % 2, side]
        )

    def stage_start(number):
        stage_copy(number, 0).start()
        left_there(1 - number // 7, number % 7).wait_recv()
        stage_copy(number, 1).start()

    def turn(number, spot):
        for side in (0, 1):
            stage_copy(number, side).wait()
        for side in (0, 1):
            lanes = pl.ds(side * total, total)
            for half in range(features // CHUNK):
                block = stage[number % 2, side, :, pl.ds(half * CHUNK, CHUNK)].T
                if spot > 3:
                    a_buf[spot, pl.ds(2 * half, 2), :, :, :, lanes] = block.reshape(
                        2, 2, 2, BLOCK, total
                    )
                else:
                    shaped = block.reshape(2, 4, BLOCK, total)
                    for item in range(4):
                        a_buf[item, spot, half, :, :, lanes] = shaped[:, item]

        @pl.when(number + 2 < 14)
        def _():
            stage_start(number + 2)

    def right_copy(layer, spot, side):
        src = own_g if side == 0 else land_g
        return pltpu.make_async_copy(
            src.at[layer, spot], g_buf.at[spot, pl.ds(side * total, total)], gl.at[spot, side]
        )

    def right_start(k):
        ch = k % COUNT
        layer = 1 - k // COUNT

        @pl.when((k < 2 * COUNT) & ((ch == 0) | (ch >= 4)))
        def _():
            spot = right_index(ch)
            right_copy(layer, spot, 0).start()
            remote(
                own_g.at[layer, spot], land_g.at[layer, spot],
                gs.at[layer, spot], gr.at[layer, spot], peer,
            ).wait_recv()
            right_copy(layer, spot, 1).start()

    RING = 12

    def first(k, par_):
        return remote(
            s1.at[k % 4], r1.at[k % RING], s1s.at[k], r1s.at[k],
            {"batch": px if par_ == 0 else py},
        )

    def second(k, par_):
        return remote(
            s2.at[k % 4], r2.at[k % RING], s2s.at[k], r2s.at[k],
            {"batch": py if par_ == 0 else px},
        )

    def third(k, step):
        layer = 1 - k // COUNT
        zt = (z + step) % 4
        return remote(
            s3.at[k % 4, zt], r3.at[core, k % COUNT, z], s3s.at[k, step],
            r3s.at[core, k % COUNT, z], {"section": layer, "batch": zt * 4 + me % 4},
        )

    def third_in(k, step, src_core):
        zs = (z + 4 - step) % 4
        return remote(
            s3.at[k % 4, zs], r3.at[src_core, k % COUNT, zs], s3s.at[k, step],
            r3s.at[src_core, k % COUNT, zs], peer,
        )

    def product(k, block, rows):
        return dot(block.reshape(rows, 2 * total), g_buf[right_index(k % COUNT)])

    def left_of(k):
        return a_buf.at[left_index(k % COUNT)]

    def ready(k, par_):
        ch = k % COUNT

        @pl.when((ch == 0) | (ch >= 4))
        def _():
            for side in (0, 1):
                right_copy(0, right_index(ch), side).wait()

        base = (k // COUNT) * 7
        if par_ == 0:

            @pl.when(ch == 0)
            def _():
                for spot in range(4):
                    turn(base + spot, spot)

            for spot, at in ((4, 4), (5, 8)):

                @pl.when(ch == at)
                def _():
                    turn(base + spot, spot)
        else:

            @pl.when(ch == 9)
            def _():
                turn(base + 6, 6)

    def part_one(k, par_):
        ready(k, par_)
        ref = left_of(k)
        block = ref[:, :, 1 - x] if par_ == 0 else ref[:, 1 - y]
        s1[k % 4] = product(k, block, 8 * BLOCK).astype(LOW).reshape(4, 2, BLOCK, CHUNK)
        first(k, par_).start()

    def part_two(k, par_):
        first(k, par_).wait()
        ref = left_of(k)
        if par_ == 0:
            block, came = ref[:, 1 - y, x], r1[k % RING, :, 1 - y]
        else:
            block, came = ref[:, y, 1 - x], r1[k % RING, :, 1 - x]
        value = product(k, block, 4 * BLOCK).reshape(4, BLOCK, CHUNK) + came.astype(FULL)
        s2[k % 4] = value.astype(LOW)
        second(k, par_).start()

    def part_three(k, par_):
        second(k, par_).wait()
        layer = 1 - k // COUNT
        ref = left_of(k)
        came = r1[k % RING, :, y] if par_ == 0 else r1[k % RING, :, x]
        value = (
            product(k, ref[:, y, x], 4 * BLOCK).reshape(4, BLOCK, CHUNK)
            + came.astype(FULL)
            + r2[k % RING].astype(FULL)
        )
        s3[k % 4] = value.astype(LOW)
        for step in (1, 2, 3):
            third(k, step).start()

        @pl.when(core != layer)
        def _():
            third(k, 0).start()

        @pl.when(core == layer)
        def _():
            r3[core, k % COUNT, z] = s3[k % 4, z]

    def part_four(k):
        layer = 1 - k // COUNT
        ch = k % COUNT
        for step in (1, 2, 3):
            third(k, step).wait_send()

        @pl.when(core != layer)
        def _():
            third(k, 0).wait_send()

        @pl.when(core == layer)
        def _():
            for step in (1, 2, 3):
                for src_core in (0, 1):
                    third_in(k, step, src_core).wait_recv()
            third_in(k, 0, 1 - core).wait_recv()
            for src_core in (0, 1):
                value = jnp.sum(r3[src_core, ch].astype(FULL), 0)

                @pl.when(ch < 4)
                def _():
                    o_out[ch, :, pl.ds(src_core * CHUNK, CHUNK)] = value

                @pl.when((ch >= 4) & (ch < 8))
                def _():
                    start = pl.multiple_of((ch - 4) * CHUNK + src_core * 4 * CHUNK, 128)
                    o_in[:, pl.ds(start, CHUNK)] = value

                @pl.when(ch == 8)
                def _():
                    o_o[:, pl.ds(src_core * CHUNK, CHUNK)] = value

                @pl.when(ch >= 9)
                def _():
                    start = pl.multiple_of((ch - 9) * CHUNK + src_core * 3 * CHUNK, 128)
                    o_qkv[:, pl.ds(start, CHUNK)] = value

    vec_cross = remote(vpar.at[1 - core], ra, vsend.at[0], vrecv.at[0], peer)
    vec_x = remote(va, rb, vsend.at[1], vrecv.at[1], {"batch": px})
    vec_y = remote(vb, rc, vsend.at[2], vrecv.at[2], {"batch": py})

    def vec_z(step, slot):
        return remote(
            vc, rz.at[slot], zsend.at[step], zrecv.at[slot],
            {"batch": ((z + step) % 4) * 4 + me % 4},
        )

    steps = 2 * COUNT + 6

    def pair(turn_index, carry):
        kk = turn_index - 1
        layer = (kk < 3).astype(jnp.int32)

        for slot, (one, two) in enumerate(((0, 4), (1, 4), (2, 5), (3, 6))):

            @pl.when((kk == one) | (kk == two))
            def _():
                done = (kk == one).astype(jnp.int32)
                given(done, slot)
                reload(done, slot)
                if slot == 3:
                    grads_given(done)

        @pl.when(kk == 0)
        def _():
            for spot in (4, 5, 6):
                left_there(1, spot).start()

        @pl.when(kk == 2)
        def _():
            for spot in range(7):
                left_there(0, spot).start()

        @pl.when(kk == -1)
        def _():
            for spot in range(4):
                left_there(1, spot).start()
            rest_of_loads()
            for copy in cots:
                copy.wait()

        for par_ in (0, 1):
            k = 2 * kk + par_

            @pl.when((k >= 0) & (k < 2 * COUNT))
            def _():
                part_one(k, par_)

        for par_ in (0, 1):
            k = 2 * kk + par_

            @pl.when((k >= 2) & (k < 2 * COUNT + 2))
            def _():
                part_two(k - 2, par_)

            @pl.when((k >= 4) & (k < 2 * COUNT + 4))
            def _():
                part_three(k - 4, par_)

            @pl.when(k >= 6)
            def _():
                part_four(k - 6)

        for slot, (one, two) in enumerate(((-1, 3), (0, 3), (1, 4), (2, 5))):

            @pl.when((kk == one) | (kk == two))
            def _():
                slots[slot](layer)

        @pl.when(kk == -1)
        def _():
            stage_start(0)
            stage_start(1)
            own_piece(1, pieces_of(0)[0]).wait()

        @pl.when((kk >= -1) & (kk < COUNT - 1))
        def _():
            for par_ in (0, 1):
                right_start(2 * kk + 2 + par_)

        @pl.when(kk == 6)
        def _():
            vec_cross.start()

        @pl.when(kk == 7)
        def _():
            vec_cross.wait()
            va[...] = vpar[core] + ra[...]
            vec_x.start()

        @pl.when(kk == 8)
        def _():
            vec_x.wait()
            vb[...] = va[...] + rb[...]
            vec_y.start()

        @pl.when(kk == 9)
        def _():
            vec_y.wait()
            vc[...] = vb[...] + rc[...]
            for step in (1, 2, 3):
                vec_z(step, z).start()

        @pl.when(kk == 11)
        def _():
            for step in (1, 2, 3):
                vec_z(step, z).wait_send()
                vec_z(step, (z + 4 - step) % 4).wait_recv()
            rz[z] = vc[...]
            o_vec[...] = jnp.sum(rz[...], 0)

        return carry

    lax.fori_loop(0, steps // 2 + 1, pair, 0)
    grads_came()
    for layer in (0, 1):
        for spot in range(7):
            left_there(layer, spot).wait_send()


def backward_both(parts, cots, qlens, plens, gcls, par, own, land, kept):
    small = parts == 16
    cot_query, cot_passage = cots
    left, h_qkv, h_pq, h_pp, h_pre, h_slope, h_ffn = kept
    total, features = left.shape[2:]
    wide = own[2].shape[1]
    shape = jax.ShapeDtypeStruct
    anywhere = pl.BlockSpec(memory_space=pl.ANY)
    vmem = pl.BlockSpec(memory_space=pltpu.VMEM)
    smem = pl.BlockSpec(memory_space=pltpu.SMEM)
    dma = pltpu.SemaphoreType.DMA
    grads = [shape(cot_query.shape, FULL), shape(cot_passage.shape, FULL)]
    if small:
        out_shape = [
            shape((BLOCK, 3 * features), FULL),
            shape((BLOCK, features), FULL),
            shape((BLOCK, wide), FULL),
            shape((4, BLOCK, features), FULL),
            shape((16, features), FULL),
            *grads,
            shape((2, 7, total, features), LOW),
            shape((2, 9, total, CHUNK), LOW),
            shape((2, 9, total, CHUNK), LOW),
        ]
        out_specs = [vmem] * 5 + [anywhere] * 5
    else:
        out_shape = [
            shape((2, 16, features), FULL),
            *grads,
            shape((2, total, 3 * features), LOW),
            shape((2, total, features), LOW),
            shape((2, total, wide), LOW),
            shape((2, total, features), LOW),
        ]
        out_specs = [vmem] + [anywhere] * 6
    scratch = [pltpu.VMEM(item.shape, item.dtype) for item in own]
    scratch += [
        pltpu.VMEM(h_qkv.shape[1:], LOW),
        pltpu.VMEM(h_pq.shape[1:], LOW),
        pltpu.VMEM(h_pp.shape[1:], LOW),
        pltpu.VMEM((total, features), FULL),
        pltpu.VMEM((total, wide), LOW),
        pltpu.VMEM((total // QLEN, QLEN, features), LOW),
        pltpu.VMEM((total, features), FULL),
        pltpu.VMEM((total, features), LOW),
        pltpu.VMEM((2, total, 256), FULL),
        pltpu.VMEM((total, features), FULL),
        pltpu.VMEM((total, features), LOW),
        pltpu.VMEM((total, features), LOW),
        pltpu.VMEM((total // QLEN, QLEN, features), FULL),
        dma((4,)),
        dma((6,)),
        dma((2,)),
        dma((2,)),
        dma((2,)),
        dma((2,)),
        dma((9,)),
    ]
    if small:
        steps = 2 * COUNT
        vector = pltpu.VMEM((16, features), FULL)
        scratch += [
            pltpu.VMEM((2, 16, features), FULL),
            pltpu.VMEM((7, 4, 2, 2, BLOCK, 2 * total), LOW),
            pltpu.VMEM((9, 2 * total, CHUNK), LOW),
            pltpu.VMEM((2, 2, total, features), LOW),
            pltpu.VMEM((4, 4, 2, BLOCK, CHUNK), LOW),
            pltpu.VMEM((12, 4, 2, BLOCK, CHUNK), LOW),
            pltpu.VMEM((4, 4, BLOCK, CHUNK), LOW),
            pltpu.VMEM((12, 4, BLOCK, CHUNK), LOW),
            pltpu.VMEM((4, 4, BLOCK, CHUNK), LOW),
            pltpu.VMEM((2, COUNT, 4, BLOCK, CHUNK), LOW),
            *[vector] * 6,
            pltpu.VMEM((4, 16, features), FULL),
            dma((steps,)),
            dma((steps,)),
            dma((steps,)),
            dma((steps,)),
            dma((steps, 4)),
            dma((2, COUNT, 4)),
            dma((3,)),
            dma((3,)),
            dma((4,)),
            dma((4,)),
            dma((2, 9)),
            dma((2, 9)),
            dma((2, 7)),
            dma((2, 7)),
            dma((2, 2)),
            dma((9, 2)),
        ]
    return pl.pallas_call(
        functools.partial(backward_kernel, parts),
        out_shape=out_shape,
        in_specs=[anywhere, anywhere, smem, smem, vmem, vmem] + [anywhere] * 15,
        out_specs=out_specs,
        scratch_shapes=scratch,
        compiler_params=pltpu.CompilerParams(
            collective_id=1, has_side_effects=True, vmem_limit_bytes=60 * 1024 * 1024
        ),
    )(cot_query, cot_passage, qlens, plens, gcls, par, *own, *land, *kept)


def per_device(
    parts,
    x_query,
    x_passage,
    len_query,
    len_passage,
    positive,
    cot_query,
    cot_passage,
    *weights,
):
    core = lax.axis_index("section")
    on_first = core == 0
    own_set = [member[0] for member in weights]
    own = [own_set[item] for item in (0, 2, 6, 8)]
    vectors = [weights[item] for item in (1, 3, 4, 5, 7, 9, 10, 11)]
    features = x_query.shape[2]
    half_q, half_p = x_query.shape[0] // 2, x_passage.shape[0] // 2
    *kept, par, l_qkv, l_o, l_in, l_out, hidden_q, hidden_p, grad_cls, loss = forward_both(
        parts,
        x_query,
        x_passage.reshape(-1, QLEN, features),
        len_query,
        len_passage,
        positive,
        vectors,
        own,
    )
    other = (l_qkv, l_o, l_in, l_out)
    hidden_q, hidden_p = hidden_q[None], hidden_p.reshape(x_passage.shape)[None]
    if parts == 16:
        loss_value = loss[0, 0]
    else:
        targets = lax.all_gather(positive, "batch", axis=0, tiled=True)
        own_q = hidden_q[0, :, 0]
        own_p = hidden_p[0, :, 0]
        last_q, last_p = (jnp.where(on_first, swap(item), item) for item in (own_q, own_p))
        cls_query = lax.all_gather(last_q, "batch", axis=0, tiled=True)
        cls_passage = lax.all_gather(last_p, "batch", axis=0, tiled=True)
        score_scale = 2.0 / math.sqrt(features)
        logits = (
            jnp.einsum("qd,pd->qp", cls_query, cls_passage, preferred_element_type=jnp.float32)
            * score_scale
        )
        term_values, grad_logits = contrast(logits, targets)
        loss_value = jnp.mean(term_values)
        mine = lax.axis_index("batch") * 2 + core
        own_logits = lax.dynamic_slice_in_dim(grad_logits, mine * half_q, half_q, 0)
        grad_cls_q = (
            jnp.einsum("qp,pd->qd", own_logits, cls_passage, preferred_element_type=jnp.float32)
            * score_scale
        )
        own_columns = lax.dynamic_slice_in_dim(grad_logits, mine * half_p, half_p, 1)
        grad_cls_p = (
            jnp.einsum("qp,qd->pd", own_columns, cls_query, preferred_element_type=jnp.float32)
            * score_scale
        )
        grad_cls = jnp.concatenate([grad_cls_q, grad_cls_p], 0)
        grad_cls = jnp.pad(grad_cls, ((0, 8 - grad_cls.shape[0]), (0, 0)))

    outs = backward_both(
        parts,
        (cot_query, cot_passage.reshape(-1, QLEN, features)),
        len_query,
        len_passage,
        grad_cls,
        par,
        own,
        other,
        kept,
    )
    groups = ((0, 2), (2, 1), (3, 1), (4, 1), (5, 4), (9, 1), (10, 1), (11, 1))
    if parts == 16:
        d_qkv, d_o, d_in, d_out, d_vec, grad_q, grad_p = outs[:7]
        d_out = d_out.reshape(-1, features)
        batch = lax.axis_index("batch")
        small = []
        for at, count in groups:
            flat = d_vec[at : at + count].reshape(-1)
            size = flat.shape[0] // parts
            small.append(lax.dynamic_slice_in_dim(flat, batch * size, size, 0))
    else:
        sums, grad_q, grad_p, g_pro, g_att, g_up, g_flo = outs
        left = kept[0]

        def total(pair):
            kept_one = jnp.where(on_first, pair[0], pair[1])
            both = kept_one + swap(jnp.where(on_first, pair[1], pair[0]))
            return lax.psum_scatter(both, "batch", scatter_dimension=0, tiled=True)

        def product(first, second):
            return jnp.einsum("rd,re->de", first, second, preferred_element_type=jnp.float32)

        d_qkv, d_o, d_in = (
            total([product(left[layer, spot], right[layer]) for layer in (0, 1)])
            for spot, right in ((6, g_pro), (5, g_att), (4, g_up))
        )
        d_out = total(
            [
                jnp.concatenate([product(left[layer, spot], g_flo[layer]) for spot in range(4)], 0)
                for layer in (0, 1)
            ]
        )
        small = [
            total([sums[layer, at : at + count].reshape(-1) for layer in (0, 1)])
            for at, count in groups
        ]
    grad_q = grad_q[None]
    grad_p = grad_p.reshape(x_passage.shape)[None]
    d_b_qv, d_b_o, d_g_attn, d_c_attn, d_b_in, d_b_out, d_g_ffn, d_c_ffn = small
    outs = (
        d_qkv, d_b_qv, d_o, d_b_o, d_g_attn, d_c_attn, d_in, d_b_in, d_out, d_b_out, d_g_ffn,
        d_c_ffn,
    )
    return (hidden_q, hidden_p, grad_q, grad_p, loss_value) + tuple(item[None] for item in outs)


def solution(mesh):
    in_specs = (
        P("batch", None, None),
        P("batch", None, None),
        P("batch"),
        P("batch"),
        P("batch"),
        P("batch", None, None),
        P("batch", None, None),
        P("section", None, None),
        P("section", None),
        P("section", None, None),
        P("section", None),
        P("section", None),
        P("section", None),
        P("section", None, None),
        P("section", None),
        P("section", None, None),
        P("section", None),
        P("section", None),
        P("section", None),
    )
    out_specs = (
        P("section", "batch", None, None),
        P("section", "batch", None, None),
        P("section", "batch", None, None),
        P("section", "batch", None, None),
        P(),
        P("section", "batch", None),
        P("section", "batch"),
        P("section", "batch", None),
        P("section", "batch"),
        P("section", "batch"),
        P("section", "batch"),
        P("section", "batch", None),
        P("section", "batch"),
        P("section", "batch", None),
        P("section", "batch"),
        P("section", "batch"),
        P("section", "batch"),
    )
    return jax.shard_map(
        functools.partial(per_device, mesh.shape["batch"]), mesh=mesh, in_specs=in_specs, out_specs=out_specs, check_vma=False
    )
```

```python
import functools
import math

import jax
import jax.numpy as jnp
from jax import lax
from jax.experimental import pallas as pl
from jax.experimental.pallas import tpu as pltpu
from jax.sharding import PartitionSpec as P

HEADS = 12
QLEN = 32
PLEN = 256


norm_eps = 1e-05


def contrast(logits, targets):
    top_score = jnp.max(logits, -1, keepdims=True)
    log_total = top_score[:, 0] + jnp.log(jnp.sum(jnp.exp(logits - top_score), -1))
    chosen = targets[:, None] == jnp.arange(logits.shape[1])[None, :]
    term_values = log_total - jnp.sum(jnp.where(chosen, logits, 0.0), -1)
    grad_logits = (jnp.exp(logits - log_total[:, None]) - chosen.astype(jnp.float32)).astype(
        jnp.bfloat16
    )
    return (term_values, grad_logits)


MESH = pl.DeviceIdType.MESH
CHUNK = 384
COUNT = 12
BLOCK = 48


def swap(value):
    return lax.ppermute(value, "section", [(0, 1), (1, 0)])


LOW = jnp.bfloat16
FULL = jnp.float32
ROWS = 32
TILE = 768
LAST = (((1,), (1,)), ((), ()))
FIRST = (((0,), (0,)), ((), ()))


def dot(left, right):
    return jnp.dot(left, right, preferred_element_type=FULL)


def dot_last(left, right):
    return lax.dot_general(left, right, LAST, preferred_element_type=FULL)


def dot_first(left, right):
    return lax.dot_general(left, right, FIRST, preferred_element_type=FULL)


UNROLL = 4
PAIRS = 3


def over(count, body, unroll=1):
    def step(index, carry):
        body(index)
        return carry

    lax.fori_loop(0, count, step, 0, unroll=unroll)


def row_range(index):
    return pl.ds(pl.multiple_of(index * ROWS, ROWS), ROWS)


def lane_range(index, width):
    return pl.ds(pl.multiple_of(index * width, 128), width)


def moments(block):
    centred = block - jnp.mean(block, -1, keepdims=True)
    spread = jnp.mean(centred * centred, -1, keepdims=True)
    inverse = lax.rsqrt(spread + norm_eps)
    return centred * inverse, inverse


def gelu_pair(block):
    size = jnp.abs(block)
    t = 1.0 / (1.0 + (0.3275911 * math.sqrt(0.5)) * size)
    bell = jnp.exp(-0.5 * block * block)
    poly = 0.5 * 1.061405429
    for term in (-1.453152027, 1.421413741, -0.284496736, 0.254829592):
        poly = poly * t + 0.5 * term
    tail = poly * t * bell
    phi = jnp.where(block > 0, 1.0 - tail, tail)
    return block * phi, phi + block * bell * (1.0 / math.sqrt(2.0 * math.pi))


def head_lanes(rows, head):
    lane = lax.broadcasted_iota(jnp.int32, (rows, 128), 1)
    return (lane < 64) if head == 0 else (lane >= 64)


def query_mask(lens, start, count):
    rows = count * QLEN
    row = lax.broadcasted_iota(jnp.int32, (rows, rows), 0)
    column = lax.broadcasted_iota(jnp.int32, (rows, rows), 1)
    limit = jnp.zeros((rows, rows), jnp.int32)
    for item in range(count):
        limit = jnp.where(column // QLEN == item, item * QLEN + lens[start + item], limit)
    return (row // QLEN == column // QLEN) & (row < limit)


VMEM_LIMIT = 58 * 1024 * 1024


def remote(src, dst, send, recv, where):
    return pltpu.make_async_remote_copy(
        src_ref=src, dst_ref=dst, send_sem=send, recv_sem=recv,
        device_id=where, device_id_type=MESH,
    )


def greet(targets):
    barrier = pltpu.get_barrier_semaphore()
    for where in targets:
        pl.semaphore_signal(barrier, inc=1, device_id=where, device_id_type=MESH)
    pl.semaphore_wait(barrier, len(targets))


def forward_kernel(
    parts, x_query, x_passage, qlens, plens, positive,
    b_qv, b_o, g_attn, c_attn, b_in, b_out, g_ffn, c_ffn, wqkv, wo, win, wout,
    o_left, o_qkv, o_pq, o_pp, o_pre, o_slope, o_ffn, both_par,
    l_qkv, l_o, l_in, l_out, hid_q, hid_p, land_a, gcls, loss,
    tok, out, bqkv, bo, bin_, bout, qkv, pq, pp, mixed, pre, normed_full, normed, up, act,
    slope, ffn, rows8, rows48, packed, every, stack,
    load, save, xload, parsend, parrecv, wsend, wrecv, hsend, hrecv, hlocal, gsend, grecv, psend, precv, asend, arecv,
):
    core = lax.axis_index("section")
    me = lax.axis_index("batch")
    peer = {"section": 1 - core}
    features = wo.shape[0]
    count_q, count_p = x_query.shape[0] // 2, x_passage.shape[0] // 2
    split = count_q * QLEN
    tall = count_p
    total = (count_q + count_p) * QLEN
    own = (wqkv, wo, win, wout)
    land = (l_qkv, l_o, l_in, l_out)
    buffers = (bqkv, bo, bin_, bout)

    gets = [
        pltpu.make_async_copy(
            x_query.at[pl.ds(core * count_q, count_q)], tok.at[0, pl.ds(0, count_q)], xload.at[0]
        ),
        pltpu.make_async_copy(
            x_passage.at[pl.ds(core * tall, tall)], tok.at[0, pl.ds(count_q, tall)], xload.at[1]
        ),
    ]
    for copy in gets:
        copy.start()

    def local(source, spot):
        return pltpu.make_async_copy(source[spot], buffers[spot], load.at[spot])

    def stash(spot):
        return pltpu.make_async_copy(buffers[spot], land[spot], load.at[4 + spot])

    def give_first(spot):
        return remote(own[spot], buffers[spot], wsend.at[spot], wrecv.at[spot], peer)

    def give_second(spot):
        return remote(own[spot], land[spot], wsend.at[spot], wrecv.at[spot], peer)

    others = [peer]
    if parts == 16:
        for step in range(1, parts):
            others.append({"batch": (me + step) % parts})

    @pl.when(core == 0)
    def _():
        for spot in range(4):
            local(own, spot).start()

    vectors = (b_qv, b_o, g_attn, c_attn, b_in, b_out, g_ffn, c_ffn)
    spot = 0
    for ref in vectors:
        for item in range(ref.shape[1] // features):
            both_par[core, spot : spot + 1] = ref[:, item * features : (item + 1) * features]
            spot += 1
    both_par[core, spot:16] = jnp.zeros((16 - spot, features), FULL)
    greet(others)
    give_par = remote(both_par.at[core], both_par.at[core], parsend, parrecv, peer)
    give_par.start()

    @pl.when(core == 0)
    def _():
        for spot in range(4):
            give_first(spot).start()

    @pl.when(core == 1)
    def _():
        for spot in range(4):
            give_second(spot).start()

    def weight_first(spot):
        @pl.when(core == 0)
        def _():
            local(own, spot).wait()

        @pl.when(core == 1)
        def _():
            give_first(spot).wait_recv()
            stash(spot).start()

    def fetch_second(spot):
        @pl.when(core == 0)
        def _():
            give_second(spot).wait_recv()
            local(land, spot).start()

        @pl.when(core == 1)
        def _():
            stash(spot).wait()
            local(own, spot).start()

    def weight(layer, spot):
        if layer == 0:
            weight_first(spot)
        else:
            local(own, spot).wait()

    saves = {}

    def keep(name, layer, source, target):
        saves[name, layer] = pltpu.make_async_copy(
            source, target, save.at[len(saves)]
        )
        saves[name, layer].start()

    places = {"act0": 0, "act1": 1, "act2": 2, "act3": 3, "normed": 4, "mixed": 5, "tok": 6}

    def left_give(layer, spot, source):
        return remote(
            source, land_a.at[layer, spot], asend.at[layer, spot], arecv.at[layer, spot], peer
        )

    def keep_left(name, layer, source):
        keep(name, layer, source, o_left.at[layer, places[name]])
        if layer == 1:
            left_give(1, places[name], source).start()

    def free(name, layer):
        if layer == 1:
            saves[name, 0].wait()

    for copy in gets:
        copy.wait()

    remote(both_par.at[core], both_par.at[1 - core], parsend, parrecv, peer).wait_recv()
    blocks = [(0, split, query_mask(qlens, core * count_q, count_q), pq, 0)]
    for item in range(count_p * QLEN // PLEN):
        row = lax.broadcasted_iota(jnp.int32, (PLEN, PLEN), 0)
        limit = plens[core * (count_p * QLEN // PLEN) + item]
        blocks.append((split + item * PLEN, PLEN, row < limit, pp, item * HEADS))

    for layer in (0, 1):
        base_row = 0
        par = both_par.at[layer]
        x = tok.at[layer].reshape(total, features)
        keep_left("tok", layer, x)
        weight(layer, 0)
        free("qkv", layer)

        def project(tile):
            lanes = lane_range(tile, features)
            bias = jnp.where(tile == 0, par[base_row : base_row + 1], 0.0)
            bias = jnp.where(tile == 2, par[base_row + 1 : base_row + 2], bias)
            qkv[:, lanes] = (dot(x[...], bqkv[:, lanes]) + bias).astype(LOW)

        over(3, project)
        keep("qkv", layer, qkv, o_qkv.at[layer])
        if layer == 1:
            fetch_second(3)
            for name, spot in places.items():
                saves[name, 0].wait()
                left_give(0, spot, o_left.at[0, spot]).start()
        for name in ("pq", "pp"):
            free(name, layer)

        def attend(index):
            tasks = []
            for step in range(PAIRS):
                for lo, rows, mask, probs, base in blocks:
                    tasks.append((index * PAIRS + step, lo, rows, mask, probs, base))

            def part(task, offset):
                hp, lo, rows = task[:3]
                return qkv[pl.ds(lo, rows), pl.ds(pl.multiple_of(offset + hp * 128, 128), 128)]

            scores = []
            for task in tasks:
                queries, keys = part(task, 0) * LOW(0.125), part(task, features)
                for head in (0, 1):
                    masked = jnp.where(head_lanes(task[2], head), keys, LOW(0))
                    scores.append(dot_last(masked, queries))
            lows = []
            for spot, value in enumerate(scores):
                hp, lo, rows, mask, probs, base = tasks[spot // 2]
                value = jnp.where(mask, value, -1000000000.0)
                weights = jnp.exp(value - jnp.max(value, 0, keepdims=True))
                inverse = 1.0 / jnp.sum(weights, 0, keepdims=True)
                low = (weights * inverse).astype(LOW)
                probs[base + 2 * hp + spot % 2] = low
                lows.append(low)
            for spot, task in enumerate(tasks):
                hp, lo, rows = task[:3]
                values = part(task, 2 * features).T
                outs = [
                    dot(values[64 * head : 64 * head + 64], lows[2 * spot + head])
                    for head in (0, 1)
                ]
                both = jnp.concatenate(outs, 0).astype(LOW).T
                mixed[pl.ds(lo, rows), pl.ds(pl.multiple_of(hp * 128, 128), 128)] = both

        over(features // 128 // PAIRS, attend)
        keep("pq", layer, pq, o_pq.at[layer])
        keep("pp", layer, pp, o_pp.at[layer])
        keep_left("mixed", layer, mixed)
        weight(layer, 1)
        free("pre", layer)
        pre[...] = (
            dot(mixed[...], bo[...]) + x[...].astype(FULL) + par[base_row + 2 : base_row + 3]
        )
        keep("pre", layer, pre, o_pre.at[layer])
        if layer == 0:
            fetch_second(0)
            fetch_second(1)

        def norm_one(index):
            rows = row_range(index)
            block = moments(pre[rows])[0] * par[base_row + 3 : base_row + 4]
            block = block + par[base_row + 4 : base_row + 5]
            normed_full[rows] = block
            normed[rows] = block.astype(LOW)

        over(total // ROWS, norm_one, UNROLL)
        keep_left("normed", layer, normed)
        weight(layer, 2)
        free("slope", layer)
        step_width = 256
        tiles = win.shape[1] // step_width

        def expand(tile):
            lanes = lane_range(tile, step_width)
            bias_lanes = lane_range(tile % 3, step_width)
            up[tile % 2] = (
                dot(normed[...], bin_[:, lanes])
                + par[pl.ds(base_row + 5 + tile // 3, 1), bias_lanes]
            )

        def bend(tile):
            lanes = lane_range(tile, step_width)
            for index in range(total // ROWS):
                rows = pl.ds(index * ROWS, ROWS)
                value, steep = gelu_pair(up[tile % 2, rows])
                act[rows, lanes] = value.astype(LOW)
                slope[rows, lanes] = steep.astype(LOW)

        expand(0)

        def grow(index):
            expand(index + 1)
            bend(index)

        over(tiles - 1, grow)
        bend(tiles - 1)
        for item in range(4):
            lanes = pl.ds(item * features, features)
            keep_left("act%d" % item, layer, act.at[:, lanes])
        keep("slope", layer, slope, o_slope.at[layer])
        weight(layer, 3)
        free("ffn", layer)
        ffn[...] = (
            dot(act[...], bout[...]) + normed_full[...] + par[base_row + 9 : base_row + 10]
        )
        keep("ffn", layer, ffn, o_ffn.at[layer])
        if layer == 0:
            fetch_second(2)
        target = tok.at[1] if layer == 0 else out
        flat = target.reshape(total, features)

        def norm_two(index):
            rows = row_range(index)
            block = moments(ffn[rows])[0] * par[base_row + 10 : base_row + 11]
            flat[rows] = (block + par[base_row + 11 : base_row + 12]).astype(LOW)

        over(total // ROWS, norm_two, UNROLL)
        sides = (
            (target.at[pl.ds(0, count_q)], hid_q.at[pl.ds(core * count_q, count_q)]),
            (target.at[pl.ds(count_q, tall)], hid_p.at[pl.ds(core * tall, tall)]),
        )

        @pl.when(core == layer)
        def _():
            for spot, (src, dst) in enumerate(sides):
                pltpu.make_async_copy(src, dst, hlocal.at[spot]).start()

        @pl.when(core != layer)
        def _():
            for spot, (src, dst) in enumerate(sides):
                remote(src, dst, hsend.at[spot], hrecv.at[spot], peer).start()

    if parts == 16:
        lead = [item * QLEN for item in range(count_q)] + [split]
        rows8[...] = jnp.zeros_like(rows8)
        for spot, row in enumerate(lead):
            rows8[spot : spot + 1] = flat[pl.ds(row, 16)].astype(FULL)[0:1]
        for tile in range(6):
            rows48[8 * tile : 8 * tile + 8] = rows8[:, 128 * tile : 128 * tile + 128]
        for item in range(count_q):
            value = positive[core * count_q + item].astype(FULL)
            rows48[8 * item + 5 : 8 * item + 6] = jnp.full((1, 128), value)
        packed[...] = rows48[...].astype(LOW)

        def share(step, slot):
            return remote(
                packed, every.at[core, slot], gsend.at[step], grecv.at[slot],
                {"batch": (me + step) % parts},
            )

        for step in range(1, parts):
            share(step, me).start()
        every[core, me] = packed[...]
        for step in range(1, parts):
            share(step, (me + parts - step) % parts).wait_recv()
        pass_on = remote(every.at[core], every.at[core], psend, precv, peer)
        pass_on.start()
        remote(every.at[core], every.at[1 - core], psend, precv, peer).wait_recv()
        pass_on.wait_send()
        for step in range(1, parts):
            share(step, me).wait_send()

        wide = 2 * parts * 8
        grid = every[...].astype(FULL).reshape(2 * parts, 48, 128)
        inner = lax.broadcasted_iota(jnp.int32, (2 * parts, 8, 128), 1)
        goal = jnp.zeros((2 * parts, 8, 128), FULL)
        for tile in range(6):
            block = grid[:, 8 * tile : 8 * tile + 8]
            stack[:, 128 * tile : 128 * tile + 128] = block.reshape(wide, 128).astype(LOW)
            if tile < count_q:
                found = jnp.sum(jnp.where(inner == 5, block, 0.0), 1, keepdims=True)
                goal = jnp.where(inner == tile, found, goal)
        row = lax.broadcasted_iota(jnp.int32, (wide, wide), 0)
        column = lax.broadcasted_iota(jnp.int32, (wide, wide), 1)
        scale = 2.0 / math.sqrt(features)
        logits = dot_last(stack[...], stack[...]) * scale
        device = column // 8
        passage = (device % parts) * 2 + device // parts
        is_passage = column % 8 == count_q
        is_query = row % 8 < count_q
        kept = jnp.where(is_passage, logits, -1e30)
        top = jnp.max(kept, -1, keepdims=True)
        log_total = top + jnp.log(jnp.sum(jnp.exp(kept - top), -1, keepdims=True))
        chosen = is_passage & (passage.astype(FULL) == goal.reshape(wide, 128)[:, 0:1])
        picked = jnp.sum(jnp.where(chosen, logits, 0.0), -1, keepdims=True)
        terms = jnp.where(is_query[:, 0:1], log_total - picked, 0.0)
        count = count_q * 2 * parts
        loss[...] = jnp.full((8, 128), jnp.sum(terms) / count)
        grads = jnp.exp(kept - log_total) - chosen.astype(FULL)
        grads = jnp.where(is_query & is_passage, grads, 0.0)
        up[0, 0:wide, 0:wide] = grads + grads.T
        mine = pl.multiple_of((core * parts + me) * 8, 8)
        picked_rows = up[0, pl.ds(mine, 8), 0:wide]
        gcls[...] = dot(picked_rows.astype(LOW), stack[...]) * scale

    for spot, (src, dst) in enumerate(sides):
        pltpu.make_async_copy(src, dst, hlocal.at[spot]).wait()
    theirs = (
        hid_q.at[pl.ds((1 - core) * count_q, count_q)],
        hid_p.at[pl.ds((1 - core) * tall, tall)],
    )
    for spot, (src, dst) in enumerate(zip((item[0] for item in sides), theirs)):
        remote(src, dst, hsend.at[spot], hrecv.at[spot], peer).wait()
    for spot in range(4):
        give_second(spot).wait_send()
    give_par.wait_send()
    for (name, layer), copy in saves.items():
        if layer == 1:
            copy.wait()
    for layer in (0, 1):
        for spot in range(7):
            left_give(layer, spot, o_left.at[layer, spot]).wait()


def forward_both(parts, x_query, x_passage, qlens, plens, positive, vectors, own):
    queries, features = x_query.shape[0], x_query.shape[2]
    passages = x_passage.shape[0]
    total = (queries + passages) // 2 * QLEN
    wide = own[2].shape[1]
    split = queries // 2 * QLEN
    heads_p = HEADS * (passages // 2 * QLEN // PLEN)
    kept = [
        ((7, total, features), LOW),
        ((total, 3 * features), LOW),
        ((HEADS, split, split), LOW),
        ((heads_p, PLEN, PLEN), LOW),
        ((total, features), FULL),
        ((total, wide), LOW),
        ((total, features), FULL),
        ((16, features), FULL),
    ]
    shape = jax.ShapeDtypeStruct
    anywhere = pl.BlockSpec(memory_space=pl.ANY)
    vmem = pl.BlockSpec(memory_space=pltpu.VMEM)
    smem = pl.BlockSpec(memory_space=pltpu.SMEM)
    dma = pltpu.SemaphoreType.DMA
    scratch = [
        pltpu.VMEM((2, total // QLEN, QLEN, features), LOW),
        pltpu.VMEM((total // QLEN, QLEN, features), LOW),
    ]
    scratch += [pltpu.VMEM(item.shape, item.dtype) for item in own]
    scratch += [pltpu.VMEM(size, kind) for size, kind in kept[1:4]]
    scratch += [
        pltpu.VMEM((total, features), LOW),
        pltpu.VMEM((total, features), FULL),
        pltpu.VMEM((total, features), FULL),
        pltpu.VMEM((total, features), LOW),
        pltpu.VMEM((2, total, 256), FULL),
        pltpu.VMEM((total, wide), LOW),
        pltpu.VMEM((total, wide), LOW),
        pltpu.VMEM((total, features), FULL),
    ]
    scratch += [
        pltpu.VMEM((8, features), FULL),
        pltpu.VMEM((48, 128), FULL),
        pltpu.VMEM((48, 128), LOW),
        pltpu.VMEM((2, 16, 48, 128), LOW),
        pltpu.VMEM((256, features), LOW),
        dma((8,)),
        dma((26,)),
        dma((2,)),
        dma,
        dma,
        dma((4,)),
        dma((4,)),
        dma((2,)),
        dma((2,)),
        dma((2,)),
        dma((16,)),
        dma((16,)),
        dma,
        dma,
        dma((2, 7)),
        dma((2, 7)),
    ]
    return pl.pallas_call(
        functools.partial(forward_kernel, parts),
        out_shape=[shape((2,) + size, kind) for size, kind in kept]
        + [shape(item.shape, item.dtype) for item in own]
        + [
            shape(x_query.shape, LOW),
            shape(x_passage.shape, LOW),
            shape((2, 7, total, features), LOW),
            shape((8, features), FULL),
            shape((8, 128), FULL),
        ],
        in_specs=[anywhere, anywhere, smem, smem, smem] + [vmem] * 8 + [anywhere] * 4,
        out_specs=[anywhere] * 7 + [vmem] + [anywhere] * 7 + [vmem] * 2,
        scratch_shapes=scratch,
        compiler_params=pltpu.CompilerParams(
            collective_id=2, has_side_effects=True, vmem_limit_bytes=VMEM_LIMIT
        ),
    )(x_query, x_passage, qlens, plens, positive, *vectors, *own)


def add_rows(block):
    return jnp.sum(block.reshape(block.shape[0] // 8, 8, block.shape[1]), 0)


def norm_back(source, grad_of, gain, total, store):
    features = source.shape[1]
    zero = jnp.zeros((8, features), FULL)

    def step(index, carry):
        rows = row_range(index)
        grad = grad_of(index)
        unit, inverse = moments(source[rows])
        scaled = grad * gain
        back = inverse * (
            scaled
            - jnp.mean(scaled, -1, keepdims=True)
            - unit * jnp.mean(scaled * unit, -1, keepdims=True)
        )
        store(rows, back)
        return (
            carry[0] + add_rows(grad * unit),
            carry[1] + add_rows(grad),
            carry[2] + add_rows(back),
        )

    sums = lax.fori_loop(0, total // ROWS, step, (zero, zero, zero), unroll=UNROLL)
    return [jnp.sum(item, 0, keepdims=True) for item in sums]


def left_index(ch):
    return (
        jnp.minimum(ch, 4) + (ch >= 8).astype(jnp.int32) + (ch >= 9).astype(jnp.int32)
    )


def right_index(ch):
    return jnp.maximum(ch - 3, 0)


def backward_kernel(parts, *refs):
    small = parts == 16
    refs = list(refs)

    def take(count):
        front = refs[:count]
        del refs[:count]
        return front

    cot_query, cot_passage, qlens, plens, gcls, par = take(6)
    own, land = take(4), take(4)
    left, h_qkv, h_pq, h_pp, h_pre, h_slope, h_ffn, land_a = take(8)
    if small:
        o_qkv, o_o, o_in, o_out, o_vec, o_gq, o_gp, land_g, own_g = take(9)
    else:
        vpar, o_gq, o_gp, f_pro, f_att, f_up, f_flo = take(7)
    buffers = take(4)
    bqkv, bo, bin_, bout = buffers
    qkv, pq, pp, source, slope, gsrc = take(6)
    attn_full, attn, steep, flow_full, flow, gmixed, grow = take(7)
    wload, fetch, cload, hsend, hrecv, hlocal, ksem = take(7)
    if small:
        vpar, a_buf, g_buf, stage, s1, r1, s2, r2, s3, r3 = take(10)
        va, ra, vb, rb, vc, rc, rz = take(7)
        s1s, r1s, s2s, r2s, s3s, r3s, vsend, vrecv, zsend, zrecv = take(10)
        gs, gr, sl, gl = take(4)

    core = lax.axis_index("section")
    me = lax.axis_index("batch")
    peer = {"section": 1 - core}
    features = gcls.shape[1]
    total = flow.shape[0]
    split = pq.shape[1]
    count_q, tall = cot_query.shape[0] // 2, cot_passage.shape[0] // 2
    heads_p = pp.shape[0]
    blocks_p = PLEN // QLEN

    def weight_copy(spot, source_set):
        return pltpu.make_async_copy(source_set[spot], buffers[spot], wload.at[spot])

    def weight_start(layer, spot):
        @pl.when(core == layer)
        def _():
            weight_copy(spot, own).start()

        @pl.when(core != layer)
        def _():
            weight_copy(spot, land).start()

    def weight_wait(spot):
        weight_copy(spot, own).wait()

    saved = ((h_ffn, source), (h_slope, slope), (h_pre, source), (h_qkv, qkv), (h_pq, pq), (h_pp, pp))

    def saved_copy(layer, spot):
        src, dst = saved[spot]
        return pltpu.make_async_copy(src.at[layer], dst, fetch.at[spot])

    cots = [
        pltpu.make_async_copy(
            cot_query.at[pl.ds(core * count_q, count_q)], gsrc.at[pl.ds(0, count_q)], cload.at[0]
        ),
        pltpu.make_async_copy(
            cot_passage.at[pl.ds(core * tall, tall)], gsrc.at[pl.ds(count_q, tall)], cload.at[1]
        ),
    ]
    saved_copy(1, 0).start()
    for copy in cots:
        copy.start()
    weight_start(1, 3)
    saved_copy(1, 1).start()

    widths = ((flow, 1), (slope, 4), (attn, 1), (qkv, 3))

    def pieces_of(slot):
        base = (0, 1, 5, 6)[slot]
        ref, count = widths[slot]
        return [(base + item, ref, ref.shape[1] // 2, item) for item in range(count)]

    def own_piece(layer, piece):
        spot, ref, width, item = piece
        lanes = pl.ds(pl.multiple_of(core * width + item * CHUNK, 128), CHUNK)
        return pltpu.make_async_copy(ref.at[:, lanes], own_g.at[layer, spot], ksem.at[spot])

    def peer_piece(layer, piece):
        spot, ref, width, item = piece
        lanes = pl.ds(pl.multiple_of((1 - core) * width + item * CHUNK, 128), CHUNK)
        return remote(
            ref.at[:, lanes], land_g.at[layer, spot], gs.at[layer, spot], gr.at[layer, spot], peer
        )

    def whole_piece(layer, slot):
        ref = widths[slot][0]
        target = (f_flo, f_up, f_att, f_pro)[slot]
        return pltpu.make_async_copy(ref, target.at[layer], ksem.at[slot])

    def give(layer, slot):
        if small:
            for piece in pieces_of(slot):
                peer_piece(layer, piece).start()
                own_piece(layer, piece).start()
        else:
            whole_piece(layer, slot).start()

    def given(layer, slot):
        if small:
            for piece in pieces_of(slot):
                peer_piece(layer, piece).wait_send()
                if slot > 0:
                    own_piece(layer, piece).wait()
                else:

                    @pl.when(layer == 0)
                    def _():
                        own_piece(layer, piece).wait()
        else:
            whole_piece(layer, slot).wait()

    def slot_zero(layer):
        saved_copy(layer, 0).wait()
        gains = par.at[layer]
        last = layer == 1

        def grad_of(index):
            block = gsrc[index].astype(FULL)
            beyond = jnp.maximum(index - count_q, 0)
            item = beyond // blocks_p
            query_limit = qlens[core * count_q + jnp.minimum(index, count_q - 1)]
            passage_limit = (
                plens[core * (tall // blocks_p) + item] - (beyond % blocks_p) * QLEN
            )
            limit = jnp.where(index < count_q, query_limit, passage_limit)
            limit = jnp.where(last, limit, QLEN)
            lead = jnp.where(index < count_q, index, count_q + item)
            starts = (index < count_q) | (beyond % blocks_p == 0)
            row = lax.broadcasted_iota(jnp.int32, block.shape, 0)
            block = jnp.where(row < limit, block, 0.0)
            extra = gcls[pl.ds(lead, 1)] * jnp.where(starts & last, 1.0, 0.0)
            return block + jnp.where(row == 0, extra, 0.0)

        def store(rows, back):
            flow_full[rows] = back
            flow[rows] = back.astype(LOW)

        gain, shift, bias = norm_back(source, grad_of, gains[10:11], total, store)
        sums = vpar.at[layer]
        sums[10:11], sums[11:12], sums[9:10] = gain, shift, bias
        give(layer, 0)
        saved_copy(layer, 2).start()

    width = 256
    tiles = bout.shape[0] // width

    def slot_one(layer):
        saved_copy(layer, 1).wait()
        weight_wait(3)
        sums = vpar.at[layer]

        def shrink(tile):
            rows_of = pl.ds(pl.multiple_of(tile * width, width), width)
            steep[tile % 2] = dot_last(flow[...], bout[rows_of])

        def bend(tile):
            lanes = lane_range(tile, width)
            acc = jnp.zeros((8, width), FULL)
            for index in range(total // ROWS):
                rows = pl.ds(index * ROWS, ROWS)
                low = (steep[tile % 2, rows] * slope[rows, lanes].astype(FULL)).astype(LOW)
                slope[rows, lanes] = low
                acc = acc + add_rows(low.astype(FULL))
            sums[pl.ds(5 + tile // 3, 1), lane_range(tile % 3, width)] = jnp.sum(
                acc, 0, keepdims=True
            )

        shrink(0)

        def both(index):
            shrink(index + 1)
            bend(index)

        over(tiles - 1, both)
        bend(tiles - 1)
        give(layer, 1)

        @pl.when(layer == 1)
        def _():
            weight_start(0, 3)

    def slot_two(layer):
        weight_wait(2)
        flow_full[...] += dot_last(slope[...], bin_[...])
        saved_copy(layer, 2).wait()
        gains, sums = par.at[layer], vpar.at[layer]

        def store(rows, back):
            attn_full[rows] = back
            attn[rows] = back.astype(LOW)

        gain, shift, bias = norm_back(
            source, lambda index: flow_full[row_range(index)], gains[3:4], total, store
        )
        sums[3:4], sums[4:5], sums[2:3] = gain, shift, bias
        give(layer, 2)
        weight_wait(1)
        gmixed[...] = dot_last(attn[...], bo[...]).astype(LOW)

        @pl.when(layer == 1)
        def _():
            weight_start(0, 2)
            weight_start(0, 1)
            saved_copy(0, 0).start()
            saved_copy(0, 1).start()

    blocks = [(0, split, pq, 0)]
    for item in range(heads_p // HEADS):
        blocks.append((split + item * PLEN, PLEN, pp, item * HEADS))

    def attend(index):
        tasks = []
        for step in range(PAIRS):
            for block in blocks:
                tasks.append((index * PAIRS + step,) + block)

        def spot_of(task, offset):
            hp, lo, rows = task[:3]
            return (pl.ds(lo, rows), pl.ds(pl.multiple_of(offset + hp * 128, 128), 128))

        grads = []
        for task in tasks:
            values, back = qkv[spot_of(task, 2 * features)], gmixed[spot_of(task, 0)]
            for head in (0, 1):
                masked = jnp.where(head_lanes(task[2], head), values, LOW(0))
                grads.append(dot_last(masked, back))
        lows = []
        for spot, grad_probs in enumerate(grads):
            hp, lo, rows, probs, base = tasks[spot // 2]
            full = probs[base + 2 * hp + spot % 2].astype(FULL)
            inner = jnp.sum(grad_probs * full, 0, keepdims=True)
            lows.append((full * (grad_probs - inner)).astype(LOW))
        for spot, task in enumerate(tasks):
            hp, lo, rows, probs, base = task
            queries, keys = qkv[spot_of(task, 0)], qkv[spot_of(task, features)]
            back = gmixed[spot_of(task, 0)]
            turned = keys.T
            outs = []
            for head in (0, 1):
                grad_scores = lows[2 * spot + head]
                outs.append(
                    (
                        dot(turned[64 * head : 64 * head + 64], grad_scores) * 0.125,
                        dot(grad_scores, queries) * 0.125,
                        dot(probs[base + 2 * hp + head], back),
                    )
                )
            first = head_lanes(rows, 0)
            both = jnp.concatenate([outs[0][0], outs[1][0]], 0)
            qkv[spot_of(task, 0)] = both.astype(LOW).T
            for item in (1, 2):
                both = jnp.where(first, outs[0][item], outs[1][item])
                qkv[spot_of(task, item * features)] = both.astype(LOW)

    def grads_here(spot):
        lo, count, target = ((0, count_q, o_gq), (count_q, tall, o_gp))[spot]
        return pltpu.make_async_copy(
            grow.at[pl.ds(lo, count)], target.at[pl.ds(core * count, count)], hlocal.at[spot]
        )

    def grads_there(spot):
        lo, count, target = ((0, count_q, o_gq), (count_q, tall, o_gp))[spot]
        return remote(
            grow.at[pl.ds(lo, count)],
            target.at[pl.ds(core * count, count)],
            hsend.at[spot],
            hrecv.at[spot],
            peer,
        )

    def slot_three(layer):
        for spot in (3, 4, 5):
            saved_copy(layer, spot).wait()
        over(features // 128 // PAIRS, attend)
        give(layer, 3)
        sums = vpar.at[layer]

        def bias_sums(index, carry):
            rows = row_range(index)
            return (
                carry[0] + add_rows(qkv[rows, pl.ds(0, features)].astype(FULL)),
                carry[1] + add_rows(qkv[rows, pl.ds(2 * features, features)].astype(FULL)),
            )

        zero = jnp.zeros((8, features), FULL)
        found = lax.fori_loop(0, total // ROWS, bias_sums, (zero, zero), unroll=2)
        sums[0:1] = jnp.sum(found[0], 0, keepdims=True)
        sums[1:2] = jnp.sum(found[1], 0, keepdims=True)
        sums[12:16] = jnp.zeros((4, features), FULL)
        weight_wait(0)
        rows_all = attn_full[...] + dot_last(qkv[...], bqkv[...])
        grow[...] = rows_all.reshape(grow.shape)
        gsrc[...] = rows_all.astype(LOW).reshape(gsrc.shape)

        @pl.when(core == layer)
        def _():
            for spot in (0, 1):
                grads_here(spot).start()

        @pl.when(core != layer)
        def _():
            for spot in (0, 1):
                grads_there(spot).start()

        @pl.when(layer == 1)
        def _():
            weight_start(0, 0)

    def grads_given(layer):
        @pl.when(core == layer)
        def _():
            for spot in (0, 1):
                grads_here(spot).wait()

        @pl.when(core != layer)
        def _():
            for spot in (0, 1):
                grads_there(spot).wait_send()

    slots = (slot_zero, slot_one, slot_two, slot_three)

    def reload(layer, slot):
        @pl.when(layer == 1)
        def _():
            if slot == 3:
                for spot in (3, 4, 5):
                    saved_copy(0, spot).start()

    def rest_of_loads():
        for spot in (2, 1, 0):
            weight_start(1, spot)
        for spot in (3, 4, 5):
            saved_copy(1, spot).start()

    def grads_came():
        lands = ((o_gq, count_q), (o_gp, tall))
        for spot, (target, count) in enumerate(lands):
            there = target.at[pl.ds((1 - core) * count, count)]
            remote(there, there, hsend.at[spot], hrecv.at[spot], peer).wait_recv()

    if not small:
        greet([peer])
        rest_of_loads()
        for copy in cots:
            copy.wait()
        for layer in (1, 0):
            for slot in range(4):
                slots[slot](layer)
                given(layer, slot)
                reload(layer, slot)
            grads_given(layer)
        grads_came()
        return

    x, y, z = me % 2, (me // 2) % 2, me // 4
    px, py = me + 1 - 2 * x, me + 2 - 4 * y
    targets = [{"batch": px}, {"batch": py}, peer]
    for step in (1, 2, 3):
        other = ((z + step) % 4) * 4 + me % 4
        targets += [{"section": sec, "batch": other} for sec in (0, 1)]
    greet(targets)

    def stage_copy(number, side):
        layer, spot = 1 - number // 7, number % 7
        src = left if side == 0 else land_a
        return pltpu.make_async_copy(
            src.at[layer, spot], stage.at[number % 2, side], sl.at[number % 2, side]
        )

    def stage_start(number):
        stage_copy(number, 0).start()
        stage_copy(number, 1).start()

    def turn(number, spot):
        for side in (0, 1):
            stage_copy(number, side).wait()
        for side in (0, 1):
            lanes = pl.ds(side * total, total)
            for half in range(features // CHUNK):
                block = stage[number % 2, side, :, pl.ds(half * CHUNK, CHUNK)].T
                if spot > 3:
                    a_buf[spot, pl.ds(2 * half, 2), :, :, :, lanes] = block.reshape(
                        2, 2, 2, BLOCK, total
                    )
                else:
                    shaped = block.reshape(2, 4, BLOCK, total)
                    for item in range(4):
                        a_buf[item, spot, half, :, :, lanes] = shaped[:, item]

        @pl.when(number + 2 < 14)
        def _():
            stage_start(number + 2)

    def right_copy(layer, spot, side):
        src = own_g if side == 0 else land_g
        return pltpu.make_async_copy(
            src.at[layer, spot], g_buf.at[spot, pl.ds(side * total, total)], gl.at[spot, side]
        )

    def right_start(k):
        ch = k % COUNT
        layer = 1 - k // COUNT

        @pl.when((k < 2 * COUNT) & ((ch == 0) | (ch >= 4)))
        def _():
            spot = right_index(ch)
            right_copy(layer, spot, 0).start()
            remote(
                own_g.at[layer, spot], land_g.at[layer, spot],
                gs.at[layer, spot], gr.at[layer, spot], peer,
            ).wait_recv()
            right_copy(layer, spot, 1).start()

    RING = 12

    def first(k, par_):
        return remote(
            s1.at[k % 4], r1.at[k % RING], s1s.at[k], r1s.at[k],
            {"batch": px if par_ == 0 else py},
        )

    def second(k, par_):
        return remote(
            s2.at[k % 4], r2.at[k % RING], s2s.at[k], r2s.at[k],
            {"batch": py if par_ == 0 else px},
        )

    def third(k, step):
        layer = 1 - k // COUNT
        zt = (z + step) % 4
        return remote(
            s3.at[k % 4, zt], r3.at[core, k % COUNT, z], s3s.at[k, step],
            r3s.at[core, k % COUNT, z], {"section": layer, "batch": zt * 4 + me % 4},
        )

    def third_in(k, step, src_core):
        zs = (z + 4 - step) % 4
        return remote(
            s3.at[k % 4, zs], r3.at[src_core, k % COUNT, zs], s3s.at[k, step],
            r3s.at[src_core, k % COUNT, zs], peer,
        )

    def product(k, block, rows):
        return dot(block.reshape(rows, 2 * total), g_buf[right_index(k % COUNT)])

    def left_of(k):
        return a_buf.at[left_index(k % COUNT)]

    def ready(k, par_):
        ch = k % COUNT

        @pl.when((ch == 0) | (ch >= 4))
        def _():
            for side in (0, 1):
                right_copy(0, right_index(ch), side).wait()

        base = (k // COUNT) * 7
        if par_ == 0:

            @pl.when(ch == 0)
            def _():
                for spot in range(4):
                    turn(base + spot, spot)

            for spot, at in ((4, 4), (5, 8)):

                @pl.when(ch == at)
                def _():
                    turn(base + spot, spot)
        else:

            @pl.when(ch == 9)
            def _():
                turn(base + 6, 6)

    def part_one(k, par_):
        ready(k, par_)
        ref = left_of(k)
        block = ref[:, :, 1 - x] if par_ == 0 else ref[:, 1 - y]
        s1[k % 4] = product(k, block, 8 * BLOCK).astype(LOW).reshape(4, 2, BLOCK, CHUNK)
        first(k, par_).start()

    def part_two(k, par_):
        first(k, par_).wait()
        ref = left_of(k)
        if par_ == 0:
            block, came = ref[:, 1 - y, x], r1[k % RING, :, 1 - y]
        else:
            block, came = ref[:, y, 1 - x], r1[k % RING, :, 1 - x]
        value = product(k, block, 4 * BLOCK).reshape(4, BLOCK, CHUNK) + came.astype(FULL)
        s2[k % 4] = value.astype(LOW)
        second(k, par_).start()

    def part_three(k, par_):
        second(k, par_).wait()
        layer = 1 - k // COUNT
        ref = left_of(k)
        came = r1[k % RING, :, y] if par_ == 0 else r1[k % RING, :, x]
        value = (
            product(k, ref[:, y, x], 4 * BLOCK).reshape(4, BLOCK, CHUNK)
            + came.astype(FULL)
            + r2[k % RING].astype(FULL)
        )
        s3[k % 4] = value.astype(LOW)
        for step in (1, 2, 3):
            third(k, step).start()

        @pl.when(core != layer)
        def _():
            third(k, 0).start()

        @pl.when(core == layer)
        def _():
            r3[core, k % COUNT, z] = s3[k % 4, z]

    def part_four(k):
        layer = 1 - k // COUNT
        ch = k % COUNT
        for step in (1, 2, 3):
            third(k, step).wait_send()

        @pl.when(core != layer)
        def _():
            third(k, 0).wait_send()

        @pl.when(core == layer)
        def _():
            for step in (1, 2, 3):
                for src_core in (0, 1):
                    third_in(k, step, src_core).wait_recv()
            third_in(k, 0, 1 - core).wait_recv()
            for src_core in (0, 1):
                value = jnp.sum(r3[src_core, ch].astype(FULL), 0)

                @pl.when(ch < 4)
                def _():
                    o_out[ch, :, pl.ds(src_core * CHUNK, CHUNK)] = value

                @pl.when((ch >= 4) & (ch < 8))
                def _():
                    start = pl.multiple_of((ch - 4) * CHUNK + src_core * 4 * CHUNK, 128)
                    o_in[:, pl.ds(start, CHUNK)] = value

                @pl.when(ch == 8)
                def _():
                    o_o[:, pl.ds(src_core * CHUNK, CHUNK)] = value

                @pl.when(ch >= 9)
                def _():
                    start = pl.multiple_of((ch - 9) * CHUNK + src_core * 3 * CHUNK, 128)
                    o_qkv[:, pl.ds(start, CHUNK)] = value

    vec_cross = remote(vpar.at[1 - core], ra, vsend.at[0], vrecv.at[0], peer)
    vec_x = remote(va, rb, vsend.at[1], vrecv.at[1], {"batch": px})
    vec_y = remote(vb, rc, vsend.at[2], vrecv.at[2], {"batch": py})

    def vec_z(step, slot):
        return remote(
            vc, rz.at[slot], zsend.at[step], zrecv.at[slot],
            {"batch": ((z + step) % 4) * 4 + me % 4},
        )

    steps = 2 * COUNT + 6

    def pair(turn_index, carry):
        kk = turn_index - 1
        layer = (kk < 3).astype(jnp.int32)

        for slot, (one, two) in enumerate(((0, 4), (1, 4), (2, 5), (3, 6))):

            @pl.when((kk == one) | (kk == two))
            def _():
                done = (kk == one).astype(jnp.int32)
                given(done, slot)
                reload(done, slot)
                if slot == 3:
                    grads_given(done)

        @pl.when(kk == -1)
        def _():
            stage_start(0)
            stage_start(1)
            rest_of_loads()
            for copy in cots:
                copy.wait()

        for par_ in (0, 1):
            k = 2 * kk + par_

            @pl.when((k >= 0) & (k < 2 * COUNT))
            def _():
                part_one(k, par_)

        for par_ in (0, 1):
            k = 2 * kk + par_

            @pl.when((k >= 2) & (k < 2 * COUNT + 2))
            def _():
                part_two(k - 2, par_)

            @pl.when((k >= 4) & (k < 2 * COUNT + 4))
            def _():
                part_three(k - 4, par_)

            @pl.when(k >= 6)
            def _():
                part_four(k - 6)

        for slot, (one, two) in enumerate(((-1, 3), (0, 3), (1, 4), (2, 5))):

            @pl.when((kk == one) | (kk == two))
            def _():
                slots[slot](layer)

        @pl.when(kk == -1)
        def _():
            own_piece(1, pieces_of(0)[0]).wait()

        @pl.when((kk >= -1) & (kk < COUNT - 1))
        def _():
            for par_ in (0, 1):
                right_start(2 * kk + 2 + par_)

        @pl.when(kk == 6)
        def _():
            vec_cross.start()

        @pl.when(kk == 7)
        def _():
            vec_cross.wait()
            va[...] = vpar[core] + ra[...]
            vec_x.start()

        @pl.when(kk == 8)
        def _():
            vec_x.wait()
            vb[...] = va[...] + rb[...]
            vec_y.start()

        @pl.when(kk == 9)
        def _():
            vec_y.wait()
            vc[...] = vb[...] + rc[...]
            for step in (1, 2, 3):
                vec_z(step, z).start()

        @pl.when(kk == 11)
        def _():
            for step in (1, 2, 3):
                vec_z(step, z).wait_send()
                vec_z(step, (z + 4 - step) % 4).wait_recv()
            rz[z] = vc[...]
            o_vec[...] = jnp.sum(rz[...], 0)

        return carry

    lax.fori_loop(0, steps // 2 + 1, pair, 0)
    grads_came()


def backward_both(parts, cots, qlens, plens, gcls, par, own, land, kept):
    small = parts == 16
    cot_query, cot_passage = cots
    left, h_qkv, h_pq, h_pp, h_pre, h_slope, h_ffn = kept[:7]
    total, features = left.shape[2:]
    wide = own[2].shape[1]
    shape = jax.ShapeDtypeStruct
    anywhere = pl.BlockSpec(memory_space=pl.ANY)
    vmem = pl.BlockSpec(memory_space=pltpu.VMEM)
    smem = pl.BlockSpec(memory_space=pltpu.SMEM)
    dma = pltpu.SemaphoreType.DMA
    grads = [shape(cot_query.shape, FULL), shape(cot_passage.shape, FULL)]
    if small:
        out_shape = [
            shape((BLOCK, 3 * features), FULL),
            shape((BLOCK, features), FULL),
            shape((BLOCK, wide), FULL),
            shape((4, BLOCK, features), FULL),
            shape((16, features), FULL),
            *grads,
            shape((2, 9, total, CHUNK), LOW),
            shape((2, 9, total, CHUNK), LOW),
        ]
        out_specs = [vmem] * 5 + [anywhere] * 4
    else:
        out_shape = [
            shape((2, 16, features), FULL),
            *grads,
            shape((2, total, 3 * features), LOW),
            shape((2, total, features), LOW),
            shape((2, total, wide), LOW),
            shape((2, total, features), LOW),
        ]
        out_specs = [vmem] + [anywhere] * 6
    scratch = [pltpu.VMEM(item.shape, item.dtype) for item in own]
    scratch += [
        pltpu.VMEM(h_qkv.shape[1:], LOW),
        pltpu.VMEM(h_pq.shape[1:], LOW),
        pltpu.VMEM(h_pp.shape[1:], LOW),
        pltpu.VMEM((total, features), FULL),
        pltpu.VMEM((total, wide), LOW),
        pltpu.VMEM((total // QLEN, QLEN, features), LOW),
        pltpu.VMEM((total, features), FULL),
        pltpu.VMEM((total, features), LOW),
        pltpu.VMEM((2, total, 256), FULL),
        pltpu.VMEM((total, features), FULL),
        pltpu.VMEM((total, features), LOW),
        pltpu.VMEM((total, features), LOW),
        pltpu.VMEM((total // QLEN, QLEN, features), FULL),
        dma((4,)),
        dma((6,)),
        dma((2,)),
        dma((2,)),
        dma((2,)),
        dma((2,)),
        dma((9,)),
    ]
    if small:
        steps = 2 * COUNT
        vector = pltpu.VMEM((16, features), FULL)
        scratch += [
            pltpu.VMEM((2, 16, features), FULL),
            pltpu.VMEM((7, 4, 2, 2, BLOCK, 2 * total), LOW),
            pltpu.VMEM((9, 2 * total, CHUNK), LOW),
            pltpu.VMEM((2, 2, total, features), LOW),
            pltpu.VMEM((4, 4, 2, BLOCK, CHUNK), LOW),
            pltpu.VMEM((12, 4, 2, BLOCK, CHUNK), LOW),
            pltpu.VMEM((4, 4, BLOCK, CHUNK), LOW),
            pltpu.VMEM((12, 4, BLOCK, CHUNK), LOW),
            pltpu.VMEM((4, 4, BLOCK, CHUNK), LOW),
            pltpu.VMEM((2, COUNT, 4, BLOCK, CHUNK), LOW),
            *[vector] * 6,
            pltpu.VMEM((4, 16, features), FULL),
            dma((steps,)),
            dma((steps,)),
            dma((steps,)),
            dma((steps,)),
            dma((steps, 4)),
            dma((2, COUNT, 4)),
            dma((3,)),
            dma((3,)),
            dma((4,)),
            dma((4,)),
            dma((2, 9)),
            dma((2, 9)),
            dma((2, 2)),
            dma((9, 2)),
        ]
    return pl.pallas_call(
        functools.partial(backward_kernel, parts),
        out_shape=out_shape,
        in_specs=[anywhere, anywhere, smem, smem, vmem, vmem] + [anywhere] * 16,
        out_specs=out_specs,
        scratch_shapes=scratch,
        compiler_params=pltpu.CompilerParams(
            collective_id=1, has_side_effects=True, vmem_limit_bytes=60 * 1024 * 1024
        ),
    )(cot_query, cot_passage, qlens, plens, gcls, par, *own, *land, *kept)


def finish_kernel(parts, *refs):
    big, vec, loss = refs[:8], refs[8], refs[9]
    outs, small, total = refs[10:18], refs[18:26], refs[26]
    held, come, go = refs[27:35], refs[35], refs[36]
    copies = []
    for src, mid, dst in zip(big, held, outs):
        pieces = 2 if src.shape[0] % 32 == 0 or len(src.shape) == 3 else 1
        size = src.shape[0] // pieces
        for item in range(pieces):
            rows, spot = pl.ds(item * size, size), len(copies)
            copies.append(
                (
                    pltpu.make_async_copy(src.at[rows], mid.at[rows], come.at[spot]),
                    pltpu.make_async_copy(mid.at[rows], dst.at[rows], go.at[spot]),
                )
            )
            copies[-1][0].start()
    me = lax.axis_index("batch")
    features = vec.shape[1]
    for at, count, out in zip((0, 2, 3, 4, 5, 9, 10, 11), (2, 1, 1, 1, 4, 1, 1, 1), small):
        size = count * features // parts
        every = parts // count
        block = vec[pl.ds(at + me // every, 1)]
        block = jnp.broadcast_to(block, (8, features))
        turned = pltpu.roll(block, (features - size * (me % every)) % features, 1)
        out[...] = turned[0:1, 0:size]
    total[...] = loss[0:1, 0:1]
    for came, left in copies:
        came.wait()
        left.start()
    for came, left in copies:
        left.wait()


def finish(parts, big, vec, loss):
    features = vec.shape[1]
    anywhere = pl.BlockSpec(memory_space=pl.ANY)
    vmem = pl.BlockSpec(memory_space=pltpu.VMEM)
    shape = jax.ShapeDtypeStruct
    return pl.pallas_call(
        functools.partial(finish_kernel, parts),
        out_shape=[shape(item.shape, item.dtype) for item in big]
        + [shape((1, count * features // parts), FULL) for count in (2, 1, 1, 1, 4, 1, 1, 1)]
        + [shape((1, 1), FULL)],
        in_specs=[anywhere] * 8 + [vmem] * 2,
        out_specs=[anywhere] * 8 + [vmem] * 9,
        scratch_shapes=[pltpu.VMEM(item.shape, item.dtype) for item in big]
        + [pltpu.SemaphoreType.DMA((16,)), pltpu.SemaphoreType.DMA((16,))],
    )(*big, vec, loss)


def per_device(
    parts,
    x_query,
    x_passage,
    len_query,
    len_passage,
    positive,
    cot_query,
    cot_passage,
    *weights,
):
    core = lax.axis_index("section")
    on_first = core == 0
    own_set = [member[0] for member in weights]
    own = [own_set[item] for item in (0, 2, 6, 8)]
    vectors = [weights[item] for item in (1, 3, 4, 5, 7, 9, 10, 11)]
    features = x_query.shape[2]
    half_q, half_p = x_query.shape[0] // 2, x_passage.shape[0] // 2
    *kept, par, l_qkv, l_o, l_in, l_out, hidden_q, hidden_p, land_a, grad_cls, loss = forward_both(
        parts,
        x_query,
        x_passage.reshape(-1, QLEN, features),
        len_query,
        len_passage,
        positive,
        vectors,
        own,
    )
    other = (l_qkv, l_o, l_in, l_out)
    if parts != 16:
        last = hidden_p.reshape(x_passage.shape)
        targets = lax.all_gather(positive, "batch", axis=0, tiled=True)
        own_q = hidden_q[:, 0]
        own_p = last[:, 0]
        last_q, last_p = (jnp.where(on_first, swap(item), item) for item in (own_q, own_p))
        cls_query = lax.all_gather(last_q, "batch", axis=0, tiled=True)
        cls_passage = lax.all_gather(last_p, "batch", axis=0, tiled=True)
        score_scale = 2.0 / math.sqrt(features)
        logits = (
            jnp.einsum("qd,pd->qp", cls_query, cls_passage, preferred_element_type=jnp.float32)
            * score_scale
        )
        term_values, grad_logits = contrast(logits, targets)
        loss_value = jnp.mean(term_values)
        mine = lax.axis_index("batch") * 2 + core
        own_logits = lax.dynamic_slice_in_dim(grad_logits, mine * half_q, half_q, 0)
        grad_cls_q = (
            jnp.einsum("qp,pd->qd", own_logits, cls_passage, preferred_element_type=jnp.float32)
            * score_scale
        )
        own_columns = lax.dynamic_slice_in_dim(grad_logits, mine * half_p, half_p, 1)
        grad_cls_p = (
            jnp.einsum("qp,qd->pd", own_columns, cls_query, preferred_element_type=jnp.float32)
            * score_scale
        )
        grad_cls = jnp.concatenate([grad_cls_q, grad_cls_p], 0)
        grad_cls = jnp.pad(grad_cls, ((0, 8 - grad_cls.shape[0]), (0, 0)))

    outs = backward_both(
        parts,
        (cot_query, cot_passage.reshape(-1, QLEN, features)),
        len_query,
        len_passage,
        grad_cls,
        par,
        own,
        other,
        kept + [land_a],
    )
    groups = ((0, 2), (2, 1), (3, 1), (4, 1), (5, 4), (9, 1), (10, 1), (11, 1))
    if parts == 16:
        d_qkv, d_o, d_in, d_out, d_vec, grad_q, grad_p = outs[:7]
        big = (hidden_q, hidden_p, grad_q, grad_p, d_qkv, d_o, d_in, d_out.reshape(-1, features))
        *final, loss = finish(parts, big, d_vec, loss)
        hidden_q, hidden_p, grad_q, grad_p, d_qkv, d_o, d_in, d_out = final[:8]
        small = [item[0] for item in final[8:]]
        loss_value = loss.reshape(())
    else:
        sums, grad_q, grad_p, g_pro, g_att, g_up, g_flo = outs
        left = kept[0]

        def total(pair):
            kept_one = jnp.where(on_first, pair[0], pair[1])
            both = kept_one + swap(jnp.where(on_first, pair[1], pair[0]))
            return lax.psum_scatter(both, "batch", scatter_dimension=0, tiled=True)

        def product(first, second):
            return jnp.einsum("rd,re->de", first, second, preferred_element_type=jnp.float32)

        d_qkv, d_o, d_in = (
            total([product(left[layer, spot], right[layer]) for layer in (0, 1)])
            for spot, right in ((6, g_pro), (5, g_att), (4, g_up))
        )
        d_out = total(
            [
                jnp.concatenate([product(left[layer, spot], g_flo[layer]) for spot in range(4)], 0)
                for layer in (0, 1)
            ]
        )
        small = [
            total([sums[layer, at : at + count].reshape(-1) for layer in (0, 1)])
            for at, count in groups
        ]
    hidden_q, hidden_p = hidden_q[None], hidden_p.reshape(x_passage.shape)[None]
    grad_q = grad_q[None]
    grad_p = grad_p.reshape(x_passage.shape)[None]
    d_b_qv, d_b_o, d_g_attn, d_c_attn, d_b_in, d_b_out, d_g_ffn, d_c_ffn = small
    outs = (
        d_qkv, d_b_qv, d_o, d_b_o, d_g_attn, d_c_attn, d_in, d_b_in, d_out, d_b_out, d_g_ffn,
        d_c_ffn,
    )
    return (hidden_q, hidden_p, grad_q, grad_p, loss_value) + tuple(item[None] for item in outs)


def solution(mesh):
    in_specs = (
        P("batch", None, None),
        P("batch", None, None),
        P("batch"),
        P("batch"),
        P("batch"),
        P("batch", None, None),
        P("batch", None, None),
        P("section", None, None),
        P("section", None),
        P("section", None, None),
        P("section", None),
        P("section", None),
        P("section", None),
        P("section", None, None),
        P("section", None),
        P("section", None, None),
        P("section", None),
        P("section", None),
        P("section", None),
    )
    out_specs = (
        P("section", "batch", None, None),
        P("section", "batch", None, None),
        P("section", "batch", None, None),
        P("section", "batch", None, None),
        P(),
        P("section", "batch", None),
        P("section", "batch"),
        P("section", "batch", None),
        P("section", "batch"),
        P("section", "batch"),
        P("section", "batch"),
        P("section", "batch", None),
        P("section", "batch"),
        P("section", "batch", None),
        P("section", "batch"),
        P("section", "batch"),
        P("section", "batch"),
    )
    return jax.shard_map(
        functools.partial(per_device, mesh.shape["batch"]), mesh=mesh, in_specs=in_specs, out_specs=out_specs, check_vma=False
    )
```

```python
import functools
import math

import jax
import jax.numpy as jnp
from jax import lax
from jax.experimental import pallas as pl
from jax.experimental.pallas import tpu as pltpu
from jax.sharding import PartitionSpec as P

HEADS = 12
QLEN = 32
PLEN = 256


norm_eps = 1e-05


def contrast(logits, targets):
    top_score = jnp.max(logits, -1, keepdims=True)
    log_total = top_score[:, 0] + jnp.log(jnp.sum(jnp.exp(logits - top_score), -1))
    chosen = targets[:, None] == jnp.arange(logits.shape[1])[None, :]
    term_values = log_total - jnp.sum(jnp.where(chosen, logits, 0.0), -1)
    grad_logits = (jnp.exp(logits - log_total[:, None]) - chosen.astype(jnp.float32)).astype(
        jnp.bfloat16
    )
    return (term_values, grad_logits)


MESH = pl.DeviceIdType.MESH
CHUNK = 384
COUNT = 12
BLOCK = 48


def swap(value):
    return lax.ppermute(value, "section", [(0, 1), (1, 0)])


LOW = jnp.bfloat16
FULL = jnp.float32
ROWS = 32
TILE = 768
LAST = (((1,), (1,)), ((), ()))
FIRST = (((0,), (0,)), ((), ()))


def dot(left, right):
    return jnp.dot(left, right, preferred_element_type=FULL)


def dot_last(left, right):
    return lax.dot_general(left, right, LAST, preferred_element_type=FULL)


def dot_first(left, right):
    return lax.dot_general(left, right, FIRST, preferred_element_type=FULL)


UNROLL = 4
PAIRS = 3


def over(count, body, unroll=1):
    def step(index, carry):
        body(index)
        return carry

    lax.fori_loop(0, count, step, 0, unroll=unroll)


def row_range(index):
    return pl.ds(pl.multiple_of(index * ROWS, ROWS), ROWS)


def lane_range(index, width):
    return pl.ds(pl.multiple_of(index * width, 128), width)


def moments(block):
    centred = block - jnp.mean(block, -1, keepdims=True)
    spread = jnp.mean(centred * centred, -1, keepdims=True)
    inverse = lax.rsqrt(spread + norm_eps)
    return centred * inverse, inverse


def gelu_pair(block):
    size = jnp.abs(block)
    t = 1.0 / (1.0 + (0.3275911 * math.sqrt(0.5)) * size)
    bell = jnp.exp(-0.5 * block * block)
    poly = 0.5 * 1.061405429
    for term in (-1.453152027, 1.421413741, -0.284496736, 0.254829592):
        poly = poly * t + 0.5 * term
    tail = poly * t * bell
    phi = jnp.where(block > 0, 1.0 - tail, tail)
    return block * phi, phi + block * bell * (1.0 / math.sqrt(2.0 * math.pi))


def head_lanes(rows, head):
    lane = lax.broadcasted_iota(jnp.int32, (rows, 128), 1)
    return (lane < 64) if head == 0 else (lane >= 64)


def query_mask(lens, start, count):
    rows = count * QLEN
    row = lax.broadcasted_iota(jnp.int32, (rows, rows), 0)
    column = lax.broadcasted_iota(jnp.int32, (rows, rows), 1)
    limit = jnp.zeros((rows, rows), jnp.int32)
    for item in range(count):
        limit = jnp.where(column // QLEN == item, item * QLEN + lens[start + item], limit)
    return (row // QLEN == column // QLEN) & (row < limit)


VMEM_LIMIT = 58 * 1024 * 1024


def remote(src, dst, send, recv, where):
    return pltpu.make_async_remote_copy(
        src_ref=src, dst_ref=dst, send_sem=send, recv_sem=recv,
        device_id=where, device_id_type=MESH,
    )


def greet(targets):
    barrier = pltpu.get_barrier_semaphore()
    for where in targets:
        pl.semaphore_signal(barrier, inc=1, device_id=where, device_id_type=MESH)
    pl.semaphore_wait(barrier, len(targets))


def forward_kernel(
    parts, x_query, x_passage, qlens, plens, positive,
    b_qv, b_o, g_attn, c_attn, b_in, b_out, g_ffn, c_ffn, wqkv, wo, win, wout,
    o_left, o_qkv, o_pq, o_pp, o_pre, o_slope, o_ffn, both_par,
    l_qkv, l_o, l_in, l_out, hid_q, hid_p, land_a, gcls, loss,
    tok, out, bqkv, bo, bin_, bout, qkv, pq, pp, mixed, pre, normed_full, normed, up, act,
    slope, ffn, rows8, rows48, packed, every, stack,
    load, save, xload, parsend, parrecv, wsend, wrecv, hsend, hrecv, hlocal, gsend, grecv, psend, precv, asend, arecv,
):
    core = lax.axis_index("section")
    me = lax.axis_index("batch")
    peer = {"section": 1 - core}
    features = wo.shape[0]
    count_q, count_p = x_query.shape[0] // 2, x_passage.shape[0] // 2
    split = count_q * QLEN
    tall = count_p
    total = (count_q + count_p) * QLEN
    own = (wqkv, wo, win, wout)
    land = (l_qkv, l_o, l_in, l_out)
    buffers = (bqkv, bo, bin_, bout)

    gets = [
        pltpu.make_async_copy(
            x_query.at[pl.ds(core * count_q, count_q)], tok.at[0, pl.ds(0, count_q)], xload.at[0]
        ),
        pltpu.make_async_copy(
            x_passage.at[pl.ds(core * tall, tall)], tok.at[0, pl.ds(count_q, tall)], xload.at[1]
        ),
    ]
    for copy in gets:
        copy.start()

    def local(source, spot):
        return pltpu.make_async_copy(source[spot], buffers[spot], load.at[spot])

    def stash(spot):
        return pltpu.make_async_copy(buffers[spot], land[spot], load.at[4 + spot])

    def give_first(spot):
        return remote(own[spot], buffers[spot], wsend.at[spot], wrecv.at[spot], peer)

    def give_second(spot):
        return remote(own[spot], land[spot], wsend.at[spot], wrecv.at[spot], peer)

    others = [peer]
    if parts == 16:
        for step in range(1, parts):
            others.append({"batch": (me + step) % parts})

    @pl.when(core == 0)
    def _():
        for spot in range(4):
            local(own, spot).start()

    vectors = (b_qv, b_o, g_attn, c_attn, b_in, b_out, g_ffn, c_ffn)
    spot = 0
    for ref in vectors:
        for item in range(ref.shape[1] // features):
            both_par[core, spot : spot + 1] = ref[:, item * features : (item + 1) * features]
            spot += 1
    both_par[core, spot:16] = jnp.zeros((16 - spot, features), FULL)
    greet(others)
    give_par = remote(both_par.at[core], both_par.at[core], parsend, parrecv, peer)
    give_par.start()

    @pl.when(core == 0)
    def _():
        for spot in range(4):
            give_first(spot).start()

    @pl.when(core == 1)
    def _():
        for spot in range(4):
            give_second(spot).start()

    def weight_first(spot):
        @pl.when(core == 0)
        def _():
            local(own, spot).wait()

        @pl.when(core == 1)
        def _():
            give_first(spot).wait_recv()
            stash(spot).start()

    def fetch_second(spot):
        @pl.when(core == 0)
        def _():
            give_second(spot).wait_recv()
            local(land, spot).start()

        @pl.when(core == 1)
        def _():
            stash(spot).wait()
            local(own, spot).start()

    def weight(layer, spot):
        if layer == 0:
            weight_first(spot)
        else:
            local(own, spot).wait()

    saves = {}

    def keep(name, layer, source, target):
        saves[name, layer] = pltpu.make_async_copy(
            source, target, save.at[len(saves)]
        )
        saves[name, layer].start()

    places = {"act0": 0, "act1": 1, "act2": 2, "act3": 3, "normed": 4, "mixed": 5, "tok": 6}

    def left_give(layer, spot, source):
        return remote(
            source, land_a.at[layer, spot], asend.at[layer, spot], arecv.at[layer, spot], peer
        )

    def keep_left(name, layer, source):
        keep(name, layer, source, o_left.at[layer, places[name]])
        if layer == 1:
            left_give(1, places[name], source).start()

    def free(name, layer):
        if layer == 1:
            saves[name, 0].wait()

    for copy in gets:
        copy.wait()

    remote(both_par.at[core], both_par.at[1 - core], parsend, parrecv, peer).wait_recv()
    blocks = [(0, split, query_mask(qlens, core * count_q, count_q), pq, 0)]
    for item in range(count_p * QLEN // PLEN):
        row = lax.broadcasted_iota(jnp.int32, (PLEN, PLEN), 0)
        limit = plens[core * (count_p * QLEN // PLEN) + item]
        blocks.append((split + item * PLEN, PLEN, row < limit, pp, item * HEADS))

    for layer in (0, 1):
        base_row = 0
        par = both_par.at[layer]
        x = tok.at[layer].reshape(total, features)
        keep_left("tok", layer, x)
        weight(layer, 0)
        free("qkv", layer)

        def project(tile):
            lanes = lane_range(tile, features)
            bias = jnp.where(tile == 0, par[base_row : base_row + 1], 0.0)
            bias = jnp.where(tile == 2, par[base_row + 1 : base_row + 2], bias)
            qkv[:, lanes] = (dot(x[...], bqkv[:, lanes]) + bias).astype(LOW)

        over(3, project)
        keep("qkv", layer, qkv, o_qkv.at[layer])
        if layer == 1:
            fetch_second(3)
            for name, spot in places.items():
                saves[name, 0].wait()
                left_give(0, spot, o_left.at[0, spot]).start()
        for name in ("pq", "pp"):
            free(name, layer)

        def attend(index):
            tasks = []
            for step in range(PAIRS):
                for lo, rows, mask, probs, base in blocks:
                    tasks.append((index * PAIRS + step, lo, rows, mask, probs, base))

            def part(task, offset):
                hp, lo, rows = task[:3]
                return qkv[pl.ds(lo, rows), pl.ds(pl.multiple_of(offset + hp * 128, 128), 128)]

            scores = []
            for task in tasks:
                queries, keys = part(task, 0) * LOW(0.125), part(task, features)
                for head in (0, 1):
                    masked = jnp.where(head_lanes(task[2], head), keys, LOW(0))
                    scores.append(dot_last(masked, queries))
            lows = []
            for spot, value in enumerate(scores):
                hp, lo, rows, mask, probs, base = tasks[spot // 2]
                value = jnp.where(mask, value, -1000000000.0)
                weights = jnp.exp(value - jnp.max(value, 0, keepdims=True))
                inverse = 1.0 / jnp.sum(weights, 0, keepdims=True)
                low = (weights * inverse).astype(LOW)
                probs[base + 2 * hp + spot % 2] = low
                lows.append(low)
            for spot, task in enumerate(tasks):
                hp, lo, rows = task[:3]
                values = part(task, 2 * features).T
                outs = [
                    dot(values[64 * head : 64 * head + 64], lows[2 * spot + head])
                    for head in (0, 1)
                ]
                both = jnp.concatenate(outs, 0).astype(LOW).T
                mixed[pl.ds(lo, rows), pl.ds(pl.multiple_of(hp * 128, 128), 128)] = both

        over(features // 128 // PAIRS, attend)
        keep("pq", layer, pq, o_pq.at[layer])
        keep("pp", layer, pp, o_pp.at[layer])
        keep_left("mixed", layer, mixed)
        weight(layer, 1)
        free("pre", layer)
        pre[...] = (
            dot(mixed[...], bo[...]) + x[...].astype(FULL) + par[base_row + 2 : base_row + 3]
        )
        keep("pre", layer, pre, o_pre.at[layer])
        if layer == 0:
            fetch_second(0)
            fetch_second(1)

        def norm_one(index):
            rows = row_range(index)
            block = moments(pre[rows])[0] * par[base_row + 3 : base_row + 4]
            block = block + par[base_row + 4 : base_row + 5]
            normed_full[rows] = block
            normed[rows] = block.astype(LOW)

        over(total // ROWS, norm_one, UNROLL)
        keep_left("normed", layer, normed)
        weight(layer, 2)
        free("slope", layer)
        step_width = 256
        tiles = win.shape[1] // step_width

        def expand(tile):
            lanes = lane_range(tile, step_width)
            bias_lanes = lane_range(tile % 3, step_width)
            up[tile % 2] = (
                dot(normed[...], bin_[:, lanes])
                + par[pl.ds(base_row + 5 + tile // 3, 1), bias_lanes]
            )

        def bend(tile):
            lanes = lane_range(tile, step_width)
            for index in range(total // ROWS):
                rows = pl.ds(index * ROWS, ROWS)
                value, steep = gelu_pair(up[tile % 2, rows])
                act[rows, lanes] = value.astype(LOW)
                slope[rows, lanes] = steep.astype(LOW)

        expand(0)

        def grow(index):
            expand(index + 1)
            bend(index)

        over(tiles - 1, grow)
        bend(tiles - 1)
        for item in range(4):
            lanes = pl.ds(item * features, features)
            keep_left("act%d" % item, layer, act.at[:, lanes])
        keep("slope", layer, slope, o_slope.at[layer])
        weight(layer, 3)
        free("ffn", layer)
        ffn[...] = (
            dot(act[...], bout[...]) + normed_full[...] + par[base_row + 9 : base_row + 10]
        )
        keep("ffn", layer, ffn, o_ffn.at[layer])
        if layer == 0:
            fetch_second(2)
        target = tok.at[1] if layer == 0 else out
        flat = target.reshape(total, features)

        def norm_two(index):
            rows = row_range(index)
            block = moments(ffn[rows])[0] * par[base_row + 10 : base_row + 11]
            flat[rows] = (block + par[base_row + 11 : base_row + 12]).astype(LOW)

        over(total // ROWS, norm_two, UNROLL)
        sides = (
            (target.at[pl.ds(0, count_q)], hid_q.at[pl.ds(core * count_q, count_q)]),
            (target.at[pl.ds(count_q, tall)], hid_p.at[pl.ds(core * tall, tall)]),
        )

        @pl.when(core == layer)
        def _():
            for spot, (src, dst) in enumerate(sides):
                pltpu.make_async_copy(src, dst, hlocal.at[spot]).start()

        @pl.when(core != layer)
        def _():
            for spot, (src, dst) in enumerate(sides):
                remote(src, dst, hsend.at[spot], hrecv.at[spot], peer).start()

    if parts == 16:
        lead = [item * QLEN for item in range(count_q)] + [split]
        rows8[...] = jnp.zeros_like(rows8)
        for spot, row in enumerate(lead):
            rows8[spot : spot + 1] = flat[pl.ds(row, 16)].astype(FULL)[0:1]
        for tile in range(6):
            rows48[8 * tile : 8 * tile + 8] = rows8[:, 128 * tile : 128 * tile + 128]
        for item in range(count_q):
            value = positive[core * count_q + item].astype(FULL)
            rows48[8 * item + 5 : 8 * item + 6] = jnp.full((1, 128), value)
        packed[...] = rows48[...].astype(LOW)

        def share(step, slot):
            return remote(
                packed, every.at[core, slot], gsend.at[step], grecv.at[slot],
                {"batch": (me + step) % parts},
            )

        for step in range(1, parts):
            share(step, me).start()
        every[core, me] = packed[...]
        for step in range(1, parts):
            share(step, (me + parts - step) % parts).wait_recv()
        pass_on = remote(every.at[core], every.at[core], psend, precv, peer)
        pass_on.start()
        remote(every.at[core], every.at[1 - core], psend, precv, peer).wait_recv()
        pass_on.wait_send()
        for step in range(1, parts):
            share(step, me).wait_send()

        wide = 2 * parts * 8
        grid = every[...].astype(FULL).reshape(2 * parts, 48, 128)
        inner = lax.broadcasted_iota(jnp.int32, (2 * parts, 8, 128), 1)
        goal = jnp.zeros((2 * parts, 8, 128), FULL)
        for tile in range(6):
            block = grid[:, 8 * tile : 8 * tile + 8]
            stack[:, 128 * tile : 128 * tile + 128] = block.reshape(wide, 128).astype(LOW)
            if tile < count_q:
                found = jnp.sum(jnp.where(inner == 5, block, 0.0), 1, keepdims=True)
                goal = jnp.where(inner == tile, found, goal)
        row = lax.broadcasted_iota(jnp.int32, (wide, wide), 0)
        column = lax.broadcasted_iota(jnp.int32, (wide, wide), 1)
        scale = 2.0 / math.sqrt(features)
        logits = dot_last(stack[...], stack[...]) * scale
        device = column // 8
        passage = (device % parts) * 2 + device // parts
        is_passage = column % 8 == count_q
        is_query = row % 8 < count_q
        kept = jnp.where(is_passage, logits, -1e30)
        top = jnp.max(kept, -1, keepdims=True)
        log_total = top + jnp.log(jnp.sum(jnp.exp(kept - top), -1, keepdims=True))
        chosen = is_passage & (passage.astype(FULL) == goal.reshape(wide, 128)[:, 0:1])
        picked = jnp.sum(jnp.where(chosen, logits, 0.0), -1, keepdims=True)
        terms = jnp.where(is_query[:, 0:1], log_total - picked, 0.0)
        count = count_q * 2 * parts
        loss[...] = jnp.full((8, 128), jnp.sum(terms) / count)
        grads = jnp.exp(kept - log_total) - chosen.astype(FULL)
        grads = jnp.where(is_query & is_passage, grads, 0.0)
        up[0, 0:wide, 0:wide] = grads + grads.T
        mine = pl.multiple_of((core * parts + me) * 8, 8)
        picked_rows = up[0, pl.ds(mine, 8), 0:wide]
        gcls[...] = dot(picked_rows.astype(LOW), stack[...]) * scale

    for spot, (src, dst) in enumerate(sides):
        pltpu.make_async_copy(src, dst, hlocal.at[spot]).wait()
    theirs = (
        hid_q.at[pl.ds((1 - core) * count_q, count_q)],
        hid_p.at[pl.ds((1 - core) * tall, tall)],
    )
    for spot, (src, dst) in enumerate(zip((item[0] for item in sides), theirs)):
        remote(src, dst, hsend.at[spot], hrecv.at[spot], peer).wait()
    for spot in range(4):
        give_second(spot).wait_send()
    give_par.wait_send()
    for (name, layer), copy in saves.items():
        if layer == 1:
            copy.wait()
    for layer in (0, 1):
        for spot in range(7):
            left_give(layer, spot, o_left.at[layer, spot]).wait()


def forward_both(parts, x_query, x_passage, qlens, plens, positive, vectors, own):
    queries, features = x_query.shape[0], x_query.shape[2]
    passages = x_passage.shape[0]
    total = (queries + passages) // 2 * QLEN
    wide = own[2].shape[1]
    split = queries // 2 * QLEN
    heads_p = HEADS * (passages // 2 * QLEN // PLEN)
    kept = [
        ((7, total, features), LOW),
        ((total, 3 * features), LOW),
        ((HEADS, split, split), LOW),
        ((heads_p, PLEN, PLEN), LOW),
        ((total, features), FULL),
        ((total, wide), LOW),
        ((total, features), FULL),
        ((16, features), FULL),
    ]
    shape = jax.ShapeDtypeStruct
    anywhere = pl.BlockSpec(memory_space=pl.ANY)
    vmem = pl.BlockSpec(memory_space=pltpu.VMEM)
    smem = pl.BlockSpec(memory_space=pltpu.SMEM)
    dma = pltpu.SemaphoreType.DMA
    scratch = [
        pltpu.VMEM((2, total // QLEN, QLEN, features), LOW),
        pltpu.VMEM((total // QLEN, QLEN, features), LOW),
    ]
    scratch += [pltpu.VMEM(item.shape, item.dtype) for item in own]
    scratch += [pltpu.VMEM(size, kind) for size, kind in kept[1:4]]
    scratch += [
        pltpu.VMEM((total, features), LOW),
        pltpu.VMEM((total, features), FULL),
        pltpu.VMEM((total, features), FULL),
        pltpu.VMEM((total, features), LOW),
        pltpu.VMEM((2, total, 256), FULL),
        pltpu.VMEM((total, wide), LOW),
        pltpu.VMEM((total, wide), LOW),
        pltpu.VMEM((total, features), FULL),
    ]
    scratch += [
        pltpu.VMEM((8, features), FULL),
        pltpu.VMEM((48, 128), FULL),
        pltpu.VMEM((48, 128), LOW),
        pltpu.VMEM((2, 16, 48, 128), LOW),
        pltpu.VMEM((256, features), LOW),
        dma((8,)),
        dma((26,)),
        dma((2,)),
        dma,
        dma,
        dma((4,)),
        dma((4,)),
        dma((2,)),
        dma((2,)),
        dma((2,)),
        dma((16,)),
        dma((16,)),
        dma,
        dma,
        dma((2, 7)),
        dma((2, 7)),
    ]
    return pl.pallas_call(
        functools.partial(forward_kernel, parts),
        out_shape=[shape((2,) + size, kind) for size, kind in kept]
        + [shape(item.shape, item.dtype) for item in own]
        + [
            shape(x_query.shape, LOW),
            shape(x_passage.shape, LOW),
            shape((2, 7, total, features), LOW),
            shape((8, features), FULL),
            shape((8, 128), FULL),
        ],
        in_specs=[anywhere, anywhere, smem, smem, smem] + [vmem] * 8 + [anywhere] * 4,
        out_specs=[anywhere] * 7 + [vmem] + [anywhere] * 7 + [vmem] * 2,
        scratch_shapes=scratch,
        compiler_params=pltpu.CompilerParams(
            collective_id=2, has_side_effects=True, vmem_limit_bytes=VMEM_LIMIT
        ),
    )(x_query, x_passage, qlens, plens, positive, *vectors, *own)


def add_rows(block):
    return jnp.sum(block.reshape(block.shape[0] // 8, 8, block.shape[1]), 0)


def norm_back(source, grad_of, gain, total, store):
    features = source.shape[1]
    zero = jnp.zeros((8, features), FULL)

    def step(index, carry):
        rows = row_range(index)
        grad = grad_of(index)
        unit, inverse = moments(source[rows])
        scaled = grad * gain
        back = inverse * (
            scaled
            - jnp.mean(scaled, -1, keepdims=True)
            - unit * jnp.mean(scaled * unit, -1, keepdims=True)
        )
        store(rows, back)
        return (
            carry[0] + add_rows(grad * unit),
            carry[1] + add_rows(grad),
            carry[2] + add_rows(back),
        )

    sums = lax.fori_loop(0, total // ROWS, step, (zero, zero, zero), unroll=UNROLL)
    return [jnp.sum(item, 0, keepdims=True) for item in sums]


LAGS = (2, 4, 6)
RING = 12
HELD = 8


def left_index(ch):
    return (
        jnp.minimum(ch, 4) + (ch >= 8).astype(jnp.int32) + (ch >= 9).astype(jnp.int32)
    )


def right_index(ch):
    return jnp.maximum(ch - 3, 0)


def backward_kernel(parts, *refs):
    small = parts == 16
    refs = list(refs)

    def take(count):
        front = refs[:count]
        del refs[:count]
        return front

    cot_query, cot_passage, qlens, plens, gcls, par = take(6)
    own, land = take(4), take(4)
    left, h_qkv, h_pq, h_pp, h_pre, h_slope, h_ffn, land_a = take(8)
    if small:
        o_qkv, o_o, o_in, o_out, o_vec, o_gq, o_gp, land_g, own_g = take(9)
    else:
        vpar, o_gq, o_gp, f_pro, f_att, f_up, f_flo = take(7)
    buffers = take(4)
    bqkv, bo, bin_, bout = buffers
    qkv, pq, pp, source, slope, gsrc = take(6)
    attn_full, attn, steep, flow_full, flow = take(5)
    gmixed = flow
    grow = flow_full.reshape(flow.shape[0] // QLEN, QLEN, flow.shape[1])
    wload, fetch, cload, hsend, hrecv, hlocal, ksem = take(7)
    if small:
        vpar, a_buf, g_buf, stage, s1, r1, s2, r2, s3, r3 = take(10)
        va, ra, vb, rb, vc, rc, rz = take(7)
        s1s, r1s, s2s, r2s, s3s, r3s, vsend, vrecv, zsend, zrecv = take(10)
        gs, gr, sl, gl = take(4)

    core = lax.axis_index("section")
    me = lax.axis_index("batch")
    peer = {"section": 1 - core}
    features = gcls.shape[1]
    total = flow.shape[0]
    split = pq.shape[1]
    count_q, tall = cot_query.shape[0] // 2, cot_passage.shape[0] // 2
    heads_p = pp.shape[0]
    blocks_p = PLEN // QLEN

    def weight_copy(spot, source_set):
        return pltpu.make_async_copy(source_set[spot], buffers[spot], wload.at[spot])

    def weight_start(layer, spot):
        @pl.when(core == layer)
        def _():
            weight_copy(spot, own).start()

        @pl.when(core != layer)
        def _():
            weight_copy(spot, land).start()

    def weight_wait(spot):
        weight_copy(spot, own).wait()

    saved = ((h_ffn, source), (h_slope, slope), (h_pre, source), (h_qkv, qkv), (h_pq, pq), (h_pp, pp))

    def saved_copy(layer, spot):
        src, dst = saved[spot]
        return pltpu.make_async_copy(src.at[layer], dst, fetch.at[spot])

    cots = [
        pltpu.make_async_copy(
            cot_query.at[pl.ds(core * count_q, count_q)], gsrc.at[pl.ds(0, count_q)], cload.at[0]
        ),
        pltpu.make_async_copy(
            cot_passage.at[pl.ds(core * tall, tall)], gsrc.at[pl.ds(count_q, tall)], cload.at[1]
        ),
    ]
    saved_copy(1, 0).start()
    for copy in cots:
        copy.start()
    weight_start(1, 3)
    saved_copy(1, 1).start()

    widths = ((flow, 1), (slope, 4), (attn, 1), (qkv, 3))

    def pieces_of(slot):
        base = (0, 1, 5, 6)[slot]
        ref, count = widths[slot]
        return [(base + item, ref, ref.shape[1] // 2, item) for item in range(count)]

    def own_piece(layer, piece):
        spot, ref, width, item = piece
        lanes = pl.ds(pl.multiple_of(core * width + item * CHUNK, 128), CHUNK)
        return pltpu.make_async_copy(ref.at[:, lanes], own_g.at[layer, spot], ksem.at[spot])

    def peer_piece(layer, piece):
        spot, ref, width, item = piece
        lanes = pl.ds(pl.multiple_of((1 - core) * width + item * CHUNK, 128), CHUNK)
        return remote(
            ref.at[:, lanes], land_g.at[layer, spot], gs.at[layer, spot], gr.at[layer, spot], peer
        )

    def whole_piece(layer, slot):
        ref = widths[slot][0]
        target = (f_flo, f_up, f_att, f_pro)[slot]
        return pltpu.make_async_copy(ref, target.at[layer], ksem.at[slot])

    def direct():
        spot, ref, width, item = pieces_of(0)[0]
        lanes = pl.ds(pl.multiple_of((1 - core) * width, 128), CHUNK)
        return remote(
            ref.at[:, lanes], g_buf.at[0, pl.ds(total, total)], gs.at[1, 0], gr.at[1, 0], peer
        )

    def give(layer, slot):
        if small and slot == 0:

            @pl.when(layer == 1)
            def _():
                direct().start()
                lanes = pl.ds(pl.multiple_of(core * CHUNK, 128), CHUNK)
                g_buf[0, pl.ds(0, total)] = flow[:, lanes]

            @pl.when(layer == 0)
            def _():
                piece = pieces_of(0)[0]
                peer_piece(layer, piece).start()
                own_piece(layer, piece).start()

        elif small:
            for piece in pieces_of(slot):
                peer_piece(layer, piece).start()
                own_piece(layer, piece).start()
        else:
            whole_piece(layer, slot).start()

    def given(layer, slot):
        if small:
            for piece in pieces_of(slot):
                peer_piece(layer, piece).wait_send()
                if slot > 0:
                    own_piece(layer, piece).wait()
                else:

                    @pl.when(layer == 0)
                    def _():
                        own_piece(layer, piece).wait()
        else:
            whole_piece(layer, slot).wait()

    def slot_zero(layer):
        saved_copy(layer, 0).wait()
        gains = par.at[layer]
        last = layer == 1

        def grad_of(index):
            block = gsrc[index].astype(FULL)
            beyond = jnp.maximum(index - count_q, 0)
            item = beyond // blocks_p
            query_limit = qlens[core * count_q + jnp.minimum(index, count_q - 1)]
            passage_limit = (
                plens[core * (tall // blocks_p) + item] - (beyond % blocks_p) * QLEN
            )
            limit = jnp.where(index < count_q, query_limit, passage_limit)
            limit = jnp.where(last, limit, QLEN)
            lead = jnp.where(index < count_q, index, count_q + item)
            starts = (index < count_q) | (beyond % blocks_p == 0)
            row = lax.broadcasted_iota(jnp.int32, block.shape, 0)
            block = jnp.where(row < limit, block, 0.0)
            extra = gcls[pl.ds(lead, 1)] * jnp.where(starts & last, 1.0, 0.0)
            return block + jnp.where(row == 0, extra, 0.0)

        def store(rows, back):
            flow_full[rows] = back
            flow[rows] = back.astype(LOW)

        gain, shift, bias = norm_back(source, grad_of, gains[10:11], total, store)
        sums = vpar.at[layer]
        sums[10:11], sums[11:12], sums[9:10] = gain, shift, bias
        give(layer, 0)
        saved_copy(layer, 2).start()

    width = 256
    tiles = bout.shape[0] // width

    def slot_one(layer):
        saved_copy(layer, 1).wait()
        weight_wait(3)
        sums = vpar.at[layer]

        def shrink(tile):
            rows_of = pl.ds(pl.multiple_of(tile * width, width), width)
            steep[tile % 2] = dot_last(flow[...], bout[rows_of])

        def bend(tile):
            lanes = lane_range(tile, width)
            acc = jnp.zeros((8, width), FULL)
            for index in range(total // ROWS):
                rows = pl.ds(index * ROWS, ROWS)
                low = (steep[tile % 2, rows] * slope[rows, lanes].astype(FULL)).astype(LOW)
                slope[rows, lanes] = low
                acc = acc + add_rows(low.astype(FULL))
            sums[pl.ds(5 + tile // 3, 1), lane_range(tile % 3, width)] = jnp.sum(
                acc, 0, keepdims=True
            )

        shrink(0)

        def both(index):
            shrink(index + 1)
            bend(index)

        over(tiles - 1, both)
        bend(tiles - 1)
        give(layer, 1)

        @pl.when(layer == 1)
        def _():
            weight_start(0, 3)

    def slot_two(layer):
        weight_wait(2)
        flow_full[...] += dot_last(slope[...], bin_[...])
        saved_copy(layer, 2).wait()
        gains, sums = par.at[layer], vpar.at[layer]

        def store(rows, back):
            attn_full[rows] = back
            attn[rows] = back.astype(LOW)

        gain, shift, bias = norm_back(
            source, lambda index: flow_full[row_range(index)], gains[3:4], total, store
        )
        sums[3:4], sums[4:5], sums[2:3] = gain, shift, bias
        give(layer, 2)
        weight_wait(1)
        gmixed[...] = dot_last(attn[...], bo[...]).astype(LOW)

        @pl.when(layer == 1)
        def _():
            weight_start(0, 2)
            weight_start(0, 1)
            saved_copy(0, 0).start()
            saved_copy(0, 1).start()

    blocks = [(0, split, pq, 0)]
    for item in range(heads_p // HEADS):
        blocks.append((split + item * PLEN, PLEN, pp, item * HEADS))

    def attend(index):
        tasks = []
        for step in range(PAIRS):
            for block in blocks:
                tasks.append((index * PAIRS + step,) + block)

        def spot_of(task, offset):
            hp, lo, rows = task[:3]
            return (pl.ds(lo, rows), pl.ds(pl.multiple_of(offset + hp * 128, 128), 128))

        grads = []
        for task in tasks:
            values, back = qkv[spot_of(task, 2 * features)], gmixed[spot_of(task, 0)]
            for head in (0, 1):
                masked = jnp.where(head_lanes(task[2], head), values, LOW(0))
                grads.append(dot_last(masked, back))
        lows = []
        for spot, grad_probs in enumerate(grads):
            hp, lo, rows, probs, base = tasks[spot // 2]
            full = probs[base + 2 * hp + spot % 2].astype(FULL)
            inner = jnp.sum(grad_probs * full, 0, keepdims=True)
            lows.append((full * (grad_probs - inner)).astype(LOW))
        for spot, task in enumerate(tasks):
            hp, lo, rows, probs, base = task
            queries, keys = qkv[spot_of(task, 0)], qkv[spot_of(task, features)]
            back = gmixed[spot_of(task, 0)]
            turned = keys.T
            outs = []
            for head in (0, 1):
                grad_scores = lows[2 * spot + head]
                outs.append(
                    (
                        dot(turned[64 * head : 64 * head + 64], grad_scores) * 0.125,
                        dot(grad_scores, queries) * 0.125,
                        dot(probs[base + 2 * hp + head], back),
                    )
                )
            first = head_lanes(rows, 0)
            both = jnp.concatenate([outs[0][0], outs[1][0]], 0)
            qkv[spot_of(task, 0)] = both.astype(LOW).T
            for item in (1, 2):
                both = jnp.where(first, outs[0][item], outs[1][item])
                qkv[spot_of(task, item * features)] = both.astype(LOW)

    def grads_here(spot):
        lo, count, target = ((0, count_q, o_gq), (count_q, tall, o_gp))[spot]
        return pltpu.make_async_copy(
            grow.at[pl.ds(lo, count)], target.at[pl.ds(core * count, count)], hlocal.at[spot]
        )

    def grads_there(spot):
        lo, count, target = ((0, count_q, o_gq), (count_q, tall, o_gp))[spot]
        return remote(
            grow.at[pl.ds(lo, count)],
            target.at[pl.ds(core * count, count)],
            hsend.at[spot],
            hrecv.at[spot],
            peer,
        )

    def slot_three(layer):
        for spot in (3, 4, 5):
            saved_copy(layer, spot).wait()
        over(features // 128 // PAIRS, attend)
        give(layer, 3)
        sums = vpar.at[layer]

        def bias_sums(index, carry):
            rows = row_range(index)
            return (
                carry[0] + add_rows(qkv[rows, pl.ds(0, features)].astype(FULL)),
                carry[1] + add_rows(qkv[rows, pl.ds(2 * features, features)].astype(FULL)),
            )

        zero = jnp.zeros((8, features), FULL)
        found = lax.fori_loop(0, total // ROWS, bias_sums, (zero, zero), unroll=2)
        sums[0:1] = jnp.sum(found[0], 0, keepdims=True)
        sums[1:2] = jnp.sum(found[1], 0, keepdims=True)
        sums[12:16] = jnp.zeros((4, features), FULL)
        weight_wait(0)
        rows_all = attn_full[...] + dot_last(qkv[...], bqkv[...])
        flow_full[...] = rows_all
        gsrc[...] = rows_all.astype(LOW).reshape(gsrc.shape)

        @pl.when(core == layer)
        def _():
            for spot in (0, 1):
                grads_here(spot).start()

        @pl.when(core != layer)
        def _():
            for spot in (0, 1):
                grads_there(spot).start()

        @pl.when(layer == 1)
        def _():
            weight_start(0, 0)

    def grads_given(layer):
        @pl.when(core == layer)
        def _():
            for spot in (0, 1):
                grads_here(spot).wait()

        @pl.when(core != layer)
        def _():
            for spot in (0, 1):
                grads_there(spot).wait_send()

    slots = (slot_zero, slot_one, slot_two, slot_three)

    def reload(layer, slot):
        @pl.when(layer == 1)
        def _():
            if slot == 3:
                for spot in (3, 4, 5):
                    saved_copy(0, spot).start()

    def rest_of_loads():
        for spot in (2, 1, 0):
            weight_start(1, spot)
        for spot in (3, 4, 5):
            saved_copy(1, spot).start()

    def grads_came():
        lands = ((o_gq, count_q), (o_gp, tall))
        for spot, (target, count) in enumerate(lands):
            there = target.at[pl.ds((1 - core) * count, count)]
            remote(there, there, hsend.at[spot], hrecv.at[spot], peer).wait_recv()

    if not small:
        greet([peer])
        rest_of_loads()
        for copy in cots:
            copy.wait()
        for layer in (1, 0):
            for slot in range(4):
                slots[slot](layer)
                given(layer, slot)
                reload(layer, slot)
            grads_given(layer)
        grads_came()
        return

    x, y, z = me % 2, (me // 2) % 2, me // 4
    px, py = me + 1 - 2 * x, me + 2 - 4 * y
    targets = [{"batch": px}, {"batch": py}, peer]
    for step in (1, 2, 3):
        other = ((z + step) % 4) * 4 + me % 4
        targets += [{"section": sec, "batch": other} for sec in (0, 1)]

    def stage_copy(number, side):
        layer, spot = 1 - number // 7, number % 7
        src = left if side == 0 else land_a
        return pltpu.make_async_copy(
            src.at[layer, spot], stage.at[number % 2, side], sl.at[number % 2, side]
        )

    def stage_start(number):
        stage_copy(number, 0).start()
        stage_copy(number, 1).start()

    def turn(number, spot):
        for side in (0, 1):
            stage_copy(number, side).wait()
        for side in (0, 1):
            lanes = pl.ds(side * total, total)
            for half in range(features // CHUNK):
                block = stage[number % 2, side, :, pl.ds(half * CHUNK, CHUNK)].T
                if spot > 3:
                    a_buf[spot, pl.ds(2 * half, 2), :, :, :, lanes] = block.reshape(
                        2, 2, 2, BLOCK, total
                    )
                else:
                    shaped = block.reshape(2, 4, BLOCK, total)
                    for item in range(4):
                        a_buf[item, spot, half, :, :, lanes] = shaped[:, item]

        if isinstance(number, int):
            stage_start(number + 2)
        else:

            @pl.when(number + 2 < 14)
            def _():
                stage_start(number + 2)

    stage_start(0)
    stage_start(1)
    for spot in range(4):
        turn(spot, spot)
    greet(targets)

    def right_copy(layer, spot, side):
        src = own_g if side == 0 else land_g
        return pltpu.make_async_copy(
            src.at[layer, spot], g_buf.at[spot, pl.ds(side * total, total)], gl.at[spot, side]
        )

    def right_start(k):
        ch = k % COUNT
        layer = 1 - k // COUNT

        @pl.when((k > 0) & (k < 2 * COUNT) & ((ch == 0) | (ch >= 4)))
        def _():
            spot = right_index(ch)
            right_copy(layer, spot, 0).start()
            remote(
                own_g.at[layer, spot], land_g.at[layer, spot],
                gs.at[layer, spot], gr.at[layer, spot], peer,
            ).wait_recv()
            right_copy(layer, spot, 1).start()

    def first(k, par_):
        return remote(
            s1.at[k % HELD], r1.at[k % RING], s1s.at[k], r1s.at[k],
            {"batch": px if par_ == 0 else py},
        )

    def second(k, par_):
        return remote(
            s2.at[k % 4], r2.at[k % HELD], s2s.at[k], r2s.at[k],
            {"batch": py if par_ == 0 else px},
        )

    def third(k, step):
        layer = 1 - k // COUNT
        zt = (z + step) % 4
        return remote(
            s3.at[k % 4, zt], r3.at[core, k % COUNT, z], s3s.at[k, step],
            r3s.at[core, k % COUNT, z], {"section": layer, "batch": zt * 4 + me % 4},
        )

    def third_in(k, step, src_core):
        zs = (z + 4 - step) % 4
        return remote(
            s3.at[k % 4, zs], r3.at[src_core, k % COUNT, zs], s3s.at[k, step],
            r3s.at[src_core, k % COUNT, zs], peer,
        )

    def product(k, block, rows):
        return dot(block.reshape(rows, 2 * total), g_buf[right_index(k % COUNT)])

    def left_of(k):
        return a_buf.at[left_index(k % COUNT)]

    def ready(k, par_):
        ch = k % COUNT

        @pl.when((k > 0) & ((ch == 0) | (ch >= 4)))
        def _():
            for side in (0, 1):
                right_copy(0, right_index(ch), side).wait()

        base = (k // COUNT) * 7
        if par_ == 0:

            @pl.when(k == 0)
            def _():
                direct().wait_recv()

            @pl.when(k == COUNT)
            def _():
                for spot in range(4):
                    turn(base + spot, spot)

            for spot, at in ((4, 4), (5, 8)):

                @pl.when(ch == at)
                def _():
                    turn(base + spot, spot)
        else:

            @pl.when(ch == 9)
            def _():
                turn(base + 6, 6)

    def part_one(k, par_):
        ready(k, par_)
        ref = left_of(k)
        block = ref[:, :, 1 - x] if par_ == 0 else ref[:, 1 - y]
        s1[k % HELD] = product(k, block, 8 * BLOCK).astype(LOW).reshape(4, 2, BLOCK, CHUNK)
        first(k, par_).start()

    def part_two(k, par_):
        first(k, par_).wait()
        ref = left_of(k)
        if par_ == 0:
            block, came = ref[:, 1 - y, x], r1[k % RING, :, 1 - y]
        else:
            block, came = ref[:, y, 1 - x], r1[k % RING, :, 1 - x]
        value = product(k, block, 4 * BLOCK).reshape(4, BLOCK, CHUNK) + came.astype(FULL)
        s2[k % 4] = value.astype(LOW)
        second(k, par_).start()

    def part_three(k, par_):
        second(k, par_).wait()
        layer = 1 - k // COUNT
        ref = left_of(k)
        came = r1[k % RING, :, y] if par_ == 0 else r1[k % RING, :, x]
        value = (
            product(k, ref[:, y, x], 4 * BLOCK).reshape(4, BLOCK, CHUNK)
            + came.astype(FULL)
            + r2[k % HELD].astype(FULL)
        )
        s3[k % 4] = value.astype(LOW)
        for step in (1, 2, 3):
            third(k, step).start()

        @pl.when(core != layer)
        def _():
            third(k, 0).start()

        @pl.when(core == layer)
        def _():
            r3[core, k % COUNT, z] = s3[k % 4, z]

    def part_four(k, par_):
        layer = 1 - k // COUNT
        ch = k % COUNT
        for step in (1, 2, 3):
            third(k, step).wait_send()

        @pl.when(core != layer)
        def _():
            third(k, 0).wait_send()

        @pl.when(core == layer)
        def _():
            for step in (1, 2, 3):
                for src_core in (0, 1):
                    third_in(k, step, src_core).wait_recv()
            third_in(k, 0, 1 - core).wait_recv()
            for src_core in (0, 1):
                value = jnp.sum(r3[src_core, ch].astype(FULL), 0)

                @pl.when(ch < 4)
                def _():
                    o_out[ch, :, pl.ds(src_core * CHUNK, CHUNK)] = value

                @pl.when((ch >= 4) & (ch < 8))
                def _():
                    start = pl.multiple_of((ch - 4) * CHUNK + src_core * 4 * CHUNK, 128)
                    o_in[:, pl.ds(start, CHUNK)] = value

                @pl.when(ch == 8)
                def _():
                    o_o[:, pl.ds(src_core * CHUNK, CHUNK)] = value

                @pl.when(ch >= 9)
                def _():
                    start = pl.multiple_of((ch - 9) * CHUNK + src_core * 3 * CHUNK, 128)
                    o_qkv[:, pl.ds(start, CHUNK)] = value

    vec_cross = remote(vpar.at[1 - core], ra, vsend.at[0], vrecv.at[0], peer)
    vec_x = remote(va, rb, vsend.at[1], vrecv.at[1], {"batch": px})
    vec_y = remote(vb, rc, vsend.at[2], vrecv.at[2], {"batch": py})

    def vec_z(step, slot):
        return remote(
            vc, rz.at[slot], zsend.at[step], zrecv.at[slot],
            {"batch": ((z + step) % 4) * 4 + me % 4},
        )

    steps = 2 * COUNT + LAGS[2]

    starts = ((-1, 3), (0, 4), (1, 6), (2, 8))

    def pair(turn_index, carry):
        kk = turn_index - 1
        layer = (kk < 3).astype(jnp.int32)

        for slot, (one, two) in enumerate(starts):

            @pl.when((kk == one + 1) | (kk == two + 1))
            def _():
                done = (kk == one + 1).astype(jnp.int32)
                given(done, slot)
                reload(done, slot)
                if slot == 3:
                    grads_given(done)

        @pl.when(kk == -1)
        def _():
            rest_of_loads()
            for copy in cots:
                copy.wait()

        for par_ in (0, 1):
            right_start(2 * kk + 2 + par_)

        for par_ in (0, 1):
            k = 2 * kk + par_
            for lag, part in zip(LAGS, (part_two, part_three, part_four)):

                @pl.when((k >= lag) & (k < 2 * COUNT + lag))
                def _():
                    part(k - lag, par_)

        for slot, (one, two) in enumerate(starts):
            if slot == 0:

                @pl.when((kk == one) | (kk == two))
                def _():
                    slots[slot](layer)

        for par_ in (0, 1):
            k = 2 * kk + 2 + par_

            @pl.when(k < 2 * COUNT)
            def _():
                part_one(k, par_)

        for slot, (one, two) in enumerate(starts):
            if slot > 0:

                @pl.when((kk == one) | (kk == two))
                def _():
                    slots[slot](layer)

        @pl.when(kk == 9)
        def _():
            vec_cross.start()

        @pl.when(kk == 10)
        def _():
            vec_cross.wait()
            va[...] = vpar[core] + ra[...]
            vec_x.start()

        @pl.when(kk == 11)
        def _():
            vec_x.wait()
            vb[...] = va[...] + rb[...]
            vec_y.start()

        @pl.when(kk == 12)
        def _():
            vec_y.wait()
            vc[...] = vb[...] + rc[...]
            for step in (1, 2, 3):
                vec_z(step, z).start()

        @pl.when(kk == 14)
        def _():
            for step in (1, 2, 3):
                vec_z(step, z).wait_send()
                vec_z(step, (z + 4 - step) % 4).wait_recv()
            rz[z] = vc[...]
            o_vec[...] = jnp.sum(rz[...], 0)

        return carry

    lax.fori_loop(0, steps // 2 + 1, pair, 0)
    grads_came()


def backward_both(parts, cots, qlens, plens, gcls, par, own, land, kept):
    small = parts == 16
    cot_query, cot_passage = cots
    left, h_qkv, h_pq, h_pp, h_pre, h_slope, h_ffn = kept[:7]
    total, features = left.shape[2:]
    wide = own[2].shape[1]
    shape = jax.ShapeDtypeStruct
    anywhere = pl.BlockSpec(memory_space=pl.ANY)
    vmem = pl.BlockSpec(memory_space=pltpu.VMEM)
    smem = pl.BlockSpec(memory_space=pltpu.SMEM)
    dma = pltpu.SemaphoreType.DMA
    grads = [shape(cot_query.shape, FULL), shape(cot_passage.shape, FULL)]
    if small:
        out_shape = [
            shape((BLOCK, 3 * features), FULL),
            shape((BLOCK, features), FULL),
            shape((BLOCK, wide), FULL),
            shape((4, BLOCK, features), FULL),
            shape((16, features), FULL),
            *grads,
            shape((2, 9, total, CHUNK), LOW),
            shape((2, 9, total, CHUNK), LOW),
        ]
        out_specs = [vmem] * 5 + [anywhere] * 4
    else:
        out_shape = [
            shape((2, 16, features), FULL),
            *grads,
            shape((2, total, 3 * features), LOW),
            shape((2, total, features), LOW),
            shape((2, total, wide), LOW),
            shape((2, total, features), LOW),
        ]
        out_specs = [vmem] + [anywhere] * 6
    scratch = [pltpu.VMEM(item.shape, item.dtype) for item in own]
    scratch += [
        pltpu.VMEM(h_qkv.shape[1:], LOW),
        pltpu.VMEM(h_pq.shape[1:], LOW),
        pltpu.VMEM(h_pp.shape[1:], LOW),
        pltpu.VMEM((total, features), FULL),
        pltpu.VMEM((total, wide), LOW),
        pltpu.VMEM((total // QLEN, QLEN, features), LOW),
        pltpu.VMEM((total, features), FULL),
        pltpu.VMEM((total, features), LOW),
        pltpu.VMEM((2, total, 256), FULL),
        pltpu.VMEM((total, features), FULL),
        pltpu.VMEM((total, features), LOW),
        dma((4,)),
        dma((6,)),
        dma((2,)),
        dma((2,)),
        dma((2,)),
        dma((2,)),
        dma((9,)),
    ]
    if small:
        steps = 2 * COUNT
        vector = pltpu.VMEM((16, features), FULL)
        scratch += [
            pltpu.VMEM((2, 16, features), FULL),
            pltpu.VMEM((7, 4, 2, 2, BLOCK, 2 * total), LOW),
            pltpu.VMEM((9, 2 * total, CHUNK), LOW),
            pltpu.VMEM((2, 2, total, features), LOW),
            pltpu.VMEM((HELD, 4, 2, BLOCK, CHUNK), LOW),
            pltpu.VMEM((RING, 4, 2, BLOCK, CHUNK), LOW),
            pltpu.VMEM((4, 4, BLOCK, CHUNK), LOW),
            pltpu.VMEM((HELD, 4, BLOCK, CHUNK), LOW),
            pltpu.VMEM((4, 4, BLOCK, CHUNK), LOW),
            pltpu.VMEM((2, COUNT, 4, BLOCK, CHUNK), LOW),
            *[vector] * 6,
            pltpu.VMEM((4, 16, features), FULL),
            dma((steps,)),
            dma((steps,)),
            dma((steps,)),
            dma((steps,)),
            dma((steps, 4)),
            dma((2, COUNT, 4)),
            dma((3,)),
            dma((3,)),
            dma((4,)),
            dma((4,)),
            dma((2, 9)),
            dma((2, 9)),
            dma((2, 2)),
            dma((9, 2)),
        ]
    return pl.pallas_call(
        functools.partial(backward_kernel, parts),
        out_shape=out_shape,
        in_specs=[anywhere, anywhere, smem, smem, vmem, vmem] + [anywhere] * 16,
        out_specs=out_specs,
        scratch_shapes=scratch,
        compiler_params=pltpu.CompilerParams(
            collective_id=1, has_side_effects=True, vmem_limit_bytes=60 * 1024 * 1024
        ),
    )(cot_query, cot_passage, qlens, plens, gcls, par, *own, *land, *kept)


def finish_kernel(parts, *refs):
    big, vec, loss = refs[:8], refs[8], refs[9]
    outs, small, total = refs[10:18], refs[18:26], refs[26]
    held, come, go = refs[27:35], refs[35], refs[36]
    copies = []
    for src, mid, dst in zip(big, held, outs):
        pieces = 2 if src.shape[0] % 32 == 0 or len(src.shape) == 3 else 1
        size = src.shape[0] // pieces
        for item in range(pieces):
            rows, spot = pl.ds(item * size, size), len(copies)
            copies.append(
                (
                    pltpu.make_async_copy(src.at[rows], mid.at[rows], come.at[spot]),
                    pltpu.make_async_copy(mid.at[rows], dst.at[rows], go.at[spot]),
                )
            )
            copies[-1][0].start()
    me = lax.axis_index("batch")
    features = vec.shape[1]
    for at, count, out in zip((0, 2, 3, 4, 5, 9, 10, 11), (2, 1, 1, 1, 4, 1, 1, 1), small):
        size = count * features // parts
        every = parts // count
        block = vec[pl.ds(at + me // every, 1)]
        block = jnp.broadcast_to(block, (8, features))
        turned = pltpu.roll(block, (features - size * (me % every)) % features, 1)
        out[...] = turned[0:1, 0:size]
    total[...] = loss[0:1, 0:1]
    for came, left in copies:
        came.wait()
        left.start()
    for came, left in copies:
        left.wait()


def finish(parts, big, vec, loss):
    features = vec.shape[1]
    anywhere = pl.BlockSpec(memory_space=pl.ANY)
    vmem = pl.BlockSpec(memory_space=pltpu.VMEM)
    shape = jax.ShapeDtypeStruct
    return pl.pallas_call(
        functools.partial(finish_kernel, parts),
        out_shape=[shape(item.shape, item.dtype) for item in big]
        + [shape((1, count * features // parts), FULL) for count in (2, 1, 1, 1, 4, 1, 1, 1)]
        + [shape((1, 1), FULL)],
        in_specs=[anywhere] * 8 + [vmem] * 2,
        out_specs=[anywhere] * 8 + [vmem] * 9,
        scratch_shapes=[pltpu.VMEM(item.shape, item.dtype) for item in big]
        + [pltpu.SemaphoreType.DMA((16,)), pltpu.SemaphoreType.DMA((16,))],
    )(*big, vec, loss)


def per_device(
    parts,
    x_query,
    x_passage,
    len_query,
    len_passage,
    positive,
    cot_query,
    cot_passage,
    *weights,
):
    core = lax.axis_index("section")
    on_first = core == 0
    own_set = [member[0] for member in weights]
    own = [own_set[item] for item in (0, 2, 6, 8)]
    vectors = [weights[item] for item in (1, 3, 4, 5, 7, 9, 10, 11)]
    features = x_query.shape[2]
    half_q, half_p = x_query.shape[0] // 2, x_passage.shape[0] // 2
    *kept, par, l_qkv, l_o, l_in, l_out, hidden_q, hidden_p, land_a, grad_cls, loss = forward_both(
        parts,
        x_query,
        x_passage.reshape(-1, QLEN, features),
        len_query,
        len_passage,
        positive,
        vectors,
        own,
    )
    other = (l_qkv, l_o, l_in, l_out)
    if parts != 16:
        last = hidden_p.reshape(x_passage.shape)
        targets = lax.all_gather(positive, "batch", axis=0, tiled=True)
        own_q = hidden_q[:, 0]
        own_p = last[:, 0]
        last_q, last_p = (jnp.where(on_first, swap(item), item) for item in (own_q, own_p))
        cls_query = lax.all_gather(last_q, "batch", axis=0, tiled=True)
        cls_passage = lax.all_gather(last_p, "batch", axis=0, tiled=True)
        score_scale = 2.0 / math.sqrt(features)
        logits = (
            jnp.einsum("qd,pd->qp", cls_query, cls_passage, preferred_element_type=jnp.float32)
            * score_scale
        )
        term_values, grad_logits = contrast(logits, targets)
        loss_value = jnp.mean(term_values)
        mine = lax.axis_index("batch") * 2 + core
        own_logits = lax.dynamic_slice_in_dim(grad_logits, mine * half_q, half_q, 0)
        grad_cls_q = (
            jnp.einsum("qp,pd->qd", own_logits, cls_passage, preferred_element_type=jnp.float32)
            * score_scale
        )
        own_columns = lax.dynamic_slice_in_dim(grad_logits, mine * half_p, half_p, 1)
        grad_cls_p = (
            jnp.einsum("qp,qd->pd", own_columns, cls_query, preferred_element_type=jnp.float32)
            * score_scale
        )
        grad_cls = jnp.concatenate([grad_cls_q, grad_cls_p], 0)
        grad_cls = jnp.pad(grad_cls, ((0, 8 - grad_cls.shape[0]), (0, 0)))

    outs = backward_both(
        parts,
        (cot_query, cot_passage.reshape(-1, QLEN, features)),
        len_query,
        len_passage,
        grad_cls,
        par,
        own,
        other,
        kept + [land_a],
    )
    groups = ((0, 2), (2, 1), (3, 1), (4, 1), (5, 4), (9, 1), (10, 1), (11, 1))
    if parts == 16:
        d_qkv, d_o, d_in, d_out, d_vec, grad_q, grad_p = outs[:7]
        big = (hidden_q, hidden_p, grad_q, grad_p, d_qkv, d_o, d_in, d_out.reshape(-1, features))
        *final, loss = finish(parts, big, d_vec, loss)
        hidden_q, hidden_p, grad_q, grad_p, d_qkv, d_o, d_in, d_out = final[:8]
        small = [item[0] for item in final[8:]]
        loss_value = loss.reshape(())
    else:
        sums, grad_q, grad_p, g_pro, g_att, g_up, g_flo = outs
        left = kept[0]

        def total(pair):
            kept_one = jnp.where(on_first, pair[0], pair[1])
            both = kept_one + swap(jnp.where(on_first, pair[1], pair[0]))
            return lax.psum_scatter(both, "batch", scatter_dimension=0, tiled=True)

        def product(first, second):
            return jnp.einsum("rd,re->de", first, second, preferred_element_type=jnp.float32)

        d_qkv, d_o, d_in = (
            total([product(left[layer, spot], right[layer]) for layer in (0, 1)])
            for spot, right in ((6, g_pro), (5, g_att), (4, g_up))
        )
        d_out = total(
            [
                jnp.concatenate([product(left[layer, spot], g_flo[layer]) for spot in range(4)], 0)
                for layer in (0, 1)
            ]
        )
        small = [
            total([sums[layer, at : at + count].reshape(-1) for layer in (0, 1)])
            for at, count in groups
        ]
    hidden_q, hidden_p = hidden_q[None], hidden_p.reshape(x_passage.shape)[None]
    grad_q = grad_q[None]
    grad_p = grad_p.reshape(x_passage.shape)[None]
    d_b_qv, d_b_o, d_g_attn, d_c_attn, d_b_in, d_b_out, d_g_ffn, d_c_ffn = small
    outs = (
        d_qkv, d_b_qv, d_o, d_b_o, d_g_attn, d_c_attn, d_in, d_b_in, d_out, d_b_out, d_g_ffn,
        d_c_ffn,
    )
    return (hidden_q, hidden_p, grad_q, grad_p, loss_value) + tuple(item[None] for item in outs)


def solution(mesh):
    in_specs = (
        P("batch", None, None),
        P("batch", None, None),
        P("batch"),
        P("batch"),
        P("batch"),
        P("batch", None, None),
        P("batch", None, None),
        P("section", None, None),
        P("section", None),
        P("section", None, None),
        P("section", None),
        P("section", None),
        P("section", None),
        P("section", None, None),
        P("section", None),
        P("section", None, None),
        P("section", None),
        P("section", None),
        P("section", None),
    )
    out_specs = (
        P("section", "batch", None, None),
        P("section", "batch", None, None),
        P("section", "batch", None, None),
        P("section", "batch", None, None),
        P(),
        P("section", "batch", None),
        P("section", "batch"),
        P("section", "batch", None),
        P("section", "batch"),
        P("section", "batch"),
        P("section", "batch"),
        P("section", "batch", None),
        P("section", "batch"),
        P("section", "batch", None),
        P("section", "batch"),
        P("section", "batch"),
        P("section", "batch"),
    )
    return jax.shard_map(
        functools.partial(per_device, mesh.shape["batch"]), mesh=mesh, in_specs=in_specs, out_specs=out_specs, check_vma=False
    )
```

```python
import functools
import math

import jax
import jax.numpy as jnp
from jax import lax
from jax.experimental import pallas as pl
from jax.experimental.pallas import tpu as pltpu
from jax.sharding import PartitionSpec as P

HEADS = 12
QLEN = 32
PLEN = 256


norm_eps = 1e-05


def contrast(logits, targets):
    top_score = jnp.max(logits, -1, keepdims=True)
    log_total = top_score[:, 0] + jnp.log(jnp.sum(jnp.exp(logits - top_score), -1))
    chosen = targets[:, None] == jnp.arange(logits.shape[1])[None, :]
    term_values = log_total - jnp.sum(jnp.where(chosen, logits, 0.0), -1)
    grad_logits = (jnp.exp(logits - log_total[:, None]) - chosen.astype(jnp.float32)).astype(
        jnp.bfloat16
    )
    return (term_values, grad_logits)


MESH = pl.DeviceIdType.MESH
CHUNK = 384
COUNT = 12
BLOCK = 48


def swap(value):
    return lax.ppermute(value, "section", [(0, 1), (1, 0)])


LOW = jnp.bfloat16
FULL = jnp.float32
ROWS = 32
TILE = 768
LAST = (((1,), (1,)), ((), ()))
FIRST = (((0,), (0,)), ((), ()))


def dot(left, right):
    return jnp.dot(left, right, preferred_element_type=FULL)


def dot_last(left, right):
    return lax.dot_general(left, right, LAST, preferred_element_type=FULL)


def dot_first(left, right):
    return lax.dot_general(left, right, FIRST, preferred_element_type=FULL)


UNROLL = 4
PAIRS = 3


def over(count, body, unroll=1):
    def step(index, carry):
        body(index)
        return carry

    lax.fori_loop(0, count, step, 0, unroll=unroll)


def row_range(index):
    return pl.ds(pl.multiple_of(index * ROWS, ROWS), ROWS)


def lane_range(index, width):
    return pl.ds(pl.multiple_of(index * width, 128), width)


def moments(block):
    centred = block - jnp.mean(block, -1, keepdims=True)
    spread = jnp.mean(centred * centred, -1, keepdims=True)
    inverse = lax.rsqrt(spread + norm_eps)
    return centred * inverse, inverse


def gelu_pair(block):
    size = jnp.abs(block)
    t = 1.0 / (1.0 + (0.3275911 * math.sqrt(0.5)) * size)
    bell = jnp.exp(-0.5 * block * block)
    poly = 0.5 * 1.061405429
    for term in (-1.453152027, 1.421413741, -0.284496736, 0.254829592):
        poly = poly * t + 0.5 * term
    tail = poly * t * bell
    phi = jnp.where(block > 0, 1.0 - tail, tail)
    return block * phi, phi + block * bell * (1.0 / math.sqrt(2.0 * math.pi))


def head_lanes(rows, head):
    lane = lax.broadcasted_iota(jnp.int32, (rows, 128), 1)
    return (lane < 64) if head == 0 else (lane >= 64)


def query_mask(lens, start, count):
    rows = count * QLEN
    row = lax.broadcasted_iota(jnp.int32, (rows, rows), 0)
    column = lax.broadcasted_iota(jnp.int32, (rows, rows), 1)
    limit = jnp.zeros((rows, rows), jnp.int32)
    for item in range(count):
        limit = jnp.where(column // QLEN == item, item * QLEN + lens[start + item], limit)
    return (row // QLEN == column // QLEN) & (row < limit)


VMEM_LIMIT = 58 * 1024 * 1024


def remote(src, dst, send, recv, where):
    return pltpu.make_async_remote_copy(
        src_ref=src, dst_ref=dst, send_sem=send, recv_sem=recv,
        device_id=where, device_id_type=MESH,
    )


def greet(targets):
    barrier = pltpu.get_barrier_semaphore()
    for where in targets:
        pl.semaphore_signal(barrier, inc=1, device_id=where, device_id_type=MESH)
    pl.semaphore_wait(barrier, len(targets))


def forward_kernel(
    parts, x_query, x_passage, qlens, plens, positive,
    b_qv, b_o, g_attn, c_attn, b_in, b_out, g_ffn, c_ffn, wqkv, wo, win, wout,
    o_left, o_qkv, o_pq, o_pp, o_pre, o_slope, o_ffn, both_par,
    l_qkv, l_o, l_in, l_out, hid_q, hid_p, land_a, gcls, loss,
    tok, out, bqkv, bo, bin_, bout, qkv, pq, pp, mixed, pre, normed_full, normed, up, act,
    slope, ffn, rows8, rows48, packed, every, stack,
    load, save, xload, parsend, parrecv, wsend, wrecv, hsend, hrecv, hlocal, gsend, grecv, psend, precv, asend, arecv,
):
    core = lax.axis_index("section")
    me = lax.axis_index("batch")
    peer = {"section": 1 - core}
    features = wo.shape[0]
    count_q, count_p = x_query.shape[0] // 2, x_passage.shape[0] // 2
    split = count_q * QLEN
    tall = count_p
    total = (count_q + count_p) * QLEN
    own = (wqkv, wo, win, wout)
    land = (l_qkv, l_o, l_in, l_out)
    buffers = (bqkv, bo, bin_, bout)

    gets = [
        pltpu.make_async_copy(
            x_query.at[pl.ds(core * count_q, count_q)], tok.at[0, pl.ds(0, count_q)], xload.at[0]
        ),
        pltpu.make_async_copy(
            x_passage.at[pl.ds(core * tall, tall)], tok.at[0, pl.ds(count_q, tall)], xload.at[1]
        ),
    ]
    for copy in gets:
        copy.start()

    def local(source, spot):
        return pltpu.make_async_copy(source[spot], buffers[spot], load.at[spot])

    def stash(spot):
        return pltpu.make_async_copy(buffers[spot], land[spot], load.at[4 + spot])

    def give_first(spot):
        return remote(own[spot], buffers[spot], wsend.at[spot], wrecv.at[spot], peer)

    def give_second(spot):
        return remote(own[spot], land[spot], wsend.at[spot], wrecv.at[spot], peer)

    others = [peer]
    if parts == 16:
        for step in range(1, parts):
            others.append({"batch": (me + step) % parts})

    @pl.when(core == 0)
    def _():
        for spot in range(4):
            local(own, spot).start()

    vectors = (b_qv, b_o, g_attn, c_attn, b_in, b_out, g_ffn, c_ffn)
    spot = 0
    for ref in vectors:
        for item in range(ref.shape[1] // features):
            both_par[core, spot : spot + 1] = ref[:, item * features : (item + 1) * features]
            spot += 1
    both_par[core, spot:16] = jnp.zeros((16 - spot, features), FULL)
    greet(others)
    give_par = remote(both_par.at[core], both_par.at[core], parsend, parrecv, peer)
    give_par.start()

    @pl.when(core == 0)
    def _():
        for spot in range(4):
            give_first(spot).start()

    @pl.when(core == 1)
    def _():
        for spot in range(4):
            give_second(spot).start()

    def weight_first(spot):
        @pl.when(core == 0)
        def _():
            local(own, spot).wait()

        @pl.when(core == 1)
        def _():
            give_first(spot).wait_recv()
            stash(spot).start()

    def fetch_second(spot):
        @pl.when(core == 0)
        def _():
            give_second(spot).wait_recv()
            local(land, spot).start()

        @pl.when(core == 1)
        def _():
            stash(spot).wait()
            local(own, spot).start()

    def weight(layer, spot):
        if layer == 0:
            weight_first(spot)
        else:
            local(own, spot).wait()

    saves = {}

    def keep(name, layer, source, target):
        saves[name, layer] = pltpu.make_async_copy(
            source, target, save.at[len(saves)]
        )
        saves[name, layer].start()

    places = {"act0": 0, "act1": 1, "act2": 2, "act3": 3, "normed": 4, "mixed": 5, "tok": 6}

    def left_give(layer, spot, source):
        return remote(
            source, land_a.at[layer, spot], asend.at[layer, spot], arecv.at[layer, spot], peer
        )

    def keep_left(name, layer, source):
        keep(name, layer, source, o_left.at[layer, places[name]])
        if layer == 1:
            left_give(1, places[name], source).start()

    def free(name, layer):
        if layer == 1:
            saves[name, 0].wait()

    for copy in gets:
        copy.wait()

    remote(both_par.at[core], both_par.at[1 - core], parsend, parrecv, peer).wait_recv()
    blocks = [(0, split, query_mask(qlens, core * count_q, count_q), pq, 0)]
    for item in range(count_p * QLEN // PLEN):
        row = lax.broadcasted_iota(jnp.int32, (PLEN, PLEN), 0)
        limit = plens[core * (count_p * QLEN // PLEN) + item]
        blocks.append((split + item * PLEN, PLEN, row < limit, pp, item * HEADS))

    for layer in (0, 1):
        base_row = 0
        par = both_par.at[layer]
        x = tok.at[layer].reshape(total, features)
        keep_left("tok", layer, x)
        weight(layer, 0)
        free("qkv", layer)

        def project(tile):
            lanes = lane_range(tile, features)
            bias = jnp.where(tile == 0, par[base_row : base_row + 1], 0.0)
            bias = jnp.where(tile == 2, par[base_row + 1 : base_row + 2], bias)
            qkv[:, lanes] = (dot(x[...], bqkv[:, lanes]) + bias).astype(LOW)

        over(3, project)
        keep("qkv", layer, qkv, o_qkv.at[layer])
        if layer == 1:
            fetch_second(3)
            for name, spot in places.items():
                saves[name, 0].wait()
                left_give(0, spot, o_left.at[0, spot]).start()
        for name in ("pq", "pp"):
            free(name, layer)

        def attend(index):
            tasks = []
            for step in range(PAIRS):
                for lo, rows, mask, probs, base in blocks:
                    tasks.append((index * PAIRS + step, lo, rows, mask, probs, base))

            def part(task, offset):
                hp, lo, rows = task[:3]
                return qkv[pl.ds(lo, rows), pl.ds(pl.multiple_of(offset + hp * 128, 128), 128)]

            scores = []
            for task in tasks:
                queries, keys = part(task, 0) * LOW(0.125), part(task, features)
                for head in (0, 1):
                    masked = jnp.where(head_lanes(task[2], head), keys, LOW(0))
                    scores.append(dot_last(masked, queries))
            lows = []
            for spot, value in enumerate(scores):
                hp, lo, rows, mask, probs, base = tasks[spot // 2]
                value = jnp.where(mask, value, -1000000000.0)
                weights = jnp.exp(value - jnp.max(value, 0, keepdims=True))
                inverse = 1.0 / jnp.sum(weights, 0, keepdims=True)
                low = (weights * inverse).astype(LOW)
                probs[base + 2 * hp + spot % 2] = low
                lows.append(low)
            for spot, task in enumerate(tasks):
                hp, lo, rows = task[:3]
                values = part(task, 2 * features).T
                outs = [
                    dot(values[64 * head : 64 * head + 64], lows[2 * spot + head])
                    for head in (0, 1)
                ]
                both = jnp.concatenate(outs, 0).astype(LOW).T
                mixed[pl.ds(lo, rows), pl.ds(pl.multiple_of(hp * 128, 128), 128)] = both

        over(features // 128 // PAIRS, attend)
        keep("pq", layer, pq, o_pq.at[layer])
        keep("pp", layer, pp, o_pp.at[layer])
        keep_left("mixed", layer, mixed)
        weight(layer, 1)
        free("pre", layer)
        pre[...] = (
            dot(mixed[...], bo[...]) + x[...].astype(FULL) + par[base_row + 2 : base_row + 3]
        )
        keep("pre", layer, pre, o_pre.at[layer])
        if layer == 0:
            fetch_second(0)
            fetch_second(1)

        def norm_one(index):
            rows = row_range(index)
            block = moments(pre[rows])[0] * par[base_row + 3 : base_row + 4]
            block = block + par[base_row + 4 : base_row + 5]
            normed_full[rows] = block
            normed[rows] = block.astype(LOW)

        over(total // ROWS, norm_one, UNROLL)
        keep_left("normed", layer, normed)
        weight(layer, 2)
        free("slope", layer)
        step_width = 256
        tiles = win.shape[1] // step_width

        def expand(tile):
            lanes = lane_range(tile, step_width)
            bias_lanes = lane_range(tile % 3, step_width)
            up[tile % 2] = (
                dot(normed[...], bin_[:, lanes])
                + par[pl.ds(base_row + 5 + tile // 3, 1), bias_lanes]
            )

        def bend(tile):
            lanes = lane_range(tile, step_width)
            for index in range(total // ROWS):
                rows = pl.ds(index * ROWS, ROWS)
                value, steep = gelu_pair(up[tile % 2, rows])
                act[rows, lanes] = value.astype(LOW)
                slope[rows, lanes] = steep.astype(LOW)

        expand(0)

        def grow(index):
            expand(index + 1)
            bend(index)

        over(tiles - 1, grow)
        bend(tiles - 1)
        for item in range(4):
            lanes = pl.ds(item * features, features)
            keep_left("act%d" % item, layer, act.at[:, lanes])
        keep("slope", layer, slope, o_slope.at[layer])
        weight(layer, 3)
        free("ffn", layer)
        ffn[...] = (
            dot(act[...], bout[...]) + normed_full[...] + par[base_row + 9 : base_row + 10]
        )
        keep("ffn", layer, ffn, o_ffn.at[layer])
        if layer == 0:
            fetch_second(2)
        target = tok.at[1] if layer == 0 else out
        flat = target.reshape(total, features)

        def norm_two(index):
            rows = row_range(index)
            block = moments(ffn[rows])[0] * par[base_row + 10 : base_row + 11]
            flat[rows] = (block + par[base_row + 11 : base_row + 12]).astype(LOW)

        over(total // ROWS, norm_two, UNROLL)
        sides = (
            (target.at[pl.ds(0, count_q)], hid_q.at[pl.ds(core * count_q, count_q)]),
            (target.at[pl.ds(count_q, tall)], hid_p.at[pl.ds(core * tall, tall)]),
        )

        @pl.when(core == layer)
        def _():
            for spot, (src, dst) in enumerate(sides):
                pltpu.make_async_copy(src, dst, hlocal.at[spot]).start()

        @pl.when(core != layer)
        def _():
            for spot, (src, dst) in enumerate(sides):
                remote(src, dst, hsend.at[spot], hrecv.at[spot], peer).start()

    if parts == 16:
        lead = [item * QLEN for item in range(count_q)] + [split]
        rows8[...] = jnp.zeros_like(rows8)
        for spot, row in enumerate(lead):
            rows8[spot : spot + 1] = flat[pl.ds(row, 16)].astype(FULL)[0:1]
        for tile in range(6):
            rows48[8 * tile : 8 * tile + 8] = rows8[:, 128 * tile : 128 * tile + 128]
        for item in range(count_q):
            value = positive[core * count_q + item].astype(FULL)
            rows48[8 * item + 5 : 8 * item + 6] = jnp.full((1, 128), value)
        packed[...] = rows48[...].astype(LOW)

        def share(step, slot):
            return remote(
                packed, every.at[core, slot], gsend.at[step], grecv.at[slot],
                {"batch": (me + step) % parts},
            )

        for step in range(1, parts):
            share(step, me).start()
        every[core, me] = packed[...]
        for step in range(1, parts):
            share(step, (me + parts - step) % parts).wait_recv()
        pass_on = remote(every.at[core], every.at[core], psend, precv, peer)
        pass_on.start()
        remote(every.at[core], every.at[1 - core], psend, precv, peer).wait_recv()
        pass_on.wait_send()
        for step in range(1, parts):
            share(step, me).wait_send()

        wide = 2 * parts * 8
        grid = every[...].astype(FULL).reshape(2 * parts, 48, 128)
        inner = lax.broadcasted_iota(jnp.int32, (2 * parts, 8, 128), 1)
        goal = jnp.zeros((2 * parts, 8, 128), FULL)
        for tile in range(6):
            block = grid[:, 8 * tile : 8 * tile + 8]
            stack[:, 128 * tile : 128 * tile + 128] = block.reshape(wide, 128).astype(LOW)
            if tile < count_q:
                found = jnp.sum(jnp.where(inner == 5, block, 0.0), 1, keepdims=True)
                goal = jnp.where(inner == tile, found, goal)
        row = lax.broadcasted_iota(jnp.int32, (wide, wide), 0)
        column = lax.broadcasted_iota(jnp.int32, (wide, wide), 1)
        scale = 2.0 / math.sqrt(features)
        logits = dot_last(stack[...], stack[...]) * scale
        device = column // 8
        passage = (device % parts) * 2 + device // parts
        is_passage = column % 8 == count_q
        is_query = row % 8 < count_q
        kept = jnp.where(is_passage, logits, -1e30)
        top = jnp.max(kept, -1, keepdims=True)
        log_total = top + jnp.log(jnp.sum(jnp.exp(kept - top), -1, keepdims=True))
        chosen = is_passage & (passage.astype(FULL) == goal.reshape(wide, 128)[:, 0:1])
        picked = jnp.sum(jnp.where(chosen, logits, 0.0), -1, keepdims=True)
        terms = jnp.where(is_query[:, 0:1], log_total - picked, 0.0)
        count = count_q * 2 * parts
        loss[...] = jnp.full((8, 128), jnp.sum(terms) / count)
        grads = jnp.exp(kept - log_total) - chosen.astype(FULL)
        grads = jnp.where(is_query & is_passage, grads, 0.0)
        up[0, 0:wide, 0:wide] = grads + grads.T
        mine = pl.multiple_of((core * parts + me) * 8, 8)
        picked_rows = up[0, pl.ds(mine, 8), 0:wide]
        gcls[...] = dot(picked_rows.astype(LOW), stack[...]) * scale

    for spot, (src, dst) in enumerate(sides):
        pltpu.make_async_copy(src, dst, hlocal.at[spot]).wait()
    theirs = (
        hid_q.at[pl.ds((1 - core) * count_q, count_q)],
        hid_p.at[pl.ds((1 - core) * tall, tall)],
    )
    for spot, (src, dst) in enumerate(zip((item[0] for item in sides), theirs)):
        remote(src, dst, hsend.at[spot], hrecv.at[spot], peer).wait()
    for spot in range(4):
        give_second(spot).wait_send()
    give_par.wait_send()
    for (name, layer), copy in saves.items():
        if layer == 1:
            copy.wait()
    for layer in (0, 1):
        for spot in range(7):
            left_give(layer, spot, o_left.at[layer, spot]).wait()


def forward_both(parts, x_query, x_passage, qlens, plens, positive, vectors, own):
    queries, features = x_query.shape[0], x_query.shape[2]
    passages = x_passage.shape[0]
    total = (queries + passages) // 2 * QLEN
    wide = own[2].shape[1]
    split = queries // 2 * QLEN
    heads_p = HEADS * (passages // 2 * QLEN // PLEN)
    kept = [
        ((7, total, features), LOW),
        ((total, 3 * features), LOW),
        ((HEADS, split, split), LOW),
        ((heads_p, PLEN, PLEN), LOW),
        ((total, features), FULL),
        ((total, wide), LOW),
        ((total, features), FULL),
        ((16, features), FULL),
    ]
    shape = jax.ShapeDtypeStruct
    anywhere = pl.BlockSpec(memory_space=pl.ANY)
    vmem = pl.BlockSpec(memory_space=pltpu.VMEM)
    smem = pl.BlockSpec(memory_space=pltpu.SMEM)
    dma = pltpu.SemaphoreType.DMA
    scratch = [
        pltpu.VMEM((2, total // QLEN, QLEN, features), LOW),
        pltpu.VMEM((total // QLEN, QLEN, features), LOW),
    ]
    scratch += [pltpu.VMEM(item.shape, item.dtype) for item in own]
    scratch += [pltpu.VMEM(size, kind) for size, kind in kept[1:4]]
    scratch += [
        pltpu.VMEM((total, features), LOW),
        pltpu.VMEM((total, features), FULL),
        pltpu.VMEM((total, features), FULL),
        pltpu.VMEM((total, features), LOW),
        pltpu.VMEM((2, total, 256), FULL),
        pltpu.VMEM((total, wide), LOW),
        pltpu.VMEM((total, wide), LOW),
        pltpu.VMEM((total, features), FULL),
    ]
    scratch += [
        pltpu.VMEM((8, features), FULL),
        pltpu.VMEM((48, 128), FULL),
        pltpu.VMEM((48, 128), LOW),
        pltpu.VMEM((2, 16, 48, 128), LOW),
        pltpu.VMEM((256, features), LOW),
        dma((8,)),
        dma((26,)),
        dma((2,)),
        dma,
        dma,
        dma((4,)),
        dma((4,)),
        dma((2,)),
        dma((2,)),
        dma((2,)),
        dma((16,)),
        dma((16,)),
        dma,
        dma,
        dma((2, 7)),
        dma((2, 7)),
    ]
    return pl.pallas_call(
        functools.partial(forward_kernel, parts),
        out_shape=[shape((2,) + size, kind) for size, kind in kept]
        + [shape(item.shape, item.dtype) for item in own]
        + [
            shape(x_query.shape, LOW),
            shape(x_passage.shape, LOW),
            shape((2, 7, total, features), LOW),
            shape((8, features), FULL),
            shape((8, 128), FULL),
        ],
        in_specs=[anywhere, anywhere, smem, smem, smem] + [vmem] * 8 + [anywhere] * 4,
        out_specs=[anywhere] * 7 + [vmem] + [anywhere] * 7 + [vmem] * 2,
        scratch_shapes=scratch,
        compiler_params=pltpu.CompilerParams(
            collective_id=2, has_side_effects=True, vmem_limit_bytes=VMEM_LIMIT
        ),
    )(x_query, x_passage, qlens, plens, positive, *vectors, *own)


def add_rows(block):
    return jnp.sum(block.reshape(block.shape[0] // 8, 8, block.shape[1]), 0)


def norm_back(source, grad_of, gain, total, store):
    features = source.shape[1]
    zero = jnp.zeros((8, features), FULL)

    def step(index, carry):
        rows = row_range(index)
        grad = grad_of(index)
        unit, inverse = moments(source[rows])
        scaled = grad * gain
        back = inverse * (
            scaled
            - jnp.mean(scaled, -1, keepdims=True)
            - unit * jnp.mean(scaled * unit, -1, keepdims=True)
        )
        store(rows, back)
        return (
            carry[0] + add_rows(grad * unit),
            carry[1] + add_rows(grad),
            carry[2] + add_rows(back),
        )

    sums = lax.fori_loop(0, total // ROWS, step, (zero, zero, zero), unroll=UNROLL)
    return [jnp.sum(item, 0, keepdims=True) for item in sums]


LAGS = (2, 4, 6)
RING = 12
HELD = 8


def left_index(ch):
    return (
        jnp.minimum(ch, 4) + (ch >= 8).astype(jnp.int32) + (ch >= 9).astype(jnp.int32)
    )


def right_index(ch):
    return jnp.maximum(ch - 3, 0)


def backward_kernel(parts, *refs):
    small = parts == 16
    refs = list(refs)

    def take(count):
        front = refs[:count]
        del refs[:count]
        return front

    cot_query, cot_passage, qlens, plens, gcls, par = take(6)
    own, land = take(4), take(4)
    left, h_qkv, h_pq, h_pp, h_pre, h_slope, h_ffn, land_a = take(8)
    if small:
        o_qkv, o_o, o_in, o_out, o_vec, o_gq, o_gp, land_g, own_g = take(9)
    else:
        vpar, o_gq, o_gp, f_pro, f_att, f_up, f_flo = take(7)
    buffers = take(4)
    bqkv, bo, bin_, bout = buffers
    qkv, pq, pp, source, slope, gsrc = take(6)
    attn_full, attn, steep, flow_full, flow = take(5)
    gmixed = flow
    grow = flow_full.reshape(flow.shape[0] // QLEN, QLEN, flow.shape[1])
    wload, fetch, cload, hsend, hrecv, hlocal, ksem = take(7)
    if small:
        vpar, a_buf, g_buf, stage, s1, r1, s2, r2, s3, r3, hold = take(11)
        va, ra, vb, rb, vc, rc, rz = take(7)
        s1s, r1s, s2s, r2s, s3s, r3s, vsend, vrecv, zsend, zrecv = take(10)
        gs, gr, sl, gl, el = take(5)

    core = lax.axis_index("section")
    me = lax.axis_index("batch")
    peer = {"section": 1 - core}
    features = gcls.shape[1]
    total = flow.shape[0]
    split = pq.shape[1]
    count_q, tall = cot_query.shape[0] // 2, cot_passage.shape[0] // 2
    heads_p = pp.shape[0]
    blocks_p = PLEN // QLEN

    def weight_copy(spot, source_set):
        return pltpu.make_async_copy(source_set[spot], buffers[spot], wload.at[spot])

    def weight_start(layer, spot):
        @pl.when(core == layer)
        def _():
            weight_copy(spot, own).start()

        @pl.when(core != layer)
        def _():
            weight_copy(spot, land).start()

    def weight_wait(spot):
        weight_copy(spot, own).wait()

    saved = ((h_ffn, source), (h_slope, slope), (h_pre, source), (h_qkv, qkv), (h_pq, pq), (h_pp, pp))

    def saved_copy(layer, spot):
        src, dst = saved[spot]
        return pltpu.make_async_copy(src.at[layer], dst, fetch.at[spot])

    cots = [
        pltpu.make_async_copy(
            cot_query.at[pl.ds(core * count_q, count_q)], gsrc.at[pl.ds(0, count_q)], cload.at[0]
        ),
        pltpu.make_async_copy(
            cot_passage.at[pl.ds(core * tall, tall)], gsrc.at[pl.ds(count_q, tall)], cload.at[1]
        ),
    ]
    def early_copy(spot, side):
        src = (left, land_a)[side]
        if spot < 2:
            dst, sem = stage.at[spot, side], sl.at[spot, side]
        else:
            lanes = pl.ds((spot - 2) * features, features)
            dst, sem = bin_.at[pl.ds(side * total, total), lanes], el.at[spot - 2, side]
        return pltpu.make_async_copy(src.at[1, spot], dst, sem)

    if small:
        x, y, z = me % 2, (me // 2) % 2, me // 4
        px, py = me + 1 - 2 * x, me + 2 - 4 * y
        targets = [{"batch": px}, {"batch": py}, peer]
        for step in (1, 2, 3):
            other = ((z + step) % 4) * 4 + me % 4
            targets += [{"section": sec, "batch": other} for sec in (0, 1)]
        barrier = pltpu.get_barrier_semaphore()
        for where in targets:
            pl.semaphore_signal(barrier, inc=1, device_id=where, device_id_type=MESH)
        for spot in range(4):
            for side in (0, 1):
                early_copy(spot, side).start()
    saved_copy(1, 0).start()
    for copy in cots:
        copy.start()
    weight_start(1, 3)
    saved_copy(1, 1).start()

    widths = ((flow, 1), (slope, 4), (attn, 1), (qkv, 3))

    def pieces_of(slot):
        base = (0, 1, 5, 6)[slot]
        ref, count = widths[slot]
        return [(base + item, ref, ref.shape[1] // 2, item) for item in range(count)]

    def own_piece(layer, piece):
        spot, ref, width, item = piece
        lanes = pl.ds(pl.multiple_of(core * width + item * CHUNK, 128), CHUNK)
        return pltpu.make_async_copy(ref.at[:, lanes], own_g.at[layer, spot], ksem.at[spot])

    def peer_piece(layer, piece):
        spot, ref, width, item = piece
        lanes = pl.ds(pl.multiple_of((1 - core) * width + item * CHUNK, 128), CHUNK)
        return remote(
            ref.at[:, lanes], land_g.at[layer, spot], gs.at[layer, spot], gr.at[layer, spot], peer
        )

    def whole_piece(layer, slot):
        ref = widths[slot][0]
        target = (f_flo, f_up, f_att, f_pro)[slot]
        return pltpu.make_async_copy(ref, target.at[layer], ksem.at[slot])

    def direct():
        spot, ref, width, item = pieces_of(0)[0]
        lanes = pl.ds(pl.multiple_of((1 - core) * width, 128), CHUNK)
        return remote(
            ref.at[:, lanes], g_buf.at[0, pl.ds(total, total)], gs.at[1, 0], gr.at[1, 0], peer
        )

    def give(layer, slot):
        if small and slot == 0:

            @pl.when(layer == 1)
            def _():
                direct().start()
                lanes = pl.ds(pl.multiple_of(core * CHUNK, 128), CHUNK)
                g_buf[0, pl.ds(0, total)] = flow[:, lanes]

            @pl.when(layer == 0)
            def _():
                piece = pieces_of(0)[0]
                peer_piece(layer, piece).start()
                own_piece(layer, piece).start()

        elif small:
            for piece in pieces_of(slot):
                peer_piece(layer, piece).start()
                own_piece(layer, piece).start()
        else:
            whole_piece(layer, slot).start()

    def given(layer, slot):
        if small:
            for piece in pieces_of(slot):
                peer_piece(layer, piece).wait_send()
                if slot > 0:
                    own_piece(layer, piece).wait()
                else:

                    @pl.when(layer == 0)
                    def _():
                        own_piece(layer, piece).wait()
        else:
            whole_piece(layer, slot).wait()

    def slot_zero(layer):
        saved_copy(layer, 0).wait()
        gains = par.at[layer]
        last = layer == 1

        def grad_of(index):
            block = gsrc[index].astype(FULL)
            beyond = jnp.maximum(index - count_q, 0)
            item = beyond // blocks_p
            query_limit = qlens[core * count_q + jnp.minimum(index, count_q - 1)]
            passage_limit = (
                plens[core * (tall // blocks_p) + item] - (beyond % blocks_p) * QLEN
            )
            limit = jnp.where(index < count_q, query_limit, passage_limit)
            limit = jnp.where(last, limit, QLEN)
            lead = jnp.where(index < count_q, index, count_q + item)
            starts = (index < count_q) | (beyond % blocks_p == 0)
            row = lax.broadcasted_iota(jnp.int32, block.shape, 0)
            block = jnp.where(row < limit, block, 0.0)
            extra = gcls[pl.ds(lead, 1)] * jnp.where(starts & last, 1.0, 0.0)
            return block + jnp.where(row == 0, extra, 0.0)

        def store(rows, back):
            flow_full[rows] = back
            flow[rows] = back.astype(LOW)

        gain, shift, bias = norm_back(source, grad_of, gains[10:11], total, store)
        sums = vpar.at[layer]
        sums[10:11], sums[11:12], sums[9:10] = gain, shift, bias
        give(layer, 0)
        saved_copy(layer, 2).start()

    width = 256
    tiles = bout.shape[0] // width

    def slot_one(layer):
        saved_copy(layer, 1).wait()
        weight_wait(3)
        sums = vpar.at[layer]

        def shrink(tile):
            rows_of = pl.ds(pl.multiple_of(tile * width, width), width)
            steep[tile % 2] = dot_last(flow[...], bout[rows_of])

        def bend(tile):
            lanes = lane_range(tile, width)
            acc = jnp.zeros((8, width), FULL)
            for index in range(total // ROWS):
                rows = pl.ds(index * ROWS, ROWS)
                low = (steep[tile % 2, rows] * slope[rows, lanes].astype(FULL)).astype(LOW)
                slope[rows, lanes] = low
                acc = acc + add_rows(low.astype(FULL))
            sums[pl.ds(5 + tile // 3, 1), lane_range(tile % 3, width)] = jnp.sum(
                acc, 0, keepdims=True
            )

        shrink(0)

        def both(index):
            shrink(index + 1)
            bend(index)

        over(tiles - 1, both)
        bend(tiles - 1)
        give(layer, 1)

        @pl.when(layer == 1)
        def _():
            weight_start(0, 3)

    def slot_two(layer):
        weight_wait(2)
        flow_full[...] += dot_last(slope[...], bin_[...])
        saved_copy(layer, 2).wait()
        gains, sums = par.at[layer], vpar.at[layer]

        def store(rows, back):
            attn_full[rows] = back
            attn[rows] = back.astype(LOW)

        gain, shift, bias = norm_back(
            source, lambda index: flow_full[row_range(index)], gains[3:4], total, store
        )
        sums[3:4], sums[4:5], sums[2:3] = gain, shift, bias
        give(layer, 2)
        weight_wait(1)
        gmixed[...] = dot_last(attn[...], bo[...]).astype(LOW)

        @pl.when(layer == 1)
        def _():
            weight_start(0, 2)
            weight_start(0, 1)
            saved_copy(0, 0).start()
            saved_copy(0, 1).start()

    blocks = [(0, split, pq, 0)]
    for item in range(heads_p // HEADS):
        blocks.append((split + item * PLEN, PLEN, pp, item * HEADS))

    def attend(index):
        tasks = []
        for step in range(PAIRS):
            for block in blocks:
                tasks.append((index * PAIRS + step,) + block)

        def spot_of(task, offset):
            hp, lo, rows = task[:3]
            return (pl.ds(lo, rows), pl.ds(pl.multiple_of(offset + hp * 128, 128), 128))

        grads = []
        for task in tasks:
            values, back = qkv[spot_of(task, 2 * features)], gmixed[spot_of(task, 0)]
            for head in (0, 1):
                masked = jnp.where(head_lanes(task[2], head), values, LOW(0))
                grads.append(dot_last(masked, back))
        lows = []
        for spot, grad_probs in enumerate(grads):
            hp, lo, rows, probs, base = tasks[spot // 2]
            full = probs[base + 2 * hp + spot % 2].astype(FULL)
            inner = jnp.sum(grad_probs * full, 0, keepdims=True)
            lows.append((full * (grad_probs - inner)).astype(LOW))
        for spot, task in enumerate(tasks):
            hp, lo, rows, probs, base = task
            queries, keys = qkv[spot_of(task, 0)], qkv[spot_of(task, features)]
            back = gmixed[spot_of(task, 0)]
            turned = keys.T
            outs = []
            for head in (0, 1):
                grad_scores = lows[2 * spot + head]
                outs.append(
                    (
                        dot(turned[64 * head : 64 * head + 64], grad_scores) * 0.125,
                        dot(grad_scores, queries) * 0.125,
                        dot(probs[base + 2 * hp + head], back),
                    )
                )
            first = head_lanes(rows, 0)
            both = jnp.concatenate([outs[0][0], outs[1][0]], 0)
            qkv[spot_of(task, 0)] = both.astype(LOW).T
            for item in (1, 2):
                both = jnp.where(first, outs[0][item], outs[1][item])
                qkv[spot_of(task, item * features)] = both.astype(LOW)

    def grads_here(spot):
        lo, count, target = ((0, count_q, o_gq), (count_q, tall, o_gp))[spot]
        return pltpu.make_async_copy(
            grow.at[pl.ds(lo, count)], target.at[pl.ds(core * count, count)], hlocal.at[spot]
        )

    def grads_there(spot):
        lo, count, target = ((0, count_q, o_gq), (count_q, tall, o_gp))[spot]
        return remote(
            grow.at[pl.ds(lo, count)],
            target.at[pl.ds(core * count, count)],
            hsend.at[spot],
            hrecv.at[spot],
            peer,
        )

    def slot_three(layer):
        for spot in (3, 4, 5):
            saved_copy(layer, spot).wait()
        over(features // 128 // PAIRS, attend)
        give(layer, 3)
        sums = vpar.at[layer]

        def bias_sums(index, carry):
            rows = row_range(index)
            return (
                carry[0] + add_rows(qkv[rows, pl.ds(0, features)].astype(FULL)),
                carry[1] + add_rows(qkv[rows, pl.ds(2 * features, features)].astype(FULL)),
            )

        zero = jnp.zeros((8, features), FULL)
        found = lax.fori_loop(0, total // ROWS, bias_sums, (zero, zero), unroll=2)
        sums[0:1] = jnp.sum(found[0], 0, keepdims=True)
        sums[1:2] = jnp.sum(found[1], 0, keepdims=True)
        sums[12:16] = jnp.zeros((4, features), FULL)
        weight_wait(0)
        rows_all = attn_full[...] + dot_last(qkv[...], bqkv[...])
        flow_full[...] = rows_all
        gsrc[...] = rows_all.astype(LOW).reshape(gsrc.shape)

        @pl.when(core == layer)
        def _():
            for spot in (0, 1):
                grads_here(spot).start()

        @pl.when(core != layer)
        def _():
            for spot in (0, 1):
                grads_there(spot).start()

        @pl.when(layer == 1)
        def _():
            weight_start(0, 0)

    def grads_given(layer):
        @pl.when(core == layer)
        def _():
            for spot in (0, 1):
                grads_here(spot).wait()

        @pl.when(core != layer)
        def _():
            for spot in (0, 1):
                grads_there(spot).wait_send()

    slots = (slot_zero, slot_one, slot_two, slot_three)

    def reload(layer, slot):
        @pl.when(layer == 1)
        def _():
            if slot == 3:
                for spot in (3, 4, 5):
                    saved_copy(0, spot).start()

    def rest_of_loads():
        for spot in (2, 1, 0):
            weight_start(1, spot)
        for spot in (3, 4, 5):
            saved_copy(1, spot).start()

    def grads_came():
        lands = ((o_gq, count_q), (o_gp, tall))
        for spot, (target, count) in enumerate(lands):
            there = target.at[pl.ds((1 - core) * count, count)]
            remote(there, there, hsend.at[spot], hrecv.at[spot], peer).wait_recv()

    if not small:
        greet([peer])
        rest_of_loads()
        for copy in cots:
            copy.wait()
        for layer in (1, 0):
            for slot in range(4):
                slots[slot](layer)
                given(layer, slot)
                reload(layer, slot)
            grads_given(layer)
        grads_came()
        return

    def stage_copy(number, side):
        layer, spot = 1 - number // 7, number % 7
        src = left if side == 0 else land_a
        return pltpu.make_async_copy(
            src.at[layer, spot], stage.at[number % 2, side], sl.at[number % 2, side]
        )

    def stage_start(number):
        stage_copy(number, 0).start()
        stage_copy(number, 1).start()

    def rotate(spot, view):
        for side in (0, 1):
            lanes = pl.ds(side * total, total)
            for half in range(features // CHUNK):
                block = view(side, half * CHUNK).T
                if spot > 3:
                    a_buf[spot, pl.ds(2 * half, 2), :, :, :, lanes] = block.reshape(
                        2, 2, 2, BLOCK, total
                    )
                else:
                    shaped = block.reshape(2, 4, BLOCK, total)
                    for item in range(4):
                        a_buf[item, spot, half, :, :, lanes] = shaped[:, item]

    def turn(number, spot):
        for side in (0, 1):
            stage_copy(number, side).wait()
        rotate(spot, lambda side, at: stage[number % 2, side, :, pl.ds(at, CHUNK)])

        @pl.when(number + 2 < 14)
        def _():
            stage_start(number + 2)

    for spot in range(4):
        for side in (0, 1):
            early_copy(spot, side).wait()
        if spot < 2:
            rotate(spot, lambda side, at: stage[spot, side, :, pl.ds(at, CHUNK)])
            stage_start(spot + 4)
        else:
            rotate(
                spot,
                lambda side, at: bin_[
                    pl.ds(side * total, total), pl.ds((spot - 2) * features + at, CHUNK)
                ],
            )
    pl.semaphore_wait(barrier, len(targets))

    def right_copy(layer, spot, side):
        src = own_g if side == 0 else land_g
        return pltpu.make_async_copy(
            src.at[layer, spot], g_buf.at[spot, pl.ds(side * total, total)], gl.at[spot, side]
        )

    def right_start(k):
        ch = k % COUNT
        layer = 1 - k // COUNT

        @pl.when((k > 0) & (k < 2 * COUNT) & ((ch == 0) | (ch >= 4)))
        def _():
            spot = right_index(ch)
            right_copy(layer, spot, 0).start()
            remote(
                own_g.at[layer, spot], land_g.at[layer, spot],
                gs.at[layer, spot], gr.at[layer, spot], peer,
            ).wait_recv()
            right_copy(layer, spot, 1).start()

    def first(k, par_):
        return remote(
            s1.at[k % HELD], r1.at[k % RING], s1s.at[k], r1s.at[k],
            {"batch": px if par_ == 0 else py},
        )

    def second(k, par_):
        return remote(
            s2.at[k % 4], r2.at[k % HELD], s2s.at[k], r2s.at[k],
            {"batch": py if par_ == 0 else px},
        )

    def third(k, step):
        layer = 1 - k // COUNT
        zt = (z + step) % 4
        return remote(
            s3.at[k % 4, zt], r3.at[core, k % COUNT, z], s3s.at[k, step],
            r3s.at[core, k % COUNT, z], {"section": layer, "batch": zt * 4 + me % 4},
        )

    def third_in(k, step, src_core):
        zs = (z + 4 - step) % 4
        return remote(
            s3.at[k % 4, zs], r3.at[src_core, k % COUNT, zs], s3s.at[k, step],
            r3s.at[src_core, k % COUNT, zs], peer,
        )

    def product(k, block, rows):
        return dot(block.reshape(rows, 2 * total), g_buf[right_index(k % COUNT)])

    def left_of(k):
        return a_buf.at[left_index(k % COUNT)]

    def ready(k, par_):
        ch = k % COUNT

        @pl.when((k > 0) & ((ch == 0) | (ch >= 4)))
        def _():
            for side in (0, 1):
                right_copy(0, right_index(ch), side).wait()

        base = (k // COUNT) * 7
        if par_ == 0:

            @pl.when(k == 0)
            def _():
                direct().wait_recv()

            @pl.when(k == COUNT)
            def _():
                for spot in range(4):
                    turn(base + spot, spot)

            for spot, at in ((4, 4), (5, 8)):

                @pl.when(ch == at)
                def _():
                    turn(base + spot, spot)
        else:

            @pl.when(ch == 9)
            def _():
                turn(base + 6, 6)

    def part_one(k, par_):
        ready(k, par_)
        ref = left_of(k)
        block = ref[:, :, 1 - x] if par_ == 0 else ref[:, 1 - y]
        s1[k % HELD] = product(k, block, 8 * BLOCK).astype(LOW).reshape(4, 2, BLOCK, CHUNK)
        first(k, par_).start()

    def part_two(k, par_):
        ref = left_of(k)
        block = ref[:, 1 - y, x] if par_ == 0 else ref[:, y, 1 - x]
        hold[...] = product(k, block, 4 * BLOCK).reshape(4, BLOCK, CHUNK)
        first(k, par_).wait()
        came = r1[k % RING, :, 1 - y] if par_ == 0 else r1[k % RING, :, 1 - x]
        s2[k % 4] = (hold[...] + came.astype(FULL)).astype(LOW)
        second(k, par_).start()

    def part_three(k, par_):
        layer = 1 - k // COUNT
        ref = left_of(k)
        came = r1[k % RING, :, y] if par_ == 0 else r1[k % RING, :, x]
        hold[...] = product(k, ref[:, y, x], 4 * BLOCK).reshape(
            4, BLOCK, CHUNK
        ) + came.astype(FULL)
        second(k, par_).wait()
        value = hold[...] + r2[k % HELD].astype(FULL)
        s3[k % 4] = value.astype(LOW)
        for step in (1, 2, 3):
            third(k, step).start()

        @pl.when(core != layer)
        def _():
            third(k, 0).start()

        @pl.when(core == layer)
        def _():
            r3[core, k % COUNT, z] = s3[k % 4, z]

    def part_four(k, par_):
        layer = 1 - k // COUNT
        ch = k % COUNT
        for step in (1, 2, 3):
            third(k, step).wait_send()

        @pl.when(core != layer)
        def _():
            third(k, 0).wait_send()

        @pl.when(core == layer)
        def _():
            for step in (1, 2, 3):
                for src_core in (0, 1):
                    third_in(k, step, src_core).wait_recv()
            third_in(k, 0, 1 - core).wait_recv()
            for src_core in (0, 1):
                value = jnp.sum(r3[src_core, ch].astype(FULL), 0)

                @pl.when(ch < 4)
                def _():
                    o_out[ch, :, pl.ds(src_core * CHUNK, CHUNK)] = value

                @pl.when((ch >= 4) & (ch < 8))
                def _():
                    start = pl.multiple_of((ch - 4) * CHUNK + src_core * 4 * CHUNK, 128)
                    o_in[:, pl.ds(start, CHUNK)] = value

                @pl.when(ch == 8)
                def _():
                    o_o[:, pl.ds(src_core * CHUNK, CHUNK)] = value

                @pl.when(ch >= 9)
                def _():
                    start = pl.multiple_of((ch - 9) * CHUNK + src_core * 3 * CHUNK, 128)
                    o_qkv[:, pl.ds(start, CHUNK)] = value

    vec_cross = remote(vpar.at[1 - core], ra, vsend.at[0], vrecv.at[0], peer)
    vec_x = remote(va, rb, vsend.at[1], vrecv.at[1], {"batch": px})
    vec_y = remote(vb, rc, vsend.at[2], vrecv.at[2], {"batch": py})

    def vec_z(step, slot):
        return remote(
            vc, rz.at[slot], zsend.at[step], zrecv.at[slot],
            {"batch": ((z + step) % 4) * 4 + me % 4},
        )

    steps = 2 * COUNT + LAGS[2]

    starts = ((-1, 3), (0, 4), (1, 6), (2, 8))

    def pair(turn_index, carry):
        kk = turn_index - 1
        layer = (kk < 3).astype(jnp.int32)

        for slot, (one, two) in enumerate(starts):

            @pl.when((kk == one + 1) | (kk == two + 1))
            def _():
                done = (kk == one + 1).astype(jnp.int32)
                given(done, slot)
                reload(done, slot)
                if slot == 3:
                    grads_given(done)

        @pl.when(kk == -1)
        def _():
            rest_of_loads()
            for copy in cots:
                copy.wait()

        for par_ in (0, 1):
            right_start(2 * kk + 2 + par_)

        stages = (part_two, part_three, part_four)

        def advance(item):
            lag, part = LAGS[item], stages[item]
            for par_ in (0, 1):
                k = 2 * kk + par_

                @pl.when((k >= lag) & (k < 2 * COUNT + lag))
                def _():
                    part(k - lag, par_)

        advance(0)
        advance(1)

        @pl.when((kk == starts[0][0]) | (kk == starts[0][1]))
        def _():
            slots[0](layer)

        for par_ in (0, 1):
            k = 2 * kk + 2 + par_

            @pl.when(k < 2 * COUNT)
            def _():
                part_one(k, par_)

        advance(2)

        for slot, (one, two) in enumerate(starts):
            if slot > 0:

                @pl.when((kk == one) | (kk == two))
                def _():
                    slots[slot](layer)

        @pl.when(kk == 9)
        def _():
            vec_cross.start()

        @pl.when(kk == 10)
        def _():
            vec_cross.wait()
            va[...] = vpar[core] + ra[...]
            vec_x.start()

        @pl.when(kk == 11)
        def _():
            vec_x.wait()
            vb[...] = va[...] + rb[...]
            vec_y.start()

        @pl.when(kk == 12)
        def _():
            vec_y.wait()
            vc[...] = vb[...] + rc[...]
            for step in (1, 2, 3):
                vec_z(step, z).start()

        @pl.when(kk == 14)
        def _():
            for step in (1, 2, 3):
                vec_z(step, z).wait_send()
                vec_z(step, (z + 4 - step) % 4).wait_recv()
            rz[z] = vc[...]
            o_vec[...] = jnp.sum(rz[...], 0)

        return carry

    lax.fori_loop(0, steps // 2 + 1, pair, 0)
    grads_came()


def backward_both(parts, cots, qlens, plens, gcls, par, own, land, kept):
    small = parts == 16
    cot_query, cot_passage = cots
    left, h_qkv, h_pq, h_pp, h_pre, h_slope, h_ffn = kept[:7]
    total, features = left.shape[2:]
    wide = own[2].shape[1]
    shape = jax.ShapeDtypeStruct
    anywhere = pl.BlockSpec(memory_space=pl.ANY)
    vmem = pl.BlockSpec(memory_space=pltpu.VMEM)
    smem = pl.BlockSpec(memory_space=pltpu.SMEM)
    dma = pltpu.SemaphoreType.DMA
    grads = [shape(cot_query.shape, FULL), shape(cot_passage.shape, FULL)]
    if small:
        out_shape = [
            shape((BLOCK, 3 * features), FULL),
            shape((BLOCK, features), FULL),
            shape((BLOCK, wide), FULL),
            shape((4, BLOCK, features), FULL),
            shape((16, features), FULL),
            *grads,
            shape((2, 9, total, CHUNK), LOW),
            shape((2, 9, total, CHUNK), LOW),
        ]
        out_specs = [vmem] * 5 + [anywhere] * 4
    else:
        out_shape = [
            shape((2, 16, features), FULL),
            *grads,
            shape((2, total, 3 * features), LOW),
            shape((2, total, features), LOW),
            shape((2, total, wide), LOW),
            shape((2, total, features), LOW),
        ]
        out_specs = [vmem] + [anywhere] * 6
    scratch = [pltpu.VMEM(item.shape, item.dtype) for item in own]
    scratch += [
        pltpu.VMEM(h_qkv.shape[1:], LOW),
        pltpu.VMEM(h_pq.shape[1:], LOW),
        pltpu.VMEM(h_pp.shape[1:], LOW),
        pltpu.VMEM((total, features), FULL),
        pltpu.VMEM((total, wide), LOW),
        pltpu.VMEM((total // QLEN, QLEN, features), LOW),
        pltpu.VMEM((total, features), FULL),
        pltpu.VMEM((total, features), LOW),
        pltpu.VMEM((2, total, 256), FULL),
        pltpu.VMEM((total, features), FULL),
        pltpu.VMEM((total, features), LOW),
        dma((4,)),
        dma((6,)),
        dma((2,)),
        dma((2,)),
        dma((2,)),
        dma((2,)),
        dma((9,)),
    ]
    if small:
        steps = 2 * COUNT
        vector = pltpu.VMEM((16, features), FULL)
        scratch += [
            pltpu.VMEM((2, 16, features), FULL),
            pltpu.VMEM((7, 4, 2, 2, BLOCK, 2 * total), LOW),
            pltpu.VMEM((9, 2 * total, CHUNK), LOW),
            pltpu.VMEM((2, 2, total, features), LOW),
            pltpu.VMEM((HELD, 4, 2, BLOCK, CHUNK), LOW),
            pltpu.VMEM((RING, 4, 2, BLOCK, CHUNK), LOW),
            pltpu.VMEM((4, 4, BLOCK, CHUNK), LOW),
            pltpu.VMEM((HELD, 4, BLOCK, CHUNK), LOW),
            pltpu.VMEM((4, 4, BLOCK, CHUNK), LOW),
            pltpu.VMEM((2, COUNT, 4, BLOCK, CHUNK), LOW),
            pltpu.VMEM((4, BLOCK, CHUNK), FULL),
            *[vector] * 6,
            pltpu.VMEM((4, 16, features), FULL),
            dma((steps,)),
            dma((steps,)),
            dma((steps,)),
            dma((steps,)),
            dma((steps, 4)),
            dma((2, COUNT, 4)),
            dma((3,)),
            dma((3,)),
            dma((4,)),
            dma((4,)),
            dma((2, 9)),
            dma((2, 9)),
            dma((2, 2)),
            dma((9, 2)),
            dma((2, 2)),
        ]
    return pl.pallas_call(
        functools.partial(backward_kernel, parts),
        out_shape=out_shape,
        in_specs=[anywhere, anywhere, smem, smem, vmem, vmem] + [anywhere] * 16,
        out_specs=out_specs,
        scratch_shapes=scratch,
        compiler_params=pltpu.CompilerParams(
            collective_id=1, has_side_effects=True, vmem_limit_bytes=60 * 1024 * 1024
        ),
    )(cot_query, cot_passage, qlens, plens, gcls, par, *own, *land, *kept)


def finish_kernel(parts, *refs):
    big, vec, loss = refs[:8], refs[8], refs[9]
    outs, small, total = refs[10:18], refs[18:26], refs[26]
    held, come, go = refs[27:35], refs[35], refs[36]
    copies = []
    for src, mid, dst in zip(big, held, outs):
        pieces = 2 if src.shape[0] % 32 == 0 or len(src.shape) == 3 else 1
        size = src.shape[0] // pieces
        for item in range(pieces):
            rows, spot = pl.ds(item * size, size), len(copies)
            copies.append(
                (
                    pltpu.make_async_copy(src.at[rows], mid.at[rows], come.at[spot]),
                    pltpu.make_async_copy(mid.at[rows], dst.at[rows], go.at[spot]),
                )
            )
            copies[-1][0].start()
    me = lax.axis_index("batch")
    features = vec.shape[1]
    for at, count, out in zip((0, 2, 3, 4, 5, 9, 10, 11), (2, 1, 1, 1, 4, 1, 1, 1), small):
        size = count * features // parts
        every = parts // count
        block = vec[pl.ds(at + me // every, 1)]
        block = jnp.broadcast_to(block, (8, features))
        turned = pltpu.roll(block, (features - size * (me % every)) % features, 1)
        out[...] = turned[0:1, 0:size]
    total[...] = loss[0:1, 0:1]
    for came, left in copies:
        came.wait()
        left.start()
    for came, left in copies:
        left.wait()


def finish(parts, big, vec, loss):
    features = vec.shape[1]
    anywhere = pl.BlockSpec(memory_space=pl.ANY)
    vmem = pl.BlockSpec(memory_space=pltpu.VMEM)
    shape = jax.ShapeDtypeStruct
    return pl.pallas_call(
        functools.partial(finish_kernel, parts),
        out_shape=[shape(item.shape, item.dtype) for item in big]
        + [shape((1, count * features // parts), FULL) for count in (2, 1, 1, 1, 4, 1, 1, 1)]
        + [shape((1, 1), FULL)],
        in_specs=[anywhere] * 8 + [vmem] * 2,
        out_specs=[anywhere] * 8 + [vmem] * 9,
        scratch_shapes=[pltpu.VMEM(item.shape, item.dtype) for item in big]
        + [pltpu.SemaphoreType.DMA((16,)), pltpu.SemaphoreType.DMA((16,))],
    )(*big, vec, loss)


def per_device(
    parts,
    x_query,
    x_passage,
    len_query,
    len_passage,
    positive,
    cot_query,
    cot_passage,
    *weights,
):
    core = lax.axis_index("section")
    on_first = core == 0
    own_set = [member[0] for member in weights]
    own = [own_set[item] for item in (0, 2, 6, 8)]
    vectors = [weights[item] for item in (1, 3, 4, 5, 7, 9, 10, 11)]
    features = x_query.shape[2]
    half_q, half_p = x_query.shape[0] // 2, x_passage.shape[0] // 2
    *kept, par, l_qkv, l_o, l_in, l_out, hidden_q, hidden_p, land_a, grad_cls, loss = forward_both(
        parts,
        x_query,
        x_passage.reshape(-1, QLEN, features),
        len_query,
        len_passage,
        positive,
        vectors,
        own,
    )
    other = (l_qkv, l_o, l_in, l_out)
    if parts != 16:
        last = hidden_p.reshape(x_passage.shape)
        targets = lax.all_gather(positive, "batch", axis=0, tiled=True)
        own_q = hidden_q[:, 0]
        own_p = last[:, 0]
        last_q, last_p = (jnp.where(on_first, swap(item), item) for item in (own_q, own_p))
        cls_query = lax.all_gather(last_q, "batch", axis=0, tiled=True)
        cls_passage = lax.all_gather(last_p, "batch", axis=0, tiled=True)
        score_scale = 2.0 / math.sqrt(features)
        logits = (
            jnp.einsum("qd,pd->qp", cls_query, cls_passage, preferred_element_type=jnp.float32)
            * score_scale
        )
        term_values, grad_logits = contrast(logits, targets)
        loss_value = jnp.mean(term_values)
        mine = lax.axis_index("batch") * 2 + core
        own_logits = lax.dynamic_slice_in_dim(grad_logits, mine * half_q, half_q, 0)
        grad_cls_q = (
            jnp.einsum("qp,pd->qd", own_logits, cls_passage, preferred_element_type=jnp.float32)
            * score_scale
        )
        own_columns = lax.dynamic_slice_in_dim(grad_logits, mine * half_p, half_p, 1)
        grad_cls_p = (
            jnp.einsum("qp,qd->pd", own_columns, cls_query, preferred_element_type=jnp.float32)
            * score_scale
        )
        grad_cls = jnp.concatenate([grad_cls_q, grad_cls_p], 0)
        grad_cls = jnp.pad(grad_cls, ((0, 8 - grad_cls.shape[0]), (0, 0)))

    outs = backward_both(
        parts,
        (cot_query, cot_passage.reshape(-1, QLEN, features)),
        len_query,
        len_passage,
        grad_cls,
        par,
        own,
        other,
        kept + [land_a],
    )
    groups = ((0, 2), (2, 1), (3, 1), (4, 1), (5, 4), (9, 1), (10, 1), (11, 1))
    if parts == 16:
        d_qkv, d_o, d_in, d_out, d_vec, grad_q, grad_p = outs[:7]
        big = (hidden_q, hidden_p, grad_q, grad_p, d_qkv, d_o, d_in, d_out.reshape(-1, features))
        *final, loss = finish(parts, big, d_vec, loss)
        hidden_q, hidden_p, grad_q, grad_p, d_qkv, d_o, d_in, d_out = final[:8]
        small = [item[0] for item in final[8:]]
        loss_value = loss.reshape(())
    else:
        sums, grad_q, grad_p, g_pro, g_att, g_up, g_flo = outs
        left = kept[0]

        def total(pair):
            kept_one = jnp.where(on_first, pair[0], pair[1])
            both = kept_one + swap(jnp.where(on_first, pair[1], pair[0]))
            return lax.psum_scatter(both, "batch", scatter_dimension=0, tiled=True)

        def product(first, second):
            return jnp.einsum("rd,re->de", first, second, preferred_element_type=jnp.float32)

        d_qkv, d_o, d_in = (
            total([product(left[layer, spot], right[layer]) for layer in (0, 1)])
            for spot, right in ((6, g_pro), (5, g_att), (4, g_up))
        )
        d_out = total(
            [
                jnp.concatenate([product(left[layer, spot], g_flo[layer]) for spot in range(4)], 0)
                for layer in (0, 1)
            ]
        )
        small = [
            total([sums[layer, at : at + count].reshape(-1) for layer in (0, 1)])
            for at, count in groups
        ]
    hidden_q, hidden_p = hidden_q[None], hidden_p.reshape(x_passage.shape)[None]
    grad_q = grad_q[None]
    grad_p = grad_p.reshape(x_passage.shape)[None]
    d_b_qv, d_b_o, d_g_attn, d_c_attn, d_b_in, d_b_out, d_g_ffn, d_c_ffn = small
    outs = (
        d_qkv, d_b_qv, d_o, d_b_o, d_g_attn, d_c_attn, d_in, d_b_in, d_out, d_b_out, d_g_ffn,
        d_c_ffn,
    )
    return (hidden_q, hidden_p, grad_q, grad_p, loss_value) + tuple(item[None] for item in outs)


def solution(mesh):
    in_specs = (
        P("batch", None, None),
        P("batch", None, None),
        P("batch"),
        P("batch"),
        P("batch"),
        P("batch", None, None),
        P("batch", None, None),
        P("section", None, None),
        P("section", None),
        P("section", None, None),
        P("section", None),
        P("section", None),
        P("section", None),
        P("section", None, None),
        P("section", None),
        P("section", None, None),
        P("section", None),
        P("section", None),
        P("section", None),
    )
    out_specs = (
        P("section", "batch", None, None),
        P("section", "batch", None, None),
        P("section", "batch", None, None),
        P("section", "batch", None, None),
        P(),
        P("section", "batch", None),
        P("section", "batch"),
        P("section", "batch", None),
        P("section", "batch"),
        P("section", "batch"),
        P("section", "batch"),
        P("section", "batch", None),
        P("section", "batch"),
        P("section", "batch", None),
        P("section", "batch"),
        P("section", "batch"),
        P("section", "batch"),
    )
    return jax.shard_map(
        functools.partial(per_device, mesh.shape["batch"]), mesh=mesh, in_specs=in_specs, out_specs=out_specs, check_vma=False
    )
```

```python
import functools
import math

import jax
import jax.numpy as jnp
from jax import lax
from jax.experimental import pallas as pl
from jax.experimental.pallas import tpu as pltpu
from jax.sharding import PartitionSpec as P

HEADS = 12
QLEN = 32
PLEN = 256


norm_eps = 1e-05


def contrast(logits, targets):
    top_score = jnp.max(logits, -1, keepdims=True)
    log_total = top_score[:, 0] + jnp.log(jnp.sum(jnp.exp(logits - top_score), -1))
    chosen = targets[:, None] == jnp.arange(logits.shape[1])[None, :]
    term_values = log_total - jnp.sum(jnp.where(chosen, logits, 0.0), -1)
    grad_logits = (jnp.exp(logits - log_total[:, None]) - chosen.astype(jnp.float32)).astype(
        jnp.bfloat16
    )
    return (term_values, grad_logits)


MESH = pl.DeviceIdType.MESH
CHUNK = 384
COUNT = 12
BLOCK = 48


def swap(value):
    return lax.ppermute(value, "section", [(0, 1), (1, 0)])


LOW = jnp.bfloat16
FULL = jnp.float32
ROWS = 32
TILE = 768
LAST = (((1,), (1,)), ((), ()))
FIRST = (((0,), (0,)), ((), ()))


def dot(left, right):
    return jnp.dot(left, right, preferred_element_type=FULL)


def dot_last(left, right):
    return lax.dot_general(left, right, LAST, preferred_element_type=FULL)


def dot_first(left, right):
    return lax.dot_general(left, right, FIRST, preferred_element_type=FULL)


UNROLL = 4
PAIRS = 3


def over(count, body, unroll=1):
    def step(index, carry):
        body(index)
        return carry

    lax.fori_loop(0, count, step, 0, unroll=unroll)


def row_range(index):
    return pl.ds(pl.multiple_of(index * ROWS, ROWS), ROWS)


def lane_range(index, width):
    return pl.ds(pl.multiple_of(index * width, 128), width)


def moments(block):
    centred = block - jnp.mean(block, -1, keepdims=True)
    spread = jnp.mean(centred * centred, -1, keepdims=True)
    inverse = lax.rsqrt(spread + norm_eps)
    return centred * inverse, inverse


def gelu_pair(block):
    size = jnp.abs(block)
    t = 1.0 / (1.0 + (0.3275911 * math.sqrt(0.5)) * size)
    bell = jnp.exp(-0.5 * block * block)
    poly = 0.5 * 1.061405429
    for term in (-1.453152027, 1.421413741, -0.284496736, 0.254829592):
        poly = poly * t + 0.5 * term
    tail = poly * t * bell
    phi = jnp.where(block > 0, 1.0 - tail, tail)
    return block * phi, phi + block * bell * (1.0 / math.sqrt(2.0 * math.pi))


def head_lanes(rows, head):
    lane = lax.broadcasted_iota(jnp.int32, (rows, 128), 1)
    return (lane < 64) if head == 0 else (lane >= 64)


def query_mask(lens, start, count):
    rows = count * QLEN
    row = lax.broadcasted_iota(jnp.int32, (rows, rows), 0)
    column = lax.broadcasted_iota(jnp.int32, (rows, rows), 1)
    limit = jnp.zeros((rows, rows), jnp.int32)
    for item in range(count):
        limit = jnp.where(column // QLEN == item, item * QLEN + lens[start + item], limit)
    return (row // QLEN == column // QLEN) & (row < limit)


VMEM_LIMIT = 58 * 1024 * 1024


def remote(src, dst, send, recv, where):
    return pltpu.make_async_remote_copy(
        src_ref=src, dst_ref=dst, send_sem=send, recv_sem=recv,
        device_id=where, device_id_type=MESH,
    )


def greet(targets):
    barrier = pltpu.get_barrier_semaphore()
    for where in targets:
        pl.semaphore_signal(barrier, inc=1, device_id=where, device_id_type=MESH)
    pl.semaphore_wait(barrier, len(targets))


def forward_kernel(
    parts, x_query, x_passage, qlens, plens, positive,
    b_qv, b_o, g_attn, c_attn, b_in, b_out, g_ffn, c_ffn, wqkv, wo, win, wout,
    o_left, o_qkv, o_pq, o_pp, o_pre, o_slope, o_ffn, both_par,
    l_qkv, l_o, l_in, l_out, hid_q, hid_p, land_a, gcls, loss,
    tok, out, bqkv, bo, bin_, bout, qkv, pq, pp, mixed, pre, normed_full, normed, up, act,
    slope, ffn, rows8, rows48, packed, every, stack,
    load, save, xload, parsend, parrecv, wsend, wrecv, hsend, hrecv, hlocal, gsend, grecv, psend, precv, asend, arecv, bsend, brecv,
):
    core = lax.axis_index("section")
    me = lax.axis_index("batch")
    peer = {"section": 1 - core}
    features = wo.shape[0]
    count_q, count_p = x_query.shape[0] // 2, x_passage.shape[0] // 2
    split = count_q * QLEN
    tall = count_p
    total = (count_q + count_p) * QLEN
    own = (wqkv, wo, win, wout)
    land = (l_qkv, l_o, l_in, l_out)
    buffers = (bqkv, bo, bin_, bout)

    gets = [
        pltpu.make_async_copy(
            x_query.at[pl.ds(core * count_q, count_q)], tok.at[0, pl.ds(0, count_q)], xload.at[0]
        ),
        pltpu.make_async_copy(
            x_passage.at[pl.ds(core * tall, tall)], tok.at[0, pl.ds(count_q, tall)], xload.at[1]
        ),
    ]
    for copy in gets:
        copy.start()

    def local(source, spot):
        return pltpu.make_async_copy(source[spot], buffers[spot], load.at[spot])

    def stash(spot):
        return pltpu.make_async_copy(buffers[spot], land[spot], load.at[4 + spot])

    def give_first(spot):
        return remote(own[spot], buffers[spot], wsend.at[spot], wrecv.at[spot], peer)

    def give_block(spot, block):
        part = pl.ds(block * features, features)
        cut = (slice(None), part) if spot == 2 else (part,)
        return remote(
            own[spot].at[cut], buffers[spot].at[cut],
            bsend.at[spot - 2, block], brecv.at[spot - 2, block], peer,
        )

    def weight_block(spot, block):
        @pl.when(core == 1)
        def _():
            give_block(spot, block).wait_recv()
            if block == 3:
                stash(spot).start()

    def give_second(spot):
        return remote(own[spot], land[spot], wsend.at[spot], wrecv.at[spot], peer)

    others = [peer]
    if parts == 16:
        for step in range(1, parts):
            others.append({"batch": (me + step) % parts})

    @pl.when(core == 0)
    def _():
        for spot in range(4):
            local(own, spot).start()

    vectors = (b_qv, b_o, g_attn, c_attn, b_in, b_out, g_ffn, c_ffn)
    spot = 0
    for ref in vectors:
        for item in range(ref.shape[1] // features):
            both_par[core, spot : spot + 1] = ref[:, item * features : (item + 1) * features]
            spot += 1
    both_par[core, spot:16] = jnp.zeros((16 - spot, features), FULL)
    greet(others)
    give_par = remote(both_par.at[core], both_par.at[core], parsend, parrecv, peer)
    give_par.start()

    @pl.when(core == 0)
    def _():
        for spot in range(2):
            give_first(spot).start()
        for spot in (2, 3):
            for block in range(4):
                give_block(spot, block).start()

    @pl.when(core == 1)
    def _():
        for spot in range(4):
            give_second(spot).start()

    def weight_first(spot):
        @pl.when(core == 0)
        def _():
            local(own, spot).wait()

        @pl.when(core == 1)
        def _():
            if spot < 2:
                give_first(spot).wait_recv()
                stash(spot).start()

        if spot >= 2:
            weight_block(spot, 0)

    def fetch_second(spot):
        @pl.when(core == 0)
        def _():
            give_second(spot).wait_recv()
            local(land, spot).start()

        @pl.when(core == 1)
        def _():
            stash(spot).wait()
            local(own, spot).start()

    def weight(layer, spot):
        if layer == 0:
            weight_first(spot)
        else:
            local(own, spot).wait()

    saves = {}

    def keep(name, layer, source, target):
        saves[name, layer] = pltpu.make_async_copy(
            source, target, save.at[len(saves)]
        )
        saves[name, layer].start()

    places = {"act0": 0, "act1": 1, "act2": 2, "act3": 3, "normed": 4, "mixed": 5, "tok": 6}

    def left_give(layer, spot, source):
        return remote(
            source, land_a.at[layer, spot], asend.at[layer, spot], arecv.at[layer, spot], peer
        )

    def keep_left(name, layer, source):
        keep(name, layer, source, o_left.at[layer, places[name]])
        if layer == 1:
            left_give(1, places[name], source).start()

    def free(name, layer):
        if layer == 1:
            saves[name, 0].wait()

    for copy in gets:
        copy.wait()

    remote(both_par.at[core], both_par.at[1 - core], parsend, parrecv, peer).wait_recv()
    blocks = [(0, split, query_mask(qlens, core * count_q, count_q), pq, 0)]
    for item in range(count_p * QLEN // PLEN):
        row = lax.broadcasted_iota(jnp.int32, (PLEN, PLEN), 0)
        limit = plens[core * (count_p * QLEN // PLEN) + item]
        blocks.append((split + item * PLEN, PLEN, row < limit, pp, item * HEADS))

    for layer in (0, 1):
        base_row = 0
        par = both_par.at[layer]
        x = tok.at[layer].reshape(total, features)
        keep_left("tok", layer, x)
        weight(layer, 0)
        free("qkv", layer)

        def project(tile):
            lanes = lane_range(tile, features)
            bias = jnp.where(tile == 0, par[base_row : base_row + 1], 0.0)
            bias = jnp.where(tile == 2, par[base_row + 1 : base_row + 2], bias)
            qkv[:, lanes] = (dot(x[...], bqkv[:, lanes]) + bias).astype(LOW)

        over(3, project)
        keep("qkv", layer, qkv, o_qkv.at[layer])
        if layer == 1:
            fetch_second(3)
            for name, spot in places.items():
                saves[name, 0].wait()
                left_give(0, spot, o_left.at[0, spot]).start()
        for name in ("pq", "pp"):
            free(name, layer)

        def attend(index):
            tasks = []
            for step in range(PAIRS):
                for lo, rows, mask, probs, base in blocks:
                    tasks.append((index * PAIRS + step, lo, rows, mask, probs, base))

            def part(task, offset):
                hp, lo, rows = task[:3]
                return qkv[pl.ds(lo, rows), pl.ds(pl.multiple_of(offset + hp * 128, 128), 128)]

            scores = []
            for task in tasks:
                queries, keys = part(task, 0) * LOW(0.125), part(task, features)
                for head in (0, 1):
                    masked = jnp.where(head_lanes(task[2], head), keys, LOW(0))
                    scores.append(dot_last(masked, queries))
            lows = []
            for spot, value in enumerate(scores):
                hp, lo, rows, mask, probs, base = tasks[spot // 2]
                value = jnp.where(mask, value, -1000000000.0)
                weights = jnp.exp(value - jnp.max(value, 0, keepdims=True))
                inverse = 1.0 / jnp.sum(weights, 0, keepdims=True)
                low = (weights * inverse).astype(LOW)
                probs[base + 2 * hp + spot % 2] = low
                lows.append(low)
            for spot, task in enumerate(tasks):
                hp, lo, rows = task[:3]
                values = part(task, 2 * features).T
                outs = [
                    dot(values[64 * head : 64 * head + 64], lows[2 * spot + head])
                    for head in (0, 1)
                ]
                both = jnp.concatenate(outs, 0).astype(LOW).T
                mixed[pl.ds(lo, rows), pl.ds(pl.multiple_of(hp * 128, 128), 128)] = both

        over(features // 128 // PAIRS, attend)
        keep("pq", layer, pq, o_pq.at[layer])
        keep("pp", layer, pp, o_pp.at[layer])
        keep_left("mixed", layer, mixed)
        weight(layer, 1)
        free("pre", layer)
        pre[...] = (
            dot(mixed[...], bo[...]) + x[...].astype(FULL) + par[base_row + 2 : base_row + 3]
        )
        keep("pre", layer, pre, o_pre.at[layer])
        if layer == 0:
            fetch_second(0)
            fetch_second(1)

        def norm_one(index):
            rows = row_range(index)
            block = moments(pre[rows])[0] * par[base_row + 3 : base_row + 4]
            block = block + par[base_row + 4 : base_row + 5]
            normed_full[rows] = block
            normed[rows] = block.astype(LOW)

        over(total // ROWS, norm_one, 12)
        keep_left("normed", layer, normed)
        weight(layer, 2)
        free("slope", layer)
        step_width = 256
        tiles = win.shape[1] // step_width

        def expand(tile):
            lanes = lane_range(tile, step_width)
            bias_lanes = lane_range(tile % 3, step_width)
            up[tile % 2] = (
                dot(normed[...], bin_[:, lanes])
                + par[pl.ds(base_row + 5 + tile // 3, 1), bias_lanes]
            )

        def bend(tile):
            lanes = lane_range(tile, step_width)
            for index in range(total // ROWS):
                rows = pl.ds(index * ROWS, ROWS)
                value, steep = gelu_pair(up[tile % 2, rows])
                act[rows, lanes] = value.astype(LOW)
                slope[rows, lanes] = steep.astype(LOW)

        expand(0)

        def grow(index):
            if layer == 0 and (index + 1) % 3 == 0:
                weight_block(2, (index + 1) // 3)
            expand(index + 1)
            bend(index)

        for index in range(tiles - 1):
            grow(index)
        bend(tiles - 1)
        for item in range(4):
            lanes = pl.ds(item * features, features)
            keep_left("act%d" % item, layer, act.at[:, lanes])
        keep("slope", layer, slope, o_slope.at[layer])
        weight(layer, 3)
        free("ffn", layer)
        ends = normed_full[...] + par[base_row + 9 : base_row + 10]
        if layer == 0:
            most = 3 * features
            for block in (1, 2):
                weight_block(3, block)
            ffn[...] = dot(act[:, :most], bout[:most]) + ends
            weight_block(3, 3)
            ffn[...] += dot(act[:, most:], bout[most:])
        else:
            ffn[...] = dot(act[...], bout[...]) + ends
        keep("ffn", layer, ffn, o_ffn.at[layer])
        if layer == 0:
            fetch_second(2)
        target = tok.at[1] if layer == 0 else out
        flat = target.reshape(total, features)

        def norm_two(index):
            rows = row_range(index)
            block = moments(ffn[rows])[0] * par[base_row + 10 : base_row + 11]
            flat[rows] = (block + par[base_row + 11 : base_row + 12]).astype(LOW)

        over(total // ROWS, norm_two, 12)
        sides = (
            (target.at[pl.ds(0, count_q)], hid_q.at[pl.ds(core * count_q, count_q)]),
            (target.at[pl.ds(count_q, tall)], hid_p.at[pl.ds(core * tall, tall)]),
        )

        @pl.when(core == layer)
        def _():
            for spot, (src, dst) in enumerate(sides):
                pltpu.make_async_copy(src, dst, hlocal.at[spot]).start()

        @pl.when(core != layer)
        def _():
            for spot, (src, dst) in enumerate(sides):
                remote(src, dst, hsend.at[spot], hrecv.at[spot], peer).start()

    if parts == 16:
        lead = [item * QLEN for item in range(count_q)] + [split]
        rows8[...] = jnp.zeros_like(rows8)
        for spot, row in enumerate(lead):
            rows8[spot : spot + 1] = flat[pl.ds(row, 16)].astype(FULL)[0:1]
        for tile in range(6):
            rows48[8 * tile : 8 * tile + 8] = rows8[:, 128 * tile : 128 * tile + 128]
        for item in range(count_q):
            value = positive[core * count_q + item].astype(FULL)
            rows48[8 * item + 5 : 8 * item + 6] = jnp.full((1, 128), value)
        packed[...] = rows48[...].astype(LOW)

        def share(step, slot):
            return remote(
                packed, every.at[core, slot], gsend.at[step], grecv.at[slot],
                {"batch": (me + step) % parts},
            )

        for step in range(1, parts):
            share(step, me).start()
        every[core, me] = packed[...]
        for step in range(1, parts):
            share(step, (me + parts - step) % parts).wait_recv()
        pass_on = remote(every.at[core], every.at[core], psend, precv, peer)
        pass_on.start()
        remote(every.at[core], every.at[1 - core], psend, precv, peer).wait_recv()
        pass_on.wait_send()
        for step in range(1, parts):
            share(step, me).wait_send()

        wide = 2 * parts * 8
        grid = every[...].astype(FULL).reshape(2 * parts, 48, 128)
        inner = lax.broadcasted_iota(jnp.int32, (2 * parts, 8, 128), 1)
        goal = jnp.zeros((2 * parts, 8, 128), FULL)
        for tile in range(6):
            block = grid[:, 8 * tile : 8 * tile + 8]
            stack[:, 128 * tile : 128 * tile + 128] = block.reshape(wide, 128).astype(LOW)
            if tile < count_q:
                found = jnp.sum(jnp.where(inner == 5, block, 0.0), 1, keepdims=True)
                goal = jnp.where(inner == tile, found, goal)
        row = lax.broadcasted_iota(jnp.int32, (wide, wide), 0)
        column = lax.broadcasted_iota(jnp.int32, (wide, wide), 1)
        scale = 2.0 / math.sqrt(features)
        logits = dot_last(stack[...], stack[...]) * scale
        device = column // 8
        passage = (device % parts) * 2 + device // parts
        is_passage = column % 8 == count_q
        is_query = row % 8 < count_q
        kept = jnp.where(is_passage, logits, -1e30)
        top = jnp.max(kept, -1, keepdims=True)
        log_total = top + jnp.log(jnp.sum(jnp.exp(kept - top), -1, keepdims=True))
        chosen = is_passage & (passage.astype(FULL) == goal.reshape(wide, 128)[:, 0:1])
        picked = jnp.sum(jnp.where(chosen, logits, 0.0), -1, keepdims=True)
        terms = jnp.where(is_query[:, 0:1], log_total - picked, 0.0)
        count = count_q * 2 * parts
        loss[...] = jnp.full((8, 128), jnp.sum(terms) / count)
        grads = jnp.exp(kept - log_total) - chosen.astype(FULL)
        grads = jnp.where(is_query & is_passage, grads, 0.0)
        up[0, 0:wide, 0:wide] = grads + grads.T
        mine = pl.multiple_of((core * parts + me) * 8, 8)
        picked_rows = up[0, pl.ds(mine, 8), 0:wide]
        gcls[...] = dot(picked_rows.astype(LOW), stack[...]) * scale

    for spot, (src, dst) in enumerate(sides):
        pltpu.make_async_copy(src, dst, hlocal.at[spot]).wait()
    theirs = (
        hid_q.at[pl.ds((1 - core) * count_q, count_q)],
        hid_p.at[pl.ds((1 - core) * tall, tall)],
    )
    for spot, (src, dst) in enumerate(zip((item[0] for item in sides), theirs)):
        remote(src, dst, hsend.at[spot], hrecv.at[spot], peer).wait()
    @pl.when(core == 0)
    def _():
        for spot in range(2):
            give_first(spot).wait_send()
        for spot in (2, 3):
            for block in range(4):
                give_block(spot, block).wait_send()

    @pl.when(core == 1)
    def _():
        for spot in range(4):
            give_second(spot).wait_send()

    give_par.wait_send()
    for (name, layer), copy in saves.items():
        if layer == 1:
            copy.wait()
    for layer in (0, 1):
        for spot in range(7):
            left_give(layer, spot, o_left.at[layer, spot]).wait()


def forward_both(parts, x_query, x_passage, qlens, plens, positive, vectors, own):
    queries, features = x_query.shape[0], x_query.shape[2]
    passages = x_passage.shape[0]
    total = (queries + passages) // 2 * QLEN
    wide = own[2].shape[1]
    split = queries // 2 * QLEN
    heads_p = HEADS * (passages // 2 * QLEN // PLEN)
    kept = [
        ((7, total, features), LOW),
        ((total, 3 * features), LOW),
        ((HEADS, split, split), LOW),
        ((heads_p, PLEN, PLEN), LOW),
        ((total, features), FULL),
        ((total, wide), LOW),
        ((total, features), FULL),
        ((16, features), FULL),
    ]
    shape = jax.ShapeDtypeStruct
    anywhere = pl.BlockSpec(memory_space=pl.ANY)
    vmem = pl.BlockSpec(memory_space=pltpu.VMEM)
    smem = pl.BlockSpec(memory_space=pltpu.SMEM)
    dma = pltpu.SemaphoreType.DMA
    scratch = [
        pltpu.VMEM((2, total // QLEN, QLEN, features), LOW),
        pltpu.VMEM((total // QLEN, QLEN, features), LOW),
    ]
    scratch += [pltpu.VMEM(item.shape, item.dtype) for item in own]
    scratch += [pltpu.VMEM(size, kind) for size, kind in kept[1:4]]
    scratch += [
        pltpu.VMEM((total, features), LOW),
        pltpu.VMEM((total, features), FULL),
        pltpu.VMEM((total, features), FULL),
        pltpu.VMEM((total, features), LOW),
        pltpu.VMEM((2, total, 256), FULL),
        pltpu.VMEM((total, wide), LOW),
        pltpu.VMEM((total, wide), LOW),
        pltpu.VMEM((total, features), FULL),
    ]
    scratch += [
        pltpu.VMEM((8, features), FULL),
        pltpu.VMEM((48, 128), FULL),
        pltpu.VMEM((48, 128), LOW),
        pltpu.VMEM((2, 16, 48, 128), LOW),
        pltpu.VMEM((256, features), LOW),
        dma((8,)),
        dma((26,)),
        dma((2,)),
        dma,
        dma,
        dma((4,)),
        dma((4,)),
        dma((2,)),
        dma((2,)),
        dma((2,)),
        dma((16,)),
        dma((16,)),
        dma,
        dma,
        dma((2, 7)),
        dma((2, 7)),
        dma((2, 4)),
        dma((2, 4)),
    ]
    return pl.pallas_call(
        functools.partial(forward_kernel, parts),
        out_shape=[shape((2,) + size, kind) for size, kind in kept]
        + [shape(item.shape, item.dtype) for item in own]
        + [
            shape(x_query.shape, LOW),
            shape(x_passage.shape, LOW),
            shape((2, 7, total, features), LOW),
            shape((8, features), FULL),
            shape((8, 128), FULL),
        ],
        in_specs=[anywhere, anywhere, smem, smem, smem] + [vmem] * 8 + [anywhere] * 4,
        out_specs=[anywhere] * 7 + [vmem] + [anywhere] * 7 + [vmem] * 2,
        scratch_shapes=scratch,
        compiler_params=pltpu.CompilerParams(
            collective_id=2, has_side_effects=True, vmem_limit_bytes=VMEM_LIMIT
        ),
    )(x_query, x_passage, qlens, plens, positive, *vectors, *own)


def add_rows(block):
    return jnp.sum(block.reshape(block.shape[0] // 8, 8, block.shape[1]), 0)


def norm_back(source, grad_of, gain, total, store):
    features = source.shape[1]
    zero = jnp.zeros((8, features), FULL)

    def step(index, carry):
        rows = row_range(index)
        grad = grad_of(index)
        unit, inverse = moments(source[rows])
        scaled = grad * gain
        back = inverse * (
            scaled
            - jnp.mean(scaled, -1, keepdims=True)
            - unit * jnp.mean(scaled * unit, -1, keepdims=True)
        )
        store(rows, back)
        return (
            carry[0] + add_rows(grad * unit),
            carry[1] + add_rows(grad),
            carry[2] + add_rows(back),
        )

    sums = lax.fori_loop(0, total // ROWS, step, (zero, zero, zero), unroll=UNROLL)
    return [jnp.sum(item, 0, keepdims=True) for item in sums]


LAGS = (2, 4, 6)
RING = 12
HELD = 8


def left_index(ch):
    return (
        jnp.minimum(ch, 4) + (ch >= 8).astype(jnp.int32) + (ch >= 9).astype(jnp.int32)
    )


def right_index(ch):
    return jnp.maximum(ch - 3, 0)


def backward_kernel(parts, *refs):
    small = parts == 16
    refs = list(refs)

    def take(count):
        front = refs[:count]
        del refs[:count]
        return front

    cot_query, cot_passage, qlens, plens, gcls, par = take(6)
    own, land = take(4), take(4)
    left, h_qkv, h_pq, h_pp, h_pre, h_slope, h_ffn, land_a = take(8)
    if small:
        o_qkv, o_o, o_in, o_out, o_vec, o_gq, o_gp, land_g, own_g = take(9)
    else:
        vpar, o_gq, o_gp, f_pro, f_att, f_up, f_flo = take(7)
    buffers = take(4)
    bqkv, bo, bin_, bout = buffers
    qkv, pq, pp, source, slope, gsrc = take(6)
    attn_full, attn, steep, flow_full, flow = take(5)
    gmixed = flow
    grow = flow_full.reshape(flow.shape[0] // QLEN, QLEN, flow.shape[1])
    wload, fetch, cload, hsend, hrecv, hlocal, ksem = take(7)
    if small:
        vpar, a_buf, g_buf, stage, s1, r1, s2, r2, s3, r3, hold = take(11)
        va, ra, vb, rb, vc, rc, rz = take(7)
        s1s, r1s, s2s, r2s, s3s, r3s, vsend, vrecv, zsend, zrecv = take(10)
        gs, gr, sl, gl, el = take(5)

    core = lax.axis_index("section")
    me = lax.axis_index("batch")
    peer = {"section": 1 - core}
    features = gcls.shape[1]
    total = flow.shape[0]
    split = pq.shape[1]
    count_q, tall = cot_query.shape[0] // 2, cot_passage.shape[0] // 2
    heads_p = pp.shape[0]
    blocks_p = PLEN // QLEN

    def weight_copy(spot, source_set):
        return pltpu.make_async_copy(source_set[spot], buffers[spot], wload.at[spot])

    def weight_start(layer, spot):
        @pl.when(core == layer)
        def _():
            weight_copy(spot, own).start()

        @pl.when(core != layer)
        def _():
            weight_copy(spot, land).start()

    def weight_wait(spot):
        weight_copy(spot, own).wait()

    saved = ((h_ffn, source), (h_slope, slope), (h_pre, source), (h_qkv, qkv), (h_pq, pq), (h_pp, pp))

    def saved_copy(layer, spot):
        src, dst = saved[spot]
        return pltpu.make_async_copy(src.at[layer], dst, fetch.at[spot])

    cots = [
        pltpu.make_async_copy(
            cot_query.at[pl.ds(core * count_q, count_q)], gsrc.at[pl.ds(0, count_q)], cload.at[0]
        ),
        pltpu.make_async_copy(
            cot_passage.at[pl.ds(core * tall, tall)], gsrc.at[pl.ds(count_q, tall)], cload.at[1]
        ),
    ]
    def early_copy(spot, side):
        src = (left, land_a)[side]
        if spot < 2:
            dst, sem = stage.at[spot, side], sl.at[spot, side]
        else:
            lanes = pl.ds((spot - 2) * features, features)
            dst, sem = bin_.at[pl.ds(side * total, total), lanes], el.at[spot - 2, side]
        return pltpu.make_async_copy(src.at[1, spot], dst, sem)

    if small:
        x, y, z = me % 2, (me // 2) % 2, me // 4
        px, py = me + 1 - 2 * x, me + 2 - 4 * y
        targets = [{"batch": px}, {"batch": py}, peer]
        for step in (1, 2, 3):
            other = ((z + step) % 4) * 4 + me % 4
            targets += [{"section": sec, "batch": other} for sec in (0, 1)]
        barrier = pltpu.get_barrier_semaphore()
        for where in targets:
            pl.semaphore_signal(barrier, inc=1, device_id=where, device_id_type=MESH)
        for spot in range(4):
            for side in (0, 1):
                early_copy(spot, side).start()
    saved_copy(1, 0).start()
    for copy in cots:
        copy.start()
    weight_start(1, 3)
    saved_copy(1, 1).start()

    widths = ((flow, 1), (slope, 4), (attn, 1), (qkv, 3))

    def pieces_of(slot):
        base = (0, 1, 5, 6)[slot]
        ref, count = widths[slot]
        return [(base + item, ref, ref.shape[1] // 2, item) for item in range(count)]

    def own_piece(layer, piece):
        spot, ref, width, item = piece
        lanes = pl.ds(pl.multiple_of(core * width + item * CHUNK, 128), CHUNK)
        return pltpu.make_async_copy(ref.at[:, lanes], own_g.at[layer, spot], ksem.at[spot])

    def peer_piece(layer, piece):
        spot, ref, width, item = piece
        lanes = pl.ds(pl.multiple_of((1 - core) * width + item * CHUNK, 128), CHUNK)
        return remote(
            ref.at[:, lanes], land_g.at[layer, spot], gs.at[layer, spot], gr.at[layer, spot], peer
        )

    def whole_piece(layer, slot):
        ref = widths[slot][0]
        target = (f_flo, f_up, f_att, f_pro)[slot]
        return pltpu.make_async_copy(ref, target.at[layer], ksem.at[slot])

    def direct():
        spot, ref, width, item = pieces_of(0)[0]
        lanes = pl.ds(pl.multiple_of((1 - core) * width, 128), CHUNK)
        return remote(
            ref.at[:, lanes], g_buf.at[0, pl.ds(total, total)], gs.at[1, 0], gr.at[1, 0], peer
        )

    def give(layer, slot):
        if small and slot == 0:

            @pl.when(layer == 1)
            def _():
                direct().start()
                lanes = pl.ds(pl.multiple_of(core * CHUNK, 128), CHUNK)
                g_buf[0, pl.ds(0, total)] = flow[:, lanes]

            @pl.when(layer == 0)
            def _():
                piece = pieces_of(0)[0]
                peer_piece(layer, piece).start()
                own_piece(layer, piece).start()

        elif small:
            for piece in pieces_of(slot):
                peer_piece(layer, piece).start()
                own_piece(layer, piece).start()
        else:
            whole_piece(layer, slot).start()

    def given(layer, slot):
        if small:
            for piece in pieces_of(slot):
                peer_piece(layer, piece).wait_send()
                if slot > 0:
                    own_piece(layer, piece).wait()
                else:

                    @pl.when(layer == 0)
                    def _():
                        own_piece(layer, piece).wait()
        else:
            whole_piece(layer, slot).wait()

    def slot_zero(layer):
        saved_copy(layer, 0).wait()
        gains = par.at[layer]
        last = layer == 1

        def grad_of(index):
            block = gsrc[index].astype(FULL)
            beyond = jnp.maximum(index - count_q, 0)
            item = beyond // blocks_p
            query_limit = qlens[core * count_q + jnp.minimum(index, count_q - 1)]
            passage_limit = (
                plens[core * (tall // blocks_p) + item] - (beyond % blocks_p) * QLEN
            )
            limit = jnp.where(index < count_q, query_limit, passage_limit)
            limit = jnp.where(last, limit, QLEN)
            lead = jnp.where(index < count_q, index, count_q + item)
            starts = (index < count_q) | (beyond % blocks_p == 0)
            row = lax.broadcasted_iota(jnp.int32, block.shape, 0)
            block = jnp.where(row < limit, block, 0.0)
            extra = gcls[pl.ds(lead, 1)] * jnp.where(starts & last, 1.0, 0.0)
            return block + jnp.where(row == 0, extra, 0.0)

        def store(rows, back):
            flow_full[rows] = back
            flow[rows] = back.astype(LOW)

        gain, shift, bias = norm_back(source, grad_of, gains[10:11], total, store)
        sums = vpar.at[layer]
        sums[10:11], sums[11:12], sums[9:10] = gain, shift, bias
        give(layer, 0)
        saved_copy(layer, 2).start()

    width = 256
    tiles = bout.shape[0] // width

    def slot_one(layer):
        saved_copy(layer, 1).wait()
        weight_wait(3)
        sums = vpar.at[layer]

        def shrink(tile):
            rows_of = pl.ds(pl.multiple_of(tile * width, width), width)
            steep[tile % 2] = dot_last(flow[...], bout[rows_of])

        def bend(tile):
            lanes = lane_range(tile, width)
            acc = jnp.zeros((8, width), FULL)
            for index in range(total // ROWS):
                rows = pl.ds(index * ROWS, ROWS)
                low = (steep[tile % 2, rows] * slope[rows, lanes].astype(FULL)).astype(LOW)
                slope[rows, lanes] = low
                acc = acc + add_rows(low.astype(FULL))
            sums[pl.ds(5 + tile // 3, 1), lane_range(tile % 3, width)] = jnp.sum(
                acc, 0, keepdims=True
            )

        shrink(0)

        def both(index):
            shrink(index + 1)
            bend(index)

        over(tiles - 1, both)
        bend(tiles - 1)
        give(layer, 1)

        @pl.when(layer == 1)
        def _():
            weight_start(0, 3)

    def slot_two(layer):
        weight_wait(2)
        flow_full[...] += dot_last(slope[...], bin_[...])
        saved_copy(layer, 2).wait()
        gains, sums = par.at[layer], vpar.at[layer]

        def store(rows, back):
            attn_full[rows] = back
            attn[rows] = back.astype(LOW)

        gain, shift, bias = norm_back(
            source, lambda index: flow_full[row_range(index)], gains[3:4], total, store
        )
        sums[3:4], sums[4:5], sums[2:3] = gain, shift, bias
        give(layer, 2)
        weight_wait(1)
        gmixed[...] = dot_last(attn[...], bo[...]).astype(LOW)

        @pl.when(layer == 1)
        def _():
            weight_start(0, 2)
            weight_start(0, 1)
            saved_copy(0, 0).start()
            saved_copy(0, 1).start()

    blocks = [(0, split, pq, 0)]
    for item in range(heads_p // HEADS):
        blocks.append((split + item * PLEN, PLEN, pp, item * HEADS))

    def attend(index):
        tasks = []
        for step in range(PAIRS):
            for block in blocks:
                tasks.append((index * PAIRS + step,) + block)

        def spot_of(task, offset):
            hp, lo, rows = task[:3]
            return (pl.ds(lo, rows), pl.ds(pl.multiple_of(offset + hp * 128, 128), 128))

        grads = []
        for task in tasks:
            values, back = qkv[spot_of(task, 2 * features)], gmixed[spot_of(task, 0)]
            for head in (0, 1):
                masked = jnp.where(head_lanes(task[2], head), values, LOW(0))
                grads.append(dot_last(masked, back))
        lows = []
        for spot, grad_probs in enumerate(grads):
            hp, lo, rows, probs, base = tasks[spot // 2]
            full = probs[base + 2 * hp + spot % 2].astype(FULL)
            inner = jnp.sum(grad_probs * full, 0, keepdims=True)
            lows.append((full * (grad_probs - inner)).astype(LOW))
        for spot, task in enumerate(tasks):
            hp, lo, rows, probs, base = task
            queries, keys = qkv[spot_of(task, 0)], qkv[spot_of(task, features)]
            back = gmixed[spot_of(task, 0)]
            turned = keys.T
            outs = []
            for head in (0, 1):
                grad_scores = lows[2 * spot + head]
                outs.append(
                    (
                        dot(turned[64 * head : 64 * head + 64], grad_scores) * 0.125,
                        dot(grad_scores, queries) * 0.125,
                        dot(probs[base + 2 * hp + head], back),
                    )
                )
            first = head_lanes(rows, 0)
            both = jnp.concatenate([outs[0][0], outs[1][0]], 0)
            qkv[spot_of(task, 0)] = both.astype(LOW).T
            for item in (1, 2):
                both = jnp.where(first, outs[0][item], outs[1][item])
                qkv[spot_of(task, item * features)] = both.astype(LOW)

    def grads_here(spot):
        lo, count, target = ((0, count_q, o_gq), (count_q, tall, o_gp))[spot]
        return pltpu.make_async_copy(
            grow.at[pl.ds(lo, count)], target.at[pl.ds(core * count, count)], hlocal.at[spot]
        )

    def grads_there(spot):
        lo, count, target = ((0, count_q, o_gq), (count_q, tall, o_gp))[spot]
        return remote(
            grow.at[pl.ds(lo, count)],
            target.at[pl.ds(core * count, count)],
            hsend.at[spot],
            hrecv.at[spot],
            peer,
        )

    def slot_three(layer):
        for spot in (3, 4, 5):
            saved_copy(layer, spot).wait()
        over(features // 128 // PAIRS, attend)
        give(layer, 3)
        sums = vpar.at[layer]

        def bias_sums(index, carry):
            rows = row_range(index)
            return (
                carry[0] + add_rows(qkv[rows, pl.ds(0, features)].astype(FULL)),
                carry[1] + add_rows(qkv[rows, pl.ds(2 * features, features)].astype(FULL)),
            )

        zero = jnp.zeros((8, features), FULL)
        found = lax.fori_loop(0, total // ROWS, bias_sums, (zero, zero), unroll=2)
        sums[0:1] = jnp.sum(found[0], 0, keepdims=True)
        sums[1:2] = jnp.sum(found[1], 0, keepdims=True)
        sums[12:16] = jnp.zeros((4, features), FULL)
        weight_wait(0)
        rows_all = attn_full[...] + dot_last(qkv[...], bqkv[...])
        flow_full[...] = rows_all
        gsrc[...] = rows_all.astype(LOW).reshape(gsrc.shape)

        @pl.when(core == layer)
        def _():
            for spot in (0, 1):
                grads_here(spot).start()

        @pl.when(core != layer)
        def _():
            for spot in (0, 1):
                grads_there(spot).start()

        @pl.when(layer == 1)
        def _():
            weight_start(0, 0)

    def grads_given(layer):
        @pl.when(core == layer)
        def _():
            for spot in (0, 1):
                grads_here(spot).wait()

        @pl.when(core != layer)
        def _():
            for spot in (0, 1):
                grads_there(spot).wait_send()

    slots = (slot_zero, slot_one, slot_two, slot_three)

    def reload(layer, slot):
        @pl.when(layer == 1)
        def _():
            if slot == 3:
                for spot in (3, 4, 5):
                    saved_copy(0, spot).start()

    def rest_of_loads():
        for spot in (2, 1, 0):
            weight_start(1, spot)
        for spot in (3, 4, 5):
            saved_copy(1, spot).start()

    def grads_came():
        lands = ((o_gq, count_q), (o_gp, tall))
        for spot, (target, count) in enumerate(lands):
            there = target.at[pl.ds((1 - core) * count, count)]
            remote(there, there, hsend.at[spot], hrecv.at[spot], peer).wait_recv()

    if not small:
        greet([peer])
        rest_of_loads()
        for copy in cots:
            copy.wait()
        for layer in (1, 0):
            for slot in range(4):
                slots[slot](layer)
                given(layer, slot)
                reload(layer, slot)
            grads_given(layer)
        grads_came()
        return

    def stage_copy(number, side):
        layer, spot = 1 - number // 7, number % 7
        src = left if side == 0 else land_a
        return pltpu.make_async_copy(
            src.at[layer, spot], stage.at[number % 2, side], sl.at[number % 2, side]
        )

    def stage_start(number):
        stage_copy(number, 0).start()
        stage_copy(number, 1).start()

    def rotate(spot, view):
        for side in (0, 1):
            lanes = pl.ds(side * total, total)
            for half in range(features // CHUNK):
                block = view(side, half * CHUNK).T
                if spot > 3:
                    a_buf[spot, pl.ds(2 * half, 2), :, :, :, lanes] = block.reshape(
                        2, 2, 2, BLOCK, total
                    )
                else:
                    shaped = block.reshape(2, 4, BLOCK, total)
                    for item in range(4):
                        a_buf[item, spot, half, :, :, lanes] = shaped[:, item]

    def turn(number, spot):
        for side in (0, 1):
            stage_copy(number, side).wait()
        rotate(spot, lambda side, at: stage[number % 2, side, :, pl.ds(at, CHUNK)])

        @pl.when(number + 2 < 14)
        def _():
            stage_start(number + 2)

    for spot in range(4):
        for side in (0, 1):
            early_copy(spot, side).wait()
        if spot < 2:
            rotate(spot, lambda side, at: stage[spot, side, :, pl.ds(at, CHUNK)])
            stage_start(spot + 4)
        else:
            rotate(
                spot,
                lambda side, at: bin_[
                    pl.ds(side * total, total), pl.ds((spot - 2) * features + at, CHUNK)
                ],
            )
    pl.semaphore_wait(barrier, len(targets))

    def right_copy(layer, spot, side):
        src = own_g if side == 0 else land_g
        return pltpu.make_async_copy(
            src.at[layer, spot], g_buf.at[spot, pl.ds(side * total, total)], gl.at[spot, side]
        )

    def right_start(k):
        ch = k % COUNT
        layer = 1 - k // COUNT

        @pl.when((k > 0) & (k < 2 * COUNT) & ((ch == 0) | (ch >= 4)))
        def _():
            spot = right_index(ch)
            right_copy(layer, spot, 0).start()
            remote(
                own_g.at[layer, spot], land_g.at[layer, spot],
                gs.at[layer, spot], gr.at[layer, spot], peer,
            ).wait_recv()
            right_copy(layer, spot, 1).start()

    def first(k, par_):
        return remote(
            s1.at[k % HELD], r1.at[k % RING], s1s.at[k], r1s.at[k],
            {"batch": px if par_ == 0 else py},
        )

    def second(k, par_):
        return remote(
            s2.at[k % 4], r2.at[k % HELD], s2s.at[k], r2s.at[k],
            {"batch": py if par_ == 0 else px},
        )

    def third(k, step):
        layer = 1 - k // COUNT
        zt = (z + step) % 4
        return remote(
            s3.at[k % 4, zt], r3.at[core, k % COUNT, z], s3s.at[k, step],
            r3s.at[core, k % COUNT, z], {"section": layer, "batch": zt * 4 + me % 4},
        )

    def third_in(k, step, src_core):
        zs = (z + 4 - step) % 4
        return remote(
            s3.at[k % 4, zs], r3.at[src_core, k % COUNT, zs], s3s.at[k, step],
            r3s.at[src_core, k % COUNT, zs], peer,
        )

    def product(k, block, rows):
        return dot(block.reshape(rows, 2 * total), g_buf[right_index(k % COUNT)])

    def left_of(k):
        return a_buf.at[left_index(k % COUNT)]

    def ready(k, par_):
        ch = k % COUNT

        @pl.when((k > 0) & ((ch == 0) | (ch >= 4)))
        def _():
            for side in (0, 1):
                right_copy(0, right_index(ch), side).wait()

        base = (k // COUNT) * 7
        if par_ == 0:

            @pl.when(k == 0)
            def _():
                direct().wait_recv()

            @pl.when(k == COUNT)
            def _():
                for spot in range(4):
                    turn(base + spot, spot)

            for spot, at in ((4, 4), (5, 8)):

                @pl.when(ch == at)
                def _():
                    turn(base + spot, spot)
        else:

            @pl.when(ch == 9)
            def _():
                turn(base + 6, 6)

    def part_one(k, par_):
        ready(k, par_)
        ref = left_of(k)
        block = ref[:, :, 1 - x] if par_ == 0 else ref[:, 1 - y]
        s1[k % HELD] = product(k, block, 8 * BLOCK).astype(LOW).reshape(4, 2, BLOCK, CHUNK)
        first(k, par_).start()

    def part_two(k, par_):
        ref = left_of(k)
        block = ref[:, 1 - y, x] if par_ == 0 else ref[:, y, 1 - x]
        hold[...] = product(k, block, 4 * BLOCK).reshape(4, BLOCK, CHUNK)
        first(k, par_).wait()
        came = r1[k % RING, :, 1 - y] if par_ == 0 else r1[k % RING, :, 1 - x]
        s2[k % 4] = (hold[...] + came.astype(FULL)).astype(LOW)
        second(k, par_).start()

    def part_three(k, par_):
        layer = 1 - k // COUNT
        ref = left_of(k)
        came = r1[k % RING, :, y] if par_ == 0 else r1[k % RING, :, x]
        hold[...] = product(k, ref[:, y, x], 4 * BLOCK).reshape(
            4, BLOCK, CHUNK
        ) + came.astype(FULL)
        second(k, par_).wait()
        value = hold[...] + r2[k % HELD].astype(FULL)
        s3[k % 4] = value.astype(LOW)
        for step in (1, 2, 3):
            third(k, step).start()

        @pl.when(core != layer)
        def _():
            third(k, 0).start()

        @pl.when(core == layer)
        def _():
            r3[core, k % COUNT, z] = s3[k % 4, z]

    def part_four(k, par_):
        layer = 1 - k // COUNT
        ch = k % COUNT
        for step in (1, 2, 3):
            third(k, step).wait_send()

        @pl.when(core != layer)
        def _():
            third(k, 0).wait_send()

        @pl.when(core == layer)
        def _():
            for step in (1, 2, 3):
                for src_core in (0, 1):
                    third_in(k, step, src_core).wait_recv()
            third_in(k, 0, 1 - core).wait_recv()
            for src_core in (0, 1):
                value = jnp.sum(r3[src_core, ch].astype(FULL), 0)

                @pl.when(ch < 4)
                def _():
                    o_out[ch, :, pl.ds(src_core * CHUNK, CHUNK)] = value

                @pl.when((ch >= 4) & (ch < 8))
                def _():
                    start = pl.multiple_of((ch - 4) * CHUNK + src_core * 4 * CHUNK, 128)
                    o_in[:, pl.ds(start, CHUNK)] = value

                @pl.when(ch == 8)
                def _():
                    o_o[:, pl.ds(src_core * CHUNK, CHUNK)] = value

                @pl.when(ch >= 9)
                def _():
                    start = pl.multiple_of((ch - 9) * CHUNK + src_core * 3 * CHUNK, 128)
                    o_qkv[:, pl.ds(start, CHUNK)] = value

    vec_cross = remote(vpar.at[1 - core], ra, vsend.at[0], vrecv.at[0], peer)
    vec_x = remote(va, rb, vsend.at[1], vrecv.at[1], {"batch": px})
    vec_y = remote(vb, rc, vsend.at[2], vrecv.at[2], {"batch": py})

    def vec_z(step, slot):
        return remote(
            vc, rz.at[slot], zsend.at[step], zrecv.at[slot],
            {"batch": ((z + step) % 4) * 4 + me % 4},
        )

    steps = 2 * COUNT + LAGS[2]

    starts = ((-1, 3), (0, 4), (1, 6), (2, 8))

    def pair(turn_index, carry):
        kk = turn_index - 1
        layer = (kk < 3).astype(jnp.int32)

        for slot, (one, two) in enumerate(starts):

            @pl.when((kk == one + 1) | (kk == two + 1))
            def _():
                done = (kk == one + 1).astype(jnp.int32)
                given(done, slot)
                reload(done, slot)
                if slot == 3:
                    grads_given(done)

        @pl.when(kk == -1)
        def _():
            rest_of_loads()
            for copy in cots:
                copy.wait()

        for par_ in (0, 1):
            right_start(2 * kk + 2 + par_)

        stages = (part_two, part_three, part_four)

        def advance(item):
            lag, part = LAGS[item], stages[item]
            for par_ in (0, 1):
                k = 2 * kk + par_

                @pl.when((k >= lag) & (k < 2 * COUNT + lag))
                def _():
                    part(k - lag, par_)

        advance(0)
        advance(1)

        @pl.when((kk == starts[0][0]) | (kk == starts[0][1]))
        def _():
            slots[0](layer)

        for par_ in (0, 1):
            k = 2 * kk + 2 + par_

            @pl.when(k < 2 * COUNT)
            def _():
                part_one(k, par_)

        advance(2)

        for slot, (one, two) in enumerate(starts):
            if slot > 0:

                @pl.when((kk == one) | (kk == two))
                def _():
                    slots[slot](layer)

        @pl.when(kk == 9)
        def _():
            vec_cross.start()

        @pl.when(kk == 10)
        def _():
            vec_cross.wait()
            va[...] = vpar[core] + ra[...]
            vec_x.start()

        @pl.when(kk == 11)
        def _():
            vec_x.wait()
            vb[...] = va[...] + rb[...]
            vec_y.start()

        @pl.when(kk == 12)
        def _():
            vec_y.wait()
            vc[...] = vb[...] + rc[...]
            for step in (1, 2, 3):
                vec_z(step, z).start()

        @pl.when(kk == 14)
        def _():
            for step in (1, 2, 3):
                vec_z(step, z).wait_send()
                vec_z(step, (z + 4 - step) % 4).wait_recv()
            rz[z] = vc[...]
            o_vec[...] = jnp.sum(rz[...], 0)

        return carry

    lax.fori_loop(0, steps // 2 + 1, pair, 0)
    grads_came()


def backward_both(parts, cots, qlens, plens, gcls, par, own, land, kept):
    small = parts == 16
    cot_query, cot_passage = cots
    left, h_qkv, h_pq, h_pp, h_pre, h_slope, h_ffn = kept[:7]
    total, features = left.shape[2:]
    wide = own[2].shape[1]
    shape = jax.ShapeDtypeStruct
    anywhere = pl.BlockSpec(memory_space=pl.ANY)
    vmem = pl.BlockSpec(memory_space=pltpu.VMEM)
    smem = pl.BlockSpec(memory_space=pltpu.SMEM)
    dma = pltpu.SemaphoreType.DMA
    grads = [shape(cot_query.shape, FULL), shape(cot_passage.shape, FULL)]
    if small:
        out_shape = [
            shape((BLOCK, 3 * features), FULL),
            shape((BLOCK, features), FULL),
            shape((BLOCK, wide), FULL),
            shape((4, BLOCK, features), FULL),
            shape((16, features), FULL),
            *grads,
            shape((2, 9, total, CHUNK), LOW),
            shape((2, 9, total, CHUNK), LOW),
        ]
        out_specs = [vmem] * 5 + [anywhere] * 4
    else:
        out_shape = [
            shape((2, 16, features), FULL),
            *grads,
            shape((2, total, 3 * features), LOW),
            shape((2, total, features), LOW),
            shape((2, total, wide), LOW),
            shape((2, total, features), LOW),
        ]
        out_specs = [vmem] + [anywhere] * 6
    scratch = [pltpu.VMEM(item.shape, item.dtype) for item in own]
    scratch += [
        pltpu.VMEM(h_qkv.shape[1:], LOW),
        pltpu.VMEM(h_pq.shape[1:], LOW),
        pltpu.VMEM(h_pp.shape[1:], LOW),
        pltpu.VMEM((total, features), FULL),
        pltpu.VMEM((total, wide), LOW),
        pltpu.VMEM((total // QLEN, QLEN, features), LOW),
        pltpu.VMEM((total, features), FULL),
        pltpu.VMEM((total, features), LOW),
        pltpu.VMEM((2, total, 256), FULL),
        pltpu.VMEM((total, features), FULL),
        pltpu.VMEM((total, features), LOW),
        dma((4,)),
        dma((6,)),
        dma((2,)),
        dma((2,)),
        dma((2,)),
        dma((2,)),
        dma((9,)),
    ]
    if small:
        steps = 2 * COUNT
        vector = pltpu.VMEM((16, features), FULL)
        scratch += [
            pltpu.VMEM((2, 16, features), FULL),
            pltpu.VMEM((7, 4, 2, 2, BLOCK, 2 * total), LOW),
            pltpu.VMEM((9, 2 * total, CHUNK), LOW),
            pltpu.VMEM((2, 2, total, features), LOW),
            pltpu.VMEM((HELD, 4, 2, BLOCK, CHUNK), LOW),
            pltpu.VMEM((RING, 4, 2, BLOCK, CHUNK), LOW),
            pltpu.VMEM((4, 4, BLOCK, CHUNK), LOW),
            pltpu.VMEM((HELD, 4, BLOCK, CHUNK), LOW),
            pltpu.VMEM((4, 4, BLOCK, CHUNK), LOW),
            pltpu.VMEM((2, COUNT, 4, BLOCK, CHUNK), LOW),
            pltpu.VMEM((4, BLOCK, CHUNK), FULL),
            *[vector] * 6,
            pltpu.VMEM((4, 16, features), FULL),
            dma((steps,)),
            dma((steps,)),
            dma((steps,)),
            dma((steps,)),
            dma((steps, 4)),
            dma((2, COUNT, 4)),
            dma((3,)),
            dma((3,)),
            dma((4,)),
            dma((4,)),
            dma((2, 9)),
            dma((2, 9)),
            dma((2, 2)),
            dma((9, 2)),
            dma((2, 2)),
        ]
    return pl.pallas_call(
        functools.partial(backward_kernel, parts),
        out_shape=out_shape,
        in_specs=[anywhere, anywhere, smem, smem, vmem, vmem] + [anywhere] * 16,
        out_specs=out_specs,
        scratch_shapes=scratch,
        compiler_params=pltpu.CompilerParams(
            collective_id=1, has_side_effects=True, vmem_limit_bytes=60 * 1024 * 1024
        ),
    )(cot_query, cot_passage, qlens, plens, gcls, par, *own, *land, *kept)


def finish_kernel(parts, *refs):
    big, vec, loss = refs[:8], refs[8], refs[9]
    outs, small, total = refs[10:18], refs[18:26], refs[26]
    held, come, go = refs[27:35], refs[35], refs[36]
    copies = []
    for src, mid, dst in zip(big, held, outs):
        spot = len(copies)
        copies.append(
            (
                pltpu.make_async_copy(src, mid, come.at[spot]),
                pltpu.make_async_copy(mid, dst, go.at[spot]),
            )
        )
        copies[-1][0].start()
    me = lax.axis_index("batch")
    features = vec.shape[1]
    for at, count, out in zip((0, 2, 3, 4, 5, 9, 10, 11), (2, 1, 1, 1, 4, 1, 1, 1), small):
        size = count * features // parts
        every = parts // count
        block = vec[pl.ds(at + me // every, 1)]
        block = jnp.broadcast_to(block, (8, features))
        turned = pltpu.roll(block, (features - size * (me % every)) % features, 1)
        out[...] = turned[0:1, 0:size]
    total[...] = loss[0:1, 0:1]
    for came, left in copies:
        came.wait()
        left.start()
    for came, left in copies:
        left.wait()


def finish(parts, big, vec, loss):
    features = vec.shape[1]
    anywhere = pl.BlockSpec(memory_space=pl.ANY)
    vmem = pl.BlockSpec(memory_space=pltpu.VMEM)
    shape = jax.ShapeDtypeStruct
    return pl.pallas_call(
        functools.partial(finish_kernel, parts),
        out_shape=[shape(item.shape, item.dtype) for item in big]
        + [shape((1, count * features // parts), FULL) for count in (2, 1, 1, 1, 4, 1, 1, 1)]
        + [shape((1, 1), FULL)],
        in_specs=[anywhere] * 8 + [vmem] * 2,
        out_specs=[anywhere] * 8 + [vmem] * 9,
        scratch_shapes=[pltpu.VMEM(item.shape, item.dtype) for item in big]
        + [pltpu.SemaphoreType.DMA((8,)), pltpu.SemaphoreType.DMA((8,))],
    )(*big, vec, loss)


def per_device(
    parts,
    x_query,
    x_passage,
    len_query,
    len_passage,
    positive,
    cot_query,
    cot_passage,
    *weights,
):
    core = lax.axis_index("section")
    on_first = core == 0
    own_set = [member[0] for member in weights]
    own = [own_set[item] for item in (0, 2, 6, 8)]
    vectors = [weights[item] for item in (1, 3, 4, 5, 7, 9, 10, 11)]
    features = x_query.shape[2]
    half_q, half_p = x_query.shape[0] // 2, x_passage.shape[0] // 2
    *kept, par, l_qkv, l_o, l_in, l_out, hidden_q, hidden_p, land_a, grad_cls, loss = forward_both(
        parts,
        x_query,
        x_passage.reshape(-1, QLEN, features),
        len_query,
        len_passage,
        positive,
        vectors,
        own,
    )
    other = (l_qkv, l_o, l_in, l_out)
    if parts != 16:
        last = hidden_p.reshape(x_passage.shape)
        targets = lax.all_gather(positive, "batch", axis=0, tiled=True)
        own_q = hidden_q[:, 0]
        own_p = last[:, 0]
        last_q, last_p = (jnp.where(on_first, swap(item), item) for item in (own_q, own_p))
        cls_query = lax.all_gather(last_q, "batch", axis=0, tiled=True)
        cls_passage = lax.all_gather(last_p, "batch", axis=0, tiled=True)
        score_scale = 2.0 / math.sqrt(features)
        logits = (
            jnp.einsum("qd,pd->qp", cls_query, cls_passage, preferred_element_type=jnp.float32)
            * score_scale
        )
        term_values, grad_logits = contrast(logits, targets)
        loss_value = jnp.mean(term_values)
        mine = lax.axis_index("batch") * 2 + core
        own_logits = lax.dynamic_slice_in_dim(grad_logits, mine * half_q, half_q, 0)
        grad_cls_q = (
            jnp.einsum("qp,pd->qd", own_logits, cls_passage, preferred_element_type=jnp.float32)
            * score_scale
        )
        own_columns = lax.dynamic_slice_in_dim(grad_logits, mine * half_p, half_p, 1)
        grad_cls_p = (
            jnp.einsum("qp,qd->pd", own_columns, cls_query, preferred_element_type=jnp.float32)
            * score_scale
        )
        grad_cls = jnp.concatenate([grad_cls_q, grad_cls_p], 0)
        grad_cls = jnp.pad(grad_cls, ((0, 8 - grad_cls.shape[0]), (0, 0)))

    outs = backward_both(
        parts,
        (cot_query, cot_passage.reshape(-1, QLEN, features)),
        len_query,
        len_passage,
        grad_cls,
        par,
        own,
        other,
        kept + [land_a],
    )
    groups = ((0, 2), (2, 1), (3, 1), (4, 1), (5, 4), (9, 1), (10, 1), (11, 1))
    if parts == 16:
        d_qkv, d_o, d_in, d_out, d_vec, grad_q, grad_p = outs[:7]
        big = (hidden_q, hidden_p, grad_q, grad_p, d_qkv, d_o, d_in, d_out.reshape(-1, features))
        *final, loss = finish(parts, big, d_vec, loss)
        hidden_q, hidden_p, grad_q, grad_p, d_qkv, d_o, d_in, d_out = final[:8]
        small = [item[0] for item in final[8:]]
        loss_value = loss.reshape(())
    else:
        sums, grad_q, grad_p, g_pro, g_att, g_up, g_flo = outs
        left = kept[0]

        def total(pair):
            kept_one = jnp.where(on_first, pair[0], pair[1])
            both = kept_one + swap(jnp.where(on_first, pair[1], pair[0]))
            return lax.psum_scatter(both, "batch", scatter_dimension=0, tiled=True)

        def product(first, second):
            return jnp.einsum("rd,re->de", first, second, preferred_element_type=jnp.float32)

        d_qkv, d_o, d_in = (
            total([product(left[layer, spot], right[layer]) for layer in (0, 1)])
            for spot, right in ((6, g_pro), (5, g_att), (4, g_up))
        )
        d_out = total(
            [
                jnp.concatenate([product(left[layer, spot], g_flo[layer]) for spot in range(4)], 0)
                for layer in (0, 1)
            ]
        )
        small = [
            total([sums[layer, at : at + count].reshape(-1) for layer in (0, 1)])
            for at, count in groups
        ]
    hidden_q, hidden_p = hidden_q[None], hidden_p.reshape(x_passage.shape)[None]
    grad_q = grad_q[None]
    grad_p = grad_p.reshape(x_passage.shape)[None]
    d_b_qv, d_b_o, d_g_attn, d_c_attn, d_b_in, d_b_out, d_g_ffn, d_c_ffn = small
    outs = (
        d_qkv, d_b_qv, d_o, d_b_o, d_g_attn, d_c_attn, d_in, d_b_in, d_out, d_b_out, d_g_ffn,
        d_c_ffn,
    )
    return (hidden_q, hidden_p, grad_q, grad_p, loss_value) + tuple(item[None] for item in outs)


def solution(mesh):
    in_specs = (
        P("batch", None, None),
        P("batch", None, None),
        P("batch"),
        P("batch"),
        P("batch"),
        P("batch", None, None),
        P("batch", None, None),
        P("section", None, None),
        P("section", None),
        P("section", None, None),
        P("section", None),
        P("section", None),
        P("section", None),
        P("section", None, None),
        P("section", None),
        P("section", None, None),
        P("section", None),
        P("section", None),
        P("section", None),
    )
    out_specs = (
        P("section", "batch", None, None),
        P("section", "batch", None, None),
        P("section", "batch", None, None),
        P("section", "batch", None, None),
        P(),
        P("section", "batch", None),
        P("section", "batch"),
        P("section", "batch", None),
        P("section", "batch"),
        P("section", "batch"),
        P("section", "batch"),
        P("section", "batch", None),
        P("section", "batch"),
        P("section", "batch", None),
        P("section", "batch"),
        P("section", "batch"),
        P("section", "batch"),
    )
    return jax.shard_map(
        functools.partial(per_device, mesh.shape["batch"]), mesh=mesh, in_specs=in_specs, out_specs=out_specs, check_vma=False
    )
```

```python
import functools
import math

import jax
import jax.numpy as jnp
from jax import lax
from jax.experimental import pallas as pl
from jax.experimental.pallas import tpu as pltpu
from jax.sharding import PartitionSpec as P

HEADS = 12
QLEN = 32
PLEN = 256


norm_eps = 1e-05


def contrast(logits, targets):
    top_score = jnp.max(logits, -1, keepdims=True)
    log_total = top_score[:, 0] + jnp.log(jnp.sum(jnp.exp(logits - top_score), -1))
    chosen = targets[:, None] == jnp.arange(logits.shape[1])[None, :]
    term_values = log_total - jnp.sum(jnp.where(chosen, logits, 0.0), -1)
    grad_logits = (jnp.exp(logits - log_total[:, None]) - chosen.astype(jnp.float32)).astype(
        jnp.bfloat16
    )
    return (term_values, grad_logits)


MESH = pl.DeviceIdType.MESH
CHUNK = 384
COUNT = 12
BLOCK = 48


def swap(value):
    return lax.ppermute(value, "section", [(0, 1), (1, 0)])


LOW = jnp.bfloat16
FULL = jnp.float32
ROWS = 32
TILE = 768
LAST = (((1,), (1,)), ((), ()))
FIRST = (((0,), (0,)), ((), ()))


def dot(left, right):
    return jnp.dot(left, right, preferred_element_type=FULL)


def dot_last(left, right):
    return lax.dot_general(left, right, LAST, preferred_element_type=FULL)


def dot_first(left, right):
    return lax.dot_general(left, right, FIRST, preferred_element_type=FULL)


UNROLL = 4
PAIRS = 3


def over(count, body, unroll=1):
    def step(index, carry):
        body(index)
        return carry

    lax.fori_loop(0, count, step, 0, unroll=unroll)


def row_range(index):
    return pl.ds(pl.multiple_of(index * ROWS, ROWS), ROWS)


def lane_range(index, width):
    return pl.ds(pl.multiple_of(index * width, 128), width)


def moments(block):
    centred = block - jnp.mean(block, -1, keepdims=True)
    spread = jnp.mean(centred * centred, -1, keepdims=True)
    inverse = lax.rsqrt(spread + norm_eps)
    return centred * inverse, inverse


def gelu_pair(block):
    size = jnp.abs(block)
    t = 1.0 / (1.0 + (0.3275911 * math.sqrt(0.5)) * size)
    bell = jnp.exp(-0.5 * block * block)
    poly = 0.5 * 1.061405429
    for term in (-1.453152027, 1.421413741, -0.284496736, 0.254829592):
        poly = poly * t + 0.5 * term
    tail = poly * t * bell
    phi = jnp.where(block > 0, 1.0 - tail, tail)
    return block * phi, phi + block * bell * (1.0 / math.sqrt(2.0 * math.pi))


def head_lanes(rows, head):
    lane = lax.broadcasted_iota(jnp.int32, (rows, 128), 1)
    return (lane < 64) if head == 0 else (lane >= 64)


def query_mask(lens, start, count):
    rows = count * QLEN
    row = lax.broadcasted_iota(jnp.int32, (rows, rows), 0)
    column = lax.broadcasted_iota(jnp.int32, (rows, rows), 1)
    limit = jnp.zeros((rows, rows), jnp.int32)
    for item in range(count):
        limit = jnp.where(column // QLEN == item, item * QLEN + lens[start + item], limit)
    return (row // QLEN == column // QLEN) & (row < limit)


VMEM_LIMIT = 58 * 1024 * 1024


def remote(src, dst, send, recv, where):
    return pltpu.make_async_remote_copy(
        src_ref=src, dst_ref=dst, send_sem=send, recv_sem=recv,
        device_id=where, device_id_type=MESH,
    )


def greet(targets):
    barrier = pltpu.get_barrier_semaphore()
    for where in targets:
        pl.semaphore_signal(barrier, inc=1, device_id=where, device_id_type=MESH)
    pl.semaphore_wait(barrier, len(targets))


def forward_kernel(
    parts, x_query, x_passage, qlens, plens, positive,
    b_qv, b_o, g_attn, c_attn, b_in, b_out, g_ffn, c_ffn, wqkv, wo, win, wout,
    o_left, o_qkv, o_pq, o_pp, o_pre, o_slope, o_ffn, both_par,
    l_qkv, l_o, l_in, l_out, hid_q, hid_p, land_a, gcls, loss,
    tok, out, bqkv, bo, bin_, bout, qkv, pq, pp, mixed, pre, normed_full, normed, up, act,
    slope, ffn, rows8, rows48, packed, every, stack,
    load, save, xload, parsend, parrecv, wsend, wrecv, hsend, hrecv, hlocal, gsend, grecv, psend, precv, asend, arecv, bsend, brecv,
):
    core = lax.axis_index("section")
    me = lax.axis_index("batch")
    peer = {"section": 1 - core}
    features = wo.shape[0]
    count_q, count_p = x_query.shape[0] // 2, x_passage.shape[0] // 2
    split = count_q * QLEN
    tall = count_p
    total = (count_q + count_p) * QLEN
    own = (wqkv, wo, win, wout)
    land = (l_qkv, l_o, l_in, l_out)
    buffers = (bqkv, bo, bin_, bout)

    gets = [
        pltpu.make_async_copy(
            x_query.at[pl.ds(core * count_q, count_q)], tok.at[0, pl.ds(0, count_q)], xload.at[0]
        ),
        pltpu.make_async_copy(
            x_passage.at[pl.ds(core * tall, tall)], tok.at[0, pl.ds(count_q, tall)], xload.at[1]
        ),
    ]
    for copy in gets:
        copy.start()

    def local(source, spot):
        return pltpu.make_async_copy(source[spot], buffers[spot], load.at[spot])

    def stash(spot):
        return pltpu.make_async_copy(buffers[spot], land[spot], load.at[4 + spot])

    def give_first(spot):
        return remote(own[spot], buffers[spot], wsend.at[spot], wrecv.at[spot], peer)

    def give_block(spot, block):
        part = pl.ds(block * features, features)
        cut = (slice(None), part) if spot == 2 else (part,)
        return remote(
            own[spot].at[cut], buffers[spot].at[cut],
            bsend.at[spot - 2, block], brecv.at[spot - 2, block], peer,
        )

    def weight_block(spot, block):
        @pl.when(core == 1)
        def _():
            give_block(spot, block).wait_recv()
            if block == 3:
                stash(spot).start()

    def give_second(spot):
        return remote(own[spot], land[spot], wsend.at[spot], wrecv.at[spot], peer)

    others = [peer]
    if parts == 16:
        for step in range(1, parts):
            others.append({"batch": (me + step) % parts})

    @pl.when(core == 0)
    def _():
        for spot in range(4):
            local(own, spot).start()

    vectors = (b_qv, b_o, g_attn, c_attn, b_in, b_out, g_ffn, c_ffn)
    spot = 0
    for ref in vectors:
        for item in range(ref.shape[1] // features):
            both_par[core, spot : spot + 1] = ref[:, item * features : (item + 1) * features]
            spot += 1
    both_par[core, spot:16] = jnp.zeros((16 - spot, features), FULL)
    greet(others)
    give_par = remote(both_par.at[core], both_par.at[core], parsend, parrecv, peer)
    give_par.start()

    @pl.when(core == 0)
    def _():
        for spot in range(2):
            give_first(spot).start()
        for spot in (2, 3):
            for block in range(4):
                give_block(spot, block).start()

    @pl.when(core == 1)
    def _():
        for spot in range(4):
            give_second(spot).start()

    def weight_first(spot):
        @pl.when(core == 0)
        def _():
            local(own, spot).wait()

        @pl.when(core == 1)
        def _():
            if spot < 2:
                give_first(spot).wait_recv()
                stash(spot).start()

        if spot >= 2:
            weight_block(spot, 0)

    def fetch_second(spot):
        @pl.when(core == 0)
        def _():
            give_second(spot).wait_recv()
            local(land, spot).start()

        @pl.when(core == 1)
        def _():
            stash(spot).wait()
            local(own, spot).start()

    def weight(layer, spot):
        if layer == 0:
            weight_first(spot)
        else:
            local(own, spot).wait()

    saves = {}

    def keep(name, layer, source, target):
        saves[name, layer] = pltpu.make_async_copy(
            source, target, save.at[len(saves)]
        )
        saves[name, layer].start()

    places = {"act0": 0, "act1": 1, "act2": 2, "act3": 3, "normed": 4, "mixed": 5, "tok": 6}

    def left_give(layer, spot, source):
        return remote(
            source, land_a.at[layer, spot], asend.at[layer, spot], arecv.at[layer, spot], peer
        )

    def keep_left(name, layer, source):
        keep(name, layer, source, o_left.at[layer, places[name]])
        if layer == 1:
            left_give(1, places[name], source).start()

    def free(name, layer):
        if layer == 1:
            saves[name, 0].wait()

    for copy in gets:
        copy.wait()

    remote(both_par.at[core], both_par.at[1 - core], parsend, parrecv, peer).wait_recv()
    blocks = [(0, split, query_mask(qlens, core * count_q, count_q), pq, 0)]
    for item in range(count_p * QLEN // PLEN):
        row = lax.broadcasted_iota(jnp.int32, (PLEN, PLEN), 0)
        limit = plens[core * (count_p * QLEN // PLEN) + item]
        blocks.append((split + item * PLEN, PLEN, row < limit, pp, item * HEADS))

    for layer in (0, 1):
        base_row = 0
        par = both_par.at[layer]
        x = tok.at[layer].reshape(total, features)
        keep_left("tok", layer, x)
        weight(layer, 0)
        free("qkv", layer)

        def project(tile):
            lanes = lane_range(tile, features)
            bias = jnp.where(tile == 0, par[base_row : base_row + 1], 0.0)
            bias = jnp.where(tile == 2, par[base_row + 1 : base_row + 2], bias)
            qkv[:, lanes] = (dot(x[...], bqkv[:, lanes]) + bias).astype(LOW)

        over(3, project)
        keep("qkv", layer, qkv, o_qkv.at[layer])
        if layer == 1:
            fetch_second(3)
            for name, spot in places.items():
                saves[name, 0].wait()
                left_give(0, spot, o_left.at[0, spot]).start()
        for name in ("pq", "pp"):
            free(name, layer)

        def attend(index):
            tasks = []
            for step in range(PAIRS):
                for lo, rows, mask, probs, base in blocks:
                    tasks.append((index * PAIRS + step, lo, rows, mask, probs, base))

            def part(task, offset):
                hp, lo, rows = task[:3]
                return qkv[pl.ds(lo, rows), pl.ds(pl.multiple_of(offset + hp * 128, 128), 128)]

            scores = []
            for task in tasks:
                queries, keys = part(task, 0) * LOW(0.125), part(task, features)
                for head in (0, 1):
                    masked = jnp.where(head_lanes(task[2], head), keys, LOW(0))
                    scores.append(dot_last(masked, queries))
            lows = []
            for spot, value in enumerate(scores):
                hp, lo, rows, mask, probs, base = tasks[spot // 2]
                value = jnp.where(mask, value, -1000000000.0)
                weights = jnp.exp(value - jnp.max(value, 0, keepdims=True))
                inverse = 1.0 / jnp.sum(weights, 0, keepdims=True)
                low = (weights * inverse).astype(LOW)
                probs[base + 2 * hp + spot % 2] = low
                lows.append(low)
            for spot, task in enumerate(tasks):
                hp, lo, rows = task[:3]
                values = part(task, 2 * features).T
                outs = [
                    dot(values[64 * head : 64 * head + 64], lows[2 * spot + head])
                    for head in (0, 1)
                ]
                both = jnp.concatenate(outs, 0).astype(LOW).T
                mixed[pl.ds(lo, rows), pl.ds(pl.multiple_of(hp * 128, 128), 128)] = both

        over(features // 128 // PAIRS, attend)
        keep("pq", layer, pq, o_pq.at[layer])
        keep("pp", layer, pp, o_pp.at[layer])
        keep_left("mixed", layer, mixed)
        weight(layer, 1)
        free("pre", layer)
        pre[...] = (
            dot(mixed[...], bo[...]) + x[...].astype(FULL) + par[base_row + 2 : base_row + 3]
        )
        keep("pre", layer, pre, o_pre.at[layer])
        if layer == 0:
            fetch_second(0)
            fetch_second(1)

        def norm_one(index):
            rows = row_range(index)
            block = moments(pre[rows])[0] * par[base_row + 3 : base_row + 4]
            block = block + par[base_row + 4 : base_row + 5]
            normed_full[rows] = block
            normed[rows] = block.astype(LOW)

        over(total // ROWS, norm_one, 12)
        keep_left("normed", layer, normed)
        weight(layer, 2)
        free("slope", layer)
        step_width = 256
        tiles = win.shape[1] // step_width

        def expand(tile):
            lanes = lane_range(tile, step_width)
            bias_lanes = lane_range(tile % 3, step_width)
            up[tile % 2] = (
                dot(normed[...], bin_[:, lanes])
                + par[pl.ds(base_row + 5 + tile // 3, 1), bias_lanes]
            )

        def bend(tile):
            lanes = lane_range(tile, step_width)
            for index in range(total // ROWS):
                rows = pl.ds(index * ROWS, ROWS)
                value, steep = gelu_pair(up[tile % 2, rows])
                act[rows, lanes] = value.astype(LOW)
                slope[rows, lanes] = steep.astype(LOW)

        expand(0)

        def grow(index):
            if layer == 0 and (index + 1) % 3 == 0:
                weight_block(2, (index + 1) // 3)
            expand(index + 1)
            bend(index)

        for index in range(tiles - 1):
            grow(index)
        bend(tiles - 1)
        for item in range(4):
            lanes = pl.ds(item * features, features)
            keep_left("act%d" % item, layer, act.at[:, lanes])
        keep("slope", layer, slope, o_slope.at[layer])
        weight(layer, 3)
        free("ffn", layer)
        ends = normed_full[...] + par[base_row + 9 : base_row + 10]
        if layer == 0:
            most = 3 * features
            for block in (1, 2):
                weight_block(3, block)
            ffn[...] = dot(act[:, :most], bout[:most]) + ends
            weight_block(3, 3)
            ffn[...] += dot(act[:, most:], bout[most:])
        else:
            ffn[...] = dot(act[...], bout[...]) + ends
        keep("ffn", layer, ffn, o_ffn.at[layer])
        if layer == 0:
            fetch_second(2)
        target = tok.at[1] if layer == 0 else out
        flat = target.reshape(total, features)

        def norm_two(index):
            rows = row_range(index)
            block = moments(ffn[rows])[0] * par[base_row + 10 : base_row + 11]
            flat[rows] = (block + par[base_row + 11 : base_row + 12]).astype(LOW)

        over(total // ROWS, norm_two, 12)
        sides = (
            (target.at[pl.ds(0, count_q)], hid_q.at[pl.ds(core * count_q, count_q)]),
            (target.at[pl.ds(count_q, tall)], hid_p.at[pl.ds(core * tall, tall)]),
        )

        @pl.when(core == layer)
        def _():
            for spot, (src, dst) in enumerate(sides):
                pltpu.make_async_copy(src, dst, hlocal.at[spot]).start()

        @pl.when(core != layer)
        def _():
            for spot, (src, dst) in enumerate(sides):
                remote(src, dst, hsend.at[spot], hrecv.at[spot], peer).start()

    if parts == 16:
        lead = [item * QLEN for item in range(count_q)] + [split]
        rows8[...] = jnp.zeros_like(rows8)
        for spot, row in enumerate(lead):
            rows8[spot : spot + 1] = flat[pl.ds(row, 16)].astype(FULL)[0:1]
        for tile in range(6):
            rows48[8 * tile : 8 * tile + 8] = rows8[:, 128 * tile : 128 * tile + 128]
        for item in range(count_q):
            value = positive[core * count_q + item].astype(FULL)
            rows48[8 * item + 5 : 8 * item + 6] = jnp.full((1, 128), value)
        packed[...] = rows48[...].astype(LOW)

        def share(step, slot):
            return remote(
                packed, every.at[core, slot], gsend.at[step], grecv.at[slot],
                {"batch": (me + step) % parts},
            )

        for step in range(1, parts):
            share(step, me).start()
        every[core, me] = packed[...]
        for step in range(1, parts):
            share(step, (me + parts - step) % parts).wait_recv()
        pass_on = remote(every.at[core], every.at[core], psend, precv, peer)
        pass_on.start()
        remote(every.at[core], every.at[1 - core], psend, precv, peer).wait_recv()
        pass_on.wait_send()
        for step in range(1, parts):
            share(step, me).wait_send()

        wide = 2 * parts * 8
        grid = every[...].astype(FULL).reshape(2 * parts, 48, 128)
        inner = lax.broadcasted_iota(jnp.int32, (2 * parts, 8, 128), 1)
        goal = jnp.zeros((2 * parts, 8, 128), FULL)
        for tile in range(6):
            block = grid[:, 8 * tile : 8 * tile + 8]
            stack[:, 128 * tile : 128 * tile + 128] = block.reshape(wide, 128).astype(LOW)
            if tile < count_q:
                found = jnp.sum(jnp.where(inner == 5, block, 0.0), 1, keepdims=True)
                goal = jnp.where(inner == tile, found, goal)
        row = lax.broadcasted_iota(jnp.int32, (wide, wide), 0)
        column = lax.broadcasted_iota(jnp.int32, (wide, wide), 1)
        scale = 2.0 / math.sqrt(features)
        logits = dot_last(stack[...], stack[...]) * scale
        device = column // 8
        passage = (device % parts) * 2 + device // parts
        is_passage = column % 8 == count_q
        is_query = row % 8 < count_q
        kept = jnp.where(is_passage, logits, -1e30)
        top = jnp.max(kept, -1, keepdims=True)
        log_total = top + jnp.log(jnp.sum(jnp.exp(kept - top), -1, keepdims=True))
        chosen = is_passage & (passage.astype(FULL) == goal.reshape(wide, 128)[:, 0:1])
        picked = jnp.sum(jnp.where(chosen, logits, 0.0), -1, keepdims=True)
        terms = jnp.where(is_query[:, 0:1], log_total - picked, 0.0)
        count = count_q * 2 * parts
        loss[...] = jnp.full((8, 128), jnp.sum(terms) / count)
        grads = jnp.exp(kept - log_total) - chosen.astype(FULL)
        grads = jnp.where(is_query & is_passage, grads, 0.0)
        up[0, 0:wide, 0:wide] = grads + grads.T
        mine = pl.multiple_of((core * parts + me) * 8, 8)
        picked_rows = up[0, pl.ds(mine, 8), 0:wide]
        gcls[...] = dot(picked_rows.astype(LOW), stack[...]) * scale

    for spot, (src, dst) in enumerate(sides):
        pltpu.make_async_copy(src, dst, hlocal.at[spot]).wait()
    theirs = (
        hid_q.at[pl.ds((1 - core) * count_q, count_q)],
        hid_p.at[pl.ds((1 - core) * tall, tall)],
    )
    for spot, (src, dst) in enumerate(zip((item[0] for item in sides), theirs)):
        remote(src, dst, hsend.at[spot], hrecv.at[spot], peer).wait()
    @pl.when(core == 0)
    def _():
        for spot in range(2):
            give_first(spot).wait_send()
        for spot in (2, 3):
            for block in range(4):
                give_block(spot, block).wait_send()

    @pl.when(core == 1)
    def _():
        for spot in range(4):
            give_second(spot).wait_send()

    give_par.wait_send()
    for (name, layer), copy in saves.items():
        if layer == 1:
            copy.wait()
    for layer in (0, 1):
        for spot in range(7):
            left_give(layer, spot, o_left.at[layer, spot]).wait()


def forward_both(parts, x_query, x_passage, qlens, plens, positive, vectors, own):
    queries, features = x_query.shape[0], x_query.shape[2]
    passages = x_passage.shape[0]
    total = (queries + passages) // 2 * QLEN
    wide = own[2].shape[1]
    split = queries // 2 * QLEN
    heads_p = HEADS * (passages // 2 * QLEN // PLEN)
    kept = [
        ((7, total, features), LOW),
        ((total, 3 * features), LOW),
        ((HEADS, split, split), LOW),
        ((heads_p, PLEN, PLEN), LOW),
        ((total, features), FULL),
        ((total, wide), LOW),
        ((total, features), FULL),
        ((16, features), FULL),
    ]
    shape = jax.ShapeDtypeStruct
    anywhere = pl.BlockSpec(memory_space=pl.ANY)
    vmem = pl.BlockSpec(memory_space=pltpu.VMEM)
    smem = pl.BlockSpec(memory_space=pltpu.SMEM)
    dma = pltpu.SemaphoreType.DMA
    scratch = [
        pltpu.VMEM((2, total // QLEN, QLEN, features), LOW),
        pltpu.VMEM((total // QLEN, QLEN, features), LOW),
    ]
    scratch += [pltpu.VMEM(item.shape, item.dtype) for item in own]
    scratch += [pltpu.VMEM(size, kind) for size, kind in kept[1:4]]
    scratch += [
        pltpu.VMEM((total, features), LOW),
        pltpu.VMEM((total, features), FULL),
        pltpu.VMEM((total, features), FULL),
        pltpu.VMEM((total, features), LOW),
        pltpu.VMEM((2, total, 256), FULL),
        pltpu.VMEM((total, wide), LOW),
        pltpu.VMEM((total, wide), LOW),
        pltpu.VMEM((total, features), FULL),
    ]
    scratch += [
        pltpu.VMEM((8, features), FULL),
        pltpu.VMEM((48, 128), FULL),
        pltpu.VMEM((48, 128), LOW),
        pltpu.VMEM((2, 16, 48, 128), LOW),
        pltpu.VMEM((256, features), LOW),
        dma((8,)),
        dma((26,)),
        dma((2,)),
        dma,
        dma,
        dma((4,)),
        dma((4,)),
        dma((2,)),
        dma((2,)),
        dma((2,)),
        dma((16,)),
        dma((16,)),
        dma,
        dma,
        dma((2, 7)),
        dma((2, 7)),
        dma((2, 4)),
        dma((2, 4)),
    ]
    return pl.pallas_call(
        functools.partial(forward_kernel, parts),
        out_shape=[shape((2,) + size, kind) for size, kind in kept]
        + [shape(item.shape, item.dtype) for item in own]
        + [
            shape(x_query.shape, LOW),
            shape(x_passage.shape, LOW),
            shape((2, 7, total, features), LOW),
            shape((8, features), FULL),
            shape((8, 128), FULL),
        ],
        in_specs=[anywhere, anywhere, smem, smem, smem] + [vmem] * 8 + [anywhere] * 4,
        out_specs=[anywhere] * 7 + [vmem] + [anywhere] * 7 + [vmem] * 2,
        scratch_shapes=scratch,
        compiler_params=pltpu.CompilerParams(
            collective_id=2, has_side_effects=True, vmem_limit_bytes=VMEM_LIMIT
        ),
    )(x_query, x_passage, qlens, plens, positive, *vectors, *own)


def add_rows(block):
    return jnp.sum(block.reshape(block.shape[0] // 8, 8, block.shape[1]), 0)


def norm_back(source, grad_of, gain, total, store):
    features = source.shape[1]
    zero = jnp.zeros((8, features), FULL)

    def step(index, carry):
        rows = row_range(index)
        grad = grad_of(index)
        unit, inverse = moments(source[rows])
        scaled = grad * gain
        back = inverse * (
            scaled
            - jnp.mean(scaled, -1, keepdims=True)
            - unit * jnp.mean(scaled * unit, -1, keepdims=True)
        )
        store(rows, back)
        return (
            carry[0] + add_rows(grad * unit),
            carry[1] + add_rows(grad),
            carry[2] + add_rows(back),
        )

    sums = lax.fori_loop(0, total // ROWS, step, (zero, zero, zero), unroll=UNROLL)
    return [jnp.sum(item, 0, keepdims=True) for item in sums]


LAGS = (2, 4, 6)
RING = 12
HELD = 8


def left_index(ch):
    return (
        jnp.minimum(ch, 4) + (ch >= 8).astype(jnp.int32) + (ch >= 9).astype(jnp.int32)
    )


def right_index(ch):
    return jnp.maximum(ch - 3, 0)


def backward_kernel(parts, *refs):
    small = parts == 16
    refs = list(refs)

    def take(count):
        front = refs[:count]
        del refs[:count]
        return front

    cot_query, cot_passage, qlens, plens, gcls, par = take(6)
    own, land = take(4), take(4)
    left, h_qkv, h_pq, h_pp, h_pre, h_slope, h_ffn, land_a = take(8)
    if small:
        o_qkv, o_o, o_in, o_out, o_vec, o_gq, o_gp, land_g, own_g = take(9)
    else:
        vpar, o_gq, o_gp, f_pro, f_att, f_up, f_flo = take(7)
    buffers = take(4)
    bqkv, bo, bin_, bout = buffers
    qkv, pq, pp, source, slope, gsrc = take(6)
    attn_full, attn, steep, flow_full, flow = take(5)
    gmixed = flow
    grow = flow_full.reshape(flow.shape[0] // QLEN, QLEN, flow.shape[1])
    wload, fetch, cload, hsend, hrecv, hlocal, ksem = take(7)
    if small:
        vpar, a_buf, g_buf, stage, s1, r1, s2, r2, s3, r3, hold = take(11)
        va, ra, vb, rb, vc, rc, rz = take(7)
        s1s, r1s, s2s, r2s, s3s, r3s, vsend, vrecv, zsend, zrecv = take(10)
        gs, gr, sl, gl, el = take(5)

    core = lax.axis_index("section")
    me = lax.axis_index("batch")
    peer = {"section": 1 - core}
    features = gcls.shape[1]
    total = flow.shape[0]
    split = pq.shape[1]
    count_q, tall = cot_query.shape[0] // 2, cot_passage.shape[0] // 2
    heads_p = pp.shape[0]
    blocks_p = PLEN // QLEN

    def weight_copy(spot, source_set):
        return pltpu.make_async_copy(source_set[spot], buffers[spot], wload.at[spot])

    def weight_start(layer, spot):
        @pl.when(core == layer)
        def _():
            weight_copy(spot, own).start()

        @pl.when(core != layer)
        def _():
            weight_copy(spot, land).start()

    def weight_wait(spot):
        weight_copy(spot, own).wait()

    saved = ((h_ffn, source), (h_slope, slope), (h_pre, source), (h_qkv, qkv), (h_pq, pq), (h_pp, pp))

    def saved_copy(layer, spot):
        src, dst = saved[spot]
        return pltpu.make_async_copy(src.at[layer], dst, fetch.at[spot])

    cots = [
        pltpu.make_async_copy(
            cot_query.at[pl.ds(core * count_q, count_q)], gsrc.at[pl.ds(0, count_q)], cload.at[0]
        ),
        pltpu.make_async_copy(
            cot_passage.at[pl.ds(core * tall, tall)], gsrc.at[pl.ds(count_q, tall)], cload.at[1]
        ),
    ]
    def early_copy(spot, side):
        src = (left, land_a)[side]
        if spot < 2:
            dst, sem = stage.at[spot, side], sl.at[spot, side]
        else:
            lanes = pl.ds((spot - 2) * features, features)
            dst, sem = bin_.at[pl.ds(side * total, total), lanes], el.at[spot - 2, side]
        return pltpu.make_async_copy(src.at[1, spot], dst, sem)

    if small:
        x, y, z = me % 2, (me // 2) % 2, me // 4
        px, py = me + 1 - 2 * x, me + 2 - 4 * y
        targets = [{"batch": px}, {"batch": py}, peer]
        for step in (1, 2, 3):
            other = ((z + step) % 4) * 4 + me % 4
            targets += [{"section": sec, "batch": other} for sec in (0, 1)]
        barrier = pltpu.get_barrier_semaphore()
        for where in targets:
            pl.semaphore_signal(barrier, inc=1, device_id=where, device_id_type=MESH)
        for spot in range(4):
            for side in (0, 1):
                early_copy(spot, side).start()
    saved_copy(1, 0).start()
    for copy in cots:
        copy.start()
    weight_start(1, 3)
    saved_copy(1, 1).start()

    widths = ((flow, 1), (slope, 4), (attn, 1), (qkv, 3))

    def pieces_of(slot):
        base = (0, 1, 5, 6)[slot]
        ref, count = widths[slot]
        return [(base + item, ref, ref.shape[1] // 2, item) for item in range(count)]

    def own_piece(layer, piece):
        spot, ref, width, item = piece
        lanes = pl.ds(pl.multiple_of(core * width + item * CHUNK, 128), CHUNK)
        return pltpu.make_async_copy(ref.at[:, lanes], own_g.at[layer, spot], ksem.at[spot])

    def peer_piece(layer, piece):
        spot, ref, width, item = piece
        lanes = pl.ds(pl.multiple_of((1 - core) * width + item * CHUNK, 128), CHUNK)
        return remote(
            ref.at[:, lanes], land_g.at[layer, spot], gs.at[layer, spot], gr.at[layer, spot], peer
        )

    def whole_piece(layer, slot):
        ref = widths[slot][0]
        target = (f_flo, f_up, f_att, f_pro)[slot]
        return pltpu.make_async_copy(ref, target.at[layer], ksem.at[slot])

    def direct():
        spot, ref, width, item = pieces_of(0)[0]
        lanes = pl.ds(pl.multiple_of((1 - core) * width, 128), CHUNK)
        return remote(
            ref.at[:, lanes], g_buf.at[0, pl.ds(total, total)], gs.at[1, 0], gr.at[1, 0], peer
        )

    def give(layer, slot):
        if small and slot == 0:

            @pl.when(layer == 1)
            def _():
                direct().start()
                lanes = pl.ds(pl.multiple_of(core * CHUNK, 128), CHUNK)
                g_buf[0, pl.ds(0, total)] = flow[:, lanes]

            @pl.when(layer == 0)
            def _():
                piece = pieces_of(0)[0]
                peer_piece(layer, piece).start()
                own_piece(layer, piece).start()

        elif small:
            for piece in pieces_of(slot):
                peer_piece(layer, piece).start()
                own_piece(layer, piece).start()
        else:
            whole_piece(layer, slot).start()

    def given(layer, slot):
        if small:
            for piece in pieces_of(slot):
                peer_piece(layer, piece).wait_send()
                if slot > 0:
                    own_piece(layer, piece).wait()
                else:

                    @pl.when(layer == 0)
                    def _():
                        own_piece(layer, piece).wait()
        else:
            whole_piece(layer, slot).wait()

    def slot_zero(layer):
        saved_copy(layer, 0).wait()
        gains = par.at[layer]
        last = layer == 1

        def grad_of(index):
            block = gsrc[index].astype(FULL)
            beyond = jnp.maximum(index - count_q, 0)
            item = beyond // blocks_p
            query_limit = qlens[core * count_q + jnp.minimum(index, count_q - 1)]
            passage_limit = (
                plens[core * (tall // blocks_p) + item] - (beyond % blocks_p) * QLEN
            )
            limit = jnp.where(index < count_q, query_limit, passage_limit)
            limit = jnp.where(last, limit, QLEN)
            lead = jnp.where(index < count_q, index, count_q + item)
            starts = (index < count_q) | (beyond % blocks_p == 0)
            row = lax.broadcasted_iota(jnp.int32, block.shape, 0)
            block = jnp.where(row < limit, block, 0.0)
            extra = gcls[pl.ds(lead, 1)] * jnp.where(starts & last, 1.0, 0.0)
            return block + jnp.where(row == 0, extra, 0.0)

        def store(rows, back):
            flow_full[rows] = back
            flow[rows] = back.astype(LOW)

        gain, shift, bias = norm_back(source, grad_of, gains[10:11], total, store)
        sums = vpar.at[layer]
        sums[10:11], sums[11:12], sums[9:10] = gain, shift, bias
        give(layer, 0)
        saved_copy(layer, 2).start()

    width = 256
    tiles = bout.shape[0] // width

    def slot_one(layer):
        saved_copy(layer, 1).wait()
        weight_wait(3)
        sums = vpar.at[layer]

        def shrink(tile):
            rows_of = pl.ds(pl.multiple_of(tile * width, width), width)
            steep[tile % 2] = dot_last(flow[...], bout[rows_of])

        def bend(tile):
            lanes = lane_range(tile, width)
            acc = jnp.zeros((8, width), FULL)
            for index in range(total // ROWS):
                rows = pl.ds(index * ROWS, ROWS)
                low = (steep[tile % 2, rows] * slope[rows, lanes].astype(FULL)).astype(LOW)
                slope[rows, lanes] = low
                acc = acc + add_rows(low.astype(FULL))
            sums[pl.ds(5 + tile // 3, 1), lane_range(tile % 3, width)] = jnp.sum(
                acc, 0, keepdims=True
            )

        shrink(0)

        def both(index):
            shrink(index + 1)
            bend(index)

        over(tiles - 1, both)
        bend(tiles - 1)
        give(layer, 1)

        @pl.when(layer == 1)
        def _():
            weight_start(0, 3)

    def slot_two(layer):
        weight_wait(2)
        flow_full[...] += dot_last(slope[...], bin_[...])
        saved_copy(layer, 2).wait()
        gains, sums = par.at[layer], vpar.at[layer]

        def store(rows, back):
            attn_full[rows] = back
            attn[rows] = back.astype(LOW)

        gain, shift, bias = norm_back(
            source, lambda index: flow_full[row_range(index)], gains[3:4], total, store
        )
        sums[3:4], sums[4:5], sums[2:3] = gain, shift, bias
        give(layer, 2)
        weight_wait(1)
        gmixed[...] = dot_last(attn[...], bo[...]).astype(LOW)

        @pl.when(layer == 1)
        def _():
            weight_start(0, 2)
            weight_start(0, 1)
            saved_copy(0, 0).start()
            saved_copy(0, 1).start()

    blocks = [(0, split, pq, 0)]
    for item in range(heads_p // HEADS):
        blocks.append((split + item * PLEN, PLEN, pp, item * HEADS))

    def attend(index):
        tasks = []
        for step in range(PAIRS):
            for block in blocks:
                tasks.append((index * PAIRS + step,) + block)

        def spot_of(task, offset):
            hp, lo, rows = task[:3]
            return (pl.ds(lo, rows), pl.ds(pl.multiple_of(offset + hp * 128, 128), 128))

        grads = []
        for task in tasks:
            values, back = qkv[spot_of(task, 2 * features)], gmixed[spot_of(task, 0)]
            for head in (0, 1):
                masked = jnp.where(head_lanes(task[2], head), values, LOW(0))
                grads.append(dot_last(masked, back))
        lows = []
        for spot, grad_probs in enumerate(grads):
            hp, lo, rows, probs, base = tasks[spot // 2]
            full = probs[base + 2 * hp + spot % 2].astype(FULL)
            inner = jnp.sum(grad_probs * full, 0, keepdims=True)
            lows.append((full * (grad_probs - inner)).astype(LOW))
        for spot, task in enumerate(tasks):
            hp, lo, rows, probs, base = task
            queries, keys = qkv[spot_of(task, 0)], qkv[spot_of(task, features)]
            back = gmixed[spot_of(task, 0)]
            turned = keys.T
            outs = []
            for head in (0, 1):
                grad_scores = lows[2 * spot + head]
                outs.append(
                    (
                        dot(turned[64 * head : 64 * head + 64], grad_scores) * 0.125,
                        dot(grad_scores, queries) * 0.125,
                        dot(probs[base + 2 * hp + head], back),
                    )
                )
            first = head_lanes(rows, 0)
            both = jnp.concatenate([outs[0][0], outs[1][0]], 0)
            qkv[spot_of(task, 0)] = both.astype(LOW).T
            for item in (1, 2):
                both = jnp.where(first, outs[0][item], outs[1][item])
                qkv[spot_of(task, item * features)] = both.astype(LOW)

    def grads_here(spot):
        lo, count, target = ((0, count_q, o_gq), (count_q, tall, o_gp))[spot]
        return pltpu.make_async_copy(
            grow.at[pl.ds(lo, count)], target.at[pl.ds(core * count, count)], hlocal.at[spot]
        )

    def grads_there(spot):
        lo, count, target = ((0, count_q, o_gq), (count_q, tall, o_gp))[spot]
        return remote(
            grow.at[pl.ds(lo, count)],
            target.at[pl.ds(core * count, count)],
            hsend.at[spot],
            hrecv.at[spot],
            peer,
        )

    def slot_three(layer):
        for spot in (3, 4, 5):
            saved_copy(layer, spot).wait()
        over(features // 128 // PAIRS, attend)
        give(layer, 3)
        sums = vpar.at[layer]

        def bias_sums(index, carry):
            rows = row_range(index)
            return (
                carry[0] + add_rows(qkv[rows, pl.ds(0, features)].astype(FULL)),
                carry[1] + add_rows(qkv[rows, pl.ds(2 * features, features)].astype(FULL)),
            )

        zero = jnp.zeros((8, features), FULL)
        found = lax.fori_loop(0, total // ROWS, bias_sums, (zero, zero), unroll=2)
        sums[0:1] = jnp.sum(found[0], 0, keepdims=True)
        sums[1:2] = jnp.sum(found[1], 0, keepdims=True)
        sums[12:16] = jnp.zeros((4, features), FULL)
        weight_wait(0)
        rows_all = attn_full[...] + dot_last(qkv[...], bqkv[...])
        flow_full[...] = rows_all
        gsrc[...] = rows_all.astype(LOW).reshape(gsrc.shape)

        @pl.when(core == layer)
        def _():
            for spot in (0, 1):
                grads_here(spot).start()

        @pl.when(core != layer)
        def _():
            for spot in (0, 1):
                grads_there(spot).start()

        @pl.when(layer == 1)
        def _():
            weight_start(0, 0)

    def grads_given(layer):
        @pl.when(core == layer)
        def _():
            for spot in (0, 1):
                grads_here(spot).wait()

        @pl.when(core != layer)
        def _():
            for spot in (0, 1):
                grads_there(spot).wait_send()

    slots = (slot_zero, slot_one, slot_two, slot_three)

    def reload(layer, slot):
        @pl.when(layer == 1)
        def _():
            if slot == 3:
                for spot in (3, 4, 5):
                    saved_copy(0, spot).start()

    def rest_of_loads():
        for spot in (2, 1, 0):
            weight_start(1, spot)
        for spot in (3, 4, 5):
            saved_copy(1, spot).start()

    def grads_came():
        lands = ((o_gq, count_q), (o_gp, tall))
        for spot, (target, count) in enumerate(lands):
            there = target.at[pl.ds((1 - core) * count, count)]
            remote(there, there, hsend.at[spot], hrecv.at[spot], peer).wait_recv()

    if not small:
        greet([peer])
        rest_of_loads()
        for copy in cots:
            copy.wait()
        for layer in (1, 0):
            for slot in range(4):
                slots[slot](layer)
                given(layer, slot)
                reload(layer, slot)
            grads_given(layer)
        grads_came()
        return

    def stage_copy(number, side):
        layer, spot = 1 - number // 7, number % 7
        src = left if side == 0 else land_a
        return pltpu.make_async_copy(
            src.at[layer, spot], stage.at[number % 2, side], sl.at[number % 2, side]
        )

    def stage_start(number):
        stage_copy(number, 0).start()
        stage_copy(number, 1).start()

    def rotate(spot, view):
        for side in (0, 1):
            lanes = pl.ds(side * total, total)
            for half in range(features // CHUNK):
                block = view(side, half * CHUNK).T
                if spot > 3:
                    a_buf[spot, pl.ds(2 * half, 2), :, :, :, lanes] = block.reshape(
                        2, 2, 2, BLOCK, total
                    )
                else:
                    shaped = block.reshape(2, 4, BLOCK, total)
                    for item in range(4):
                        a_buf[item, spot, half, :, :, lanes] = shaped[:, item]

    def turn(number, spot):
        for side in (0, 1):
            stage_copy(number, side).wait()
        rotate(spot, lambda side, at: stage[number % 2, side, :, pl.ds(at, CHUNK)])

        @pl.when(number + 2 < 14)
        def _():
            stage_start(number + 2)

    for spot in range(4):
        for side in (0, 1):
            early_copy(spot, side).wait()
        if spot < 2:
            rotate(spot, lambda side, at: stage[spot, side, :, pl.ds(at, CHUNK)])
            stage_start(spot + 4)
        else:
            rotate(
                spot,
                lambda side, at: bin_[
                    pl.ds(side * total, total), pl.ds((spot - 2) * features + at, CHUNK)
                ],
            )
    pl.semaphore_wait(barrier, len(targets))

    def right_copy(layer, spot, side):
        src = own_g if side == 0 else land_g
        return pltpu.make_async_copy(
            src.at[layer, spot], g_buf.at[spot, pl.ds(side * total, total)], gl.at[spot, side]
        )

    def right_start(k):
        ch = k % COUNT
        layer = 1 - k // COUNT

        @pl.when((k > 0) & (k < 2 * COUNT) & ((ch == 0) | (ch >= 4)))
        def _():
            spot = right_index(ch)
            right_copy(layer, spot, 0).start()
            remote(
                own_g.at[layer, spot], land_g.at[layer, spot],
                gs.at[layer, spot], gr.at[layer, spot], peer,
            ).wait_recv()
            right_copy(layer, spot, 1).start()

    def first(k, par_):
        return remote(
            s1.at[k % HELD], r1.at[k % RING], s1s.at[k], r1s.at[k],
            {"batch": px if par_ == 0 else py},
        )

    def second(k, par_):
        return remote(
            s2.at[k % 4], r2.at[k % HELD], s2s.at[k], r2s.at[k],
            {"batch": py if par_ == 0 else px},
        )

    def third(k, step):
        layer = 1 - k // COUNT
        zt = (z + step) % 4
        return remote(
            s3.at[k % 4, zt], r3.at[core, k % COUNT, z], s3s.at[k, step],
            r3s.at[core, k % COUNT, z], {"section": layer, "batch": zt * 4 + me % 4},
        )

    def third_in(k, step, src_core):
        zs = (z + 4 - step) % 4
        return remote(
            s3.at[k % 4, zs], r3.at[src_core, k % COUNT, zs], s3s.at[k, step],
            r3s.at[src_core, k % COUNT, zs], peer,
        )

    def product(k, block, rows):
        return dot(block.reshape(rows, 2 * total), g_buf[right_index(k % COUNT)])

    def left_of(k):
        return a_buf.at[left_index(k % COUNT)]

    def ready(k, par_):
        ch = k % COUNT

        @pl.when((k > 0) & ((ch == 0) | (ch >= 4)))
        def _():
            for side in (0, 1):
                right_copy(0, right_index(ch), side).wait()

        base = (k // COUNT) * 7
        if par_ == 0:

            @pl.when(k == 0)
            def _():
                direct().wait_recv()

            @pl.when(k == COUNT)
            def _():
                for spot in range(4):
                    turn(base + spot, spot)

            for spot, at in ((4, 4), (5, 8)):

                @pl.when(ch == at)
                def _():
                    turn(base + spot, spot)
        else:

            @pl.when(ch == 9)
            def _():
                turn(base + 6, 6)

    def part_one(k, par_):
        ready(k, par_)
        ref = left_of(k)
        block = ref[:, :, 1 - x] if par_ == 0 else ref[:, 1 - y]
        s1[k % HELD] = product(k, block, 8 * BLOCK).astype(LOW).reshape(4, 2, BLOCK, CHUNK)
        first(k, par_).start()

    def part_two(k, par_):
        ref = left_of(k)
        block = ref[:, 1 - y, x] if par_ == 0 else ref[:, y, 1 - x]
        hold[...] = product(k, block, 4 * BLOCK).reshape(4, BLOCK, CHUNK)
        first(k, par_).wait()
        came = r1[k % RING, :, 1 - y] if par_ == 0 else r1[k % RING, :, 1 - x]
        s2[k % 4] = (hold[...] + came.astype(FULL)).astype(LOW)
        second(k, par_).start()

    def part_three(k, par_):
        layer = 1 - k // COUNT
        ref = left_of(k)
        came = r1[k % RING, :, y] if par_ == 0 else r1[k % RING, :, x]
        hold[...] = product(k, ref[:, y, x], 4 * BLOCK).reshape(
            4, BLOCK, CHUNK
        ) + came.astype(FULL)
        second(k, par_).wait()
        value = hold[...] + r2[k % HELD].astype(FULL)
        s3[k % 4] = value.astype(LOW)
        for step in (1, 2, 3):
            third(k, step).start()

        @pl.when(core != layer)
        def _():
            third(k, 0).start()

        @pl.when(core == layer)
        def _():
            r3[core, k % COUNT, z] = s3[k % 4, z]

    def part_four(k, par_):
        layer = 1 - k // COUNT
        ch = k % COUNT
        for step in (1, 2, 3):
            third(k, step).wait_send()

        @pl.when(core != layer)
        def _():
            third(k, 0).wait_send()

        @pl.when(core == layer)
        def _():
            for step in (1, 2, 3):
                for src_core in (0, 1):
                    third_in(k, step, src_core).wait_recv()
            third_in(k, 0, 1 - core).wait_recv()
            for src_core in (0, 1):
                value = jnp.sum(r3[src_core, ch].astype(FULL), 0)

                @pl.when(ch < 4)
                def _():
                    o_out[ch, :, pl.ds(src_core * CHUNK, CHUNK)] = value

                @pl.when((ch >= 4) & (ch < 8))
                def _():
                    start = pl.multiple_of((ch - 4) * CHUNK + src_core * 4 * CHUNK, 128)
                    o_in[:, pl.ds(start, CHUNK)] = value

                @pl.when(ch == 8)
                def _():
                    o_o[:, pl.ds(src_core * CHUNK, CHUNK)] = value

                @pl.when(ch >= 9)
                def _():
                    start = pl.multiple_of((ch - 9) * CHUNK + src_core * 3 * CHUNK, 128)
                    o_qkv[:, pl.ds(start, CHUNK)] = value

    vec_cross = remote(vpar.at[1 - core], ra, vsend.at[0], vrecv.at[0], peer)
    vec_x = remote(va, rb, vsend.at[1], vrecv.at[1], {"batch": px})
    vec_y = remote(vb, rc, vsend.at[2], vrecv.at[2], {"batch": py})

    def vec_z(step, slot):
        return remote(
            vc, rz.at[slot], zsend.at[step], zrecv.at[slot],
            {"batch": ((z + step) % 4) * 4 + me % 4},
        )

    steps = 2 * COUNT + LAGS[2]

    starts = ((-1, 3), (0, 4), (1, 5), (2, 6))

    def pair(turn_index, carry):
        kk = turn_index - 1
        layer = (kk < 3).astype(jnp.int32)

        for slot, (one, two) in enumerate(starts):

            @pl.when((kk == one + 1) | (kk == two + 1))
            def _():
                done = (kk == one + 1).astype(jnp.int32)
                given(done, slot)
                reload(done, slot)
                if slot == 3:
                    grads_given(done)

        @pl.when(kk == -1)
        def _():
            rest_of_loads()
            for copy in cots:
                copy.wait()

        for par_ in (0, 1):
            right_start(2 * kk + 2 + par_)

        stages = (part_two, part_three, part_four)

        def advance(item):
            lag, part = LAGS[item], stages[item]
            for par_ in (0, 1):
                k = 2 * kk + par_

                @pl.when((k >= lag) & (k < 2 * COUNT + lag))
                def _():
                    part(k - lag, par_)

        advance(0)
        advance(1)

        @pl.when((kk == starts[0][0]) | (kk == starts[0][1]))
        def _():
            slots[0](layer)

        for par_ in (0, 1):
            k = 2 * kk + 2 + par_

            @pl.when(k < 2 * COUNT)
            def _():
                part_one(k, par_)

        advance(2)

        for slot, (one, two) in enumerate(starts):
            if slot > 0:

                @pl.when((kk == one) | (kk == two))
                def _():
                    slots[slot](layer)

        @pl.when(kk == 7)
        def _():
            vec_cross.start()

        @pl.when(kk == 8)
        def _():
            vec_cross.wait()
            va[...] = vpar[core] + ra[...]
            vec_x.start()

        @pl.when(kk == 9)
        def _():
            vec_x.wait()
            vb[...] = va[...] + rb[...]
            vec_y.start()

        @pl.when(kk == 10)
        def _():
            vec_y.wait()
            vc[...] = vb[...] + rc[...]
            for step in (1, 2, 3):
                vec_z(step, z).start()

        @pl.when(kk == 12)
        def _():
            for step in (1, 2, 3):
                vec_z(step, z).wait_send()
                vec_z(step, (z + 4 - step) % 4).wait_recv()
            rz[z] = vc[...]
            o_vec[...] = jnp.sum(rz[...], 0)

        return carry

    lax.fori_loop(0, steps // 2 + 1, pair, 0)
    grads_came()


def backward_both(parts, cots, qlens, plens, gcls, par, own, land, kept):
    small = parts == 16
    cot_query, cot_passage = cots
    left, h_qkv, h_pq, h_pp, h_pre, h_slope, h_ffn = kept[:7]
    total, features = left.shape[2:]
    wide = own[2].shape[1]
    shape = jax.ShapeDtypeStruct
    anywhere = pl.BlockSpec(memory_space=pl.ANY)
    vmem = pl.BlockSpec(memory_space=pltpu.VMEM)
    smem = pl.BlockSpec(memory_space=pltpu.SMEM)
    dma = pltpu.SemaphoreType.DMA
    grads = [shape(cot_query.shape, FULL), shape(cot_passage.shape, FULL)]
    if small:
        out_shape = [
            shape((BLOCK, 3 * features), FULL),
            shape((BLOCK, features), FULL),
            shape((BLOCK, wide), FULL),
            shape((4, BLOCK, features), FULL),
            shape((16, features), FULL),
            *grads,
            shape((2, 9, total, CHUNK), LOW),
            shape((2, 9, total, CHUNK), LOW),
        ]
        out_specs = [vmem] * 5 + [anywhere] * 4
    else:
        out_shape = [
            shape((2, 16, features), FULL),
            *grads,
            shape((2, total, 3 * features), LOW),
            shape((2, total, features), LOW),
            shape((2, total, wide), LOW),
            shape((2, total, features), LOW),
        ]
        out_specs = [vmem] + [anywhere] * 6
    scratch = [pltpu.VMEM(item.shape, item.dtype) for item in own]
    scratch += [
        pltpu.VMEM(h_qkv.shape[1:], LOW),
        pltpu.VMEM(h_pq.shape[1:], LOW),
        pltpu.VMEM(h_pp.shape[1:], LOW),
        pltpu.VMEM((total, features), FULL),
        pltpu.VMEM((total, wide), LOW),
        pltpu.VMEM((total // QLEN, QLEN, features), LOW),
        pltpu.VMEM((total, features), FULL),
        pltpu.VMEM((total, features), LOW),
        pltpu.VMEM((2, total, 256), FULL),
        pltpu.VMEM((total, features), FULL),
        pltpu.VMEM((total, features), LOW),
        dma((4,)),
        dma((6,)),
        dma((2,)),
        dma((2,)),
        dma((2,)),
        dma((2,)),
        dma((9,)),
    ]
    if small:
        steps = 2 * COUNT
        vector = pltpu.VMEM((16, features), FULL)
        scratch += [
            pltpu.VMEM((2, 16, features), FULL),
            pltpu.VMEM((7, 4, 2, 2, BLOCK, 2 * total), LOW),
            pltpu.VMEM((9, 2 * total, CHUNK), LOW),
            pltpu.VMEM((2, 2, total, features), LOW),
            pltpu.VMEM((HELD, 4, 2, BLOCK, CHUNK), LOW),
            pltpu.VMEM((RING, 4, 2, BLOCK, CHUNK), LOW),
            pltpu.VMEM((4, 4, BLOCK, CHUNK), LOW),
            pltpu.VMEM((HELD, 4, BLOCK, CHUNK), LOW),
            pltpu.VMEM((4, 4, BLOCK, CHUNK), LOW),
            pltpu.VMEM((2, COUNT, 4, BLOCK, CHUNK), LOW),
            pltpu.VMEM((4, BLOCK, CHUNK), FULL),
            *[vector] * 6,
            pltpu.VMEM((4, 16, features), FULL),
            dma((steps,)),
            dma((steps,)),
            dma((steps,)),
            dma((steps,)),
            dma((steps, 4)),
            dma((2, COUNT, 4)),
            dma((3,)),
            dma((3,)),
            dma((4,)),
            dma((4,)),
            dma((2, 9)),
            dma((2, 9)),
            dma((2, 2)),
            dma((9, 2)),
            dma((2, 2)),
        ]
    return pl.pallas_call(
        functools.partial(backward_kernel, parts),
        out_shape=out_shape,
        in_specs=[anywhere, anywhere, smem, smem, vmem, vmem] + [anywhere] * 16,
        out_specs=out_specs,
        scratch_shapes=scratch,
        compiler_params=pltpu.CompilerParams(
            collective_id=1, has_side_effects=True, vmem_limit_bytes=60 * 1024 * 1024
        ),
    )(cot_query, cot_passage, qlens, plens, gcls, par, *own, *land, *kept)


def finish_kernel(parts, *refs):
    big, vec, loss = refs[:8], refs[8], refs[9]
    outs, small, total = refs[10:18], refs[18:26], refs[26]
    held, come, go = refs[27:35], refs[35], refs[36]
    copies = []
    for src, mid, dst in zip(big, held, outs):
        spot = len(copies)
        copies.append(
            (
                pltpu.make_async_copy(src, mid, come.at[spot]),
                pltpu.make_async_copy(mid, dst, go.at[spot]),
            )
        )
        copies[-1][0].start()
    me = lax.axis_index("batch")
    features = vec.shape[1]
    for at, count, out in zip((0, 2, 3, 4, 5, 9, 10, 11), (2, 1, 1, 1, 4, 1, 1, 1), small):
        size = count * features // parts
        every = parts // count
        block = vec[pl.ds(at + me // every, 1)]
        block = jnp.broadcast_to(block, (8, features))
        turned = pltpu.roll(block, (features - size * (me % every)) % features, 1)
        out[...] = turned[0:1, 0:size]
    total[...] = loss[0:1, 0:1]
    for came, left in copies:
        came.wait()
        left.start()
    for came, left in copies:
        left.wait()


def finish(parts, big, vec, loss):
    features = vec.shape[1]
    anywhere = pl.BlockSpec(memory_space=pl.ANY)
    vmem = pl.BlockSpec(memory_space=pltpu.VMEM)
    shape = jax.ShapeDtypeStruct
    return pl.pallas_call(
        functools.partial(finish_kernel, parts),
        out_shape=[shape(item.shape, item.dtype) for item in big]
        + [shape((1, count * features // parts), FULL) for count in (2, 1, 1, 1, 4, 1, 1, 1)]
        + [shape((1, 1), FULL)],
        in_specs=[anywhere] * 8 + [vmem] * 2,
        out_specs=[anywhere] * 8 + [vmem] * 9,
        scratch_shapes=[pltpu.VMEM(item.shape, item.dtype) for item in big]
        + [pltpu.SemaphoreType.DMA((8,)), pltpu.SemaphoreType.DMA((8,))],
    )(*big, vec, loss)


def per_device(
    parts,
    x_query,
    x_passage,
    len_query,
    len_passage,
    positive,
    cot_query,
    cot_passage,
    *weights,
):
    core = lax.axis_index("section")
    on_first = core == 0
    own_set = [member[0] for member in weights]
    own = [own_set[item] for item in (0, 2, 6, 8)]
    vectors = [weights[item] for item in (1, 3, 4, 5, 7, 9, 10, 11)]
    features = x_query.shape[2]
    half_q, half_p = x_query.shape[0] // 2, x_passage.shape[0] // 2
    *kept, par, l_qkv, l_o, l_in, l_out, hidden_q, hidden_p, land_a, grad_cls, loss = forward_both(
        parts,
        x_query,
        x_passage.reshape(-1, QLEN, features),
        len_query,
        len_passage,
        positive,
        vectors,
        own,
    )
    other = (l_qkv, l_o, l_in, l_out)
    if parts != 16:
        last = hidden_p.reshape(x_passage.shape)
        targets = lax.all_gather(positive, "batch", axis=0, tiled=True)
        own_q = hidden_q[:, 0]
        own_p = last[:, 0]
        last_q, last_p = (jnp.where(on_first, swap(item), item) for item in (own_q, own_p))
        cls_query = lax.all_gather(last_q, "batch", axis=0, tiled=True)
        cls_passage = lax.all_gather(last_p, "batch", axis=0, tiled=True)
        score_scale = 2.0 / math.sqrt(features)
        logits = (
            jnp.einsum("qd,pd->qp", cls_query, cls_passage, preferred_element_type=jnp.float32)
            * score_scale
        )
        term_values, grad_logits = contrast(logits, targets)
        loss_value = jnp.mean(term_values)
        mine = lax.axis_index("batch") * 2 + core
        own_logits = lax.dynamic_slice_in_dim(grad_logits, mine * half_q, half_q, 0)
        grad_cls_q = (
            jnp.einsum("qp,pd->qd", own_logits, cls_passage, preferred_element_type=jnp.float32)
            * score_scale
        )
        own_columns = lax.dynamic_slice_in_dim(grad_logits, mine * half_p, half_p, 1)
        grad_cls_p = (
            jnp.einsum("qp,qd->pd", own_columns, cls_query, preferred_element_type=jnp.float32)
            * score_scale
        )
        grad_cls = jnp.concatenate([grad_cls_q, grad_cls_p], 0)
        grad_cls = jnp.pad(grad_cls, ((0, 8 - grad_cls.shape[0]), (0, 0)))

    outs = backward_both(
        parts,
        (cot_query, cot_passage.reshape(-1, QLEN, features)),
        len_query,
        len_passage,
        grad_cls,
        par,
        own,
        other,
        kept + [land_a],
    )
    groups = ((0, 2), (2, 1), (3, 1), (4, 1), (5, 4), (9, 1), (10, 1), (11, 1))
    if parts == 16:
        d_qkv, d_o, d_in, d_out, d_vec, grad_q, grad_p = outs[:7]
        big = (hidden_q, hidden_p, grad_q, grad_p, d_qkv, d_o, d_in, d_out.reshape(-1, features))
        *final, loss = finish(parts, big, d_vec, loss)
        hidden_q, hidden_p, grad_q, grad_p, d_qkv, d_o, d_in, d_out = final[:8]
        small = [item[0] for item in final[8:]]
        loss_value = loss.reshape(())
    else:
        sums, grad_q, grad_p, g_pro, g_att, g_up, g_flo = outs
        left = kept[0]

        def total(pair):
            kept_one = jnp.where(on_first, pair[0], pair[1])
            both = kept_one + swap(jnp.where(on_first, pair[1], pair[0]))
            return lax.psum_scatter(both, "batch", scatter_dimension=0, tiled=True)

        def product(first, second):
            return jnp.einsum("rd,re->de", first, second, preferred_element_type=jnp.float32)

        d_qkv, d_o, d_in = (
            total([product(left[layer, spot], right[layer]) for layer in (0, 1)])
            for spot, right in ((6, g_pro), (5, g_att), (4, g_up))
        )
        d_out = total(
            [
                jnp.concatenate([product(left[layer, spot], g_flo[layer]) for spot in range(4)], 0)
                for layer in (0, 1)
            ]
        )
        small = [
            total([sums[layer, at : at + count].reshape(-1) for layer in (0, 1)])
            for at, count in groups
        ]
    hidden_q, hidden_p = hidden_q[None], hidden_p.reshape(x_passage.shape)[None]
    grad_q = grad_q[None]
    grad_p = grad_p.reshape(x_passage.shape)[None]
    d_b_qv, d_b_o, d_g_attn, d_c_attn, d_b_in, d_b_out, d_g_ffn, d_c_ffn = small
    outs = (
        d_qkv, d_b_qv, d_o, d_b_o, d_g_attn, d_c_attn, d_in, d_b_in, d_out, d_b_out, d_g_ffn,
        d_c_ffn,
    )
    return (hidden_q, hidden_p, grad_q, grad_p, loss_value) + tuple(item[None] for item in outs)


def solution(mesh):
    in_specs = (
        P("batch", None, None),
        P("batch", None, None),
        P("batch"),
        P("batch"),
        P("batch"),
        P("batch", None, None),
        P("batch", None, None),
        P("section", None, None),
        P("section", None),
        P("section", None, None),
        P("section", None),
        P("section", None),
        P("section", None),
        P("section", None, None),
        P("section", None),
        P("section", None, None),
        P("section", None),
        P("section", None),
        P("section", None),
    )
    out_specs = (
        P("section", "batch", None, None),
        P("section", "batch", None, None),
        P("section", "batch", None, None),
        P("section", "batch", None, None),
        P(),
        P("section", "batch", None),
        P("section", "batch"),
        P("section", "batch", None),
        P("section", "batch"),
        P("section", "batch"),
        P("section", "batch"),
        P("section", "batch", None),
        P("section", "batch"),
        P("section", "batch", None),
        P("section", "batch"),
        P("section", "batch"),
        P("section", "batch"),
    )
    return jax.shard_map(
        functools.partial(per_device, mesh.shape["batch"]), mesh=mesh, in_specs=in_specs, out_specs=out_specs, check_vma=False
    )
```

```python
import functools
import math

import jax
import jax.numpy as jnp
from jax import lax
from jax.experimental import pallas as pl
from jax.experimental.pallas import tpu as pltpu
from jax.sharding import PartitionSpec as P

HEADS = 12
QLEN = 32
PLEN = 256


norm_eps = 1e-05


def contrast(logits, targets):
    top_score = jnp.max(logits, -1, keepdims=True)
    log_total = top_score[:, 0] + jnp.log(jnp.sum(jnp.exp(logits - top_score), -1))
    chosen = targets[:, None] == jnp.arange(logits.shape[1])[None, :]
    term_values = log_total - jnp.sum(jnp.where(chosen, logits, 0.0), -1)
    grad_logits = (jnp.exp(logits - log_total[:, None]) - chosen.astype(jnp.float32)).astype(
        jnp.bfloat16
    )
    return (term_values, grad_logits)


MESH = pl.DeviceIdType.MESH
CHUNK = 384
COUNT = 12
BLOCK = 48


def swap(value):
    return lax.ppermute(value, "section", [(0, 1), (1, 0)])


LOW = jnp.bfloat16
FULL = jnp.float32
ROWS = 32
TILE = 768
LAST = (((1,), (1,)), ((), ()))
FIRST = (((0,), (0,)), ((), ()))


def dot(left, right):
    return jnp.dot(left, right, preferred_element_type=FULL)


def dot_last(left, right):
    return lax.dot_general(left, right, LAST, preferred_element_type=FULL)


def dot_first(left, right):
    return lax.dot_general(left, right, FIRST, preferred_element_type=FULL)


UNROLL = 4
PAIRS = 3


def over(count, body, unroll=1):
    def step(index, carry):
        body(index)
        return carry

    lax.fori_loop(0, count, step, 0, unroll=unroll)


def row_range(index):
    return pl.ds(pl.multiple_of(index * ROWS, ROWS), ROWS)


def lane_range(index, width):
    return pl.ds(pl.multiple_of(index * width, 128), width)


def moments(block):
    centred = block - jnp.mean(block, -1, keepdims=True)
    spread = jnp.mean(centred * centred, -1, keepdims=True)
    inverse = lax.rsqrt(spread + norm_eps)
    return centred * inverse, inverse


def gelu_pair(block):
    size = jnp.abs(block)
    t = 1.0 / (1.0 + (0.3275911 * math.sqrt(0.5)) * size)
    bell = jnp.exp(-0.5 * block * block)
    poly = 0.5 * 1.061405429
    for term in (-1.453152027, 1.421413741, -0.284496736, 0.254829592):
        poly = poly * t + 0.5 * term
    tail = poly * t * bell
    phi = jnp.where(block > 0, 1.0 - tail, tail)
    return block * phi, phi + block * bell * (1.0 / math.sqrt(2.0 * math.pi))


def head_lanes(rows, head):
    lane = lax.broadcasted_iota(jnp.int32, (rows, 128), 1)
    return (lane < 64) if head == 0 else (lane >= 64)


def query_mask(lens, start, count):
    rows = count * QLEN
    row = lax.broadcasted_iota(jnp.int32, (rows, rows), 0)
    column = lax.broadcasted_iota(jnp.int32, (rows, rows), 1)
    limit = jnp.zeros((rows, rows), jnp.int32)
    for item in range(count):
        limit = jnp.where(column // QLEN == item, item * QLEN + lens[start + item], limit)
    return (row // QLEN == column // QLEN) & (row < limit)


VMEM_LIMIT = 58 * 1024 * 1024


def remote(src, dst, send, recv, where):
    return pltpu.make_async_remote_copy(
        src_ref=src, dst_ref=dst, send_sem=send, recv_sem=recv,
        device_id=where, device_id_type=MESH,
    )


def greet(targets):
    barrier = pltpu.get_barrier_semaphore()
    for where in targets:
        pl.semaphore_signal(barrier, inc=1, device_id=where, device_id_type=MESH)
    pl.semaphore_wait(barrier, len(targets))


def forward_kernel(
    parts, x_query, x_passage, qlens, plens, positive,
    b_qv, b_o, g_attn, c_attn, b_in, b_out, g_ffn, c_ffn, wqkv, wo, win, wout,
    o_left, o_qkv, o_pq, o_pp, o_pre, o_slope, o_ffn, both_par,
    l_qkv, l_o, l_in, l_out, hid_q, hid_p, land_a, gcls, loss,
    tok, out, bqkv, bo, bin_, bout, qkv, pq, pp, mixed, pre, normed_full, normed, up, act,
    slope, ffn, rows8, rows48, packed, every, stack,
    load, save, xload, parsend, parrecv, wsend, wrecv, hsend, hrecv, hlocal, gsend, grecv, psend, precv, asend, arecv, bsend, brecv,
):
    core = lax.axis_index("section")
    me = lax.axis_index("batch")
    peer = {"section": 1 - core}
    features = wo.shape[0]
    count_q, count_p = x_query.shape[0] // 2, x_passage.shape[0] // 2
    split = count_q * QLEN
    tall = count_p
    total = (count_q + count_p) * QLEN
    own = (wqkv, wo, win, wout)
    land = (l_qkv, l_o, l_in, l_out)
    buffers = (bqkv, bo, bin_, bout)

    gets = [
        pltpu.make_async_copy(
            x_query.at[pl.ds(core * count_q, count_q)], tok.at[0, pl.ds(0, count_q)], xload.at[0]
        ),
        pltpu.make_async_copy(
            x_passage.at[pl.ds(core * tall, tall)], tok.at[0, pl.ds(count_q, tall)], xload.at[1]
        ),
    ]
    for copy in gets:
        copy.start()

    def local(source, spot):
        return pltpu.make_async_copy(source[spot], buffers[spot], load.at[spot])

    def stash(spot):
        return pltpu.make_async_copy(buffers[spot], land[spot], load.at[4 + spot])

    def give_first(spot):
        return remote(own[spot], buffers[spot], wsend.at[spot], wrecv.at[spot], peer)

    def give_block(spot, block):
        part = pl.ds(block * features, features)
        cut = (slice(None), part) if spot == 2 else (part,)
        return remote(
            own[spot].at[cut], buffers[spot].at[cut],
            bsend.at[spot - 2, block], brecv.at[spot - 2, block], peer,
        )

    def weight_block(spot, block):
        @pl.when(core == 1)
        def _():
            give_block(spot, block).wait_recv()
            if block == 3:
                stash(spot).start()

    def give_second(spot):
        return remote(own[spot], land[spot], wsend.at[spot], wrecv.at[spot], peer)

    others = [peer]
    if parts == 16:
        for step in range(1, parts):
            others.append({"batch": (me + step) % parts})

    @pl.when(core == 0)
    def _():
        for spot in range(4):
            local(own, spot).start()

    vectors = (b_qv, b_o, g_attn, c_attn, b_in, b_out, g_ffn, c_ffn)
    spot = 0
    for ref in vectors:
        for item in range(ref.shape[1] // features):
            both_par[core, spot : spot + 1] = ref[:, item * features : (item + 1) * features]
            spot += 1
    both_par[core, spot:16] = jnp.zeros((16 - spot, features), FULL)
    greet(others)
    give_par = remote(both_par.at[core], both_par.at[core], parsend, parrecv, peer)
    give_par.start()

    @pl.when(core == 0)
    def _():
        for spot in range(2):
            give_first(spot).start()
        for spot in (2, 3):
            for block in range(4):
                give_block(spot, block).start()

    @pl.when(core == 1)
    def _():
        for spot in range(4):
            give_second(spot).start()

    def weight_first(spot):
        @pl.when(core == 0)
        def _():
            local(own, spot).wait()

        @pl.when(core == 1)
        def _():
            if spot < 2:
                give_first(spot).wait_recv()
                stash(spot).start()

        if spot >= 2:
            weight_block(spot, 0)

    def fetch_second(spot):
        @pl.when(core == 0)
        def _():
            give_second(spot).wait_recv()
            local(land, spot).start()

        @pl.when(core == 1)
        def _():
            stash(spot).wait()
            local(own, spot).start()

    def weight(layer, spot):
        if layer == 0:
            weight_first(spot)
        else:
            local(own, spot).wait()

    saves = {}

    def keep(name, layer, source, target):
        saves[name, layer] = pltpu.make_async_copy(
            source, target, save.at[len(saves)]
        )
        saves[name, layer].start()

    places = {"act0": 0, "act1": 1, "act2": 2, "act3": 3, "normed": 4, "mixed": 5, "tok": 6}

    def left_give(layer, spot, source):
        return remote(
            source, land_a.at[layer, spot], asend.at[layer, spot], arecv.at[layer, spot], peer
        )

    def keep_left(name, layer, source):
        keep(name, layer, source, o_left.at[layer, places[name]])
        if layer == 1:
            left_give(1, places[name], source).start()

    def free(name, layer):
        if layer == 1:
            saves[name, 0].wait()

    for copy in gets:
        copy.wait()

    remote(both_par.at[core], both_par.at[1 - core], parsend, parrecv, peer).wait_recv()
    blocks = [(0, split, query_mask(qlens, core * count_q, count_q), pq, 0)]
    for item in range(count_p * QLEN // PLEN):
        row = lax.broadcasted_iota(jnp.int32, (PLEN, PLEN), 0)
        limit = plens[core * (count_p * QLEN // PLEN) + item]
        blocks.append((split + item * PLEN, PLEN, row < limit, pp, item * HEADS))

    for layer in (0, 1):
        base_row = 0
        par = both_par.at[layer]
        x = tok.at[layer].reshape(total, features)
        keep_left("tok", layer, x)
        weight(layer, 0)
        free("qkv", layer)

        def project(tile):
            lanes = lane_range(tile, features)
            bias = jnp.where(tile == 0, par[base_row : base_row + 1], 0.0)
            bias = jnp.where(tile == 2, par[base_row + 1 : base_row + 2], bias)
            qkv[:, lanes] = (dot(x[...], bqkv[:, lanes]) + bias).astype(LOW)

        over(3, project)
        keep("qkv", layer, qkv, o_qkv.at[layer])
        if layer == 1:
            fetch_second(3)
            for name, spot in places.items():
                saves[name, 0].wait()
                left_give(0, spot, o_left.at[0, spot]).start()
        for name in ("pq", "pp"):
            free(name, layer)

        def attend(index):
            tasks = []
            for step in range(6):
                for lo, rows, mask, probs, base in blocks:
                    tasks.append((index * 6 + step, lo, rows, mask, probs, base))

            def part(task, offset):
                hp, lo, rows = task[:3]
                return qkv[pl.ds(lo, rows), pl.ds(pl.multiple_of(offset + hp * 128, 128), 128)]

            scores = []
            for task in tasks:
                queries, keys = part(task, 0) * LOW(0.125), part(task, features)
                for head in (0, 1):
                    masked = jnp.where(head_lanes(task[2], head), keys, LOW(0))
                    scores.append(dot_last(masked, queries))
            lows = []
            for spot, value in enumerate(scores):
                hp, lo, rows, mask, probs, base = tasks[spot // 2]
                value = jnp.where(mask, value, -1000000000.0)
                weights = jnp.exp(value - jnp.max(value, 0, keepdims=True))
                inverse = 1.0 / jnp.sum(weights, 0, keepdims=True)
                low = (weights * inverse).astype(LOW)
                probs[base + 2 * hp + spot % 2] = low
                lows.append(low)
            for spot, task in enumerate(tasks):
                hp, lo, rows = task[:3]
                values = part(task, 2 * features).T
                outs = [
                    dot(values[64 * head : 64 * head + 64], lows[2 * spot + head])
                    for head in (0, 1)
                ]
                both = jnp.concatenate(outs, 0).astype(LOW).T
                mixed[pl.ds(lo, rows), pl.ds(pl.multiple_of(hp * 128, 128), 128)] = both

        attend(0)
        keep("pq", layer, pq, o_pq.at[layer])
        keep("pp", layer, pp, o_pp.at[layer])
        keep_left("mixed", layer, mixed)
        weight(layer, 1)
        free("pre", layer)
        pre[...] = (
            dot(mixed[...], bo[...]) + x[...].astype(FULL) + par[base_row + 2 : base_row + 3]
        )
        keep("pre", layer, pre, o_pre.at[layer])
        if layer == 0:
            fetch_second(0)
            fetch_second(1)

        def norm_one(index):
            rows = row_range(index)
            block = moments(pre[rows])[0] * par[base_row + 3 : base_row + 4]
            block = block + par[base_row + 4 : base_row + 5]
            normed_full[rows] = block
            normed[rows] = block.astype(LOW)

        over(total // ROWS, norm_one, 12)
        keep_left("normed", layer, normed)
        weight(layer, 2)
        free("slope", layer)
        step_width = 256
        tiles = win.shape[1] // step_width

        def expand(tile):
            lanes = lane_range(tile, step_width)
            bias_lanes = lane_range(tile % 3, step_width)
            up[tile % 2] = (
                dot(normed[...], bin_[:, lanes])
                + par[pl.ds(base_row + 5 + tile // 3, 1), bias_lanes]
            )

        def bend(tile):
            lanes = lane_range(tile, step_width)
            for index in range(total // ROWS):
                rows = pl.ds(index * ROWS, ROWS)
                value, steep = gelu_pair(up[tile % 2, rows])
                act[rows, lanes] = value.astype(LOW)
                slope[rows, lanes] = steep.astype(LOW)

        expand(0)

        def grow(index):
            if layer == 0 and (index + 1) % 3 == 0:
                weight_block(2, (index + 1) // 3)
            expand(index + 1)
            bend(index)

        for index in range(tiles - 1):
            grow(index)
        bend(tiles - 1)
        for item in range(4):
            lanes = pl.ds(item * features, features)
            keep_left("act%d" % item, layer, act.at[:, lanes])
        keep("slope", layer, slope, o_slope.at[layer])
        weight(layer, 3)
        free("ffn", layer)
        ends = normed_full[...] + par[base_row + 9 : base_row + 10]
        if layer == 0:
            most = 3 * features
            for block in (1, 2):
                weight_block(3, block)
            ffn[...] = dot(act[:, :most], bout[:most]) + ends
            weight_block(3, 3)
            ffn[...] += dot(act[:, most:], bout[most:])
        else:
            ffn[...] = dot(act[...], bout[...]) + ends
        keep("ffn", layer, ffn, o_ffn.at[layer])
        if layer == 0:
            fetch_second(2)
        target = tok.at[1] if layer == 0 else out
        flat = target.reshape(total, features)

        def norm_two(index):
            rows = row_range(index)
            block = moments(ffn[rows])[0] * par[base_row + 10 : base_row + 11]
            flat[rows] = (block + par[base_row + 11 : base_row + 12]).astype(LOW)

        over(total // ROWS, norm_two, 12)
        sides = (
            (target.at[pl.ds(0, count_q)], hid_q.at[pl.ds(core * count_q, count_q)]),
            (target.at[pl.ds(count_q, tall)], hid_p.at[pl.ds(core * tall, tall)]),
        )

        @pl.when(core == layer)
        def _():
            for spot, (src, dst) in enumerate(sides):
                pltpu.make_async_copy(src, dst, hlocal.at[spot]).start()

        @pl.when(core != layer)
        def _():
            for spot, (src, dst) in enumerate(sides):
                remote(src, dst, hsend.at[spot], hrecv.at[spot], peer).start()

    if parts == 16:
        lead = [item * QLEN for item in range(count_q)] + [split]
        rows8[...] = jnp.zeros_like(rows8)
        for spot, row in enumerate(lead):
            rows8[spot : spot + 1] = flat[pl.ds(row, 16)].astype(FULL)[0:1]
        for tile in range(6):
            rows48[8 * tile : 8 * tile + 8] = rows8[:, 128 * tile : 128 * tile + 128]
        for item in range(count_q):
            value = positive[core * count_q + item].astype(FULL)
            rows48[8 * item + 5 : 8 * item + 6] = jnp.full((1, 128), value)
        packed[...] = rows48[...].astype(LOW)

        def share(step, slot):
            return remote(
                packed, every.at[core, slot], gsend.at[step], grecv.at[slot],
                {"batch": (me + step) % parts},
            )

        for step in range(1, parts):
            share(step, me).start()
        every[core, me] = packed[...]
        for step in range(1, parts):
            share(step, (me + parts - step) % parts).wait_recv()
        pass_on = remote(every.at[core], every.at[core], psend, precv, peer)
        pass_on.start()
        remote(every.at[core], every.at[1 - core], psend, precv, peer).wait_recv()
        pass_on.wait_send()
        for step in range(1, parts):
            share(step, me).wait_send()

        wide = 2 * parts * 8
        grid = every[...].astype(FULL).reshape(2 * parts, 48, 128)
        inner = lax.broadcasted_iota(jnp.int32, (2 * parts, 8, 128), 1)
        goal = jnp.zeros((2 * parts, 8, 128), FULL)
        for tile in range(6):
            block = grid[:, 8 * tile : 8 * tile + 8]
            stack[:, 128 * tile : 128 * tile + 128] = block.reshape(wide, 128).astype(LOW)
            if tile < count_q:
                found = jnp.sum(jnp.where(inner == 5, block, 0.0), 1, keepdims=True)
                goal = jnp.where(inner == tile, found, goal)
        row = lax.broadcasted_iota(jnp.int32, (wide, wide), 0)
        column = lax.broadcasted_iota(jnp.int32, (wide, wide), 1)
        scale = 2.0 / math.sqrt(features)
        logits = dot_last(stack[...], stack[...]) * scale
        device = column // 8
        passage = (device % parts) * 2 + device // parts
        is_passage = column % 8 == count_q
        is_query = row % 8 < count_q
        kept = jnp.where(is_passage, logits, -1e30)
        top = jnp.max(kept, -1, keepdims=True)
        log_total = top + jnp.log(jnp.sum(jnp.exp(kept - top), -1, keepdims=True))
        chosen = is_passage & (passage.astype(FULL) == goal.reshape(wide, 128)[:, 0:1])
        picked = jnp.sum(jnp.where(chosen, logits, 0.0), -1, keepdims=True)
        terms = jnp.where(is_query[:, 0:1], log_total - picked, 0.0)
        count = count_q * 2 * parts
        loss[...] = jnp.full((8, 128), jnp.sum(terms) / count)
        grads = jnp.exp(kept - log_total) - chosen.astype(FULL)
        grads = jnp.where(is_query & is_passage, grads, 0.0)
        up[0, 0:wide, 0:wide] = grads + grads.T
        mine = pl.multiple_of((core * parts + me) * 8, 8)
        picked_rows = up[0, pl.ds(mine, 8), 0:wide]
        gcls[...] = dot(picked_rows.astype(LOW), stack[...]) * scale

    for spot, (src, dst) in enumerate(sides):
        pltpu.make_async_copy(src, dst, hlocal.at[spot]).wait()
    theirs = (
        hid_q.at[pl.ds((1 - core) * count_q, count_q)],
        hid_p.at[pl.ds((1 - core) * tall, tall)],
    )
    for spot, (src, dst) in enumerate(zip((item[0] for item in sides), theirs)):
        remote(src, dst, hsend.at[spot], hrecv.at[spot], peer).wait()
    @pl.when(core == 0)
    def _():
        for spot in range(2):
            give_first(spot).wait_send()
        for spot in (2, 3):
            for block in range(4):
                give_block(spot, block).wait_send()

    @pl.when(core == 1)
    def _():
        for spot in range(4):
            give_second(spot).wait_send()

    give_par.wait_send()
    for (name, layer), copy in saves.items():
        if layer == 1:
            copy.wait()
    for layer in (0, 1):
        for spot in range(7):
            left_give(layer, spot, o_left.at[layer, spot]).wait()


def forward_both(parts, x_query, x_passage, qlens, plens, positive, vectors, own):
    queries, features = x_query.shape[0], x_query.shape[2]
    passages = x_passage.shape[0]
    total = (queries + passages) // 2 * QLEN
    wide = own[2].shape[1]
    split = queries // 2 * QLEN
    heads_p = HEADS * (passages // 2 * QLEN // PLEN)
    kept = [
        ((7, total, features), LOW),
        ((total, 3 * features), LOW),
        ((HEADS, split, split), LOW),
        ((heads_p, PLEN, PLEN), LOW),
        ((total, features), FULL),
        ((total, wide), LOW),
        ((total, features), FULL),
        ((16, features), FULL),
    ]
    shape = jax.ShapeDtypeStruct
    anywhere = pl.BlockSpec(memory_space=pl.ANY)
    vmem = pl.BlockSpec(memory_space=pltpu.VMEM)
    smem = pl.BlockSpec(memory_space=pltpu.SMEM)
    dma = pltpu.SemaphoreType.DMA
    scratch = [
        pltpu.VMEM((2, total // QLEN, QLEN, features), LOW),
        pltpu.VMEM((total // QLEN, QLEN, features), LOW),
    ]
    scratch += [pltpu.VMEM(item.shape, item.dtype) for item in own]
    scratch += [pltpu.VMEM(size, kind) for size, kind in kept[1:4]]
    scratch += [
        pltpu.VMEM((total, features), LOW),
        pltpu.VMEM((total, features), FULL),
        pltpu.VMEM((total, features), FULL),
        pltpu.VMEM((total, features), LOW),
        pltpu.VMEM((2, total, 256), FULL),
        pltpu.VMEM((total, wide), LOW),
        pltpu.VMEM((total, wide), LOW),
        pltpu.VMEM((total, features), FULL),
    ]
    scratch += [
        pltpu.VMEM((8, features), FULL),
        pltpu.VMEM((48, 128), FULL),
        pltpu.VMEM((48, 128), LOW),
        pltpu.VMEM((2, 16, 48, 128), LOW),
        pltpu.VMEM((256, features), LOW),
        dma((8,)),
        dma((26,)),
        dma((2,)),
        dma,
        dma,
        dma((4,)),
        dma((4,)),
        dma((2,)),
        dma((2,)),
        dma((2,)),
        dma((16,)),
        dma((16,)),
        dma,
        dma,
        dma((2, 7)),
        dma((2, 7)),
        dma((2, 4)),
        dma((2, 4)),
    ]
    return pl.pallas_call(
        functools.partial(forward_kernel, parts),
        out_shape=[shape((2,) + size, kind) for size, kind in kept]
        + [shape(item.shape, item.dtype) for item in own]
        + [
            shape(x_query.shape, LOW),
            shape(x_passage.shape, LOW),
            shape((2, 7, total, features), LOW),
            shape((8, features), FULL),
            shape((8, 128), FULL),
        ],
        in_specs=[anywhere, anywhere, smem, smem, smem] + [vmem] * 8 + [anywhere] * 4,
        out_specs=[anywhere] * 7 + [vmem] + [anywhere] * 7 + [vmem] * 2,
        scratch_shapes=scratch,
        compiler_params=pltpu.CompilerParams(
            collective_id=2, has_side_effects=True, vmem_limit_bytes=VMEM_LIMIT
        ),
    )(x_query, x_passage, qlens, plens, positive, *vectors, *own)


def add_rows(block):
    return jnp.sum(block.reshape(block.shape[0] // 8, 8, block.shape[1]), 0)


def norm_back(source, grad_of, gain, total, store):
    features = source.shape[1]
    zero = jnp.zeros((8, features), FULL)

    def step(index, carry):
        rows = row_range(index)
        grad = grad_of(index)
        unit, inverse = moments(source[rows])
        scaled = grad * gain
        back = inverse * (
            scaled
            - jnp.mean(scaled, -1, keepdims=True)
            - unit * jnp.mean(scaled * unit, -1, keepdims=True)
        )
        store(rows, back)
        return (
            carry[0] + add_rows(grad * unit),
            carry[1] + add_rows(grad),
            carry[2] + add_rows(back),
        )

    sums = lax.fori_loop(0, total // ROWS, step, (zero, zero, zero), unroll=UNROLL)
    return [jnp.sum(item, 0, keepdims=True) for item in sums]


LAGS = (2, 4, 6)
RING = 12
HELD = 8


def left_index(ch):
    return (
        jnp.minimum(ch, 4) + (ch >= 8).astype(jnp.int32) + (ch >= 9).astype(jnp.int32)
    )


def right_index(ch):
    return jnp.maximum(ch - 3, 0)


def backward_kernel(parts, *refs):
    small = parts == 16
    refs = list(refs)

    def take(count):
        front = refs[:count]
        del refs[:count]
        return front

    cot_query, cot_passage, qlens, plens, gcls, par = take(6)
    own, land = take(4), take(4)
    left, h_qkv, h_pq, h_pp, h_pre, h_slope, h_ffn, land_a = take(8)
    if small:
        o_qkv, o_o, o_in, o_out, o_vec, o_gq, o_gp, land_g, own_g = take(9)
    else:
        vpar, o_gq, o_gp, f_pro, f_att, f_up, f_flo = take(7)
    buffers = take(4)
    bqkv, bo, bin_, bout = buffers
    qkv, pq, pp, source, slope, gsrc = take(6)
    attn_full, attn, steep, flow_full, flow = take(5)
    gmixed = flow
    grow = flow_full.reshape(flow.shape[0] // QLEN, QLEN, flow.shape[1])
    wload, fetch, cload, hsend, hrecv, hlocal, ksem = take(7)
    if small:
        vpar, a_buf, g_buf, stage, s1, r1, s2, r2, s3, r3, hold = take(11)
        va, ra, vb, rb, vc, rc, rz = take(7)
        s1s, r1s, s2s, r2s, s3s, r3s, vsend, vrecv, zsend, zrecv = take(10)
        gs, gr, sl, gl, el = take(5)

    core = lax.axis_index("section")
    me = lax.axis_index("batch")
    peer = {"section": 1 - core}
    features = gcls.shape[1]
    total = flow.shape[0]
    split = pq.shape[1]
    count_q, tall = cot_query.shape[0] // 2, cot_passage.shape[0] // 2
    heads_p = pp.shape[0]
    blocks_p = PLEN // QLEN

    def weight_copy(spot, source_set):
        return pltpu.make_async_copy(source_set[spot], buffers[spot], wload.at[spot])

    def weight_start(layer, spot):
        @pl.when(core == layer)
        def _():
            weight_copy(spot, own).start()

        @pl.when(core != layer)
        def _():
            weight_copy(spot, land).start()

    def weight_wait(spot):
        weight_copy(spot, own).wait()

    saved = ((h_ffn, source), (h_slope, slope), (h_pre, source), (h_qkv, qkv), (h_pq, pq), (h_pp, pp))

    def saved_copy(layer, spot):
        src, dst = saved[spot]
        return pltpu.make_async_copy(src.at[layer], dst, fetch.at[spot])

    cots = [
        pltpu.make_async_copy(
            cot_query.at[pl.ds(core * count_q, count_q)], gsrc.at[pl.ds(0, count_q)], cload.at[0]
        ),
        pltpu.make_async_copy(
            cot_passage.at[pl.ds(core * tall, tall)], gsrc.at[pl.ds(count_q, tall)], cload.at[1]
        ),
    ]
    def early_copy(spot, side):
        src = (left, land_a)[side]
        if spot < 2:
            dst, sem = stage.at[spot, side], sl.at[spot, side]
        else:
            lanes = pl.ds((spot - 2) * features, features)
            dst, sem = bin_.at[pl.ds(side * total, total), lanes], el.at[spot - 2, side]
        return pltpu.make_async_copy(src.at[1, spot], dst, sem)

    if small:
        x, y, z = me % 2, (me // 2) % 2, me // 4
        px, py = me + 1 - 2 * x, me + 2 - 4 * y
        targets = [{"batch": px}, {"batch": py}, peer]
        for step in (1, 2, 3):
            other = ((z + step) % 4) * 4 + me % 4
            targets += [{"section": sec, "batch": other} for sec in (0, 1)]
        barrier = pltpu.get_barrier_semaphore()
        for where in targets:
            pl.semaphore_signal(barrier, inc=1, device_id=where, device_id_type=MESH)
        for spot in range(4):
            for side in (0, 1):
                early_copy(spot, side).start()
    saved_copy(1, 0).start()
    for copy in cots:
        copy.start()
    if not small:
        saved_copy(1, 1).start()
    weight_start(1, 3)

    widths = ((flow, 1), (slope, 4), (attn, 1), (qkv, 3))

    def pieces_of(slot):
        base = (0, 1, 5, 6)[slot]
        ref, count = widths[slot]
        return [(base + item, ref, ref.shape[1] // 2, item) for item in range(count)]

    def own_piece(layer, piece):
        spot, ref, width, item = piece
        lanes = pl.ds(pl.multiple_of(core * width + item * CHUNK, 128), CHUNK)
        return pltpu.make_async_copy(ref.at[:, lanes], own_g.at[layer, spot], ksem.at[spot])

    def peer_piece(layer, piece):
        spot, ref, width, item = piece
        lanes = pl.ds(pl.multiple_of((1 - core) * width + item * CHUNK, 128), CHUNK)
        return remote(
            ref.at[:, lanes], land_g.at[layer, spot], gs.at[layer, spot], gr.at[layer, spot], peer
        )

    def whole_piece(layer, slot):
        ref = widths[slot][0]
        target = (f_flo, f_up, f_att, f_pro)[slot]
        return pltpu.make_async_copy(ref, target.at[layer], ksem.at[slot])

    def direct():
        spot, ref, width, item = pieces_of(0)[0]
        lanes = pl.ds(pl.multiple_of((1 - core) * width, 128), CHUNK)
        return remote(
            ref.at[:, lanes], g_buf.at[0, pl.ds(total, total)], gs.at[1, 0], gr.at[1, 0], peer
        )

    def give(layer, slot):
        if small and slot == 0:

            @pl.when(layer == 1)
            def _():
                direct().start()
                lanes = pl.ds(pl.multiple_of(core * CHUNK, 128), CHUNK)
                g_buf[0, pl.ds(0, total)] = flow[:, lanes]

            @pl.when(layer == 0)
            def _():
                piece = pieces_of(0)[0]
                peer_piece(layer, piece).start()
                own_piece(layer, piece).start()

        elif small:
            for piece in pieces_of(slot):
                peer_piece(layer, piece).start()
                own_piece(layer, piece).start()
        else:
            whole_piece(layer, slot).start()

    def given(layer, slot):
        if small:
            for piece in pieces_of(slot):
                peer_piece(layer, piece).wait_send()
                if slot > 0:
                    own_piece(layer, piece).wait()
                else:

                    @pl.when(layer == 0)
                    def _():
                        own_piece(layer, piece).wait()
        else:
            whole_piece(layer, slot).wait()

    def slot_zero(layer):
        saved_copy(layer, 0).wait()
        gains = par.at[layer]
        last = layer == 1

        def grad_of(index):
            block = gsrc[index].astype(FULL)
            beyond = jnp.maximum(index - count_q, 0)
            item = beyond // blocks_p
            query_limit = qlens[core * count_q + jnp.minimum(index, count_q - 1)]
            passage_limit = (
                plens[core * (tall // blocks_p) + item] - (beyond % blocks_p) * QLEN
            )
            limit = jnp.where(index < count_q, query_limit, passage_limit)
            limit = jnp.where(last, limit, QLEN)
            lead = jnp.where(index < count_q, index, count_q + item)
            starts = (index < count_q) | (beyond % blocks_p == 0)
            row = lax.broadcasted_iota(jnp.int32, block.shape, 0)
            block = jnp.where(row < limit, block, 0.0)
            extra = gcls[pl.ds(lead, 1)] * jnp.where(starts & last, 1.0, 0.0)
            return block + jnp.where(row == 0, extra, 0.0)

        def store(rows, back):
            flow_full[rows] = back
            flow[rows] = back.astype(LOW)

        gain, shift, bias = norm_back(source, grad_of, gains[10:11], total, store)
        sums = vpar.at[layer]
        sums[10:11], sums[11:12], sums[9:10] = gain, shift, bias
        give(layer, 0)
        saved_copy(layer, 2).start()

    width = 256
    tiles = bout.shape[0] // width

    def slot_one(layer):
        saved_copy(layer, 1).wait()
        weight_wait(3)
        sums = vpar.at[layer]

        def shrink(tile):
            rows_of = pl.ds(pl.multiple_of(tile * width, width), width)
            steep[tile % 2] = dot_last(flow[...], bout[rows_of])

        def bend(tile):
            lanes = lane_range(tile, width)
            acc = jnp.zeros((8, width), FULL)
            for index in range(total // ROWS):
                rows = pl.ds(index * ROWS, ROWS)
                low = (steep[tile % 2, rows] * slope[rows, lanes].astype(FULL)).astype(LOW)
                slope[rows, lanes] = low
                acc = acc + add_rows(low.astype(FULL))
            sums[pl.ds(5 + tile // 3, 1), lane_range(tile % 3, width)] = jnp.sum(
                acc, 0, keepdims=True
            )

        shrink(0)

        def both(index):
            shrink(index + 1)
            bend(index)

        over(tiles - 1, both)
        bend(tiles - 1)
        give(layer, 1)

        @pl.when(layer == 1)
        def _():
            weight_start(0, 3)

    def slot_two(layer):
        weight_wait(2)
        flow_full[...] += dot_last(slope[...], bin_[...])
        saved_copy(layer, 2).wait()
        gains, sums = par.at[layer], vpar.at[layer]

        def store(rows, back):
            attn_full[rows] = back
            attn[rows] = back.astype(LOW)

        gain, shift, bias = norm_back(
            source, lambda index: flow_full[row_range(index)], gains[3:4], total, store
        )
        sums[3:4], sums[4:5], sums[2:3] = gain, shift, bias
        give(layer, 2)
        weight_wait(1)
        gmixed[...] = dot_last(attn[...], bo[...]).astype(LOW)

        @pl.when(layer == 1)
        def _():
            weight_start(0, 2)
            weight_start(0, 1)
            saved_copy(0, 0).start()
            saved_copy(0, 1).start()

    blocks = [(0, split, pq, 0)]
    for item in range(heads_p // HEADS):
        blocks.append((split + item * PLEN, PLEN, pp, item * HEADS))

    def attend(index):
        tasks = []
        for step in range(PAIRS):
            for block in blocks:
                tasks.append((index * PAIRS + step,) + block)

        def spot_of(task, offset):
            hp, lo, rows = task[:3]
            return (pl.ds(lo, rows), pl.ds(pl.multiple_of(offset + hp * 128, 128), 128))

        grads = []
        for task in tasks:
            values, back = qkv[spot_of(task, 2 * features)], gmixed[spot_of(task, 0)]
            for head in (0, 1):
                masked = jnp.where(head_lanes(task[2], head), values, LOW(0))
                grads.append(dot_last(masked, back))
        lows = []
        for spot, grad_probs in enumerate(grads):
            hp, lo, rows, probs, base = tasks[spot // 2]
            full = probs[base + 2 * hp + spot % 2].astype(FULL)
            inner = jnp.sum(grad_probs * full, 0, keepdims=True)
            lows.append((full * (grad_probs - inner)).astype(LOW))
        for spot, task in enumerate(tasks):
            hp, lo, rows, probs, base = task
            queries, keys = qkv[spot_of(task, 0)], qkv[spot_of(task, features)]
            back = gmixed[spot_of(task, 0)]
            turned = keys.T
            outs = []
            for head in (0, 1):
                grad_scores = lows[2 * spot + head]
                outs.append(
                    (
                        dot(turned[64 * head : 64 * head + 64], grad_scores) * 0.125,
                        dot(grad_scores, queries) * 0.125,
                        dot(probs[base + 2 * hp + head], back),
                    )
                )
            first = head_lanes(rows, 0)
            both = jnp.concatenate([outs[0][0], outs[1][0]], 0)
            qkv[spot_of(task, 0)] = both.astype(LOW).T
            for item in (1, 2):
                both = jnp.where(first, outs[0][item], outs[1][item])
                qkv[spot_of(task, item * features)] = both.astype(LOW)

    def grads_here(spot):
        lo, count, target = ((0, count_q, o_gq), (count_q, tall, o_gp))[spot]
        return pltpu.make_async_copy(
            grow.at[pl.ds(lo, count)], target.at[pl.ds(core * count, count)], hlocal.at[spot]
        )

    def grads_there(spot):
        lo, count, target = ((0, count_q, o_gq), (count_q, tall, o_gp))[spot]
        return remote(
            grow.at[pl.ds(lo, count)],
            target.at[pl.ds(core * count, count)],
            hsend.at[spot],
            hrecv.at[spot],
            peer,
        )

    def slot_three(layer):
        for spot in (3, 4, 5):
            saved_copy(layer, spot).wait()
        over(features // 128 // PAIRS, attend)
        give(layer, 3)
        sums = vpar.at[layer]

        def bias_sums(index, carry):
            rows = row_range(index)
            return (
                carry[0] + add_rows(qkv[rows, pl.ds(0, features)].astype(FULL)),
                carry[1] + add_rows(qkv[rows, pl.ds(2 * features, features)].astype(FULL)),
            )

        zero = jnp.zeros((8, features), FULL)
        found = lax.fori_loop(0, total // ROWS, bias_sums, (zero, zero), unroll=2)
        sums[0:1] = jnp.sum(found[0], 0, keepdims=True)
        sums[1:2] = jnp.sum(found[1], 0, keepdims=True)
        sums[12:16] = jnp.zeros((4, features), FULL)
        weight_wait(0)
        rows_all = attn_full[...] + dot_last(qkv[...], bqkv[...])
        flow_full[...] = rows_all
        gsrc[...] = rows_all.astype(LOW).reshape(gsrc.shape)

        @pl.when(core == layer)
        def _():
            for spot in (0, 1):
                grads_here(spot).start()

        @pl.when(core != layer)
        def _():
            for spot in (0, 1):
                grads_there(spot).start()

        @pl.when(layer == 1)
        def _():
            weight_start(0, 0)

    def grads_given(layer):
        @pl.when(core == layer)
        def _():
            for spot in (0, 1):
                grads_here(spot).wait()

        @pl.when(core != layer)
        def _():
            for spot in (0, 1):
                grads_there(spot).wait_send()

    slots = (slot_zero, slot_one, slot_two, slot_three)

    def reload(layer, slot):
        @pl.when(layer == 1)
        def _():
            if slot == 3:
                for spot in (3, 4, 5):
                    saved_copy(0, spot).start()

    def rest_of_loads():
        for spot in (2, 1, 0):
            weight_start(1, spot)
        for spot in (3, 4, 5):
            saved_copy(1, spot).start()

    def grads_came():
        lands = ((o_gq, count_q), (o_gp, tall))
        for spot, (target, count) in enumerate(lands):
            there = target.at[pl.ds((1 - core) * count, count)]
            remote(there, there, hsend.at[spot], hrecv.at[spot], peer).wait_recv()

    if not small:
        greet([peer])
        rest_of_loads()
        for copy in cots:
            copy.wait()
        for layer in (1, 0):
            for slot in range(4):
                slots[slot](layer)
                given(layer, slot)
                reload(layer, slot)
            grads_given(layer)
        grads_came()
        return

    def stage_copy(number, side):
        layer, spot = 1 - number // 7, number % 7
        src = left if side == 0 else land_a
        return pltpu.make_async_copy(
            src.at[layer, spot], stage.at[number % 2, side], sl.at[number % 2, side]
        )

    def stage_start(number):
        stage_copy(number, 0).start()
        stage_copy(number, 1).start()

    def rotate(spot, view):
        for side in (0, 1):
            lanes = pl.ds(side * total, total)
            for half in range(features // CHUNK):
                block = view(side, half * CHUNK).T
                if spot > 3:
                    a_buf[spot, pl.ds(2 * half, 2), :, :, :, lanes] = block.reshape(
                        2, 2, 2, BLOCK, total
                    )
                else:
                    shaped = block.reshape(2, 4, BLOCK, total)
                    for item in range(4):
                        a_buf[item, spot, half, :, :, lanes] = shaped[:, item]

    def turn(number, spot):
        for side in (0, 1):
            stage_copy(number, side).wait()
        rotate(spot, lambda side, at: stage[number % 2, side, :, pl.ds(at, CHUNK)])

        @pl.when(number + 2 < 14)
        def _():
            stage_start(number + 2)

    for spot in range(4):
        for side in (0, 1):
            early_copy(spot, side).wait()
        if spot < 2:
            rotate(spot, lambda side, at: stage[spot, side, :, pl.ds(at, CHUNK)])
            stage_start(spot + 4)
        else:
            rotate(
                spot,
                lambda side, at: bin_[
                    pl.ds(side * total, total), pl.ds((spot - 2) * features + at, CHUNK)
                ],
            )
    pl.semaphore_wait(barrier, len(targets))

    def right_copy(layer, spot, side):
        src = own_g if side == 0 else land_g
        return pltpu.make_async_copy(
            src.at[layer, spot], g_buf.at[spot, pl.ds(side * total, total)], gl.at[spot, side]
        )

    def right_start(k):
        ch = k % COUNT
        layer = 1 - k // COUNT

        @pl.when((k > 0) & (k < 2 * COUNT) & ((ch == 0) | (ch >= 4)))
        def _():
            spot = right_index(ch)
            right_copy(layer, spot, 0).start()
            remote(
                own_g.at[layer, spot], land_g.at[layer, spot],
                gs.at[layer, spot], gr.at[layer, spot], peer,
            ).wait_recv()
            right_copy(layer, spot, 1).start()

    def first(k, par_):
        return remote(
            s1.at[k % HELD], r1.at[k % RING], s1s.at[k], r1s.at[k],
            {"batch": px if par_ == 0 else py},
        )

    def second(k, par_):
        return remote(
            s2.at[k % 4], r2.at[k % HELD], s2s.at[k], r2s.at[k],
            {"batch": py if par_ == 0 else px},
        )

    def third(k, step):
        layer = 1 - k // COUNT
        zt = (z + step) % 4
        return remote(
            s3.at[k % 4, zt], r3.at[core, k % COUNT, z], s3s.at[k, step],
            r3s.at[core, k % COUNT, z], {"section": layer, "batch": zt * 4 + me % 4},
        )

    def third_in(k, step, src_core):
        zs = (z + 4 - step) % 4
        return remote(
            s3.at[k % 4, zs], r3.at[src_core, k % COUNT, zs], s3s.at[k, step],
            r3s.at[src_core, k % COUNT, zs], peer,
        )

    def product(k, block, rows):
        return dot(block.reshape(rows, 2 * total), g_buf[right_index(k % COUNT)])

    def left_of(k):
        return a_buf.at[left_index(k % COUNT)]

    def ready(k, par_):
        ch = k % COUNT

        @pl.when((k > 0) & ((ch == 0) | (ch >= 4)))
        def _():
            for side in (0, 1):
                right_copy(0, right_index(ch), side).wait()

        base = (k // COUNT) * 7
        if par_ == 0:

            @pl.when(k == 0)
            def _():
                direct().wait_recv()

            @pl.when(k == COUNT)
            def _():
                for spot in range(4):
                    turn(base + spot, spot)

            for spot, at in ((4, 4), (5, 8)):

                @pl.when(ch == at)
                def _():
                    turn(base + spot, spot)
        else:

            @pl.when(ch == 9)
            def _():
                turn(base + 6, 6)

    def part_one(k, par_):
        ready(k, par_)
        ref = left_of(k)
        block = ref[:, :, 1 - x] if par_ == 0 else ref[:, 1 - y]
        s1[k % HELD] = product(k, block, 8 * BLOCK).astype(LOW).reshape(4, 2, BLOCK, CHUNK)
        first(k, par_).start()

    def part_two(k, par_):
        ref = left_of(k)
        block = ref[:, 1 - y, x] if par_ == 0 else ref[:, y, 1 - x]
        hold[...] = product(k, block, 4 * BLOCK).reshape(4, BLOCK, CHUNK)
        first(k, par_).wait()
        came = r1[k % RING, :, 1 - y] if par_ == 0 else r1[k % RING, :, 1 - x]
        s2[k % 4] = (hold[...] + came.astype(FULL)).astype(LOW)
        second(k, par_).start()

    def part_three(k, par_):
        layer = 1 - k // COUNT
        ref = left_of(k)
        came = r1[k % RING, :, y] if par_ == 0 else r1[k % RING, :, x]
        hold[...] = product(k, ref[:, y, x], 4 * BLOCK).reshape(
            4, BLOCK, CHUNK
        ) + came.astype(FULL)
        second(k, par_).wait()
        value = hold[...] + r2[k % HELD].astype(FULL)
        s3[k % 4] = value.astype(LOW)
        for step in (1, 2, 3):
            third(k, step).start()

        @pl.when(core != layer)
        def _():
            third(k, 0).start()

        @pl.when(core == layer)
        def _():
            r3[core, k % COUNT, z] = s3[k % 4, z]

    def part_four(k, par_):
        layer = 1 - k // COUNT
        ch = k % COUNT
        for step in (1, 2, 3):
            third(k, step).wait_send()

        @pl.when(core != layer)
        def _():
            third(k, 0).wait_send()

        @pl.when(core == layer)
        def _():
            for step in (1, 2, 3):
                for src_core in (0, 1):
                    third_in(k, step, src_core).wait_recv()
            third_in(k, 0, 1 - core).wait_recv()
            for src_core in (0, 1):
                value = jnp.sum(r3[src_core, ch].astype(FULL), 0)

                @pl.when(ch < 4)
                def _():
                    o_out[ch, :, pl.ds(src_core * CHUNK, CHUNK)] = value

                @pl.when((ch >= 4) & (ch < 8))
                def _():
                    start = pl.multiple_of((ch - 4) * CHUNK + src_core * 4 * CHUNK, 128)
                    o_in[:, pl.ds(start, CHUNK)] = value

                @pl.when(ch == 8)
                def _():
                    o_o[:, pl.ds(src_core * CHUNK, CHUNK)] = value

                @pl.when(ch >= 9)
                def _():
                    start = pl.multiple_of((ch - 9) * CHUNK + src_core * 3 * CHUNK, 128)
                    o_qkv[:, pl.ds(start, CHUNK)] = value

    vec_cross = remote(vpar.at[1 - core], ra, vsend.at[0], vrecv.at[0], peer)
    vec_x = remote(va, rb, vsend.at[1], vrecv.at[1], {"batch": px})
    vec_y = remote(vb, rc, vsend.at[2], vrecv.at[2], {"batch": py})

    def vec_z(step, slot):
        return remote(
            vc, rz.at[slot], zsend.at[step], zrecv.at[slot],
            {"batch": ((z + step) % 4) * 4 + me % 4},
        )

    steps = 2 * COUNT + LAGS[2]

    starts = ((-1, 3), (0, 4), (1, 5), (2, 6))

    def pair(turn_index, carry):
        kk = turn_index - 1
        layer = (kk < 3).astype(jnp.int32)

        for slot, (one, two) in enumerate(starts):

            @pl.when((kk == one + 1) | (kk == two + 1))
            def _():
                done = (kk == one + 1).astype(jnp.int32)
                given(done, slot)
                reload(done, slot)
                if slot == 3:
                    grads_given(done)

        @pl.when(kk == -1)
        def _():
            saved_copy(1, 1).start()
            rest_of_loads()
            for copy in cots:
                copy.wait()

        for par_ in (0, 1):
            right_start(2 * kk + 2 + par_)

        stages = (part_two, part_three, part_four)

        def advance(item):
            lag, part = LAGS[item], stages[item]
            for par_ in (0, 1):
                k = 2 * kk + par_

                @pl.when((k >= lag) & (k < 2 * COUNT + lag))
                def _():
                    part(k - lag, par_)

        advance(0)
        advance(1)

        @pl.when((kk == starts[0][0]) | (kk == starts[0][1]))
        def _():
            slots[0](layer)

        for par_ in (0, 1):
            k = 2 * kk + 2 + par_

            @pl.when(k < 2 * COUNT)
            def _():
                part_one(k, par_)

        advance(2)

        for slot, (one, two) in enumerate(starts):
            if slot > 0:

                @pl.when((kk == one) | (kk == two))
                def _():
                    slots[slot](layer)

        @pl.when(kk == 7)
        def _():
            vec_cross.start()

        @pl.when(kk == 8)
        def _():
            vec_cross.wait()
            va[...] = vpar[core] + ra[...]
            vec_x.start()

        @pl.when(kk == 9)
        def _():
            vec_x.wait()
            vb[...] = va[...] + rb[...]
            vec_y.start()

        @pl.when(kk == 10)
        def _():
            vec_y.wait()
            vc[...] = vb[...] + rc[...]
            for step in (1, 2, 3):
                vec_z(step, z).start()

        @pl.when(kk == 12)
        def _():
            for step in (1, 2, 3):
                vec_z(step, z).wait_send()
                vec_z(step, (z + 4 - step) % 4).wait_recv()
            rz[z] = vc[...]
            o_vec[...] = jnp.sum(rz[...], 0)

        return carry

    lax.fori_loop(0, steps // 2 + 1, pair, 0)
    grads_came()


def backward_both(parts, cots, qlens, plens, gcls, par, own, land, kept):
    small = parts == 16
    cot_query, cot_passage = cots
    left, h_qkv, h_pq, h_pp, h_pre, h_slope, h_ffn = kept[:7]
    total, features = left.shape[2:]
    wide = own[2].shape[1]
    shape = jax.ShapeDtypeStruct
    anywhere = pl.BlockSpec(memory_space=pl.ANY)
    vmem = pl.BlockSpec(memory_space=pltpu.VMEM)
    smem = pl.BlockSpec(memory_space=pltpu.SMEM)
    dma = pltpu.SemaphoreType.DMA
    grads = [shape(cot_query.shape, FULL), shape(cot_passage.shape, FULL)]
    if small:
        out_shape = [
            shape((BLOCK, 3 * features), FULL),
            shape((BLOCK, features), FULL),
            shape((BLOCK, wide), FULL),
            shape((4, BLOCK, features), FULL),
            shape((16, features), FULL),
            *grads,
            shape((2, 9, total, CHUNK), LOW),
            shape((2, 9, total, CHUNK), LOW),
        ]
        out_specs = [vmem] * 5 + [anywhere] * 4
    else:
        out_shape = [
            shape((2, 16, features), FULL),
            *grads,
            shape((2, total, 3 * features), LOW),
            shape((2, total, features), LOW),
            shape((2, total, wide), LOW),
            shape((2, total, features), LOW),
        ]
        out_specs = [vmem] + [anywhere] * 6
    scratch = [pltpu.VMEM(item.shape, item.dtype) for item in own]
    scratch += [
        pltpu.VMEM(h_qkv.shape[1:], LOW),
        pltpu.VMEM(h_pq.shape[1:], LOW),
        pltpu.VMEM(h_pp.shape[1:], LOW),
        pltpu.VMEM((total, features), FULL),
        pltpu.VMEM((total, wide), LOW),
        pltpu.VMEM((total // QLEN, QLEN, features), LOW),
        pltpu.VMEM((total, features), FULL),
        pltpu.VMEM((total, features), LOW),
        pltpu.VMEM((2, total, 256), FULL),
        pltpu.VMEM((total, features), FULL),
        pltpu.VMEM((total, features), LOW),
        dma((4,)),
        dma((6,)),
        dma((2,)),
        dma((2,)),
        dma((2,)),
        dma((2,)),
        dma((9,)),
    ]
    if small:
        steps = 2 * COUNT
        vector = pltpu.VMEM((16, features), FULL)
        scratch += [
            pltpu.VMEM((2, 16, features), FULL),
            pltpu.VMEM((7, 4, 2, 2, BLOCK, 2 * total), LOW),
            pltpu.VMEM((9, 2 * total, CHUNK), LOW),
            pltpu.VMEM((2, 2, total, features), LOW),
            pltpu.VMEM((HELD, 4, 2, BLOCK, CHUNK), LOW),
            pltpu.VMEM((RING, 4, 2, BLOCK, CHUNK), LOW),
            pltpu.VMEM((4, 4, BLOCK, CHUNK), LOW),
            pltpu.VMEM((HELD, 4, BLOCK, CHUNK), LOW),
            pltpu.VMEM((4, 4, BLOCK, CHUNK), LOW),
            pltpu.VMEM((2, COUNT, 4, BLOCK, CHUNK), LOW),
            pltpu.VMEM((4, BLOCK, CHUNK), FULL),
            *[vector] * 6,
            pltpu.VMEM((4, 16, features), FULL),
            dma((steps,)),
            dma((steps,)),
            dma((steps,)),
            dma((steps,)),
            dma((steps, 4)),
            dma((2, COUNT, 4)),
            dma((3,)),
            dma((3,)),
            dma((4,)),
            dma((4,)),
            dma((2, 9)),
            dma((2, 9)),
            dma((2, 2)),
            dma((9, 2)),
            dma((2, 2)),
        ]
    return pl.pallas_call(
        functools.partial(backward_kernel, parts),
        out_shape=out_shape,
        in_specs=[anywhere, anywhere, smem, smem, vmem, vmem] + [anywhere] * 16,
        out_specs=out_specs,
        scratch_shapes=scratch,
        compiler_params=pltpu.CompilerParams(
            collective_id=1, has_side_effects=True, vmem_limit_bytes=60 * 1024 * 1024
        ),
    )(cot_query, cot_passage, qlens, plens, gcls, par, *own, *land, *kept)


def finish_kernel(parts, *refs):
    big, vec, loss = refs[:8], refs[8], refs[9]
    outs, small, total = refs[10:18], refs[18:26], refs[26]
    held, come, go = refs[27:35], refs[35], refs[36]
    copies = []
    for src, mid, dst in zip(big, held, outs):
        spot = len(copies)
        copies.append(
            (
                pltpu.make_async_copy(src, mid, come.at[spot]),
                pltpu.make_async_copy(mid, dst, go.at[spot]),
            )
        )
        copies[-1][0].start()
    me = lax.axis_index("batch")
    features = vec.shape[1]
    for at, count, out in zip((0, 2, 3, 4, 5, 9, 10, 11), (2, 1, 1, 1, 4, 1, 1, 1), small):
        size = count * features // parts
        every = parts // count
        block = vec[pl.ds(at + me // every, 1)]
        block = jnp.broadcast_to(block, (8, features))
        turned = pltpu.roll(block, (features - size * (me % every)) % features, 1)
        out[...] = turned[0:1, 0:size]
    total[...] = loss[0:1, 0:1]
    for came, left in copies:
        came.wait()
        left.start()
    for came, left in copies:
        left.wait()


def finish(parts, big, vec, loss):
    features = vec.shape[1]
    anywhere = pl.BlockSpec(memory_space=pl.ANY)
    vmem = pl.BlockSpec(memory_space=pltpu.VMEM)
    shape = jax.ShapeDtypeStruct
    return pl.pallas_call(
        functools.partial(finish_kernel, parts),
        out_shape=[shape(item.shape, item.dtype) for item in big]
        + [shape((1, count * features // parts), FULL) for count in (2, 1, 1, 1, 4, 1, 1, 1)]
        + [shape((1, 1), FULL)],
        in_specs=[anywhere] * 8 + [vmem] * 2,
        out_specs=[anywhere] * 8 + [vmem] * 9,
        scratch_shapes=[pltpu.VMEM(item.shape, item.dtype) for item in big]
        + [pltpu.SemaphoreType.DMA((8,)), pltpu.SemaphoreType.DMA((8,))],
    )(*big, vec, loss)


def per_device(
    parts,
    x_query,
    x_passage,
    len_query,
    len_passage,
    positive,
    cot_query,
    cot_passage,
    *weights,
):
    core = lax.axis_index("section")
    on_first = core == 0
    own_set = [member[0] for member in weights]
    own = [own_set[item] for item in (0, 2, 6, 8)]
    vectors = [weights[item] for item in (1, 3, 4, 5, 7, 9, 10, 11)]
    features = x_query.shape[2]
    half_q, half_p = x_query.shape[0] // 2, x_passage.shape[0] // 2
    *kept, par, l_qkv, l_o, l_in, l_out, hidden_q, hidden_p, land_a, grad_cls, loss = forward_both(
        parts,
        x_query,
        x_passage.reshape(-1, QLEN, features),
        len_query,
        len_passage,
        positive,
        vectors,
        own,
    )
    other = (l_qkv, l_o, l_in, l_out)
    if parts != 16:
        last = hidden_p.reshape(x_passage.shape)
        targets = lax.all_gather(positive, "batch", axis=0, tiled=True)
        own_q = hidden_q[:, 0]
        own_p = last[:, 0]
        last_q, last_p = (jnp.where(on_first, swap(item), item) for item in (own_q, own_p))
        cls_query = lax.all_gather(last_q, "batch", axis=0, tiled=True)
        cls_passage = lax.all_gather(last_p, "batch", axis=0, tiled=True)
        score_scale = 2.0 / math.sqrt(features)
        logits = (
            jnp.einsum("qd,pd->qp", cls_query, cls_passage, preferred_element_type=jnp.float32)
            * score_scale
        )
        term_values, grad_logits = contrast(logits, targets)
        loss_value = jnp.mean(term_values)
        mine = lax.axis_index("batch") * 2 + core
        own_logits = lax.dynamic_slice_in_dim(grad_logits, mine * half_q, half_q, 0)
        grad_cls_q = (
            jnp.einsum("qp,pd->qd", own_logits, cls_passage, preferred_element_type=jnp.float32)
            * score_scale
        )
        own_columns = lax.dynamic_slice_in_dim(grad_logits, mine * half_p, half_p, 1)
        grad_cls_p = (
            jnp.einsum("qp,qd->pd", own_columns, cls_query, preferred_element_type=jnp.float32)
            * score_scale
        )
        grad_cls = jnp.concatenate([grad_cls_q, grad_cls_p], 0)
        grad_cls = jnp.pad(grad_cls, ((0, 8 - grad_cls.shape[0]), (0, 0)))

    outs = backward_both(
        parts,
        (cot_query, cot_passage.reshape(-1, QLEN, features)),
        len_query,
        len_passage,
        grad_cls,
        par,
        own,
        other,
        kept + [land_a],
    )
    groups = ((0, 2), (2, 1), (3, 1), (4, 1), (5, 4), (9, 1), (10, 1), (11, 1))
    if parts == 16:
        d_qkv, d_o, d_in, d_out, d_vec, grad_q, grad_p = outs[:7]
        big = (hidden_q, hidden_p, grad_q, grad_p, d_qkv, d_o, d_in, d_out.reshape(-1, features))
        *final, loss = finish(parts, big, d_vec, loss)
        hidden_q, hidden_p, grad_q, grad_p, d_qkv, d_o, d_in, d_out = final[:8]
        small = [item[0] for item in final[8:]]
        loss_value = loss.reshape(())
    else:
        sums, grad_q, grad_p, g_pro, g_att, g_up, g_flo = outs
        left = kept[0]

        def total(pair):
            kept_one = jnp.where(on_first, pair[0], pair[1])
            both = kept_one + swap(jnp.where(on_first, pair[1], pair[0]))
            return lax.psum_scatter(both, "batch", scatter_dimension=0, tiled=True)

        def product(first, second):
            return jnp.einsum("rd,re->de", first, second, preferred_element_type=jnp.float32)

        d_qkv, d_o, d_in = (
            total([product(left[layer, spot], right[layer]) for layer in (0, 1)])
            for spot, right in ((6, g_pro), (5, g_att), (4, g_up))
        )
        d_out = total(
            [
                jnp.concatenate([product(left[layer, spot], g_flo[layer]) for spot in range(4)], 0)
                for layer in (0, 1)
            ]
        )
        small = [
            total([sums[layer, at : at + count].reshape(-1) for layer in (0, 1)])
            for at, count in groups
        ]
    hidden_q, hidden_p = hidden_q[None], hidden_p.reshape(x_passage.shape)[None]
    grad_q = grad_q[None]
    grad_p = grad_p.reshape(x_passage.shape)[None]
    d_b_qv, d_b_o, d_g_attn, d_c_attn, d_b_in, d_b_out, d_g_ffn, d_c_ffn = small
    outs = (
        d_qkv, d_b_qv, d_o, d_b_o, d_g_attn, d_c_attn, d_in, d_b_in, d_out, d_b_out, d_g_ffn,
        d_c_ffn,
    )
    return (hidden_q, hidden_p, grad_q, grad_p, loss_value) + tuple(item[None] for item in outs)


def solution(mesh):
    in_specs = (
        P("batch", None, None),
        P("batch", None, None),
        P("batch"),
        P("batch"),
        P("batch"),
        P("batch", None, None),
        P("batch", None, None),
        P("section", None, None),
        P("section", None),
        P("section", None, None),
        P("section", None),
        P("section", None),
        P("section", None),
        P("section", None, None),
        P("section", None),
        P("section", None, None),
        P("section", None),
        P("section", None),
        P("section", None),
    )
    out_specs = (
        P("section", "batch", None, None),
        P("section", "batch", None, None),
        P("section", "batch", None, None),
        P("section", "batch", None, None),
        P(),
        P("section", "batch", None),
        P("section", "batch"),
        P("section", "batch", None),
        P("section", "batch"),
        P("section", "batch"),
        P("section", "batch"),
        P("section", "batch", None),
        P("section", "batch"),
        P("section", "batch", None),
        P("section", "batch"),
        P("section", "batch"),
        P("section", "batch"),
    )
    return jax.shard_map(
        functools.partial(per_device, mesh.shape["batch"]), mesh=mesh, in_specs=in_specs, out_specs=out_specs, check_vma=False
    )
```
